32 devices in a mesh: gx: 4 (over y, core), gy: 8 (over z, x).
Axes of the slice: x: 2, y: 2, z: 4, core: 2. Of those that a mesh axis runs over, the one named last changes fastest.
Arguments:
- hidden_in: bfloat16 [16384, 768], P(('gx', 'gy')), may hold values from -6 to 6
- route: int32 [16384, 1], P(('gx', 'gy')), may hold values from 0 to 7; in each aligned block of 512 rows (0 to 511, 512 to 1023, ...) at most 128 rows name the same one
- piece_ids: int32 [16384], P(('gx', 'gy')), may hold values from 0 to 1, as said below
- buckets: int32 [1023], replicated, may hold values from 0 to 31
- rel_table: bfloat16 [32, 12], replicated, may hold values from -4 to 4
- gain_attn: bfloat16 [2, 768], replicated, may hold values from 0.25 to 1.75
- gain_ffn: bfloat16 [2, 768], replicated, may hold values from 0.25 to 1.75
- w_query: bfloat16 [2, 768, 768], P(None, 'gx', 'gy'), may hold values from -0.21875 to 0.21875
- w_key: bfloat16 [2, 768, 768], P(None, 'gx', 'gy'), may hold values from -0.21875 to 0.21875
- w_value: bfloat16 [2, 768, 768], P(None, 'gx', 'gy'), may hold values from -0.21875 to 0.21875
- w_output: bfloat16 [2, 768, 768], P(None, 'gx', 'gy'), may hold values from -0.875 to 0.875
- w_router: bfloat16 [2, 768, 8], P(None, 'gx', 'gy'), may hold values from -0.15625 to 0.15625
- w_in: bfloat16 [2, 8, 768, 3072], P(None, 'gy', None, 'gx'), may hold values from -0.21875 to 0.21875
- w_out: bfloat16 [2, 8, 768, 3072], P(None, 'gy', None, 'gx'), may hold values from -1.5 to 1.5
- cotangent: bfloat16 [16384, 768], P(('gx', 'gy')), may hold values from -6 to 6
Outputs:
- hidden_out: float32 [16384, 768], P(('gx', 'gy'))
- grad_input: float32 [16384, 768], P(('gx', 'gy'))
- grad_rel_table: float32 [32, 12], replicated
- grad_gain_attn: float32 [2, 768], replicated
- grad_gain_ffn: float32 [2, 768], replicated
- grad_w_query: float32 [2, 768, 768], P(None, 'gx', 'gy')
- grad_w_key: float32 [2, 768, 768], P(None, 'gx', 'gy')
- grad_w_value: float32 [2, 768, 768], P(None, 'gx', 'gy')
- grad_w_output: float32 [2, 768, 768], P(None, 'gx', 'gy')
- grad_w_router: float32 [2, 768, 8], P(None, 'gx', 'gy')
- grad_w_in: float32 [2, 8, 768, 3072], P(None, 'gy', None, 'gx')
- grad_w_out: float32 [2, 8, 768, 3072], P(None, 'gy', None, 'gx')
The draws below stay inside these ranges and needn't reach their ends.
Inputs may be any that keep to these rules, and one draw needn't show every extreme that they name: `route`: within the rows of one device (aligned blocks of 512 tokens, one sequence), no expert is named by more than 128 tokens. `piece_ids`: each sequence is cut into windows of 512 tokens; window w of a sequence holds one picture piece of exactly 256 consecutive tokens with id w + 1, at an offset of 0 to 256 within it; all other tokens have id 0.
All inputs are finite; a program needn't handle non-finite values.
Results may differ from the reference program's by a relative error of at most 0.025.
Values may be sent and summed in bfloat16 or wider, within the bound.
A program may use at most 320 MiB of HBM per device.

```python
import math
import jax
import jax.numpy as jnp
import numpy as np
from jax import lax

D = 768
HEADS = 12
FF = 3072
NB = 32
LAYERS = 2
PIECE = 256
TOK_DEV = 512
EXPERTS = 8
TOKENS = 16384
CAP = 128


def draw_piece_ids(key, part):
    key = jax.random.fold_in(key, 11)
    windows = TOKENS // (2 * PIECE)
    offsets = jax.random.randint(key, (windows, 1), 0, PIECE + 1)
    positions = jnp.arange(2 * PIECE, dtype=jnp.int32)[None, :]
    inside = (positions >= offsets) & (positions < offsets + PIECE)
    window_id = (jnp.arange(windows, dtype=jnp.int32) % (TOK_DEV // (2 * PIECE)) + 1)[:, None]
    return jnp.where(inside, window_id, 0).reshape(TOKENS).astype(jnp.int32)


def set_ends(entries, own_key, smallest, largest):
    spot = [jax.random.randint(jax.random.fold_in(own_key, axis), (), 0, length) for axis, length in enumerate(entries.shape)]
    longest = entries.shape.index(max(entries.shape))
    next_to = spot[:longest] + [(spot[longest] + 1) % entries.shape[longest]] + spot[longest + 1:]
    return entries.at[tuple(spot)].set(smallest).at[tuple(next_to)].set(largest)


def block_levels(stream_key, shape, split, smallest, top_value):
    def one(dim, blocks):
        heights = jax.random.uniform(jax.random.fold_in(jax.random.fold_in(stream_key, 6), dim), (blocks,), jnp.float32, smallest / len(split), top_value / len(split))
        return jnp.repeat(jnp.exp(heights), shape[dim] // blocks).reshape((-1,) + (1,) * (len(shape) - dim - 1))

    factor_of = one(*split[0])
    for cut in split[1:]:
        factor_of = factor_of * one(*cut)
    return factor_of


def deal_out(key, own, number, rows, amount, top, bound, slope):
    sequence = jax.random.permutation(key, amount)
    heavy_load, ordinary = load_shares(amount, rows * top, bound, slope, True), load_shares(amount, rows * top, bound, slope, False)
    places = jnp.arange(amount)

    def named(lengths, rotation):
        used = int((lengths > 0).sum())
        fixed = max(1, used // 4)
        passed = fixed + (places - fixed + rotation * (used - fixed)) % max(1, amount - fixed)
        return jnp.zeros((amount,), jnp.int32).at[sequence[jnp.where(places < fixed, places, passed)]].set(jnp.asarray(lengths, jnp.int32))

    lengths = jnp.where(number % 4 == 0, named(heavy_load, number // 4), named(ordinary, number - number // 4 - 1))
    mixed = jax.random.permutation(jax.random.fold_in(own, 3), amount)
    source_of, receiver = mixed[0:amount // 2 * 2:2], mixed[1:amount // 2 * 2:2]
    slack = jnp.minimum(lengths[source_of] - 1, bound - lengths[receiver]) // 2
    slack = jnp.where((source_of == sequence[0]) | (receiver == sequence[0]) | (lengths[receiver] == 0), 0, jnp.maximum(slack, 0))
    passed = jax.random.randint(jax.random.fold_in(own, 4), (amount // 2,), 0, 1 << 20) % (slack + 1)
    lengths = lengths.at[source_of].add(-passed).at[receiver].add(passed)
    labels = jnp.searchsorted(jnp.cumsum(lengths), jnp.arange(rows * top), side="right").astype(jnp.int32)
    grid = labels.reshape(top, rows).T
    grid = grid[jax.random.permutation(jax.random.fold_in(own, 1), rows)]
    rotation = jax.random.randint(jax.random.fold_in(own, 2), (rows, 1), 0, top)
    return jnp.take_along_axis(grid, (jnp.arange(top)[None, :] + rotation) % top, axis=1)


def load_shares(number_of, total, limit, skew, full):
    portions = [(1 << 20) // math.isqrt(standing ** skew) + 1 for standing in range(1, number_of + 1)]
    largest = limit if full else min(limit, max(-(-total // number_of), total * portions[0] // sum(portions)))
    least = 1 if total - largest >= number_of - 1 else 0
    given, surplus = [largest] + [least] * (number_of - 1), total - largest - least * (number_of - 1)
    while surplus > 0:
        free = [i for i in range(1, number_of) if given[i] < largest] or [i for i in range(1, number_of) if given[i] < limit]
        whole, budget = sum([portions[i] for i in free]), surplus
        for i in free:
            addition = min(limit - given[i], max(1, budget * portions[i] // whole), surplus)
            given[i] = given[i] + addition
            surplus = surplus - addition
    return np.array(given)


def scatter_about(own_key, shape, deviation, most, pieces=(), kind=jnp.bfloat16):
    gain = block_levels(own_key, shape, pieces, -0.22, 0.18) if pieces else 1.0
    values = jax.random.normal(own_key, shape, jnp.float32) * deviation * gain
    return jnp.minimum(jnp.maximum(values, -most), most).astype(kind)


def setup_inputs(seed: int = 0) -> dict:
    splits = jax.random.split(jax.random.key(seed), 16)
    hidden_in = scatter_about(splits[0], (TOKENS, D), 1.0, 6.0, ((0, 32),))
    route_keys = jax.random.split(jax.random.fold_in(splits[1], 1), TOKENS // TOK_DEV)
    route_turns = jax.random.permutation(jax.random.fold_in(splits[1], 3), TOKENS // TOK_DEV)
    route = jax.vmap(lambda own, number: deal_out(jax.random.fold_in(splits[1], 2), own, number, TOK_DEV, EXPERTS, 1, CAP, 1))(route_keys, route_turns).reshape((TOKENS, 1))
    piece_ids = draw_piece_ids(jax.random.fold_in(splits[15], 71), 0)
    buckets = set_ends(jax.random.randint(splits[3], (2 * TOK_DEV - 1,), 0, NB), jax.random.fold_in(splits[3], 1), 0, NB - 1).astype(jnp.int32)
    rel_table = scatter_about(splits[4], (NB, HEADS), 1.0, 4.0)
    gain_attn = jnp.clip(1.0 + 0.15 * jax.random.normal(splits[5], (LAYERS, D), jnp.float32), 0.25, 1.75).astype(jnp.bfloat16)
    gain_ffn = jnp.clip(1.0 + 0.15 * jax.random.normal(splits[6], (LAYERS, D), jnp.float32), 0.25, 1.75).astype(jnp.bfloat16)
    w_query = scatter_about(splits[7], (LAYERS, D, D), D ** -0.5, 0.21875, ((1, 4), (2, 8)))
    w_key = scatter_about(splits[8], (LAYERS, D, D), D ** -0.5, 0.21875, ((1, 4), (2, 8)))
    w_value = scatter_about(splits[9], (LAYERS, D, D), D ** -0.5, 0.21875, ((1, 4), (2, 8)))
    w_output = scatter_about(splits[10], (LAYERS, D, D), (D // 16) ** -0.5, 0.875, ((1, 4), (2, 8)))
    w_router = scatter_about(splits[11], (LAYERS, D, EXPERTS), (D * 16 // 9) ** -0.5, 0.15625, ((1, 4), (2, 8)))
    w_in = scatter_about(splits[12], (LAYERS, EXPERTS, D, FF), D ** -0.5, 0.21875, ((1, 8), (3, 4)))
    w_out = scatter_about(splits[13], (LAYERS, EXPERTS, D, FF), (max(FF * 3 // (EXPERTS * EXPERTS * 8), 1)) ** -0.5, 1.5, ((1, 8), (3, 4)))
    cotangent = scatter_about(splits[14], (TOKENS, D), 1.0, 6.0, ((0, 32),))
    return dict(hidden_in=hidden_in, route=route, piece_ids=piece_ids, buckets=buckets, rel_table=rel_table, gain_attn=gain_attn, gain_ffn=gain_ffn, w_query=w_query, w_key=w_key, w_value=w_value, w_output=w_output, w_router=w_router, w_in=w_in, w_out=w_out, cotangent=cotangent)


eps_norm = 1e-06
highest = lax.Precision.HIGHEST

@jax.custom_vjp
def low(v):
    return lax.optimization_barrier(v.astype(jnp.bfloat16)).astype(jnp.float32)

@jax.custom_vjp
def low_back(v):
    return v

def low_keep(v):
    return (low(v), None)

def low_pass(kept, grad):
    return (grad,)

def back_keep(v):
    return (v, None)

def back_low(kept, grad):
    return (low(grad),)
low.defvjp(low_keep, low_pass)
low_back.defvjp(back_keep, back_low)

def rms_scale(hidden, gain_vec):
    return hidden * lax.rsqrt(lax.optimization_barrier(jnp.mean(hidden * hidden, axis=-1, keepdims=True)) + eps_norm) * gain_vec

def single_sequence_input(params, hidden, route_ids, piece_row, bucket_row):
    rel_table, gain_attn, gain_ffn, w_query, w_key, w_value, w_output, w_router, w_in, w_out = params
    seq_len, feat_width = hidden.shape
    num_heads = rel_table.shape[1]
    head_dim = feat_width // num_heads
    num_experts = w_router.shape[2]
    capacity = 2 * seq_len // num_experts
    attn_scale = head_dim ** (-0.5)
    places = jnp.arange(seq_len, dtype=jnp.int32)
    allowed = (places[None, :] <= places[:, None]) | (piece_row[:, None] == piece_row[None, :]) & (piece_row[:, None] > 0)
    offsets = places[:, None] - places[None, :] + (seq_len - 1)
    rel_bias = jnp.transpose(rel_table[bucket_row[offsets]], (2, 0, 1))
    expert_of = route_ids[:, 0]
    chosen = (expert_of[:, None] == jnp.arange(num_experts, dtype=jnp.int32)[None, :]).astype(jnp.int32)
    ranked = lax.optimization_barrier(jnp.sum((jnp.cumsum(chosen, axis=0) - 1) * chosen, axis=1))
    slot_of = ranked * num_experts + expert_of
    placing = (slot_of[:, None] == jnp.arange(capacity * num_experts, dtype=jnp.int32)[None, :]).astype(jnp.float32)
    chosen_f = chosen.astype(jnp.float32)
    for layer_idx in range(w_query.shape[0]):
        normed = low(rms_scale(hidden, gain_attn[layer_idx]))
        q_all = low(low_back(jnp.dot(normed, w_query[layer_idx], precision=highest))).reshape(seq_len, num_heads, head_dim)
        k_all = low(low_back(jnp.dot(normed, w_key[layer_idx], precision=highest))).reshape(seq_len, num_heads, head_dim)
        v_all = low(low_back(jnp.dot(normed, w_value[layer_idx], precision=highest))).reshape(seq_len, num_heads, head_dim)
        scores = low_back(jnp.einsum('qhd,khd->hqk', q_all, k_all, precision=highest) * attn_scale + rel_bias)
        scores = jnp.where(allowed[None], scores, -jnp.inf)
        attn_probs = low(jax.nn.softmax(scores, axis=-1))
        attended = low(low_back(jnp.einsum('hqk,khd->qhd', attn_probs, v_all, precision=highest).reshape(seq_len, feat_width)))
        middle = hidden + low_back(jnp.dot(attended, w_output[layer_idx], precision=highest))
        ffn_in = low(rms_scale(middle, gain_ffn[layer_idx]))
        logits = low_back(jnp.dot(ffn_in, w_router[layer_idx], precision=highest))
        gate_value = lax.optimization_barrier(jnp.sum(jax.nn.softmax(logits, axis=-1) * chosen_f, axis=1))
        sent_rows = jnp.dot(placing.T, low_back(ffn_in), precision=highest).reshape(capacity, num_experts, feat_width)
        pre_act = low_back(jnp.einsum('ced,edf->cef', sent_rows, w_in[layer_idx], precision=highest))
        activated = low(jax.nn.gelu(pre_act, approximate=True))
        made_rows = low(low_back(jnp.einsum('cef,edf->ced', activated, w_out[layer_idx], precision=highest)))
        combined = jnp.dot(placing, made_rows.reshape(capacity * num_experts, feat_width), precision=highest)
        hidden = middle + gate_value[:, None] * combined
    return hidden

def reference(hidden_in, route, piece_ids, buckets, rel_table, gain_attn, gain_ffn, w_query, w_key, w_value, w_output, w_router, w_in, w_out, cotangent):
    weights = tuple((group_member.astype(jnp.float32) for group_member in (rel_table, gain_attn, gain_ffn, w_query, w_key, w_value, w_output, w_router, w_in, w_out)))
    per_round = max(1, min(8, 4096 // TOK_DEV))
    rounds_all = TOKENS // (TOK_DEV * per_round)

    def one_round(params, hidden_blk, route_blk, piece_blk):

        def single(hidden_one, route_one, piece_one):
            return single_sequence_input(params, hidden_one, route_one, piece_one, buckets)
        return jax.vmap(single)(hidden_blk, route_blk, piece_blk)
    checked = jax.checkpoint(one_round)

    def forward(params, hidden_all):
        hidden_blocks = hidden_all.reshape(rounds_all, per_round, TOK_DEV, D)
        route_blocks = route.reshape(rounds_all, per_round, TOK_DEV, 1)
        piece_blocks = piece_ids.reshape(rounds_all, per_round, TOK_DEV)

        def apply_round(inputs):
            return checked(params, inputs[0], inputs[1], inputs[2])
        results = lax.map(apply_round, (hidden_blocks, route_blocks, piece_blocks))
        return results.reshape(TOKENS, D)
    hidden_out, pull_back = jax.vjp(forward, weights, hidden_in.astype(jnp.float32))
    grad_weights, d_input = pull_back(cotangent.astype(jnp.float32))
    return (hidden_out, d_input, grad_weights[0], grad_weights[1], grad_weights[2], grad_weights[3], grad_weights[4], grad_weights[5], grad_weights[6], grad_weights[7], grad_weights[8], grad_weights[9])
```

```python
from functools import partial

import jax
import jax.numpy as jnp
from jax import lax
from jax.experimental import pallas as pl
from jax.experimental.pallas import tpu as pltpu
from jax.sharding import PartitionSpec as P

eps_norm = 1e-06
highest = lax.Precision.HIGHEST
f32 = jnp.float32
bf16 = jnp.bfloat16
masked_out = -1e30
vmem_bytes = 56 * 1024 * 1024


def whole(shape):
    zeros = (0,) * len(shape)
    return pl.BlockSpec(shape, lambda *_: zeros, pipeline_mode=pl.Buffered(1))


def whole_of(arrays):
    return [whole(array.shape) for array in arrays]


def params():
    return pltpu.CompilerParams(vmem_limit_bytes=vmem_bytes)


def dot(lhs, rhs, lhs_dim=1, rhs_dim=0):
    return lax.dot_general(
        lhs, rhs, (((lhs_dim,), (rhs_dim,)), ((), ())), preferred_element_type=f32
    )


def rms_factor(hidden):
    return lax.rsqrt(jnp.mean(hidden * hidden, axis=-1, keepdims=True) + eps_norm)


def rms_pull(hidden, gain_row, d_normed):
    factor = rms_factor(hidden)
    scaled = gain_row * d_normed
    inner = jnp.mean(hidden * scaled, axis=-1, keepdims=True)
    d_hidden = factor * scaled - hidden * (factor * factor * factor * inner)
    d_gain = jnp.sum(d_normed * hidden * factor, axis=0, keepdims=True)
    return d_hidden, d_gain


def placing_rows(slot_row, slots):
    places = lax.broadcasted_iota(jnp.int32, (slots, slot_row.shape[1]), 0)
    return (places == slot_row).astype(f32).astype(bf16)


def placing_cols(slot_col, slots):
    places = lax.broadcasted_iota(jnp.int32, (slot_col.shape[0], slots), 1)
    return (places == slot_col).astype(f32).astype(bf16)


def bias_kernel(offsets_ref, piece_col_ref, piece_row_ref, bias_ref):
    seq_len = piece_col_ref.shape[0]
    row = jnp.broadcast_to(offsets_ref[0], (seq_len, 2 * seq_len))
    shifted = pltpu.roll(row, seq_len + 1, 1, stride=1, stride_axis=0)[:, :seq_len]
    key_pos = lax.broadcasted_iota(jnp.int32, (seq_len, seq_len), 0)
    query_pos = lax.broadcasted_iota(jnp.int32, (seq_len, seq_len), 1)
    piece_col = piece_col_ref[...]
    same = (piece_col == piece_row_ref[...]) & (piece_col > 0)
    allowed = (key_pos <= query_pos) | same
    bias_ref[0] = jnp.where(allowed, shifted, masked_out).astype(bf16)


def bias_of(offsets, piece_ids):
    heads, seq_len = offsets.shape[0], piece_ids.shape[0]
    return pl.pallas_call(
        bias_kernel,
        grid=(heads,),
        in_specs=[
            pl.BlockSpec((1, 1, 2 * seq_len), lambda h: (h, 0, 0)),
            whole((seq_len, 1)),
            whole((1, seq_len)),
        ],
        out_specs=pl.BlockSpec((1, seq_len, seq_len), lambda h: (h, 0, 0)),
        out_shape=jax.ShapeDtypeStruct((heads, seq_len, seq_len), bf16),
        compiler_params=params(),
        name="bias_table",
    )(offsets[:, None, :], piece_ids[:, None], piece_ids[None, :])


def half_masks(rows, width):
    lane = lax.broadcasted_iota(jnp.int32, (rows, width), 1)
    return lane < (width // 2)


def forward_kernel(
    head_dim,
    hidden_ref,
    gain_attn_ref,
    gain_ffn_ref,
    wq_ref,
    wk_ref,
    wv_ref,
    wo_ref,
    wr_ref,
    slot_row_ref,
    bias_ref,
    q_ref,
    k_ref,
    v_ref,
    att_ref,
    lse_ref,
    middle_ref,
    logits_ref,
    sent_ref,
):
    pair, pairs = pl.program_id(0), pl.num_programs(0)
    seq_len = hidden_ref.shape[0]
    width = 2 * head_dim
    step = min(256, seq_len)

    @pl.when(pair == 0)
    def _():
        hidden = hidden_ref[...].astype(f32)
        normed = (hidden * rms_factor(hidden) * gain_attn_ref[...]).astype(bf16)
        q_ref[...] = dot(normed, wq_ref[...]).astype(bf16)
        k_ref[...] = dot(normed, wk_ref[...]).astype(bf16)
        v_ref[...] = dot(normed, wv_ref[...]).astype(bf16)

    lanes = pl.ds(pl.multiple_of(pair * width, width), width)
    q2 = q_ref[:, lanes] * jnp.asarray(head_dim**-0.5, bf16)
    k2 = k_ref[:, lanes]
    v2t = v_ref[:, lanes].T
    first = half_masks(seq_len, width)
    for half in range(2):
        q_one = jnp.where(first if half == 0 else ~first, q2, jnp.zeros_like(q2))
        v_one = v2t[half * head_dim : (half + 1) * head_dim]
        for start in range(0, seq_len, step):
            cols = slice(start, start + step)
            scores = dot(k2, q_one[cols], 1, 1) + bias_ref[half, :, cols].astype(f32)
            top = jnp.max(scores, axis=0, keepdims=True)
            raised = jnp.exp(scores - top)
            total = jnp.sum(raised, axis=0, keepdims=True)
            probs = (raised * (1.0 / total)).astype(bf16)
            rows = pl.ds(pl.multiple_of(pair * width + half * head_dim, head_dim), head_dim)
            att_ref[rows, cols] = dot(v_one, probs).astype(bf16)
            lse_ref[0, half : half + 1, cols] = top + jnp.log(total)

    @pl.when(pair == pairs - 1)
    def _():
        middle = hidden_ref[...].astype(f32) + dot(att_ref[...].T, wo_ref[...])
        middle_ref[...] = middle
        ffn_in = (middle * rms_factor(middle) * gain_ffn_ref[...]).astype(bf16)
        logits_ref[...] = dot(ffn_in, wr_ref[...])
        placing = placing_rows(slot_row_ref[...], sent_ref.shape[0])
        sent_ref[...] = dot(placing, ffn_in).astype(bf16)


def attention_forward(hidden, gain_attn, gain_ffn, mats, slot_row, bias):
    seq_len, width = hidden.shape
    heads = bias.shape[0]
    head_dim = width // heads
    experts = mats[4].shape[1]
    slots = 2 * seq_len
    ins = (hidden, gain_attn, gain_ffn, *mats, slot_row)
    tall = jax.ShapeDtypeStruct((seq_len, width), bf16)
    outs = (
        tall,
        tall,
        tall,
        jax.ShapeDtypeStruct((width, seq_len), bf16),
        jax.ShapeDtypeStruct((heads // 2, 2, seq_len), f32),
        jax.ShapeDtypeStruct((seq_len, width), f32),
        jax.ShapeDtypeStruct((seq_len, experts), f32),
        jax.ShapeDtypeStruct((slots, width), bf16),
    )
    out_specs = whole_of(outs)
    out_specs[4] = pl.BlockSpec((1, 2, seq_len), lambda p: (p, 0, 0))
    return pl.pallas_call(
        partial(forward_kernel, head_dim),
        grid=(heads // 2,),
        in_specs=whole_of(ins) + [pl.BlockSpec((2, seq_len, seq_len), lambda p: (p, 0, 0))],
        out_specs=out_specs,
        out_shape=outs,
        compiler_params=params(),
        name="attention_forward",
    )(*ins, bias)


def diagonal_fold(values, seq_len):
    rows, wide = seq_len, 2 * seq_len
    folded = None
    tile = 128
    count = seq_len // tile
    for row_tile in range(count):
        piece = values[row_tile * tile : (row_tile + 1) * tile].astype(f32)
        before = (count - 1 - row_tile) * tile
        after = wide - seq_len - before
        parts = []
        if before:
            parts.append(jnp.zeros((tile, before), f32))
        parts.append(piece)
        if after:
            parts.append(jnp.zeros((tile, after), f32))
        padded = jnp.concatenate(parts, axis=1)
        folded = padded if folded is None else folded + padded
    rows = tile
    while rows > 1:
        rows //= 2
        folded = pltpu.roll(folded[:rows], rows, 1) + folded[rows:]
    return folded


def backward_kernel(
    head_dim,
    d_back_ref,
    slot_col_ref,
    d_logits_ref,
    grad_ref,
    middle_ref,
    hidden_ref,
    gain_attn_ref,
    gain_ffn_ref,
    wq_ref,
    wk_ref,
    wv_ref,
    wo_ref,
    wr_ref,
    q_ref,
    k_ref,
    v_ref,
    att_ref,
    bias_ref,
    lse_ref,
    grad_new_ref,
    gwq_ref,
    gwk_ref,
    gwv_ref,
    gwo_ref,
    gwr_ref,
    gga_ref,
    ggf_ref,
    offsets_ref,
    d_att_s,
    d_middle_s,
    dqt_s,
    dk_s,
    dv_s,
    probs_s,
    scores_s,
):
    pair, pairs = pl.program_id(0), pl.num_programs(0)
    seq_len = hidden_ref.shape[0]
    width = 2 * head_dim
    step = min(256, seq_len)
    scale = head_dim**-0.5

    @pl.when(pair == 0)
    def _():
        placing = placing_cols(slot_col_ref[...], d_back_ref.shape[0])
        d_logits = d_logits_ref[...]
        d_ffn = dot(placing, d_back_ref[...]) + dot(d_logits, wr_ref[...], 1, 1)
        middle = middle_ref[...]
        gain_row = gain_ffn_ref[...]
        ffn_in = (middle * rms_factor(middle) * gain_row).astype(bf16)
        gwr_ref[...] = dot(ffn_in, d_logits, 0, 0)
        d_middle, d_gain = rms_pull(middle, gain_row, d_ffn)
        ggf_ref[...] = d_gain
        d_middle = d_middle + grad_ref[...]
        d_middle_s[...] = d_middle
        d_low = d_middle.astype(bf16)
        gwo_ref[...] = dot(att_ref[...], d_low).astype(bf16)
        d_att_s[...] = dot(d_low, wo_ref[...], 1, 1).astype(bf16)

    lanes = pl.ds(pl.multiple_of(pair * width, width), width)
    q2 = q_ref[:, lanes] * jnp.asarray(scale, bf16)
    k2 = k_ref[:, lanes]
    v2 = v_ref[:, lanes]
    da2 = d_att_s[:, lanes]
    k2t = k2.T
    first = half_masks(seq_len, width)
    d_key = jnp.zeros((seq_len, width), f32)
    d_value = jnp.zeros((seq_len, width), f32)
    for half in range(2):
        mask = first if half == 0 else ~first
        q_one = jnp.where(mask, q2, jnp.zeros_like(q2))
        da_one = jnp.where(mask, da2, jnp.zeros_like(da2))
        k_one = k2t[half * head_dim : (half + 1) * head_dim]
        rows = pl.ds(pl.multiple_of(pair * width + half * head_dim, head_dim), head_dim)
        for start in range(0, seq_len, step):
            cols = slice(start, start + step)
            scores = dot(k2, q_one[cols], 1, 1) + bias_ref[half, :, cols].astype(f32)
            probs = jnp.exp(scores - lse_ref[0, half : half + 1, cols])
            d_probs = dot(v2, da_one[cols], 1, 1)
            inner = jnp.sum(probs * d_probs, axis=0, keepdims=True)
            d_scores = (probs * (d_probs - inner)).astype(bf16)
            probs_s[:, cols] = probs.astype(bf16)
            scores_s[:, cols] = d_scores
            dqt_s[rows, cols] = (dot(k_one, d_scores) * scale).astype(bf16)
        d_key = d_key + dot(scores_s[...], q_one)
        d_value = d_value + dot(probs_s[...], da_one)
        offsets_ref[0, half : half + 1, :] = diagonal_fold(scores_s[...], seq_len)
    dk_s[:, lanes] = d_key.astype(bf16)
    dv_s[:, lanes] = d_value.astype(bf16)

    @pl.when(pair == pairs - 1)
    def _():
        hidden = hidden_ref[...].astype(f32)
        gain_row = gain_attn_ref[...]
        normed_t = (hidden * rms_factor(hidden) * gain_row).astype(bf16).T
        d_query = dqt_s[...].T
        d_normed = dot(d_query, wq_ref[...], 1, 1)
        gwq_ref[...] = dot(normed_t, d_query).astype(bf16)
        d_normed = d_normed + dot(dk_s[...], wk_ref[...], 1, 1)
        gwk_ref[...] = dot(normed_t, dk_s[...]).astype(bf16)
        d_normed = d_normed + dot(dv_s[...], wv_ref[...], 1, 1)
        gwv_ref[...] = dot(normed_t, dv_s[...]).astype(bf16)
        d_hidden, d_gain = rms_pull(hidden, gain_row, d_normed)
        gga_ref[...] = d_gain
        grad_new_ref[...] = d_hidden + d_middle_s[...]


def attention_backward(
    d_back, slot_col, d_logits, grad_now, middle, hidden, gains, mats, q_k_v, attended, bias, lse
):
    seq_len, width = hidden.shape
    heads = bias.shape[0]
    head_dim = width // heads
    experts = mats[4].shape[1]
    ins = (
        d_back,
        slot_col,
        d_logits,
        grad_now,
        middle,
        hidden,
        *gains,
        *mats,
        *q_k_v,
        attended,
    )
    square = jax.ShapeDtypeStruct((width, width), bf16)
    row = jax.ShapeDtypeStruct((1, width), f32)
    outs = (
        jax.ShapeDtypeStruct((seq_len, width), f32),
        square,
        square,
        square,
        square,
        jax.ShapeDtypeStruct((width, experts), f32),
        row,
        row,
        jax.ShapeDtypeStruct((heads // 2, 2, 2 * seq_len), f32),
    )
    out_specs = whole_of(outs)
    out_specs[8] = pl.BlockSpec((1, 2, 2 * seq_len), lambda p: (p, 0, 0))
    return pl.pallas_call(
        partial(backward_kernel, head_dim),
        grid=(heads // 2,),
        in_specs=whole_of(ins)
        + [
            pl.BlockSpec((2, seq_len, seq_len), lambda p: (p, 0, 0)),
            pl.BlockSpec((1, 2, seq_len), lambda p: (p, 0, 0)),
        ],
        out_specs=out_specs,
        out_shape=outs,
        scratch_shapes=[
            pltpu.VMEM((seq_len, width), bf16),
            pltpu.VMEM((seq_len, width), f32),
            pltpu.VMEM((width, seq_len), bf16),
            pltpu.VMEM((seq_len, width), bf16),
            pltpu.VMEM((seq_len, width), bf16),
            pltpu.VMEM((seq_len, seq_len), bf16),
            pltpu.VMEM((seq_len, seq_len), bf16),
        ],
        compiler_params=params(),
        name="attention_backward",
    )(*ins, bias, lse)


def combine_kernel(returned_ref, slot_col_ref, chosen_ref, logits_ref, middle_ref, comb_ref, out_ref):
    placing = placing_cols(slot_col_ref[...], returned_ref.shape[0])
    combined = dot(placing, returned_ref[...])
    comb_ref[...] = combined
    gate = jnp.sum(jax.nn.softmax(logits_ref[...], axis=-1) * chosen_ref[...], axis=1, keepdims=True)
    out_ref[...] = middle_ref[...] + gate * combined


def combine(returned, slot_col, chosen_f, logits, middle):
    outs = (jax.ShapeDtypeStruct(middle.shape, f32),) * 2
    ins = (returned, slot_col, chosen_f, logits, middle)
    return pl.pallas_call(
        combine_kernel,
        in_specs=whole_of(ins),
        out_specs=whole_of(outs),
        out_shape=outs,
        grid=(1,),
        compiler_params=params(),
        name="combine",
    )(*ins)


def spread_kernel(grad_ref, comb_ref, slot_row_ref, chosen_ref, logits_ref, d_sent_ref, d_logits_ref):
    grad_now = grad_ref[...].astype(f32)
    d_gate = jnp.sum(grad_now * comb_ref[...], axis=1, keepdims=True)
    shares = jax.nn.softmax(logits_ref[...], axis=-1)
    chosen = chosen_ref[...]
    gate = jnp.sum(shares * chosen, axis=1, keepdims=True)
    d_logits_ref[...] = (d_gate * shares * (chosen - gate)).astype(bf16)
    placing = placing_rows(slot_row_ref[...], d_sent_ref.shape[0])
    d_sent_ref[...] = dot(placing, (gate * grad_now).astype(bf16)).astype(bf16)


def spread(grad_now, combined, slot_row, chosen_f, logits):
    seq_len, width = grad_now.shape
    outs = (
        jax.ShapeDtypeStruct((2 * seq_len, width), bf16),
        jax.ShapeDtypeStruct(logits.shape, bf16),
    )
    ins = (grad_now, combined, slot_row, chosen_f, logits)
    return pl.pallas_call(
        spread_kernel,
        in_specs=whole_of(ins),
        out_specs=whole_of(outs),
        out_shape=outs,
        grid=(1,),
        compiler_params=params(),
        name="spread",
    )(*ins)


def gelu_tanh(pre_vals):
    return jax.nn.gelu(pre_vals, approximate=True)


def body(
    hidden_in,
    route,
    piece_ids,
    buckets,
    rel_table,
    gain_attn,
    gain_ffn,
    w_query,
    w_key,
    w_value,
    w_output,
    w_router,
    w_in,
    w_out,
    cotangent,
):
    count_x = lax.axis_size("gx")
    count_y = lax.axis_size("gy")
    seq_len, width = hidden_in.shape
    layers = w_query.shape[0]
    heads = rel_table.shape[1]
    experts = w_router.shape[2] * count_y
    capacity = 2 * seq_len // experts
    expert_of = route[:, 0]
    chosen = (expert_of[:, None] == jnp.arange(experts, dtype=jnp.int32)[None, :]).astype(jnp.int32)
    ranked = jnp.sum((jnp.cumsum(chosen, axis=0) - 1) * chosen, axis=1)
    slot_of = expert_of * capacity + ranked
    slot_row, slot_col = slot_of[None, :], slot_of[:, None]
    chosen_f = chosen.astype(f32)
    bucket_onehot = (
        buckets[:, None] == jnp.arange(rel_table.shape[0], dtype=jnp.int32)[None, :]
    ).astype(f32)
    bucket_onehot = jnp.pad(bucket_onehot, ((0, 1), (0, 0)))
    offsets = jnp.dot(bucket_onehot, rel_table.astype(f32), precision=highest).T
    bias = bias_of(offsets, piece_ids)
    gain_attn_f = gain_attn.astype(f32)
    gain_ffn_f = gain_ffn.astype(f32)

    tall, wide = w_query.shape[1], w_query.shape[2]

    def gather_mats(layer):
        packed = jnp.concatenate(
            [w_query[layer], w_key[layer], w_value[layer], w_output[layer]], axis=1
        )
        everything = lax.all_gather(packed, ("gx", "gy"), axis=0, tiled=False)
        parted = everything.reshape(count_x, count_y, tall, 4, wide)
        mats = parted.transpose(3, 0, 2, 1, 4).reshape(4, width, width)
        router = lax.all_gather(
            lax.all_gather(w_router[layer], "gy", axis=1, tiled=True), "gx", axis=0, tiled=True
        )
        return (mats[0], mats[1], mats[2], mats[3], router)

    hidden = hidden_in
    kept = []
    for layer in range(layers):
        mats = gather_mats(layer)
        gains = (gain_attn_f[layer][None], gain_ffn_f[layer][None])
        q, k, v, attended, lse, middle, logits, sent = attention_forward(
            hidden, gains[0], gains[1], mats, slot_row, bias
        )
        arrived = lax.all_to_all(
            sent.reshape(experts, capacity, width), "gy", split_axis=0, concat_axis=0, tiled=True
        ).reshape(experts * capacity, width)
        full_in = lax.all_gather(w_in[layer, 0], "gx", axis=1, tiled=True)
        full_out = lax.all_gather(w_out[layer, 0], "gx", axis=1, tiled=True)
        pre_act = dot(arrived, full_in)
        activated = gelu_tanh(pre_act).astype(bf16)
        made = dot(activated, full_out, 1, 1).astype(bf16)
        returned = lax.all_to_all(
            made.reshape(experts, capacity, width), "gy", split_axis=0, concat_axis=0, tiled=True
        ).reshape(experts * capacity, width)
        combined, hidden_next = combine(returned, slot_col, chosen_f, logits, middle)
        kept.append(
            (hidden, gains, mats, (q, k, v), attended, lse, middle, logits, combined)
            + (arrived, full_in, full_out, pre_act, activated)
        )
        hidden = hidden_next

    grad_now = cotangent
    table_sums = None
    parts = []
    for layer in reversed(range(layers)):
        (prior, gains, mats, q_k_v, attended, lse, middle, logits, combined) = kept[layer][:9]
        (arrived, full_in, full_out, pre_act, activated) = kept[layer][9:]
        d_sent, d_logits = spread(grad_now, combined, slot_row, chosen_f, logits)
        d_arrived = lax.all_to_all(
            d_sent.reshape(experts, capacity, width), "gy", split_axis=0, concat_axis=0, tiled=True
        ).reshape(experts * capacity, width)
        d_activated = dot(d_arrived, full_out)
        d_pre = jax.vjp(gelu_tanh, pre_act)[1](d_activated)[0].astype(bf16)
        d_rows = dot(d_pre, full_in, 1, 1).astype(bf16)
        grad_out_part = lax.psum_scatter(
            dot(d_arrived, activated, 0, 0).astype(bf16), "gx", scatter_dimension=1, tiled=True
        )
        grad_in_part = lax.psum_scatter(
            dot(arrived, d_pre, 0, 0).astype(bf16), "gx", scatter_dimension=1, tiled=True
        )
        d_back = lax.all_to_all(
            d_rows.reshape(experts, capacity, width), "gy", split_axis=0, concat_axis=0, tiled=True
        ).reshape(experts * capacity, width)
        grad_now, gwq, gwk, gwv, gwo, gwr, gga, ggf, offset_sums = attention_backward(
            d_back,
            slot_col,
            d_logits,
            grad_now.astype(f32),
            middle,
            prior,
            gains,
            mats,
            q_k_v,
            attended,
            bias,
            lse,
        )
        table_sums = offset_sums if table_sums is None else table_sums + offset_sums
        stacked = jnp.stack([gwq, gwk, gwv, gwo]).reshape(4, count_x, tall, count_y, wide)
        blocked = stacked.transpose(1, 3, 2, 0, 4).reshape(count_x * count_y, tall, 4 * wide)
        summed = lax.psum_scatter(blocked, ("gx", "gy"), scatter_dimension=0, tiled=True)[0]
        summed = summed.astype(f32).reshape(tall, 4, wide)
        parts.append((summed, gwr, gga, ggf, grad_in_part, grad_out_part))
    parts = parts[::-1]
    d_table = jnp.dot(
        table_sums.reshape(heads, 2 * seq_len), bucket_onehot, precision=highest
    ).T
    router_sum, d_table, gga_all, ggf_all = lax.psum(
        (
            jnp.stack([part[1] for part in parts]),
            d_table,
            jnp.concatenate([part[2] for part in parts]),
            jnp.concatenate([part[3] for part in parts]),
        ),
        ("gx", "gy"),
    )
    wide_router = w_router.shape[2]
    router_mine = lax.dynamic_slice(
        router_sum,
        (0, lax.axis_index("gx") * tall, lax.axis_index("gy") * wide_router),
        (layers, tall, wide_router),
    )
    attn_grads = [jnp.stack([part[0][:, index] for part in parts]) for index in range(4)]
    grad_in = jnp.stack([part[4] for part in parts]).astype(f32)[:, None]
    grad_out = jnp.stack([part[5] for part in parts]).astype(f32)[:, None]
    return (
        hidden,
        grad_now,
        d_table,
        gga_all,
        ggf_all,
        *attn_grads,
        router_mine,
        grad_in,
        grad_out,
    )


def solution(mesh):
    rows = P(("gx", "gy"), None)
    square = P(None, "gx", "gy")
    expert = P(None, "gy", None, "gx")
    return jax.shard_map(
        body,
        mesh=mesh,
        in_specs=(rows, rows, P(("gx", "gy")), P(), P(), P(), P())
        + (square,) * 5
        + (expert, expert, rows),
        out_specs=(rows, rows, P(), P(), P()) + (square,) * 5 + (expert, expert),
        check_vma=False,
    )
```

```python
from functools import partial

import jax
import jax.numpy as jnp
from jax import lax
from jax.experimental import pallas as pl
from jax.experimental.pallas import tpu as pltpu
from jax.sharding import PartitionSpec as P

eps_norm = 1e-06
highest = lax.Precision.HIGHEST
f32 = jnp.float32
bf16 = jnp.bfloat16
masked_out = -1e30
MESH = pl.DeviceIdType.MESH
vmem_spec = pl.BlockSpec(memory_space=pltpu.VMEM)
any_spec = pl.BlockSpec(memory_space=pl.ANY)
vmem_bytes = 56 * 1024 * 1024


def whole(shape):
    zeros = (0,) * len(shape)
    return pl.BlockSpec(shape, lambda *_: zeros, pipeline_mode=pl.Buffered(1))


def whole_of(arrays):
    return [whole(array.shape) for array in arrays]


def params():
    return pltpu.CompilerParams(vmem_limit_bytes=vmem_bytes)


def dot(lhs, rhs, lhs_dim=1, rhs_dim=0):
    return lax.dot_general(
        lhs, rhs, (((lhs_dim,), (rhs_dim,)), ((), ())), preferred_element_type=f32
    )


def rms_factor(hidden):
    return lax.rsqrt(jnp.mean(hidden * hidden, axis=-1, keepdims=True) + eps_norm)


def rms_pull(hidden, gain_row, d_normed):
    factor = rms_factor(hidden)
    scaled = gain_row * d_normed
    inner = jnp.mean(hidden * scaled, axis=-1, keepdims=True)
    d_hidden = factor * scaled - hidden * (factor * factor * factor * inner)
    d_gain = jnp.sum(d_normed * hidden * factor, axis=0, keepdims=True)
    return d_hidden, d_gain


def xor_of(index, other, bits):
    total = 0
    for bit in range(bits):
        power = 1 << bit
        total = total + ((index // power + other // power) % 2) * power
    return total


def placing_rows(slot_row, slots):
    places = lax.broadcasted_iota(jnp.int32, (slots, slot_row.shape[1]), 0)
    return (places == slot_row).astype(f32).astype(bf16)


def placing_cols(slot_col, slots):
    places = lax.broadcasted_iota(jnp.int32, (slot_col.shape[0], slots), 1)
    return (places == slot_col).astype(f32).astype(bf16)


def bias_kernel(offsets_ref, piece_col_ref, piece_row_ref, bias_ref):
    seq_len = piece_col_ref.shape[0]
    row = jnp.broadcast_to(offsets_ref[0], (seq_len, 2 * seq_len))
    shifted = pltpu.roll(row, seq_len + 1, 1, stride=1, stride_axis=0)[:, :seq_len]
    key_pos = lax.broadcasted_iota(jnp.int32, (seq_len, seq_len), 0)
    query_pos = lax.broadcasted_iota(jnp.int32, (seq_len, seq_len), 1)
    piece_col = piece_col_ref[...]
    same = (piece_col == piece_row_ref[...]) & (piece_col > 0)
    allowed = (key_pos <= query_pos) | same
    bias_ref[0] = jnp.where(allowed, shifted, masked_out).astype(bf16)


def bias_of(offsets, piece_ids):
    heads, seq_len = offsets.shape[0], piece_ids.shape[0]
    return pl.pallas_call(
        bias_kernel,
        grid=(heads,),
        in_specs=[
            pl.BlockSpec((1, 1, 2 * seq_len), lambda h: (h, 0, 0)),
            whole((seq_len, 1)),
            whole((1, seq_len)),
        ],
        out_specs=pl.BlockSpec((1, seq_len, seq_len), lambda h: (h, 0, 0)),
        out_shape=jax.ShapeDtypeStruct((heads, seq_len, seq_len), bf16),
        compiler_params=params(),
        name="bias_table",
    )(offsets[:, None, :], piece_ids[:, None], piece_ids[None, :])


def half_masks(rows, width):
    lane = lax.broadcasted_iota(jnp.int32, (rows, width), 1)
    return lane < (width // 2)


def unblock(grid_shape, blocks_ref, mats_ref, router_ref):
    count_x, count_y = grid_shape
    tall = mats_ref.shape[1] // count_x
    wide = mats_ref.shape[2] // count_y
    router_rows = []
    for first in range(count_x):
        block_rows = [first * count_y + second for second in range(count_y)]
        rows = slice(first * tall, (first + 1) * tall)
        for which in range(4):
            lanes = slice(which * wide, (which + 1) * wide)
            mats_ref[which, rows, :] = jnp.concatenate(
                [blocks_ref[block, :tall, lanes] for block in block_rows], axis=1
            )
        router_rows.append(
            jnp.concatenate([blocks_ref[block, tall : tall + 1, :tall] for block in block_rows], axis=0)
        )
    router_ref[...] = jnp.concatenate(router_rows, axis=1)


def forward_kernel(
    head_dim,
    grid_shape,
    hidden_ref,
    gain_attn_ref,
    gain_ffn_ref,
    slot_row_ref,
    blocks_ref,
    bias_ref,
    mats_ref,
    router_ref,
    q_ref,
    k_ref,
    v_ref,
    att_ref,
    lse_ref,
    middle_ref,
    logits_ref,
    sent_ref,
):
    pair, pairs = pl.program_id(0), pl.num_programs(0)
    seq_len = hidden_ref.shape[0]
    width = 2 * head_dim
    step = min(256, seq_len)

    @pl.when(pair == 0)
    def _():
        unblock(grid_shape, blocks_ref, mats_ref, router_ref)
        hidden = hidden_ref[...].astype(f32)
        normed = (hidden * rms_factor(hidden) * gain_attn_ref[...]).astype(bf16)
        q_ref[...] = dot(normed, mats_ref[0]).astype(bf16)
        k_ref[...] = dot(normed, mats_ref[1]).astype(bf16)
        v_ref[...] = dot(normed, mats_ref[2]).astype(bf16)

    lanes = pl.ds(pl.multiple_of(pair * width, width), width)
    q2 = q_ref[:, lanes] * jnp.asarray(head_dim**-0.5, bf16)
    k2 = k_ref[:, lanes]
    v2t = v_ref[:, lanes].T
    first = half_masks(seq_len, width)
    for half in range(2):
        q_one = jnp.where(first if half == 0 else ~first, q2, jnp.zeros_like(q2))
        v_one = v2t[half * head_dim : (half + 1) * head_dim]
        for start in range(0, seq_len, step):
            cols = slice(start, start + step)
            scores = dot(k2, q_one[cols], 1, 1) + bias_ref[half, :, cols].astype(f32)
            top = jnp.max(scores, axis=0, keepdims=True)
            raised = jnp.exp(scores - top)
            total = jnp.sum(raised, axis=0, keepdims=True)
            probs = (raised * (1.0 / total)).astype(bf16)
            rows = pl.ds(pl.multiple_of(pair * width + half * head_dim, head_dim), head_dim)
            att_ref[rows, cols] = dot(v_one, probs).astype(bf16)
            lse_ref[0, half : half + 1, cols] = top + jnp.log(total)

    @pl.when(pair == pairs - 1)
    def _():
        middle = hidden_ref[...].astype(f32) + dot(att_ref[...].T, mats_ref[3])
        middle_ref[...] = middle
        ffn_in = (middle * rms_factor(middle) * gain_ffn_ref[...]).astype(bf16)
        logits_ref[...] = dot(ffn_in, router_ref[...], 1, 1)
        placing = placing_rows(slot_row_ref[...], sent_ref.shape[0])
        sent_ref[...] = dot(placing, ffn_in).astype(bf16)


def attention_forward(hidden, gain_attn, gain_ffn, blocks, slot_row, bias, grid_shape, experts):
    seq_len, width = hidden.shape
    heads = bias.shape[0]
    head_dim = width // heads
    slots = 2 * seq_len
    ins = (hidden, gain_attn, gain_ffn, slot_row, blocks)
    tall = jax.ShapeDtypeStruct((seq_len, width), bf16)
    outs = (
        jax.ShapeDtypeStruct((4, width, width), bf16),
        jax.ShapeDtypeStruct((experts, width), bf16),
        tall,
        tall,
        tall,
        jax.ShapeDtypeStruct((width, seq_len), bf16),
        jax.ShapeDtypeStruct((heads // 2, 2, seq_len), f32),
        jax.ShapeDtypeStruct((seq_len, width), f32),
        jax.ShapeDtypeStruct((seq_len, experts), f32),
        jax.ShapeDtypeStruct((slots, width), bf16),
    )
    out_specs = whole_of(outs)
    out_specs[6] = pl.BlockSpec((1, 2, seq_len), lambda p: (p, 0, 0))
    return pl.pallas_call(
        partial(forward_kernel, head_dim, grid_shape),
        grid=(heads // 2,),
        in_specs=whole_of(ins) + [pl.BlockSpec((2, seq_len, seq_len), lambda p: (p, 0, 0))],
        out_specs=out_specs,
        out_shape=outs,
        compiler_params=params(),
        name="attention_forward",
    )(*ins, bias)


def diagonal_fold(values, seq_len):
    rows, wide = seq_len, 2 * seq_len
    folded = None
    tile = 128
    count = seq_len // tile
    for row_tile in range(count):
        piece = values[row_tile * tile : (row_tile + 1) * tile].astype(f32)
        before = (count - 1 - row_tile) * tile
        after = wide - seq_len - before
        parts = []
        if before:
            parts.append(jnp.zeros((tile, before), f32))
        parts.append(piece)
        if after:
            parts.append(jnp.zeros((tile, after), f32))
        padded = jnp.concatenate(parts, axis=1)
        folded = padded if folded is None else folded + padded
    rows = tile
    while rows > 1:
        rows //= 2
        folded = pltpu.roll(folded[:rows], rows, 1) + folded[rows:]
    return folded


def reblock(grid_shape, blocks_ref, which, values):
    count_x, count_y = grid_shape
    tall = values.shape[0] // count_x
    wide = values.shape[1] // count_y
    for first in range(count_x):
        for second in range(count_y):
            blocks_ref[first * count_y + second, :, which * wide : (which + 1) * wide] = values[
                first * tall : (first + 1) * tall, second * wide : (second + 1) * wide
            ]


def backward_kernel(
    head_dim,
    grid_shape,
    d_back_ref,
    slot_col_ref,
    d_logits_ref,
    grad_ref,
    middle_ref,
    hidden_ref,
    gain_attn_ref,
    gain_ffn_ref,
    mats_ref,
    router_ref,
    q_ref,
    k_ref,
    v_ref,
    att_ref,
    bias_ref,
    lse_ref,
    grad_new_ref,
    blocks_ref,
    gwr_ref,
    gga_ref,
    ggf_ref,
    offsets_ref,
    d_att_s,
    d_middle_s,
    dqt_s,
    dk_s,
    dv_s,
    probs_s,
    scores_s,
):
    pair, pairs = pl.program_id(0), pl.num_programs(0)
    seq_len = hidden_ref.shape[0]
    width = 2 * head_dim
    step = min(256, seq_len)
    scale = head_dim**-0.5

    @pl.when(pair == 0)
    def _():
        placing = placing_cols(slot_col_ref[...], d_back_ref.shape[0])
        d_logits = d_logits_ref[...]
        d_ffn = dot(placing, d_back_ref[...]) + dot(d_logits, router_ref[...])
        middle = middle_ref[...]
        gain_row = gain_ffn_ref[...]
        ffn_in = (middle * rms_factor(middle) * gain_row).astype(bf16)
        gwr_ref[...] = dot(d_logits, ffn_in, 0, 0)
        d_middle, d_gain = rms_pull(middle, gain_row, d_ffn)
        ggf_ref[...] = d_gain
        d_middle = d_middle + grad_ref[...]
        d_middle_s[...] = d_middle
        d_low = d_middle.astype(bf16)
        reblock(grid_shape, blocks_ref, 3, dot(att_ref[...], d_low).astype(bf16))
        d_att_s[...] = dot(d_low, mats_ref[3], 1, 1).astype(bf16)

    lanes = pl.ds(pl.multiple_of(pair * width, width), width)
    q2 = q_ref[:, lanes] * jnp.asarray(scale, bf16)
    k2 = k_ref[:, lanes]
    v2 = v_ref[:, lanes]
    da2 = d_att_s[:, lanes]
    k2t = k2.T
    first = half_masks(seq_len, width)
    d_key = jnp.zeros((seq_len, width), f32)
    d_value = jnp.zeros((seq_len, width), f32)
    for half in range(2):
        mask = first if half == 0 else ~first
        q_one = jnp.where(mask, q2, jnp.zeros_like(q2))
        da_one = jnp.where(mask, da2, jnp.zeros_like(da2))
        k_one = k2t[half * head_dim : (half + 1) * head_dim]
        rows = pl.ds(pl.multiple_of(pair * width + half * head_dim, head_dim), head_dim)
        for start in range(0, seq_len, step):
            cols = slice(start, start + step)
            scores = dot(k2, q_one[cols], 1, 1) + bias_ref[half, :, cols].astype(f32)
            probs = jnp.exp(scores - lse_ref[0, half : half + 1, cols])
            d_probs = dot(v2, da_one[cols], 1, 1)
            inner = jnp.sum(probs * d_probs, axis=0, keepdims=True)
            d_scores = (probs * (d_probs - inner)).astype(bf16)
            probs_s[:, cols] = probs.astype(bf16)
            scores_s[:, cols] = d_scores
            dqt_s[rows, cols] = (dot(k_one, d_scores) * scale).astype(bf16)
        d_key = d_key + dot(scores_s[...], q_one)
        d_value = d_value + dot(probs_s[...], da_one)
        offsets_ref[0, half : half + 1, :] = diagonal_fold(scores_s[...], seq_len)
    dk_s[:, lanes] = d_key.astype(bf16)
    dv_s[:, lanes] = d_value.astype(bf16)

    @pl.when(pair == pairs - 1)
    def _():
        hidden = hidden_ref[...].astype(f32)
        gain_row = gain_attn_ref[...]
        normed_t = (hidden * rms_factor(hidden) * gain_row).astype(bf16).T
        d_query = dqt_s[...].T
        d_normed = dot(d_query, mats_ref[0], 1, 1)
        reblock(grid_shape, blocks_ref, 0, dot(normed_t, d_query).astype(bf16))
        d_normed = d_normed + dot(dk_s[...], mats_ref[1], 1, 1)
        reblock(grid_shape, blocks_ref, 1, dot(normed_t, dk_s[...]).astype(bf16))
        d_normed = d_normed + dot(dv_s[...], mats_ref[2], 1, 1)
        reblock(grid_shape, blocks_ref, 2, dot(normed_t, dv_s[...]).astype(bf16))
        d_hidden, d_gain = rms_pull(hidden, gain_row, d_normed)
        gga_ref[...] = d_gain
        grad_new_ref[...] = d_hidden + d_middle_s[...]


def attention_backward(
    d_back,
    slot_col,
    d_logits,
    grad_now,
    middle,
    hidden,
    gains,
    mats,
    q_k_v,
    attended,
    bias,
    lse,
    grid_shape,
):
    seq_len, width = hidden.shape
    heads = bias.shape[0]
    head_dim = width // heads
    experts = mats[1].shape[0]
    count_x, count_y = grid_shape
    ins = (
        d_back,
        slot_col,
        d_logits,
        grad_now,
        middle,
        hidden,
        *gains,
        *mats,
        *q_k_v,
        attended,
    )
    row = jax.ShapeDtypeStruct((1, width), f32)
    outs = (
        jax.ShapeDtypeStruct((seq_len, width), f32),
        jax.ShapeDtypeStruct(
            (count_x * count_y, width // count_x, 4 * (width // count_y)), bf16
        ),
        jax.ShapeDtypeStruct((experts, width), f32),
        row,
        row,
        jax.ShapeDtypeStruct((heads // 2, 2, 2 * seq_len), f32),
    )
    out_specs = whole_of(outs)
    out_specs[5] = pl.BlockSpec((1, 2, 2 * seq_len), lambda p: (p, 0, 0))
    return pl.pallas_call(
        partial(backward_kernel, head_dim, grid_shape),
        grid=(heads // 2,),
        in_specs=whole_of(ins)
        + [
            pl.BlockSpec((2, seq_len, seq_len), lambda p: (p, 0, 0)),
            pl.BlockSpec((1, 2, seq_len), lambda p: (p, 0, 0)),
        ],
        out_specs=out_specs,
        out_shape=outs,
        scratch_shapes=[
            pltpu.VMEM((seq_len, width), bf16),
            pltpu.VMEM((seq_len, width), f32),
            pltpu.VMEM((width, seq_len), bf16),
            pltpu.VMEM((seq_len, width), bf16),
            pltpu.VMEM((seq_len, width), bf16),
            pltpu.VMEM((seq_len, seq_len), bf16),
            pltpu.VMEM((seq_len, seq_len), bf16),
        ],
        compiler_params=params(),
        name="attention_backward",
    )(*ins, bias, lse)


def spread_kernel(grad_ref, comb_ref, slot_row_ref, chosen_ref, logits_ref, d_sent_ref, d_logits_ref):
    grad_now = grad_ref[...].astype(f32)
    d_gate = jnp.sum(grad_now * comb_ref[...], axis=1, keepdims=True)
    shares = jax.nn.softmax(logits_ref[...], axis=-1)
    chosen = chosen_ref[...]
    gate = jnp.sum(shares * chosen, axis=1, keepdims=True)
    d_logits_ref[...] = (d_gate * shares * (chosen - gate)).astype(bf16)
    placing = placing_rows(slot_row_ref[...], d_sent_ref.shape[0])
    d_sent_ref[...] = dot(placing, (gate * grad_now).astype(bf16)).astype(bf16)


def spread(grad_now, combined, slot_row, chosen_f, logits):
    seq_len, width = grad_now.shape
    outs = (
        jax.ShapeDtypeStruct((2 * seq_len, width), bf16),
        jax.ShapeDtypeStruct(logits.shape, bf16),
    )
    ins = (grad_now, combined, slot_row, chosen_f, logits)
    return pl.pallas_call(
        spread_kernel,
        in_specs=whole_of(ins),
        out_specs=whole_of(outs),
        out_shape=outs,
        grid=(1,),
        compiler_params=params(),
        name="spread",
    )(*ins)


def greet(peers):
    barrier = pltpu.get_barrier_semaphore()
    for peer in peers:
        pl.semaphore_signal(barrier, inc=1, device_id=peer, device_id_type=MESH)
    pl.semaphore_wait(barrier, len(peers))


class Exchange:
    def __init__(self, members, rows, src, dst, send_sems, recv_sems):
        self.me = lax.axis_index("gy")
        self.bits = members.bit_length() - 1
        self.rows, self.src, self.dst = rows, src, dst
        self.send_sems, self.recv_sems = send_sems, recv_sems

    def block(self, index):
        return pl.ds(pl.multiple_of(index * self.rows, self.rows), self.rows)

    def copy(self, apart):
        peer = xor_of(self.me, apart, self.bits)
        return pltpu.make_async_remote_copy(
            src_ref=self.src.at[self.block(peer), :],
            dst_ref=self.dst.at[self.block(self.me), :],
            send_sem=self.send_sems.at[apart],
            recv_sem=self.recv_sems.at[apart],
            device_id={"gy": peer},
            device_id_type=MESH,
        )

    def keep_own(self):
        self.dst[self.block(self.me), :] = self.src[self.block(self.me), :]


def peers_along_gy(members):
    me = lax.axis_index("gy")
    bits = members.bit_length() - 1
    return [{"gy": xor_of(me, apart, bits)} for apart in range(1, members)]


def gelu_and_slope(pre):
    inner_scale = 0.7978845608028654
    square = pre * pre
    bent = jnp.tanh(inner_scale * pre * (1.0 + 0.044715 * square))
    act = 0.5 * pre * (1.0 + bent)
    slope = 0.5 * (1.0 + bent) + 0.5 * pre * (1.0 - bent * bent) * (
        inner_scale * (1.0 + 3 * 0.044715 * square)
    )
    return act, slope


def gelu_only(pre):
    inner_scale = 0.7978845608028654
    return 0.5 * pre * (1.0 + jnp.tanh(inner_scale * pre * (1.0 + 0.044715 * pre * pre)))


def chunk_of(members, rows):
    return max(1, min(members, 256 // rows))


def expert_forward_kernel(
    members,
    sent_ref,
    slot_col_ref,
    chosen_ref,
    logits_ref,
    middle_ref,
    win_ref,
    wout_ref,
    arrived_ref,
    comb_ref,
    out_ref,
    win_s,
    wout_s,
    made_s,
    returned_s,
    w_sems,
    send_sems,
    recv_sems,
    back_send_sems,
    back_recv_sems,
):
    slots = sent_ref.shape[0]
    rows = slots // members
    group = chunk_of(members, rows)
    chunks = members // group
    chunk_bits = chunks.bit_length() - 1
    hidden_units = win_s.shape[1]
    tile = min(768, hidden_units)
    load_in = pltpu.make_async_copy(win_ref, win_s, w_sems.at[0])
    load_out = pltpu.make_async_copy(wout_ref, wout_s, w_sems.at[1])
    load_in.start()
    load_out.start()
    greet(peers_along_gy(members))
    there = Exchange(members, rows, sent_ref, arrived_ref, send_sems, recv_sems)
    back = Exchange(members, rows, made_s, returned_s, back_send_sems, back_recv_sems)
    for apart in range(members - 1, 0, -1):
        there.copy(apart).start()
    there.keep_own()
    load_in.wait()
    load_out.wait()
    my_chunk = there.me // group

    def chunk_rows(index):
        start = xor_of(my_chunk, index, chunk_bits) * (group * rows)
        return pl.ds(pl.multiple_of(start, group * rows), group * rows)

    def work(index, first):
        for member in range(first, group):
            there.copy(index * group + member).wait_recv()
        here = chunk_rows(index)
        taken = arrived_ref[here, :]
        total = jnp.zeros((group * rows, taken.shape[1]), f32)
        for start in range(0, hidden_units, tile):
            units = slice(start, start + tile)
            act = gelu_only(dot(taken, win_s[:, units])).astype(bf16)
            total = total + dot(act, wout_s[:, units], 1, 1)
        made_s[here, :] = total.astype(bf16)
        for member in range(first, group):
            back.copy(index * group + member).start()

    work(0, 1)
    back.keep_own()

    @pl.loop(1, chunks)
    def _(index):
        work(index, 0)

    slot_col = slot_col_ref[...]
    width = arrived_ref.shape[1]
    comb_ref[...] = jnp.zeros_like(comb_ref)

    def gather_back(index, first):
        for member in range(first, group):
            back.copy(index * group + member).wait_recv()
        start = xor_of(my_chunk, index, chunk_bits) * (group * rows)
        places = lax.broadcasted_iota(jnp.int32, (slot_col.shape[0], group * rows), 1) + start
        placing = (places == slot_col).astype(f32).astype(bf16)
        comb_ref[...] += dot(placing, returned_s[chunk_rows(index), :])

    gather_back(0, 1)

    @pl.loop(1, chunks)
    def _(index):
        gather_back(index, 0)

    gate = jnp.sum(jax.nn.softmax(logits_ref[...], axis=-1) * chosen_ref[...], axis=1, keepdims=True)
    out_ref[...] = middle_ref[...] + gate * comb_ref[...]

    @pl.loop(1, members)
    def _(apart):
        there.copy(apart).wait_send()
        back.copy(apart).wait_send()


def expert_params(identifier):
    return pltpu.CompilerParams(
        vmem_limit_bytes=vmem_bytes, collective_id=identifier, has_side_effects=True
    )


def expert_forward(sent, slot_col, chosen_f, logits, middle, full_in, full_out, members):
    slots, width = sent.shape
    outs = (
        jax.ShapeDtypeStruct(sent.shape, bf16),
        jax.ShapeDtypeStruct(middle.shape, f32),
        jax.ShapeDtypeStruct(middle.shape, f32),
    )
    ins = (sent, slot_col, chosen_f, logits, middle)
    sems = pltpu.SemaphoreType.DMA((members,))
    return pl.pallas_call(
        partial(expert_forward_kernel, members),
        in_specs=[vmem_spec] * len(ins) + [any_spec] * 2,
        out_specs=[vmem_spec] * 3,
        out_shape=outs,
        scratch_shapes=[
            pltpu.VMEM(full_in.shape, bf16),
            pltpu.VMEM(full_out.shape, bf16),
            pltpu.VMEM(sent.shape, bf16),
            pltpu.VMEM(sent.shape, bf16),
            pltpu.SemaphoreType.DMA((2,)),
            sems,
            sems,
            sems,
            sems,
        ],
        compiler_params=expert_params(1),
        name="expert_forward",
    )(*ins, full_in, full_out)


def expert_backward_kernel(
    members,
    d_sent_ref,
    arrived_ref,
    win_ref,
    wout_ref,
    d_back_ref,
    gin_ref,
    gout_ref,
    win_s,
    wout_s,
    d_arrived_s,
    d_rows_s,
    act_s,
    slope_s,
    w_sems,
    send_sems,
    recv_sems,
    back_send_sems,
    back_recv_sems,
):
    slots = d_sent_ref.shape[0]
    rows = slots // members
    group = chunk_of(members, rows)
    chunks = members // group
    chunk_bits = chunks.bit_length() - 1
    hidden_units = win_s.shape[1]
    tile = min(768, hidden_units)
    load_in = pltpu.make_async_copy(win_ref, win_s, w_sems.at[0])
    load_out = pltpu.make_async_copy(wout_ref, wout_s, w_sems.at[1])
    load_in.start()
    load_out.start()
    greet(peers_along_gy(members))
    there = Exchange(members, rows, d_sent_ref, d_arrived_s, send_sems, recv_sems)
    back = Exchange(members, rows, d_rows_s, d_back_ref, back_send_sems, back_recv_sems)
    for apart in range(members - 1, 0, -1):
        there.copy(apart).start()
    there.keep_own()
    my_chunk = there.me // group
    load_in.wait()

    @pl.loop(0, slots // 256)
    def _(index):
        here = pl.ds(pl.multiple_of(index * 256, 256), 256)
        taken = arrived_ref[here, :]
        for start in range(0, hidden_units, tile):
            units = slice(start, start + tile)
            act, slope = gelu_and_slope(dot(taken, win_s[:, units]))
            act_s[here, units] = act.astype(bf16)
            slope_s[here, units] = slope.astype(bf16)

    load_out.wait()

    def chunk_rows(index):
        start = xor_of(my_chunk, index, chunk_bits) * (group * rows)
        return pl.ds(pl.multiple_of(start, group * rows), group * rows)

    def work(index, first):
        for member in range(first, group):
            there.copy(index * group + member).wait_recv()
        here = chunk_rows(index)
        taken = d_arrived_s[here, :]
        total = jnp.zeros((group * rows, taken.shape[1]), f32)
        for start in range(0, hidden_units, tile):
            units = slice(start, start + tile)
            d_pre = (dot(taken, wout_s[:, units]) * slope_s[here, units].astype(f32)).astype(bf16)
            slope_s[here, units] = d_pre
            total = total + dot(d_pre, win_s[:, units], 1, 1)
        d_rows_s[here, :] = total.astype(bf16)
        for member in range(first, group):
            back.copy(index * group + member).start()

    work(0, 1)
    back.keep_own()

    @pl.loop(1, chunks)
    def _(index):
        work(index, 0)

    for lhs_ref, rhs_ref, out_ref in (
        (d_arrived_s, act_s, gout_ref),
        (arrived_ref, slope_s, gin_ref),
    ):
        lhs = lhs_ref[...].T

        @pl.loop(0, hidden_units // tile)
        def _(index, lhs=lhs, rhs_ref=rhs_ref, out_ref=out_ref):
            units = pl.ds(pl.multiple_of(index * tile, tile), tile)
            out_ref[:, units] = dot(lhs, rhs_ref[:, units]).astype(bf16)

    @pl.loop(1, members)
    def _(apart):
        back.copy(apart).wait_recv()
        there.copy(apart).wait_send()
        back.copy(apart).wait_send()


def expert_backward(d_sent, arrived, full_in, full_out, members):
    outs = (
        jax.ShapeDtypeStruct(d_sent.shape, bf16),
        jax.ShapeDtypeStruct(full_in.shape, bf16),
        jax.ShapeDtypeStruct(full_out.shape, bf16),
    )
    slots = d_sent.shape[0]
    sems = pltpu.SemaphoreType.DMA((members,))
    return pl.pallas_call(
        partial(expert_backward_kernel, members),
        in_specs=[vmem_spec] * 2 + [any_spec] * 2,
        out_specs=[vmem_spec] * 3,
        out_shape=outs,
        scratch_shapes=[
            pltpu.VMEM(full_in.shape, bf16),
            pltpu.VMEM(full_out.shape, bf16),
            pltpu.VMEM(d_sent.shape, bf16),
            pltpu.VMEM(d_sent.shape, bf16),
            pltpu.VMEM((slots, full_in.shape[1]), bf16),
            pltpu.VMEM((slots, full_in.shape[1]), bf16),
            pltpu.SemaphoreType.DMA((2,)),
            sems,
            sems,
            sems,
            sems,
        ],
        compiler_params=expert_params(2),
        name="expert_backward",
    )(d_sent, arrived, full_in, full_out)


def body(
    hidden_in,
    route,
    piece_ids,
    buckets,
    rel_table,
    gain_attn,
    gain_ffn,
    w_query,
    w_key,
    w_value,
    w_output,
    w_router,
    w_in,
    w_out,
    cotangent,
):
    count_x = lax.axis_size("gx")
    count_y = lax.axis_size("gy")
    seq_len, width = hidden_in.shape
    layers = w_query.shape[0]
    heads = rel_table.shape[1]
    experts = w_router.shape[2] * count_y
    capacity = 2 * seq_len // experts
    expert_of = route[:, 0]
    chosen = (expert_of[:, None] == jnp.arange(experts, dtype=jnp.int32)[None, :]).astype(jnp.int32)
    ranked = jnp.sum((jnp.cumsum(chosen, axis=0) - 1) * chosen, axis=1)
    slot_of = expert_of * capacity + ranked
    slot_row, slot_col = slot_of[None, :], slot_of[:, None]
    chosen_f = chosen.astype(f32)
    bucket_onehot = (
        buckets[:, None] == jnp.arange(rel_table.shape[0], dtype=jnp.int32)[None, :]
    ).astype(f32)
    bucket_onehot = jnp.pad(bucket_onehot, ((0, 1), (0, 0)))
    offsets = jnp.dot(bucket_onehot, rel_table.astype(f32), precision=highest).T
    bias = bias_of(offsets, piece_ids)
    gain_attn_f = gain_attn.astype(f32)
    gain_ffn_f = gain_ffn.astype(f32)

    tall, wide = w_query.shape[1], w_query.shape[2]

    grid_shape = (count_x, count_y)
    tile_rows = 16

    def gather_blocks(layer):
        packed = jnp.concatenate(
            [w_query[layer], w_key[layer], w_value[layer], w_output[layer]], axis=1
        )
        router_row = jnp.pad(w_router[layer].T, ((0, tile_rows - 1), (0, 4 * wide - tall)))
        packed = jnp.concatenate([packed, router_row], axis=0)
        return lax.all_gather(packed, ("gx", "gy"), axis=0, tiled=False)

    hidden = hidden_in
    kept = []
    for layer in range(layers):
        blocks = gather_blocks(layer)
        gains = (gain_attn_f[layer][None], gain_ffn_f[layer][None])
        mats, router, q, k, v, attended, lse, middle, logits, sent = attention_forward(
            hidden, gains[0], gains[1], blocks, slot_row, bias, grid_shape, experts
        )
        full_in = lax.all_gather(w_in[layer, 0], "gx", axis=1, tiled=True)
        full_out = lax.all_gather(w_out[layer, 0], "gx", axis=1, tiled=True)
        arrived, combined, hidden_next = expert_forward(
            sent, slot_col, chosen_f, logits, middle, full_in, full_out, count_y
        )
        kept.append(
            (hidden, gains, (mats, router), (q, k, v), attended, lse, middle, logits, combined)
            + (arrived, full_in, full_out)
        )
        hidden = hidden_next

    grad_now = cotangent
    table_sums = None
    parts = []
    for layer in reversed(range(layers)):
        (prior, gains, mats, q_k_v, attended, lse, middle, logits, combined) = kept[layer][:9]
        (arrived, full_in, full_out) = kept[layer][9:]
        d_sent, d_logits = spread(grad_now, combined, slot_row, chosen_f, logits)
        d_back, grad_in_full, grad_out_full = expert_backward(
            d_sent, arrived, full_in, full_out, count_y
        )
        grad_out_part = lax.psum_scatter(grad_out_full, "gx", scatter_dimension=1, tiled=True)
        grad_in_part = lax.psum_scatter(grad_in_full, "gx", scatter_dimension=1, tiled=True)
        grad_now, blocked, gwr, gga, ggf, offset_sums = attention_backward(
            d_back,
            slot_col,
            d_logits,
            grad_now.astype(f32),
            middle,
            prior,
            gains,
            mats,
            q_k_v,
            attended,
            bias,
            lse,
            grid_shape,
        )
        table_sums = offset_sums if table_sums is None else table_sums + offset_sums
        summed = lax.psum_scatter(blocked, ("gx", "gy"), scatter_dimension=0, tiled=True)[0]
        summed = summed.astype(f32).reshape(tall, 4, wide)
        parts.append((summed, gwr, gga, ggf, grad_in_part, grad_out_part))
    parts = parts[::-1]
    d_table = jnp.dot(
        table_sums.reshape(heads, 2 * seq_len), bucket_onehot, precision=highest
    ).T
    router_sum, d_table, gga_all, ggf_all = lax.psum(
        (
            jnp.stack([part[1] for part in parts]),
            d_table,
            jnp.concatenate([part[2] for part in parts]),
            jnp.concatenate([part[3] for part in parts]),
        ),
        ("gx", "gy"),
    )
    wide_router = w_router.shape[2]
    router_mine = lax.dynamic_slice(
        router_sum,
        (0, lax.axis_index("gy") * wide_router, lax.axis_index("gx") * tall),
        (layers, wide_router, tall),
    ).transpose(0, 2, 1)
    attn_grads = [jnp.stack([part[0][:, index] for part in parts]) for index in range(4)]
    grad_in = jnp.stack([part[4] for part in parts]).astype(f32)[:, None]
    grad_out = jnp.stack([part[5] for part in parts]).astype(f32)[:, None]
    return (
        hidden,
        grad_now,
        d_table,
        gga_all,
        ggf_all,
        *attn_grads,
        router_mine,
        grad_in,
        grad_out,
    )


def solution(mesh):
    rows = P(("gx", "gy"), None)
    square = P(None, "gx", "gy")
    expert = P(None, "gy", None, "gx")
    return jax.shard_map(
        body,
        mesh=mesh,
        in_specs=(rows, rows, P(("gx", "gy")), P(), P(), P(), P())
        + (square,) * 5
        + (expert, expert, rows),
        out_specs=(rows, rows, P(), P(), P()) + (square,) * 5 + (expert, expert),
        check_vma=False,
    )
```

```python
from functools import partial

import jax
import jax.numpy as jnp
from jax import lax
from jax.experimental import pallas as pl
from jax.experimental.pallas import tpu as pltpu
from jax.sharding import PartitionSpec as P

eps_norm = 1e-06
highest = lax.Precision.HIGHEST
f32 = jnp.float32
bf16 = jnp.bfloat16
masked_out = -1e30
tile_rows = 16
MESH = pl.DeviceIdType.MESH
vmem_spec = pl.BlockSpec(memory_space=pltpu.VMEM)
any_spec = pl.BlockSpec(memory_space=pl.ANY)
vmem_bytes = 56 * 1024 * 1024


def whole(shape):
    zeros = (0,) * len(shape)
    return pl.BlockSpec(shape, lambda *_: zeros, pipeline_mode=pl.Buffered(1))


def whole_of(arrays):
    return [whole(array.shape) for array in arrays]


def params(identifier=None):
    if identifier is None:
        return pltpu.CompilerParams(vmem_limit_bytes=vmem_bytes)
    return pltpu.CompilerParams(
        vmem_limit_bytes=vmem_bytes, collective_id=identifier, has_side_effects=True
    )


def lasting(microseconds):
    return pl.CostEstimate(
        flops=int(microseconds * 1e9), bytes_accessed=1 << 20, transcendentals=0
    )


def dot(lhs, rhs, lhs_dim=1, rhs_dim=0):
    return lax.dot_general(
        lhs, rhs, (((lhs_dim,), (rhs_dim,)), ((), ())), preferred_element_type=f32
    )


def rms_factor(hidden):
    return lax.rsqrt(jnp.mean(hidden * hidden, axis=-1, keepdims=True) + eps_norm)


def rms_pull(hidden, gain_row, d_normed):
    factor = rms_factor(hidden)
    scaled = gain_row * d_normed
    inner = jnp.mean(hidden * scaled, axis=-1, keepdims=True)
    d_hidden = factor * scaled - hidden * (factor * factor * factor * inner)
    d_gain = jnp.sum(d_normed * hidden * factor, axis=0, keepdims=True)
    return d_hidden, d_gain


def xor_of(index, other, bits):
    total = 0
    for bit in range(bits):
        power = 1 << bit
        total = total + ((index // power + other // power) % 2) * power
    return total


def placing_rows(slot_row, slots):
    places = lax.broadcasted_iota(jnp.int32, (slots, slot_row.shape[1]), 0)
    return (places == slot_row).astype(f32).astype(bf16)


def placing_cols(slot_col, slots):
    places = lax.broadcasted_iota(jnp.int32, (slot_col.shape[0], slots), 1)
    return (places == slot_col).astype(f32).astype(bf16)


def greet(peers):
    barrier = pltpu.get_barrier_semaphore()
    for peer in peers:
        pl.semaphore_signal(barrier, inc=1, device_id=peer, device_id_type=MESH)
    pl.semaphore_wait(barrier, len(peers))


def bits_of(count):
    return count.bit_length() - 1


class Place:
    def __init__(self, grid_shape):
        self.count_y, self.count_z = grid_shape[0] // 2, grid_shape[1] // 2
        first, second = lax.axis_index("gx"), lax.axis_index("gy")
        self.c, self.y = first % 2, first // 2
        self.x, self.z = second % 2, second // 2

    def core_peer(self):
        return {"gx": self.y * 2 + 1 - self.c}

    def x_peer(self):
        return {"gy": self.z * 2 + 1 - self.x}

    def y_at(self, apart):
        return xor_of(self.y, apart, bits_of(self.count_y))

    def y_peer(self, apart):
        return {"gx": self.y_at(apart) * 2 + self.c}

    def y_peers(self):
        return [self.y_peer(apart) for apart in range(1, self.count_y)]

    def z_at(self, apart):
        return xor_of(self.z, apart, bits_of(self.count_z))

    def z_peer(self, apart):
        return {"gy": self.z_at(apart) * 2 + self.x}

    def z_peers(self):
        return [self.z_peer(apart) for apart in range(1, self.count_z)]


def send(src, dst, sems, index, peer):
    return pltpu.make_async_remote_copy(
        src_ref=src,
        dst_ref=dst,
        send_sem=sems[0].at[index],
        recv_sem=sems[1].at[index],
        device_id=peer,
        device_id_type=MESH,
    )


def start_all(copies):
    for copy in copies:
        copy.start()


def wait_all(copies):
    for copy in copies:
        copy.wait()


def gather_z(place, src, landing, sems):
    return [
        send(src, landing, sems, apart - 1, place.z_peer(apart)) for apart in range(1, place.count_z)
    ]


def gather_copies(grid_shape):
    return grid_shape[1] // 2 - 1, 2 * (grid_shape[0] // 2 - 1) + 3


def gather_second(place, column, full, split, sems):
    y, c, x = place.y, place.c, place.x
    upper, lower = pl.ds(0, split), pl.ds(split, full.shape[4] - split)
    copies = [
        send(column.at[:, upper], full.at[y, c, :, x, upper], sems, 0, place.x_peer())
    ]
    for apart in range(1, place.count_y):
        copies.append(
            send(column.at[:, lower], full.at[y, c, :, x, lower], sems, apart, place.y_peer(apart))
        )
    return copies


def gather_third(place, full, split, sems):
    y, c, x = place.y, place.c, place.x
    upper, lower = pl.ds(0, split), pl.ds(split, full.shape[4] - split)
    base = place.count_y
    ref = full.at[:, c, :, x, lower]
    copies = [send(ref, ref, sems, base, place.x_peer())]
    ref = full.at[y, c, :, :, upper]
    for apart in range(1, place.count_y):
        copies.append(send(ref, ref, sems, base + apart, place.y_peer(apart)))
    return copies


def gather_core(place, full, sems):
    ref = full.at[:, place.c]
    return [send(ref, ref, sems, 2 * place.count_y, place.core_peer())]


def whole_blocks(shape, split):
    count_y, _, count_z, _, tall, lanes = shape
    low = tall - split
    return [
        (count_y, count_z, 2, tall, lanes),
        (count_y - 1, count_z, 2, split, lanes),
        (count_y, count_z, low, lanes),
        (count_z, split, lanes),
        (count_y - 1, count_z, low, lanes),
        (count_z - 1, split, lanes),
        (count_z - 1, low, lanes),
    ]


def scatter_copies(grid_shape):
    return 1 + 2 * (grid_shape[0] // 2) + 2 * (grid_shape[1] // 2 - 1)


def add_low(dst, dst_at, *terms):
    total = terms[0].astype(f32)
    for term in terms[1:]:
        total = total + term.astype(f32)
    dst[dst_at] = total.astype(bf16)


class Scatter:
    def __init__(self, place, src, landings, sems, split):
        self.place, self.src, self.sems = place, src, sems
        self.first, self.up2, self.low2, self.up3, self.low3, self.up4, self.low4 = landings
        tall = src.shape[4]
        self.upper, self.lower = pl.ds(0, split), pl.ds(split, tall - split)

    def copies(self, stage):
        at, sems = self.place, self.sems
        count_y, count_z = at.count_y, at.count_z
        if stage == 0:
            return [send(self.src.at[:, 1 - at.c], self.first, sems, 0, at.core_peer())]
        if stage == 1:
            copies = [send(self.first.at[:, :, 1 - at.x, self.lower], self.low2, sems, 1, at.x_peer())]
            for apart in range(1, count_y):
                src = self.first.at[at.y_at(apart), :, :, self.upper]
                dst = self.up2.at[apart - 1]
                copies.append(send(src, dst, sems, 1 + apart, at.y_peer(apart)))
            return copies
        if stage == 2:
            base = 1 + count_y
            copies = [send(self.up2.at[0, :, 1 - at.x], self.up3, sems, base, at.x_peer())]
            for apart in range(1, count_y):
                src, dst = self.low2.at[at.y_at(apart)], self.low3.at[apart - 1]
                copies.append(send(src, dst, sems, base + apart, at.y_peer(apart)))
            return copies
        base = 2 * count_y
        copies = []
        for apart in range(1, count_z):
            there = at.z_at(apart)
            for src, dst, more in (
                (self.up3.at[there], self.up4.at[apart - 1], 0),
                (self.low3.at[0, there], self.low4.at[apart - 1], 1),
            ):
                index = base + 2 * apart - 1 + more
                copies.append(send(src, dst, sems, index, at.z_peer(apart)))
        return copies

    def add(self, stage):
        at = self.place
        count_y, count_z = at.count_y, at.count_z
        if stage == 0:

            @pl.loop(0, count_y * count_z)
            def _(index):
                y, z = index // count_z, index % count_z
                add_low(self.first, (y, z), self.first[y, z], self.src[y, at.c, z])

        elif stage == 1:

            @pl.loop(0, count_z)
            def _(z):
                for x in range(2):
                    terms = [self.up2[apart, z, x] for apart in range(count_y - 1)]
                    add_low(self.up2, (0, z, x), self.first[at.y, z, x, self.upper], *terms)

                @pl.loop(0, count_y)
                def _(y):
                    add_low(self.low2, (y, z), self.first[y, z, at.x, self.lower], self.low2[y, z])

        elif stage == 2:

            @pl.loop(0, count_z)
            def _(z):
                add_low(self.up3, (z,), self.up3[z], self.up2[0, z, at.x])
                terms = [self.low3[apart, z] for apart in range(count_y - 1)]
                add_low(self.low3, (0, z), self.low2[at.y, z], *terms)

    def result(self):
        at = self.place
        upper, lower = self.up3[at.z].astype(f32), self.low3[0, at.z].astype(f32)
        for apart in range(at.count_z - 1):
            upper = upper + self.up4[apart].astype(f32)
            lower = lower + self.low4[apart].astype(f32)
        return upper, lower


class SmallSum:
    def __init__(self, grid_shape, totals, landing, sems):
        self.totals, self.landing, self.sems = totals, landing, sems
        self.peers = []
        for name, count in (("gx", grid_shape[0]), ("gy", grid_shape[1])):
            me = lax.axis_index(name)
            for bit in range(bits_of(count)):
                self.peers.append({name: xor_of(me, 1 << bit, bits_of(count))})
        self.done = 0

    def copy(self):
        step = self.done
        return send(self.totals.at[step], self.landing.at[step], self.sems, step, self.peers[step])

    def begin(self):
        self.copy().start()

    def advance(self):
        if self.done == len(self.peers):
            return
        self.copy().wait()
        step = self.done
        self.totals[step + 1] = self.totals[step] + self.landing[step]
        self.done += 1
        if self.done < len(self.peers):
            self.begin()


def small_steps(grid_shape):
    return bits_of(grid_shape[0]) + bits_of(grid_shape[1])


def final_kernel(grid_shape, layers, *refs):
    refs = list(refs)
    take = refs.pop
    blocks = [take(0) for _ in range(layers)]
    small_ref = take(0)
    outs = [take(0) for _ in range(4)]
    small_out_ref = take(0)
    landings = [[take(0) for _ in range(7)] for _ in range(layers)]
    totals, landing = take(0), take(0)
    sems = [(take(0), take(0)) for _ in range(layers)]
    small_sems = (take(0), take(0))
    place = Place(grid_shape)
    tall, wide = outs[0].shape[1:]
    split = tall // 2
    sums = [Scatter(place, blocks[l], landings[l], sems[l], split) for l in range(layers)][::-1]
    small = SmallSum(grid_shape, totals, landing, small_sems)
    totals[0] = small_ref[...]
    greet([place.core_peer(), place.x_peer()] + place.y_peers() + place.z_peers())
    small.begin()
    for one in sums:
        start_all(one.copies(0))
    for stage in range(4):
        for one in sums:
            small.advance()
            wait_all(one.copies(stage))
            if stage < 3:
                one.add(stage)
                start_all(one.copies(stage + 1))
    while small.done < len(small.peers):
        small.advance()
    small_out_ref[...] = totals[len(small.peers)]
    for layer, one in enumerate(sums[::-1]):
        for part, rows in zip(one.result(), (slice(0, split), slice(split, tall))):
            for which in range(4):
                outs[which][layer, rows, :] = part[:, which * wide : (which + 1) * wide]


def final_sums(blocks, small, grid_shape, wide):
    layers = len(blocks)
    shape = blocks[0].shape
    tall = shape[4]
    landings = [pltpu.VMEM(one, bf16) for one in whole_blocks(shape, tall // 2)]
    steps = small_steps(grid_shape)
    sems = pltpu.SemaphoreType.DMA((scatter_copies(grid_shape),))
    small_sems = pltpu.SemaphoreType.DMA((steps,))
    outs = [jax.ShapeDtypeStruct((layers, tall, wide), f32)] * 4
    outs.append(jax.ShapeDtypeStruct(small.shape, f32))
    return pl.pallas_call(
        partial(final_kernel, grid_shape, layers),
        in_specs=[vmem_spec] * (layers + 1),
        out_specs=[vmem_spec] * len(outs),
        out_shape=outs,
        scratch_shapes=landings * layers
        + [pltpu.VMEM((steps + 1, *small.shape), f32), pltpu.VMEM((steps, *small.shape), f32)]
        + [sems, sems] * layers
        + [small_sems, small_sems],
        compiler_params=params(20),
        cost_estimate=lasting(60),
        name="final_sums",
    )(*blocks, small)


def unblock(grid_shape, blocks_ref, mats_ref, router_ref):
    count_x, count_y = grid_shape
    tall = mats_ref.shape[1] // count_x
    wide = mats_ref.shape[2] // count_y
    router_rows = []
    for first in range(count_x):
        spots = [(first // 2, first % 2, second // 2, second % 2) for second in range(count_y)]
        rows = slice(first * tall, (first + 1) * tall)
        for which in range(4):
            lanes = slice(which * wide, (which + 1) * wide)
            mats_ref[which, rows, :] = jnp.concatenate(
                [blocks_ref[(*spot, slice(0, tall), lanes)] for spot in spots], axis=1
            )
        router_rows.append(
            jnp.concatenate(
                [blocks_ref[(*spot, slice(tall, tall + 1), slice(0, tall))] for spot in spots],
                axis=0,
            )
        )
    router_ref[...] = jnp.concatenate(router_rows, axis=1)


def start_kernel(
    grid_shape,
    wq_ref,
    wk_ref,
    wv_ref,
    wo_ref,
    router_rows_ref,
    buckets_ref,
    table_ref,
    piece_col_ref,
    piece_row_ref,
    route_col_ref,
    route_row_ref,
    mats_ref,
    router_ref,
    later_ref,
    bias_ref,
    slot_col_ref,
    slot_row_ref,
    chosen_ref,
    full_s,
    column_s,
    z_send,
    z_recv,
    send_sems,
    recv_sems,
):
    place = Place(grid_shape)
    layers, tall, wide = wq_ref.shape
    split = tall // 2
    y, c, z, x = place.y, place.c, place.z, place.x

    def packed(layer):
        return jnp.concatenate([ref[layer] for ref in (wq_ref, wk_ref, wv_ref, wo_ref)], axis=1)

    column_s[z, :tall] = packed(0)
    column_s[z, tall:] = router_rows_ref[0]
    greet([place.core_peer(), place.x_peer()] + place.y_peers() + place.z_peers())
    first = gather_z(place, column_s.at[z], column_s.at[z], (z_send, z_recv))
    start_all(first)
    for layer in range(1, layers):
        later_ref[layer - 1, :tall] = packed(layer)
        later_ref[layer - 1, tall:] = router_rows_ref[layer]

    seq_len, experts = chosen_ref.shape
    capacity = 2 * seq_len // experts
    heads = bias_ref.shape[0]
    buckets_all = buckets_ref[...]
    in_bucket = lax.broadcasted_iota(jnp.int32, (2 * seq_len, table_ref.shape[1]), 1) == buckets_all
    offsets = dot(table_ref[...], in_bucket.astype(f32).astype(bf16), 1, 1)
    key_pos = lax.broadcasted_iota(jnp.int32, (seq_len, seq_len), 0)
    query_pos = lax.broadcasted_iota(jnp.int32, (seq_len, seq_len), 1)
    piece_col = piece_col_ref[...]
    same = (piece_col == piece_row_ref[...]) & (piece_col > 0)
    allowed = (key_pos <= query_pos) | same

    def bias_for(head):
        row = jnp.broadcast_to(offsets[head : head + 1], (seq_len, 2 * seq_len))
        shifted = pltpu.roll(row, seq_len + 1, 1, stride=1, stride_axis=0)[:, :seq_len]
        bias_ref[head] = jnp.where(allowed, shifted, masked_out).astype(bf16)

    for head in range(heads // 2):
        bias_for(head)
    wait_all(first)
    sems = (send_sems, recv_sems)
    second = gather_second(place, column_s, full_s, split, sems)
    start_all(second)
    full_s[y, c, :, x] = column_s[...]
    for head in range(heads // 2, heads):
        bias_for(head)
    wait_all(second)
    third = gather_third(place, full_s, split, sems)
    start_all(third)

    route_col, route_row = route_col_ref[...], route_row_ref[...]
    chosen = (lax.broadcasted_iota(jnp.int32, (seq_len, experts), 1) == route_col).astype(f32)
    chosen_t = (lax.broadcasted_iota(jnp.int32, (experts, seq_len), 0) == route_row).astype(f32)
    chosen_ref[...] = chosen
    earlier = (key_pos < query_pos).astype(f32).astype(bf16)
    before_t = dot(chosen_t.astype(bf16), earlier)
    rank_row = jnp.sum(before_t * chosen_t, axis=0, keepdims=True)
    slot_row_ref[...] = route_row * capacity + rank_row.astype(jnp.int32)
    later = (key_pos > query_pos).astype(f32).astype(bf16)
    before = dot(later, chosen.astype(bf16))
    rank_col = jnp.sum(before * chosen, axis=1, keepdims=True)
    slot_col_ref[...] = route_col * capacity + rank_col.astype(jnp.int32)

    wait_all(third)
    fourth = gather_core(place, full_s, sems)
    start_all(fourth)
    wait_all(fourth)
    unblock(grid_shape, full_s, mats_ref, router_ref)


def start(mats, router_rows, buckets, table_t, piece_ids, route, grid_shape):
    layers, tall, wide = mats[0].shape
    seq_len = piece_ids.shape[0]
    heads = table_t.shape[0]
    width = tall * grid_shape[0]
    experts = grid_shape[1]
    block = (router_rows.shape[1] + tall, 4 * wide)
    half = (grid_shape[0] // 2, 2, grid_shape[1] // 2, 2)
    ins = (
        *mats,
        router_rows,
        buckets,
        table_t,
        piece_ids[:, None],
        piece_ids[None, :],
        route,
        route.reshape(1, seq_len),
    )
    outs = (
        jax.ShapeDtypeStruct((4, width, width), bf16),
        jax.ShapeDtypeStruct((experts, width), bf16),
        jax.ShapeDtypeStruct((layers - 1, *block), bf16),
        jax.ShapeDtypeStruct((heads, seq_len, seq_len), bf16),
        jax.ShapeDtypeStruct((seq_len, 1), jnp.int32),
        jax.ShapeDtypeStruct((1, seq_len), jnp.int32),
        jax.ShapeDtypeStruct((seq_len, experts), f32),
    )
    along_z, others = gather_copies(grid_shape)
    return pl.pallas_call(
        partial(start_kernel, grid_shape),
        in_specs=[vmem_spec] * len(ins),
        out_specs=[vmem_spec] * len(outs),
        out_shape=outs,
        scratch_shapes=[
            pltpu.VMEM((*half, *block), bf16),
            pltpu.VMEM((half[2], *block), bf16),
            pltpu.SemaphoreType.DMA((along_z,)),
            pltpu.SemaphoreType.DMA((along_z,)),
            pltpu.SemaphoreType.DMA((others,)),
            pltpu.SemaphoreType.DMA((others,)),
        ],
        compiler_params=params(0),
        cost_estimate=lasting(45),
        name="start",
    )(*ins)


def half_masks(rows, width):
    lane = lax.broadcasted_iota(jnp.int32, (rows, width), 1)
    return lane < (width // 2)


def forward_kernel(
    head_dim,
    grid_shape,
    blocked,
    sends,
    hidden_ref,
    gain_attn_ref,
    gain_ffn_ref,
    slot_row_ref,
    *refs,
):
    refs = list(refs)
    take = refs.pop
    blocks_ref = take(0) if blocked else None
    mats_ref, router_ref = (None, None) if blocked else (take(0), take(0))
    next_ref = take(0) if sends else None
    bias_ref = take(0)
    if blocked:
        mats_ref, router_ref = take(0), take(0)
    q_ref, k_ref, v_ref, att_ref, lse_ref, middle_ref, logits_ref, sent_ref = (
        take(0) for _ in range(8)
    )
    pair, pairs = pl.program_id(0), pl.num_programs(0)
    seq_len = hidden_ref.shape[0]
    width = 2 * head_dim
    step = min(256, seq_len)

    if sends:
        column_ref, z_send, z_recv, own_sem = refs
        place = Place(grid_shape)
        own = pltpu.make_async_copy(next_ref, column_ref.at[place.z], own_sem)
        copies = gather_z(place, next_ref, column_ref.at[place.z], (z_send, z_recv))

        @pl.when(pair == 0)
        def _():
            greet(place.z_peers())
            own.start()
            start_all(copies)

    @pl.when(pair == 0)
    def _():
        if blocked:
            unblock(grid_shape, blocks_ref, mats_ref, router_ref)
        hidden = hidden_ref[...].astype(f32)
        normed = (hidden * rms_factor(hidden) * gain_attn_ref[...]).astype(bf16)
        q_ref[...] = dot(normed, mats_ref[0]).astype(bf16)
        k_ref[...] = dot(normed, mats_ref[1]).astype(bf16)
        v_ref[...] = dot(normed, mats_ref[2]).astype(bf16)

    lanes = pl.ds(pl.multiple_of(pair * width, width), width)
    q2 = q_ref[:, lanes] * jnp.asarray(head_dim**-0.5, bf16)
    k2 = k_ref[:, lanes]
    v2t = v_ref[:, lanes].T
    first = half_masks(seq_len, width)
    for half in range(2):
        q_one = jnp.where(first if half == 0 else ~first, q2, jnp.zeros_like(q2))
        v_one = v2t[half * head_dim : (half + 1) * head_dim]
        for begin in range(0, seq_len, step):
            cols = slice(begin, begin + step)
            scores = dot(k2, q_one[cols], 1, 1) + bias_ref[half, :, cols].astype(f32)
            top = jnp.max(scores, axis=0, keepdims=True)
            raised = jnp.exp(scores - top)
            total = jnp.sum(raised, axis=0, keepdims=True)
            probs = (raised * (1.0 / total)).astype(bf16)
            rows = pl.ds(pl.multiple_of(pair * width + half * head_dim, head_dim), head_dim)
            att_ref[rows, cols] = dot(v_one, probs).astype(bf16)
            lse_ref[0, half : half + 1, cols] = top + jnp.log(total)

    @pl.when(pair == pairs - 1)
    def _():
        middle = hidden_ref[...].astype(f32) + dot(att_ref[...].T, mats_ref[3])
        middle_ref[...] = middle
        ffn_in = (middle * rms_factor(middle) * gain_ffn_ref[...]).astype(bf16)
        logits_ref[...] = dot(ffn_in, router_ref[...], 1, 1)
        placing = placing_rows(slot_row_ref[...], sent_ref.shape[0])
        sent_ref[...] = dot(placing, ffn_in).astype(bf16)

    if sends:

        @pl.when(pair == pairs - 1)
        def _():
            own.wait()
            wait_all(copies)


def attention_forward(
    hidden, gain_attn, gain_ffn, slot_row, bias, grid_shape, identifier, blocks=None, mats=None, following=None
):
    seq_len, width = hidden.shape
    heads = bias.shape[0]
    head_dim = width // heads
    slots = 2 * seq_len
    experts = grid_shape[1]
    blocked, sends = blocks is not None, following is not None
    ins = [hidden, gain_attn, gain_ffn, slot_row] + ([blocks] if blocked else list(mats))
    in_specs = whole_of(ins)
    if sends:
        ins.append(following)
        in_specs.append(any_spec)
    ins.append(bias)
    in_specs.append(pl.BlockSpec((2, seq_len, seq_len), lambda p: (p, 0, 0)))
    tall = jax.ShapeDtypeStruct((seq_len, width), bf16)
    outs = [
        tall,
        tall,
        tall,
        jax.ShapeDtypeStruct((width, seq_len), bf16),
        jax.ShapeDtypeStruct((heads // 2, 2, seq_len), f32),
        jax.ShapeDtypeStruct((seq_len, width), f32),
        jax.ShapeDtypeStruct((seq_len, experts), f32),
        jax.ShapeDtypeStruct((slots, width), bf16),
    ]
    out_specs = whole_of(outs)
    out_specs[4] = pl.BlockSpec((1, 2, seq_len), lambda p: (p, 0, 0))
    if blocked:
        more = [
            jax.ShapeDtypeStruct((4, width, width), bf16),
            jax.ShapeDtypeStruct((experts, width), bf16),
        ]
        outs = more + outs
        out_specs = whole_of(more) + out_specs
    scratch = []
    if sends:
        along_z = grid_shape[1] // 2
        outs.append(jax.ShapeDtypeStruct((along_z, *following.shape), bf16))
        out_specs.append(any_spec)
        sems = pltpu.SemaphoreType.DMA((along_z - 1,))
        scratch = [sems, sems, pltpu.SemaphoreType.DMA]
    got = pl.pallas_call(
        partial(forward_kernel, head_dim, grid_shape, blocked, sends),
        grid=(heads // 2,),
        in_specs=in_specs,
        out_specs=out_specs,
        out_shape=outs,
        scratch_shapes=scratch,
        compiler_params=params(identifier if sends else None),
        cost_estimate=lasting(25),
        name="attention_forward",
    )(*ins)
    column = got[-1] if sends else None
    got = got[:-1] if sends else got
    return (tuple(mats) + tuple(got) if not blocked else tuple(got)), column


def diagonal_fold(values, seq_len):
    rows, wide = seq_len, 2 * seq_len
    folded = None
    tile = 128
    count = seq_len // tile
    for row_tile in range(count):
        piece = values[row_tile * tile : (row_tile + 1) * tile].astype(f32)
        before = (count - 1 - row_tile) * tile
        after = wide - seq_len - before
        parts = []
        if before:
            parts.append(jnp.zeros((tile, before), f32))
        parts.append(piece)
        if after:
            parts.append(jnp.zeros((tile, after), f32))
        padded = jnp.concatenate(parts, axis=1)
        folded = padded if folded is None else folded + padded
    rows = tile
    while rows > 1:
        rows //= 2
        folded = pltpu.roll(folded[:rows], rows, 1) + folded[rows:]
    return folded


def reblock(grid_shape, blocks_ref, which, values):
    count_x, count_y = grid_shape
    tall = values.shape[0] // count_x
    wide = values.shape[1] // count_y
    for first in range(count_x):
        for second in range(count_y):
            spot = (first // 2, first % 2, second // 2, second % 2)
            lanes = slice(which * wide, (which + 1) * wide)
            blocks_ref[(*spot, slice(None), lanes)] = values[
                first * tall : (first + 1) * tall, second * wide : (second + 1) * wide
            ]


def spread_into(grad_now, comb_ref, slot_row_ref, chosen_ref, logits_ref, d_sent_ref, d_logits_ref):
    d_gate = jnp.sum(grad_now * comb_ref[...], axis=1, keepdims=True)
    shares = jax.nn.softmax(logits_ref[...], axis=-1)
    chosen = chosen_ref[...]
    gate = jnp.sum(shares * chosen, axis=1, keepdims=True)
    d_logits_ref[...] = (d_gate * shares * (chosen - gate)).astype(bf16)
    placing = placing_rows(slot_row_ref[...], d_sent_ref.shape[0])
    d_sent_ref[...] = dot(placing, (gate * grad_now).astype(bf16)).astype(bf16)


def backward_kernel(
    head_dim,
    grid_shape,
    spreads,
    unread,
    d_back_ref,
    slot_col_ref,
    d_logits_ref,
    grad_ref,
    middle_ref,
    hidden_ref,
    gain_attn_ref,
    gain_ffn_ref,
    mats_ref,
    router_ref,
    q_ref,
    k_ref,
    v_ref,
    att_ref,
    *refs,
):
    refs = list(refs)
    take = refs.pop
    spread_in = [take(0) for _ in range(4)] if spreads else []
    bias_ref, lse_ref = take(0), take(0)
    del refs[:unread]
    grad_new_ref, blocks_ref, gwr_ref, gga_ref, ggf_ref, offsets_ref = (take(0) for _ in range(6))
    spread_out = [take(0) for _ in range(2)] if spreads else []
    d_att_s, d_middle_s, dqt_s, dk_s, dv_s, probs_s, scores_s = refs
    pair, pairs = pl.program_id(0), pl.num_programs(0)
    seq_len = hidden_ref.shape[0]
    width = 2 * head_dim
    step = min(256, seq_len)
    scale = head_dim**-0.5

    @pl.when(pair == 0)
    def _():
        placing = placing_cols(slot_col_ref[...], d_back_ref.shape[0])
        d_logits = d_logits_ref[...]
        d_ffn = dot(placing, d_back_ref[...]) + dot(d_logits, router_ref[...])
        middle = middle_ref[...]
        gain_row = gain_ffn_ref[...]
        ffn_in = (middle * rms_factor(middle) * gain_row).astype(bf16)
        gwr_ref[...] = dot(d_logits, ffn_in, 0, 0)
        d_middle, d_gain = rms_pull(middle, gain_row, d_ffn)
        ggf_ref[...] = d_gain
        d_middle = d_middle + grad_ref[...].astype(f32)
        d_middle_s[...] = d_middle
        d_low = d_middle.astype(bf16)
        reblock(grid_shape, blocks_ref, 3, dot(att_ref[...], d_low).astype(bf16))
        d_att_s[...] = dot(d_low, mats_ref[3], 1, 1).astype(bf16)

    lanes = pl.ds(pl.multiple_of(pair * width, width), width)
    q2 = q_ref[:, lanes] * jnp.asarray(scale, bf16)
    k2 = k_ref[:, lanes]
    v2 = v_ref[:, lanes]
    da2 = d_att_s[:, lanes]
    k2t = k2.T
    first = half_masks(seq_len, width)
    d_key = jnp.zeros((seq_len, width), f32)
    d_value = jnp.zeros((seq_len, width), f32)
    for half in range(2):
        mask = first if half == 0 else ~first
        q_one = jnp.where(mask, q2, jnp.zeros_like(q2))
        da_one = jnp.where(mask, da2, jnp.zeros_like(da2))
        k_one = k2t[half * head_dim : (half + 1) * head_dim]
        rows = pl.ds(pl.multiple_of(pair * width + half * head_dim, head_dim), head_dim)
        for start in range(0, seq_len, step):
            cols = slice(start, start + step)
            scores = dot(k2, q_one[cols], 1, 1) + bias_ref[half, :, cols].astype(f32)
            probs = jnp.exp(scores - lse_ref[0, half : half + 1, cols])
            d_probs = dot(v2, da_one[cols], 1, 1)
            inner = jnp.sum(probs * d_probs, axis=0, keepdims=True)
            d_scores = (probs * (d_probs - inner)).astype(bf16)
            probs_s[:, cols] = probs.astype(bf16)
            scores_s[:, cols] = d_scores
            dqt_s[rows, cols] = (dot(k_one, d_scores) * scale).astype(bf16)
        d_key = d_key + dot(scores_s[...], q_one)
        d_value = d_value + dot(probs_s[...], da_one)
        offsets_ref[0, half : half + 1, :] = diagonal_fold(scores_s[...], seq_len)
    dk_s[:, lanes] = d_key.astype(bf16)
    dv_s[:, lanes] = d_value.astype(bf16)

    @pl.when(pair == pairs - 1)
    def _():
        hidden = hidden_ref[...].astype(f32)
        gain_row = gain_attn_ref[...]
        normed_t = (hidden * rms_factor(hidden) * gain_row).astype(bf16).T
        d_query = dqt_s[...].T
        d_normed = dot(d_query, mats_ref[0], 1, 1)
        reblock(grid_shape, blocks_ref, 0, dot(normed_t, d_query).astype(bf16))
        d_normed = d_normed + dot(dk_s[...], mats_ref[1], 1, 1)
        reblock(grid_shape, blocks_ref, 1, dot(normed_t, dk_s[...]).astype(bf16))
        d_normed = d_normed + dot(dv_s[...], mats_ref[2], 1, 1)
        reblock(grid_shape, blocks_ref, 2, dot(normed_t, dv_s[...]).astype(bf16))
        d_hidden, d_gain = rms_pull(hidden, gain_row, d_normed)
        gga_ref[...] = d_gain
        grad_new = d_hidden + d_middle_s[...]
        grad_new_ref[...] = grad_new
        if spreads:
            spread_into(grad_new, *spread_in, *spread_out)


def attention_backward(
    d_back,
    slot_col,
    d_logits,
    grad_now,
    middle,
    hidden,
    gains,
    mats,
    q_k_v,
    attended,
    bias,
    lse,
    grid_shape,
    below=None,
    after=(),
):
    seq_len, width = hidden.shape
    heads = bias.shape[0]
    head_dim = width // heads
    experts = mats[1].shape[0]
    count_x, count_y = grid_shape
    ins = (
        d_back,
        slot_col,
        d_logits,
        grad_now,
        middle,
        hidden,
        *gains,
        *mats,
        *q_k_v,
        attended,
    )
    spreads = below is not None
    if spreads:
        ins = ins + tuple(below)
    row = jax.ShapeDtypeStruct((1, width), f32)
    outs = (
        jax.ShapeDtypeStruct((seq_len, width), f32),
        jax.ShapeDtypeStruct(
            (count_x // 2, 2, count_y // 2, 2, width // count_x, 4 * (width // count_y)), bf16
        ),
        jax.ShapeDtypeStruct((experts, width), f32),
        row,
        row,
        jax.ShapeDtypeStruct((heads // 2, 2, 2 * seq_len), f32),
    )
    if spreads:
        outs = outs + (
            jax.ShapeDtypeStruct((2 * seq_len, width), bf16),
            jax.ShapeDtypeStruct(d_logits.shape, bf16),
        )
    out_specs = whole_of(outs)
    out_specs[5] = pl.BlockSpec((1, 2, 2 * seq_len), lambda p: (p, 0, 0))
    return pl.pallas_call(
        partial(backward_kernel, head_dim, grid_shape, spreads, len(after)),
        grid=(heads // 2,),
        in_specs=whole_of(ins)
        + [
            pl.BlockSpec((2, seq_len, seq_len), lambda p: (p, 0, 0)),
            pl.BlockSpec((1, 2, seq_len), lambda p: (p, 0, 0)),
        ]
        + [any_spec] * len(after),
        out_specs=out_specs,
        out_shape=outs,
        scratch_shapes=[
            pltpu.VMEM((seq_len, width), bf16),
            pltpu.VMEM((seq_len, width), f32),
            pltpu.VMEM((width, seq_len), bf16),
            pltpu.VMEM((seq_len, width), bf16),
            pltpu.VMEM((seq_len, width), bf16),
            pltpu.VMEM((seq_len, seq_len), bf16),
            pltpu.VMEM((seq_len, seq_len), bf16),
        ],
        compiler_params=params(),
        cost_estimate=lasting(32),
        name="attention_backward",
    )(*ins, bias, lse, *after)


class Exchange:
    def __init__(self, members, rows, src, dst, send_sems, recv_sems):
        self.me = lax.axis_index("gy")
        self.bits = members.bit_length() - 1
        self.rows, self.src, self.dst = rows, src, dst
        self.send_sems, self.recv_sems = send_sems, recv_sems

    def block(self, index):
        return pl.ds(pl.multiple_of(index * self.rows, self.rows), self.rows)

    def copy(self, apart):
        peer = xor_of(self.me, apart, self.bits)
        return pltpu.make_async_remote_copy(
            src_ref=self.src.at[self.block(peer), :],
            dst_ref=self.dst.at[self.block(self.me), :],
            send_sem=self.send_sems.at[apart],
            recv_sem=self.recv_sems.at[apart],
            device_id={"gy": peer},
            device_id_type=MESH,
        )

    def keep_own(self):
        self.dst[self.block(self.me), :] = self.src[self.block(self.me), :]


def peers_along_gy(members):
    me = lax.axis_index("gy")
    bits = members.bit_length() - 1
    return [{"gy": xor_of(me, apart, bits)} for apart in range(1, members)]


def gelu_and_slope(pre):
    inner_scale = 0.7978845608028654
    square = pre * pre
    bent = jnp.tanh(inner_scale * pre * (1.0 + 0.044715 * square))
    act = 0.5 * pre * (1.0 + bent)
    slope = 0.5 * (1.0 + bent) + 0.5 * pre * (1.0 - bent * bent) * (
        inner_scale * (1.0 + 3 * 0.044715 * square)
    )
    return act, slope


def gelu_only(pre):
    inner_scale = 0.7978845608028654
    return 0.5 * pre * (1.0 + jnp.tanh(inner_scale * pre * (1.0 + 0.044715 * pre * pre)))


def chunk_of(members, rows):
    return max(1, min(members, 256 // rows))


def expert_forward_kernel(
    grid_shape,
    gathers,
    spreads,
    sent_ref,
    slot_col_ref,
    chosen_ref,
    logits_ref,
    middle_ref,
    win_ref,
    wout_ref,
    *refs,
):
    refs = list(refs)
    take = refs.pop
    column_ref = take(0) if gathers else None
    cotangent_ref, slot_row_ref = (take(0), take(0)) if spreads else (None, None)
    arrived_ref, comb_ref, out_ref = (take(0) for _ in range(3))
    full_ref = take(0) if gathers else None
    spread_out = [take(0) for _ in range(2)] if spreads else []
    win_s, wout_s, made_s, returned_s, w_sems = (take(0) for _ in range(5))
    send_sems, recv_sems, back_send_sems, back_recv_sems = (take(0) for _ in range(4))
    members = grid_shape[1]
    slots = sent_ref.shape[0]
    rows = slots // members
    group = chunk_of(members, rows)
    chunks = members // group
    chunk_bits = chunks.bit_length() - 1
    hidden_units = win_s.shape[1]
    tile = min(768, hidden_units)
    load_in = pltpu.make_async_copy(win_ref, win_s, w_sems.at[0])
    load_out = pltpu.make_async_copy(wout_ref, wout_s, w_sems.at[1])
    load_in.start()
    load_out.start()
    place = Place(grid_shape)
    more_peers = [place.core_peer()] + place.y_peers() if gathers else []
    greet(peers_along_gy(members) + more_peers)
    there = Exchange(members, rows, sent_ref, arrived_ref, send_sems, recv_sems)
    back = Exchange(members, rows, made_s, returned_s, back_send_sems, back_recv_sems)
    for apart in range(members - 1, 0, -1):
        there.copy(apart).start()
    there.keep_own()
    if gathers:
        own_sem, *sems = refs
        split = (full_ref.shape[4] - tile_rows) // 2
        own = pltpu.make_async_copy(
            column_ref, full_ref.at[place.y, place.c, :, place.x], own_sem
        )
        own.start()
        second = gather_second(place, column_ref, full_ref, split, sems)
        third = gather_third(place, full_ref, split, sems)
        fourth = gather_core(place, full_ref, sems)
        start_all(second)
    load_in.wait()
    load_out.wait()
    my_chunk = there.me // group

    def chunk_rows(index):
        start = xor_of(my_chunk, index, chunk_bits) * (group * rows)
        return pl.ds(pl.multiple_of(start, group * rows), group * rows)

    def work(index, first):
        for member in range(first, group):
            there.copy(index * group + member).wait_recv()
        here = chunk_rows(index)
        taken = arrived_ref[here, :]
        total = jnp.zeros((group * rows, taken.shape[1]), f32)
        for start in range(0, hidden_units, tile):
            units = slice(start, start + tile)
            act = gelu_only(dot(taken, win_s[:, units])).astype(bf16)
            total = total + dot(act, wout_s[:, units], 1, 1)
        made_s[here, :] = total.astype(bf16)
        for member in range(first, group):
            back.copy(index * group + member).start()

    work(0, 1)
    back.keep_own()
    half = chunks // 2

    @pl.loop(1, half)
    def _(index):
        work(index, 0)

    if gathers:
        own.wait()
        wait_all(second)
        start_all(third)

    @pl.loop(half, chunks)
    def _(index):
        work(index, 0)

    if gathers:
        wait_all(third)
        start_all(fourth)
    slot_col = slot_col_ref[...]
    comb_ref[...] = jnp.zeros_like(comb_ref)

    def gather_back(index, first):
        for member in range(first, group):
            back.copy(index * group + member).wait_recv()
        begin = xor_of(my_chunk, index, chunk_bits) * (group * rows)
        places = lax.broadcasted_iota(jnp.int32, (slot_col.shape[0], group * rows), 1) + begin
        placing = (places == slot_col).astype(f32).astype(bf16)
        comb_ref[...] += dot(placing, returned_s[chunk_rows(index), :])

    gather_back(0, 1)

    @pl.loop(1, chunks)
    def _(index):
        gather_back(index, 0)

    gate = jnp.sum(jax.nn.softmax(logits_ref[...], axis=-1) * chosen_ref[...], axis=1, keepdims=True)
    out_ref[...] = middle_ref[...] + gate * comb_ref[...]
    if spreads:
        spread_into(
            cotangent_ref[...].astype(f32), comb_ref, slot_row_ref, chosen_ref, logits_ref, *spread_out
        )
    if gathers:
        wait_all(fourth)

    @pl.loop(1, members)
    def _(apart):
        there.copy(apart).wait_send()
        back.copy(apart).wait_send()


def expert_forward(
    sent, slot_col, chosen_f, logits, middle, full_in, full_out, grid_shape, identifier, column=None, spread_from=None
):
    members = grid_shape[1]
    gathers, spreads = column is not None, spread_from is not None
    ins = [sent, slot_col, chosen_f, logits, middle, full_in, full_out]
    in_specs = [vmem_spec] * 5 + [any_spec] * 2
    outs = [
        jax.ShapeDtypeStruct(sent.shape, bf16),
        jax.ShapeDtypeStruct(middle.shape, f32),
        jax.ShapeDtypeStruct(middle.shape, f32),
    ]
    out_specs = [vmem_spec] * 3
    sems = pltpu.SemaphoreType.DMA((members,))
    scratch = [
        pltpu.VMEM(full_in.shape, bf16),
        pltpu.VMEM(full_out.shape, bf16),
        pltpu.VMEM(sent.shape, bf16),
        pltpu.VMEM(sent.shape, bf16),
        pltpu.SemaphoreType.DMA((2,)),
        sems,
        sems,
        sems,
        sems,
    ]
    if gathers:
        ins.append(column)
        in_specs.append(any_spec)
        half = (grid_shape[0] // 2, 2, grid_shape[1] // 2, 2)
        outs.append(jax.ShapeDtypeStruct((*half, *column.shape[1:]), bf16))
        out_specs.append(any_spec)
        others = pltpu.SemaphoreType.DMA((gather_copies(grid_shape)[1],))
        scratch += [pltpu.SemaphoreType.DMA, others, others]
    if spreads:
        ins += list(spread_from)
        in_specs += [vmem_spec] * 2
        outs += [
            jax.ShapeDtypeStruct(sent.shape, bf16),
            jax.ShapeDtypeStruct(logits.shape, bf16),
        ]
        out_specs += [vmem_spec] * 2
    return pl.pallas_call(
        partial(expert_forward_kernel, grid_shape, gathers, spreads),
        in_specs=in_specs,
        out_specs=out_specs,
        out_shape=outs,
        scratch_shapes=scratch,
        compiler_params=params(identifier),
        cost_estimate=lasting(75),
        name="expert_forward",
    )(*ins)


def expert_backward_kernel(
    members,
    d_sent_ref,
    arrived_ref,
    win_ref,
    wout_ref,
    d_back_ref,
    gin_ref,
    gout_ref,
    win_s,
    wout_s,
    d_arrived_s,
    d_rows_s,
    act_s,
    slope_s,
    w_sems,
    send_sems,
    recv_sems,
    back_send_sems,
    back_recv_sems,
):
    slots = d_sent_ref.shape[0]
    rows = slots // members
    group = chunk_of(members, rows)
    chunks = members // group
    chunk_bits = chunks.bit_length() - 1
    hidden_units = win_s.shape[1]
    tile = min(768, hidden_units)
    load_in = pltpu.make_async_copy(win_ref, win_s, w_sems.at[0])
    load_out = pltpu.make_async_copy(wout_ref, wout_s, w_sems.at[1])
    load_in.start()
    load_out.start()
    greet(peers_along_gy(members))
    there = Exchange(members, rows, d_sent_ref, d_arrived_s, send_sems, recv_sems)
    back = Exchange(members, rows, d_rows_s, d_back_ref, back_send_sems, back_recv_sems)
    for apart in range(members - 1, 0, -1):
        there.copy(apart).start()
    there.keep_own()
    my_chunk = there.me // group
    load_in.wait()

    @pl.loop(0, slots // 256)
    def _(index):
        here = pl.ds(pl.multiple_of(index * 256, 256), 256)
        taken = arrived_ref[here, :]
        for start in range(0, hidden_units, tile):
            units = slice(start, start + tile)
            act, slope = gelu_and_slope(dot(taken, win_s[:, units]))
            act_s[here, units] = act.astype(bf16)
            slope_s[here, units] = slope.astype(bf16)

    load_out.wait()

    def chunk_rows(index):
        start = xor_of(my_chunk, index, chunk_bits) * (group * rows)
        return pl.ds(pl.multiple_of(start, group * rows), group * rows)

    def work(index, first):
        for member in range(first, group):
            there.copy(index * group + member).wait_recv()
        here = chunk_rows(index)
        taken = d_arrived_s[here, :]
        total = jnp.zeros((group * rows, taken.shape[1]), f32)
        for start in range(0, hidden_units, tile):
            units = slice(start, start + tile)
            d_pre = (dot(taken, wout_s[:, units]) * slope_s[here, units].astype(f32)).astype(bf16)
            slope_s[here, units] = d_pre
            total = total + dot(d_pre, win_s[:, units], 1, 1)
        d_rows_s[here, :] = total.astype(bf16)
        for member in range(first, group):
            back.copy(index * group + member).start()

    work(0, 1)
    back.keep_own()

    @pl.loop(1, chunks)
    def _(index):
        work(index, 0)

    for lhs_ref, rhs_ref, out_ref in (
        (d_arrived_s, act_s, gout_ref),
        (arrived_ref, slope_s, gin_ref),
    ):
        lhs = lhs_ref[...].T

        @pl.loop(0, hidden_units // tile)
        def _(index, lhs=lhs, rhs_ref=rhs_ref, out_ref=out_ref):
            units = pl.ds(pl.multiple_of(index * tile, tile), tile)
            out_ref[:, units] = dot(lhs, rhs_ref[:, units]).astype(bf16)

    @pl.loop(1, members)
    def _(apart):
        back.copy(apart).wait_recv()
        there.copy(apart).wait_send()
        back.copy(apart).wait_send()


def expert_backward(d_sent, arrived, full_in, full_out, members, identifier):
    outs = (
        jax.ShapeDtypeStruct(d_sent.shape, bf16),
        jax.ShapeDtypeStruct(full_in.shape, bf16),
        jax.ShapeDtypeStruct(full_out.shape, bf16),
    )
    slots = d_sent.shape[0]
    sems = pltpu.SemaphoreType.DMA((members,))
    return pl.pallas_call(
        partial(expert_backward_kernel, members),
        in_specs=[vmem_spec] * 2 + [any_spec] * 2,
        out_specs=[vmem_spec] * 3,
        out_shape=outs,
        scratch_shapes=[
            pltpu.VMEM(full_in.shape, bf16),
            pltpu.VMEM(full_out.shape, bf16),
            pltpu.VMEM(d_sent.shape, bf16),
            pltpu.VMEM(d_sent.shape, bf16),
            pltpu.VMEM((slots, full_in.shape[1]), bf16),
            pltpu.VMEM((slots, full_in.shape[1]), bf16),
            pltpu.SemaphoreType.DMA((2,)),
            sems,
            sems,
            sems,
            sems,
        ],
        compiler_params=params(10 + identifier),
        cost_estimate=lasting(85),
        name="expert_backward",
    )(d_sent, arrived, full_in, full_out)


def body(
    hidden_in,
    route,
    piece_ids,
    buckets,
    rel_table,
    gain_attn,
    gain_ffn,
    w_query,
    w_key,
    w_value,
    w_output,
    w_router,
    w_in,
    w_out,
    cotangent,
):
    count_x = lax.axis_size("gx")
    count_y = lax.axis_size("gy")
    seq_len, width = hidden_in.shape
    layers = w_query.shape[0]
    heads = rel_table.shape[1]
    experts = w_router.shape[2] * count_y
    capacity = 2 * seq_len // experts
    wide_router = w_router.shape[2]
    tall, wide = w_query.shape[1], w_query.shape[2]
    grid_shape = (count_x, count_y)
    router_rows = jnp.pad(
        w_router.transpose(0, 2, 1), ((0, 0), (0, tile_rows - wide_router), (0, 4 * wide - tall))
    )
    buckets_col = jnp.pad(buckets, (0, 1), constant_values=-1)[:, None]
    mats, router, later, bias, slot_col, slot_row, chosen_f = start(
        (w_query, w_key, w_value, w_output),
        router_rows,
        buckets_col,
        rel_table.T,
        piece_ids,
        route,
        grid_shape,
    )
    gain_attn_f = gain_attn.astype(f32)
    gain_ffn_f = gain_ffn.astype(f32)

    hidden = hidden_in
    kept = []
    blocks = None
    for layer in range(layers):
        last = layer == layers - 1
        gains = (gain_attn_f[layer][None], gain_ffn_f[layer][None])
        (mats, router, q, k, v, attended, lse, middle, logits, sent), column = attention_forward(
            hidden,
            gains[0],
            gains[1],
            slot_row,
            bias,
            grid_shape,
            1 + layer,
            blocks=blocks,
            mats=(mats, router) if blocks is None else None,
            following=None if last else later[layer],
        )
        full_in = lax.all_gather(w_in[layer, 0], "gx", axis=1, tiled=True)
        full_out = lax.all_gather(w_out[layer, 0], "gx", axis=1, tiled=True)
        got = expert_forward(
            sent,
            slot_col,
            chosen_f,
            logits,
            middle,
            full_in,
            full_out,
            grid_shape,
            5 + layer,
            column=column,
            spread_from=(cotangent, slot_row) if last else None,
        )
        arrived, combined, hidden_next = got[:3]
        if last:
            d_sent, d_logits = got[3:]
        else:
            blocks = got[3]
        kept.append(
            (hidden, gains, (mats, router), (q, k, v), attended, lse, middle, logits, combined)
            + (arrived, full_in, full_out)
        )
        hidden = hidden_next

    grad_now = cotangent
    table_sums = None
    parts = []
    for layer in reversed(range(layers)):
        (prior, gains, mats, q_k_v, attended, lse, middle, logits, combined) = kept[layer][:9]
        (arrived, full_in, full_out) = kept[layer][9:]
        d_back, grad_in_full, grad_out_full = expert_backward(
            d_sent, arrived, full_in, full_out, count_y, layer
        )
        grad_out_part = lax.psum_scatter(grad_out_full, "gx", scatter_dimension=1, tiled=True)
        grad_in_part = lax.psum_scatter(grad_in_full, "gx", scatter_dimension=1, tiled=True)
        below = None
        if layer > 0:
            below = (kept[layer - 1][8], slot_row, chosen_f, kept[layer - 1][7])
        got = attention_backward(
            d_back,
            slot_col,
            d_logits,
            grad_now,
            middle,
            prior,
            gains,
            mats,
            q_k_v,
            attended,
            bias,
            lse,
            grid_shape,
            below=below,
            after=[array for part in parts for array in part[4:6]],
        )
        grad_now, blocked, gwr, gga, ggf, offset_sums = got[:6]
        if layer > 0:
            d_sent, d_logits = got[6:]
        table_sums = offset_sums if table_sums is None else table_sums + offset_sums
        parts.append((blocked, gwr, gga, ggf, grad_in_part, grad_out_part))
    parts = parts[::-1]
    bucket_onehot = (
        buckets_col == jnp.arange(rel_table.shape[0], dtype=jnp.int32)[None, :]
    ).astype(f32)
    d_table = jnp.dot(
        table_sums.reshape(heads, 2 * seq_len), bucket_onehot, precision=highest
    ).T
    buckets_count = rel_table.shape[0]
    small = jnp.concatenate(
        [part[1] for part in parts]
        + [part[2] for part in parts]
        + [part[3] for part in parts]
        + [jnp.pad(d_table.reshape(1, -1), ((0, 0), (0, width - d_table.size)))]
    )
    small = jnp.pad(small, ((0, -small.shape[0] % 8), (0, 0)))
    *attn_grads, small = final_sums([part[0] for part in parts], small, grid_shape, wide)
    router_sum = small[: layers * experts].reshape(layers, experts, width)
    base = layers * experts
    gga_all, ggf_all = small[base : base + layers], small[base + layers : base + 2 * layers]
    d_table = small[base + 2 * layers, : heads * buckets_count].reshape(buckets_count, heads)
    router_mine = lax.dynamic_slice(
        router_sum,
        (0, lax.axis_index("gy") * wide_router, lax.axis_index("gx") * tall),
        (layers, wide_router, tall),
    ).transpose(0, 2, 1)
    grad_in = jnp.stack([part[4] for part in parts]).astype(f32)[:, None]
    grad_out = jnp.stack([part[5] for part in parts]).astype(f32)[:, None]
    return (
        hidden,
        grad_now,
        d_table,
        gga_all,
        ggf_all,
        *attn_grads,
        router_mine,
        grad_in,
        grad_out,
    )


def solution(mesh):
    rows = P(("gx", "gy"), None)
    square = P(None, "gx", "gy")
    expert = P(None, "gy", None, "gx")
    return jax.shard_map(
        body,
        mesh=mesh,
        in_specs=(rows, rows, P(("gx", "gy")), P(), P(), P(), P())
        + (square,) * 5
        + (expert, expert, rows),
        out_specs=(rows, rows, P(), P(), P()) + (square,) * 5 + (expert, expert),
        check_vma=False,
    )
```

```python
from functools import partial

import jax
import jax.numpy as jnp
from jax import lax
from jax.experimental import pallas as pl
from jax.experimental.pallas import tpu as pltpu
from jax.sharding import PartitionSpec as P

eps_norm = 1e-06
highest = lax.Precision.HIGHEST
f32 = jnp.float32
bf16 = jnp.bfloat16
masked_out = -1e30
tile_rows = 16
MESH = pl.DeviceIdType.MESH
vmem_spec = pl.BlockSpec(memory_space=pltpu.VMEM)
any_spec = pl.BlockSpec(memory_space=pl.ANY)
vmem_bytes = 56 * 1024 * 1024


def whole(shape):
    zeros = (0,) * len(shape)
    return pl.BlockSpec(shape, lambda *_: zeros, pipeline_mode=pl.Buffered(1))


def whole_of(arrays):
    return [whole(array.shape) for array in arrays]


def params(identifier=None):
    if identifier is None:
        return pltpu.CompilerParams(vmem_limit_bytes=vmem_bytes)
    return pltpu.CompilerParams(
        vmem_limit_bytes=vmem_bytes, collective_id=identifier, has_side_effects=True
    )


def lasting(microseconds):
    return pl.CostEstimate(
        flops=int(microseconds * 1e9), bytes_accessed=1 << 20, transcendentals=0
    )


def dot(lhs, rhs, lhs_dim=1, rhs_dim=0):
    return lax.dot_general(
        lhs, rhs, (((lhs_dim,), (rhs_dim,)), ((), ())), preferred_element_type=f32
    )


def rms_factor(hidden):
    return lax.rsqrt(jnp.mean(hidden * hidden, axis=-1, keepdims=True) + eps_norm)


def rms_pull(hidden, gain_row, d_normed):
    factor = rms_factor(hidden)
    scaled = gain_row * d_normed
    inner = jnp.mean(hidden * scaled, axis=-1, keepdims=True)
    d_hidden = factor * scaled - hidden * (factor * factor * factor * inner)
    d_gain = jnp.sum(d_normed * hidden * factor, axis=0, keepdims=True)
    return d_hidden, d_gain


def xor_of(index, other, bits):
    total = 0
    for bit in range(bits):
        power = 1 << bit
        total = total + ((index // power + other // power) % 2) * power
    return total


def placing_rows(slot_row, slots):
    places = lax.broadcasted_iota(jnp.int32, (slots, slot_row.shape[1]), 0)
    return (places == slot_row).astype(f32).astype(bf16)


def placing_cols(slot_col, slots):
    places = lax.broadcasted_iota(jnp.int32, (slot_col.shape[0], slots), 1)
    return (places == slot_col).astype(f32).astype(bf16)


def greet(peers):
    barrier = pltpu.get_barrier_semaphore()
    for peer in peers:
        pl.semaphore_signal(barrier, inc=1, device_id=peer, device_id_type=MESH)
    pl.semaphore_wait(barrier, len(peers))


def bits_of(count):
    return count.bit_length() - 1


class Place:
    def __init__(self, grid_shape):
        self.count_y, self.count_z = grid_shape[0] // 2, grid_shape[1] // 2
        first, second = lax.axis_index("gx"), lax.axis_index("gy")
        self.c, self.y = first % 2, first // 2
        self.x, self.z = second % 2, second // 2

    def core_peer(self):
        return {"gx": self.y * 2 + 1 - self.c}

    def x_peer(self):
        return {"gy": self.z * 2 + 1 - self.x}

    def y_at(self, apart):
        return xor_of(self.y, apart, bits_of(self.count_y))

    def y_peer(self, apart):
        return {"gx": self.y_at(apart) * 2 + self.c}

    def y_peers(self):
        return [self.y_peer(apart) for apart in range(1, self.count_y)]

    def z_at(self, apart):
        return xor_of(self.z, apart, bits_of(self.count_z))

    def z_peer(self, apart):
        return {"gy": self.z_at(apart) * 2 + self.x}

    def z_peers(self):
        return [self.z_peer(apart) for apart in range(1, self.count_z)]


def send(src, dst, sems, index, peer):
    return pltpu.make_async_remote_copy(
        src_ref=src,
        dst_ref=dst,
        send_sem=sems[0].at[index],
        recv_sem=sems[1].at[index],
        device_id=peer,
        device_id_type=MESH,
    )


def start_all(copies):
    for copy in copies:
        copy.start()


def wait_all(copies):
    for copy in copies:
        copy.wait()


def gather_z(place, src, landing, sems):
    return [
        send(src, landing, sems, apart - 1, place.z_peer(apart)) for apart in range(1, place.count_z)
    ]


def gather_copies(grid_shape):
    return grid_shape[1] // 2 - 1, 2 * (grid_shape[0] // 2 - 1) + 3


def gather_second(place, column, full, split, sems):
    y, c, x = place.y, place.c, place.x
    upper, lower = pl.ds(0, split), pl.ds(split, full.shape[4] - split)
    copies = [
        send(column.at[:, upper], full.at[y, c, :, x, upper], sems, 0, place.x_peer())
    ]
    for apart in range(1, place.count_y):
        copies.append(
            send(column.at[:, lower], full.at[y, c, :, x, lower], sems, apart, place.y_peer(apart))
        )
    return copies


def gather_third(place, full, split, sems):
    y, c, x = place.y, place.c, place.x
    upper, lower = pl.ds(0, split), pl.ds(split, full.shape[4] - split)
    base = place.count_y
    ref = full.at[:, c, :, x, lower]
    copies = [send(ref, ref, sems, base, place.x_peer())]
    ref = full.at[y, c, :, :, upper]
    for apart in range(1, place.count_y):
        copies.append(send(ref, ref, sems, base + apart, place.y_peer(apart)))
    return copies


def gather_core(place, full, sems):
    ref = full.at[:, place.c]
    return [send(ref, ref, sems, 2 * place.count_y, place.core_peer())]


def whole_blocks(shape, split):
    count_y, _, count_z, _, tall, lanes = shape
    low = tall - split
    return [
        (count_y, count_z, 2, tall, lanes),
        (count_y - 1, count_z, 2, split, lanes),
        (count_y, count_z, low, lanes),
        (count_z, split, lanes),
        (count_y - 1, count_z, low, lanes),
        (count_z - 1, split, lanes),
        (count_z - 1, low, lanes),
    ]


def scatter_copies(grid_shape):
    return 1 + 2 * (grid_shape[0] // 2) + 2 * (grid_shape[1] // 2 - 1)


def add_low(dst, dst_at, *terms):
    total = terms[0].astype(f32)
    for term in terms[1:]:
        total = total + term.astype(f32)
    dst[dst_at] = total.astype(bf16)


class Scatter:
    def __init__(self, place, src, landings, sems, split):
        self.place, self.src, self.sems = place, src, sems
        self.first, self.up2, self.low2, self.up3, self.low3, self.up4, self.low4 = landings
        tall = src.shape[4]
        self.upper, self.lower = pl.ds(0, split), pl.ds(split, tall - split)

    def copies(self, stage):
        at, sems = self.place, self.sems
        count_y, count_z = at.count_y, at.count_z
        if stage == 0:
            return [send(self.src.at[:, 1 - at.c], self.first, sems, 0, at.core_peer())]
        if stage == 1:
            copies = [send(self.first.at[:, :, 1 - at.x, self.lower], self.low2, sems, 1, at.x_peer())]
            for apart in range(1, count_y):
                src = self.first.at[at.y_at(apart), :, :, self.upper]
                dst = self.up2.at[apart - 1]
                copies.append(send(src, dst, sems, 1 + apart, at.y_peer(apart)))
            return copies
        if stage == 2:
            base = 1 + count_y
            copies = [send(self.up2.at[0, :, 1 - at.x], self.up3, sems, base, at.x_peer())]
            for apart in range(1, count_y):
                src, dst = self.low2.at[at.y_at(apart)], self.low3.at[apart - 1]
                copies.append(send(src, dst, sems, base + apart, at.y_peer(apart)))
            return copies
        base = 2 * count_y
        copies = []
        for apart in range(1, count_z):
            there = at.z_at(apart)
            for src, dst, more in (
                (self.up3.at[there], self.up4.at[apart - 1], 0),
                (self.low3.at[0, there], self.low4.at[apart - 1], 1),
            ):
                index = base + 2 * apart - 1 + more
                copies.append(send(src, dst, sems, index, at.z_peer(apart)))
        return copies

    def add(self, stage):
        at = self.place
        count_y, count_z = at.count_y, at.count_z
        if stage == 0:

            @pl.loop(0, count_y * count_z)
            def _(index):
                y, z = index // count_z, index % count_z
                add_low(self.first, (y, z), self.first[y, z], self.src[y, at.c, z])

        elif stage == 1:

            @pl.loop(0, count_z)
            def _(z):
                for x in range(2):
                    terms = [self.up2[apart, z, x] for apart in range(count_y - 1)]
                    add_low(self.up2, (0, z, x), self.first[at.y, z, x, self.upper], *terms)

                @pl.loop(0, count_y)
                def _(y):
                    add_low(self.low2, (y, z), self.first[y, z, at.x, self.lower], self.low2[y, z])

        elif stage == 2:

            @pl.loop(0, count_z)
            def _(z):
                add_low(self.up3, (z,), self.up3[z], self.up2[0, z, at.x])
                terms = [self.low3[apart, z] for apart in range(count_y - 1)]
                add_low(self.low3, (0, z), self.low2[at.y, z], *terms)

    def result(self):
        at = self.place
        upper, lower = self.up3[at.z].astype(f32), self.low3[0, at.z].astype(f32)
        for apart in range(at.count_z - 1):
            upper = upper + self.up4[apart].astype(f32)
            lower = lower + self.low4[apart].astype(f32)
        return upper, lower


class SmallSum:
    def __init__(self, grid_shape, totals, landing, sems):
        self.totals, self.landing, self.sems = totals, landing, sems
        self.peers = []
        for name, count in (("gx", grid_shape[0]), ("gy", grid_shape[1])):
            me = lax.axis_index(name)
            for bit in range(bits_of(count)):
                self.peers.append({name: xor_of(me, 1 << bit, bits_of(count))})
        self.done = 0

    def copy(self):
        step = self.done
        return send(self.totals.at[step], self.landing.at[step], self.sems, step, self.peers[step])

    def begin(self):
        self.copy().start()

    def advance(self):
        if self.done == len(self.peers):
            return
        self.copy().wait()
        step = self.done
        self.totals[step + 1] = self.totals[step] + self.landing[step]
        self.done += 1
        if self.done < len(self.peers):
            self.begin()


def small_steps(grid_shape):
    return bits_of(grid_shape[0]) + bits_of(grid_shape[1])


def final_kernel(grid_shape, layers, buckets_count, *refs):
    refs = list(refs)
    take = refs.pop
    blocks_ref = take(0)
    partial_refs = [(take(0), take(0)) for _ in range(layers - 1)]
    router_refs, gga_refs, ggf_refs, offset_refs = ([take(0) for _ in range(layers)] for _ in range(4))
    buckets_ref, slot_col_ref, chosen_ref, logits_ref, middle_ref = (take(0) for _ in range(5))
    first_ref, second_ref = take(0), take(0)
    outs = [take(0) for _ in range(4)]
    small_out_ref, result_ref = take(0), take(0)
    landings = [take(0) for _ in range(7)]
    z_landings = [(take(0), take(0)) for _ in range(layers - 1)]
    totals, landing, returned_s = take(0), take(0), take(0)
    sems = [(take(0), take(0)) for _ in range(layers)]
    small_sems, collect_sems = (take(0), take(0)), take(0)
    place = Place(grid_shape)
    tall, wide = outs[0].shape[1:]
    split = tall // 2
    members = grid_shape[1]
    slots = returned_s.shape[0]
    upper_layers = []
    for layer in range(1, layers):
        upper, lower = partial_refs[layer - 1]
        places = (None, None, None, upper, lower, *z_landings[layer - 1])
        upper_layers.append(Scatter(place, blocks_ref, places, sems[layer], split))
    lowest = Scatter(place, blocks_ref, landings, sems[0], split)
    collected = collect(
        lax.axis_index("gy"), members, slots // members, first_ref, second_ref, returned_s, collect_sems
    )
    start_all(collected)
    greet([place.core_peer(), place.x_peer()] + place.y_peers() + place.z_peers())
    start_all(lowest.copies(0))
    for one in upper_layers:
        start_all(one.copies(3))

    experts = router_refs[0].shape[0]
    totals[0] = jnp.zeros(totals.shape[1:], f32)
    row = 0
    for refs_of in (router_refs, gga_refs, ggf_refs):
        for ref in refs_of:
            totals[0, row : row + ref.shape[0], :] = ref[...]
            row += ref.shape[0]
    heads = offset_refs[0].shape[0]
    offsets = offset_refs[0][...]
    for ref in offset_refs[1:]:
        offsets = offsets + ref[...]
    in_bucket = (
        lax.broadcasted_iota(jnp.int32, (buckets_count, offsets.shape[1]), 0) == buckets_ref[...]
    ).astype(f32)
    totals[0, row : row + heads, :buckets_count] = lax.dot_general(
        offsets, in_bucket, (((1,), (1,)), ((), ())), precision=highest, preferred_element_type=f32
    )
    small = SmallSum(grid_shape, totals, landing, small_sems)
    small.begin()
    wait_all(lowest.copies(0))
    lowest.add(0)
    start_all(lowest.copies(1))
    small.advance()
    wait_all(collected)
    placing = placing_cols(slot_col_ref[...], slots)
    gate = jnp.sum(jax.nn.softmax(logits_ref[...], axis=-1) * chosen_ref[...], axis=1, keepdims=True)
    result_ref[...] = middle_ref[...] + gate * dot(placing, returned_s[...])
    small.advance()
    wait_all(lowest.copies(1))
    lowest.add(1)
    start_all(lowest.copies(2))
    small.advance()

    def finish(layer, one):
        for part, rows in zip(one.result(), (slice(0, split), slice(split, tall))):
            for which in range(4):
                outs[which][layer, rows, :] = part[:, which * wide : (which + 1) * wide]

    for layer, one in enumerate(upper_layers):
        wait_all(one.copies(3))
        finish(layer + 1, one)
    wait_all(lowest.copies(2))
    lowest.add(2)
    start_all(lowest.copies(3))
    while small.done < len(small.peers):
        small.advance()
    small_out_ref[...] = totals[len(small.peers)]
    wait_all(lowest.copies(3))
    finish(0, lowest)


def final_sums(blocks, partials, smalls, finishing, returned, grid_shape, wide, buckets_count):
    layers = len(partials) + 1
    shape = blocks.shape
    tall = shape[4]
    width = finishing[-1].shape[1]
    landings = [pltpu.VMEM(one, bf16) for one in whole_blocks(shape, tall // 2)]
    steps = small_steps(grid_shape)
    rows = sum(one.shape[0] for one in smalls[: 3 * layers]) + smalls[3 * layers].shape[0]
    small_shape = (rows + -rows % 8, width)
    sems = pltpu.SemaphoreType.DMA((scatter_copies(grid_shape),))
    small_sems = pltpu.SemaphoreType.DMA((steps,))
    outs = [jax.ShapeDtypeStruct((layers, tall, wide), f32)] * 4
    outs += [jax.ShapeDtypeStruct(small_shape, f32), jax.ShapeDtypeStruct(finishing[-1].shape, f32)]
    ins = [blocks, *[array for pair in partials for array in pair], *smalls, *finishing]
    return pl.pallas_call(
        partial(final_kernel, grid_shape, layers, buckets_count),
        in_specs=[vmem_spec] * len(ins) + [any_spec] * 2,
        out_specs=[vmem_spec] * len(outs),
        out_shape=outs,
        scratch_shapes=landings
        + landings[5:] * (layers - 1)
        + [pltpu.VMEM((steps + 1, *small_shape), f32), pltpu.VMEM((steps, *small_shape), f32)]
        + [pltpu.VMEM(returned[0].shape, bf16)]
        + [sems, sems] * layers
        + [small_sems, small_sems, pltpu.SemaphoreType.DMA((grid_shape[1],))],
        compiler_params=params(24),
        cost_estimate=lasting(60),
        name="final_sums",
    )(*ins, *returned)


def unblock(grid_shape, blocks_ref, mats_ref, router_ref):
    count_x, count_y = grid_shape
    tall = mats_ref.shape[1] // count_x
    wide = mats_ref.shape[2] // count_y
    router_rows = []
    for first in range(count_x):
        spots = [(first // 2, first % 2, second // 2, second % 2) for second in range(count_y)]
        rows = slice(first * tall, (first + 1) * tall)
        for which in range(4):
            lanes = slice(which * wide, (which + 1) * wide)
            mats_ref[which, rows, :] = jnp.concatenate(
                [blocks_ref[(*spot, slice(0, tall), lanes)] for spot in spots], axis=1
            )
        router_rows.append(
            jnp.concatenate(
                [blocks_ref[(*spot, slice(tall, tall + 1), slice(0, tall))] for spot in spots],
                axis=0,
            )
        )
    router_ref[...] = jnp.concatenate(router_rows, axis=1)


def turned(row):
    return jnp.broadcast_to(row, (128, row.shape[1])).T[:, 0:1]


def start_kernel(
    grid_shape,
    wq_ref,
    wk_ref,
    wv_ref,
    wo_ref,
    router_rows_ref,
    buckets_ref,
    table_ref,
    piece_row_ref,
    route_row_ref,
    cotangent_ref,
    mats_ref,
    router_ref,
    later_ref,
    bias_ref,
    slot_col_ref,
    slot_row_ref,
    chosen_ref,
    spread_ref,
    full_s,
    column_s,
    later_send,
    later_recv,
    z_send,
    z_recv,
    send_sems,
    recv_sems,
):
    place = Place(grid_shape)
    layers, tall, wide = wq_ref.shape
    split = tall // 2
    y, c, z, x = place.y, place.c, place.z, place.x

    def packed(layer):
        return jnp.concatenate([ref[layer] for ref in (wq_ref, wk_ref, wv_ref, wo_ref)], axis=1)

    column_s[z, :tall] = packed(0)
    column_s[z, tall:] = router_rows_ref[0]
    greet([place.core_peer(), place.x_peer()] + place.y_peers() + place.z_peers())
    first = gather_z(place, column_s.at[z], column_s.at[z], (z_send, z_recv))
    start_all(first)
    along_z = []
    for layer in range(1, layers):
        later_ref[layer - 1, z, :tall] = packed(layer)
        later_ref[layer - 1, z, tall:] = router_rows_ref[layer]
        mine = later_ref.at[layer - 1, z]
        along_z += gather_z(place, mine, mine, (later_send.at[layer - 1], later_recv.at[layer - 1]))

    seq_len, experts = chosen_ref.shape
    capacity = 2 * seq_len // experts
    heads = bias_ref.shape[0]
    buckets_count = table_ref.shape[1]
    in_bucket = (
        lax.broadcasted_iota(jnp.int32, (buckets_count, 2 * seq_len), 0) == buckets_ref[...]
    )
    offsets = dot(table_ref[...], in_bucket.astype(f32).astype(bf16))
    key_pos = lax.broadcasted_iota(jnp.int32, (seq_len, seq_len), 0)
    query_pos = lax.broadcasted_iota(jnp.int32, (seq_len, seq_len), 1)
    route_row, piece_row = route_row_ref[...], piece_row_ref[...]
    route_col, piece_col = turned(route_row), turned(piece_row)
    chosen = (lax.broadcasted_iota(jnp.int32, (seq_len, experts), 1) == route_col).astype(f32)
    chosen_t = (lax.broadcasted_iota(jnp.int32, (experts, seq_len), 0) == route_row).astype(f32)
    chosen_ref[...] = chosen
    earlier = (key_pos < query_pos).astype(f32).astype(bf16)
    before_t = dot(chosen_t.astype(bf16), earlier)
    rank_row = jnp.sum(before_t * chosen_t, axis=0, keepdims=True)
    slot_row_ref[...] = route_row * capacity + rank_row.astype(jnp.int32)
    later = (key_pos > query_pos).astype(f32).astype(bf16)
    before = dot(later, chosen.astype(bf16))
    rank_col = jnp.sum(before * chosen, axis=1, keepdims=True)
    slot_col_ref[...] = route_col * capacity + rank_col.astype(jnp.int32)
    placing = placing_rows(slot_row_ref[...], spread_ref.shape[0])
    spread_ref[...] = dot(placing, cotangent_ref[...]).astype(bf16)

    same = (piece_col == piece_row) & (piece_col > 0)
    allowed = (key_pos <= query_pos) | same

    def bias_for(head):
        row = jnp.broadcast_to(offsets[head : head + 1], (seq_len, 2 * seq_len))
        shifted = pltpu.roll(row, seq_len + 1, 1, stride=1, stride_axis=0)[:, :seq_len]
        bias_ref[head] = jnp.where(allowed, shifted, masked_out).astype(bf16)

    for head in range(heads // 2):
        bias_for(head)
    wait_all(first)
    sems = (send_sems, recv_sems)
    second = gather_second(place, column_s, full_s, split, sems)
    start_all(second)
    start_all(along_z)
    full_s[y, c, :, x] = column_s[...]
    for head in range(heads // 2, heads):
        bias_for(head)
    wait_all(second)
    third = gather_third(place, full_s, split, sems)
    start_all(third)

    wait_all(third)
    fourth = gather_core(place, full_s, sems)
    start_all(fourth)
    wait_all(fourth)
    unblock(grid_shape, full_s, mats_ref, router_ref)
    wait_all(along_z)


def start(mats, router_rows, buckets, table_t, piece_ids, route, cotangent, grid_shape):
    layers, tall, wide = mats[0].shape
    seq_len = piece_ids.shape[0]
    heads = table_t.shape[0]
    width = tall * grid_shape[0]
    experts = grid_shape[1]
    block = (router_rows.shape[1] + tall, 4 * wide)
    half = (grid_shape[0] // 2, 2, grid_shape[1] // 2, 2)
    ins = (
        *mats,
        router_rows,
        buckets,
        table_t,
        piece_ids[None, :],
        route.reshape(1, seq_len),
        cotangent,
    )
    outs = (
        jax.ShapeDtypeStruct((4, width, width), bf16),
        jax.ShapeDtypeStruct((experts, width), bf16),
        jax.ShapeDtypeStruct((layers - 1, half[2], *block), bf16),
        jax.ShapeDtypeStruct((heads, seq_len, seq_len), bf16),
        jax.ShapeDtypeStruct((seq_len, 1), jnp.int32),
        jax.ShapeDtypeStruct((1, seq_len), jnp.int32),
        jax.ShapeDtypeStruct((seq_len, experts), f32),
        jax.ShapeDtypeStruct((2 * seq_len, width), bf16),
    )
    along_z, others = gather_copies(grid_shape)
    return pl.pallas_call(
        partial(start_kernel, grid_shape),
        in_specs=[vmem_spec] * len(ins),
        out_specs=[vmem_spec] * len(outs),
        out_shape=outs,
        scratch_shapes=[
            pltpu.VMEM((*half, *block), bf16),
            pltpu.VMEM((half[2], *block), bf16),
            pltpu.SemaphoreType.DMA((layers - 1, along_z)),
            pltpu.SemaphoreType.DMA((layers - 1, along_z)),
            pltpu.SemaphoreType.DMA((along_z,)),
            pltpu.SemaphoreType.DMA((along_z,)),
            pltpu.SemaphoreType.DMA((others,)),
            pltpu.SemaphoreType.DMA((others,)),
        ],
        compiler_params=params(0),
        cost_estimate=lasting(45),
        name="start",
    )(*ins)


def half_masks(rows, width):
    lane = lax.broadcasted_iota(jnp.int32, (rows, width), 1)
    return lane < (width // 2)


def gates_of(logits, slot_col, chosen, gates_ref):
    experts = gates_ref.shape[0]
    seq_len = slot_col.shape[0]
    capacity = 2 * seq_len // experts
    gate = jnp.sum(jax.nn.softmax(logits, axis=-1) * chosen, axis=1, keepdims=True)
    places = lax.broadcasted_iota(jnp.int32, (seq_len, 2 * seq_len), 1)
    row = jnp.sum(jnp.where(places == slot_col, gate, 0.0), axis=0, keepdims=True)
    gates_ref[...] = jnp.zeros_like(gates_ref)
    for expert in range(experts):
        mine = row[:, expert * capacity : (expert + 1) * capacity]
        gates_ref[expert, :, :capacity] = jnp.broadcast_to(mine, (gates_ref.shape[1], capacity))


def forward_kernel(
    head_dim,
    grid_shape,
    blocked,
    last,
    hidden_ref,
    gain_attn_ref,
    gain_ffn_ref,
    slot_row_ref,
    slot_col_ref,
    chosen_ref,
    *refs,
):
    refs = list(refs)
    take = refs.pop
    blocks_ref = take(0) if blocked else None
    mats_ref, router_ref = (None, None) if blocked else (take(0), take(0))
    spread_ref = take(0)
    bias_ref = take(0)
    if blocked:
        mats_ref, router_ref = take(0), take(0)
    q_ref, k_ref, v_ref, att_ref, lse_ref, middle_ref, logits_ref, sent_ref = (
        take(0) for _ in range(8)
    )
    gates_ref = take(0) if last else None
    far_ref, send_sems, recv_sems, own_sem = refs
    pair, pairs = pl.program_id(0), pl.num_programs(0)
    seq_len = hidden_ref.shape[0]
    width = 2 * head_dim
    step = min(256, seq_len)

    members = grid_shape[1]
    spread = Exchange(members, spread_ref.shape[0] // members, spread_ref, far_ref, send_sems, recv_sems)
    mine = spread.block(spread.me)
    own = None
    if not last:
        own = pltpu.make_async_copy(spread_ref.at[mine, :], far_ref.at[mine, :], own_sem)
    aparts = part_of(members, not last)

    @pl.when(pair == 0)
    def _():
        greet([spread.peer(apart) for apart in aparts])
        start_all([spread.copy(apart) for apart in aparts])
        if not last:
            own.start()

    @pl.when(pair == 0)
    def _():
        if blocked:
            unblock(grid_shape, blocks_ref, mats_ref, router_ref)
        hidden = hidden_ref[...].astype(f32)
        normed = (hidden * rms_factor(hidden) * gain_attn_ref[...]).astype(bf16)
        q_ref[...] = dot(normed, mats_ref[0]).astype(bf16)
        k_ref[...] = dot(normed, mats_ref[1]).astype(bf16)
        v_ref[...] = dot(normed, mats_ref[2]).astype(bf16)

    lanes = pl.ds(pl.multiple_of(pair * width, width), width)
    q2 = q_ref[:, lanes] * jnp.asarray(head_dim**-0.5, bf16)
    k2 = k_ref[:, lanes]
    v2t = v_ref[:, lanes].T
    first = half_masks(seq_len, width)
    for half in range(2):
        q_one = jnp.where(first if half == 0 else ~first, q2, jnp.zeros_like(q2))
        v_one = v2t[half * head_dim : (half + 1) * head_dim]
        for begin in range(0, seq_len, step):
            cols = slice(begin, begin + step)
            scores = dot(k2, q_one[cols], 1, 1) + bias_ref[half, :, cols].astype(f32)
            top = jnp.max(scores, axis=0, keepdims=True)
            raised = jnp.exp(scores - top)
            total = jnp.sum(raised, axis=0, keepdims=True)
            probs = (raised * (1.0 / total)).astype(bf16)
            rows = pl.ds(pl.multiple_of(pair * width + half * head_dim, head_dim), head_dim)
            att_ref[rows, cols] = dot(v_one, probs).astype(bf16)
            lse_ref[0, half : half + 1, cols] = top + jnp.log(total)

    @pl.when(pair == pairs - 1)
    def _():
        middle = hidden_ref[...].astype(f32) + dot(att_ref[...].T, mats_ref[3])
        middle_ref[...] = middle
        ffn_in = (middle * rms_factor(middle) * gain_ffn_ref[...]).astype(bf16)
        logits = dot(ffn_in, router_ref[...], 1, 1)
        logits_ref[...] = logits
        if gates_ref is not None:
            gates_of(logits, slot_col_ref[...], chosen_ref[...], gates_ref)
        placing = placing_rows(slot_row_ref[...], sent_ref.shape[0])
        sent_ref[...] = dot(placing, ffn_in).astype(bf16)

    @pl.when(pair == pairs - 1)
    def _():
        wait_all([spread.copy(apart) for apart in aparts])
        if not last:
            own.wait()


def attention_forward(
    hidden,
    gain_attn,
    gain_ffn,
    slots_and_chosen,
    bias,
    grid_shape,
    identifier,
    spread,
    last,
    blocks=None,
    mats=None,
):
    seq_len, width = hidden.shape
    heads = bias.shape[0]
    head_dim = width // heads
    slots = 2 * seq_len
    experts = grid_shape[1]
    blocked = blocks is not None
    ins = [hidden, gain_attn, gain_ffn, *slots_and_chosen] + ([blocks] if blocked else list(mats))
    in_specs = whole_of(ins)
    ins.append(spread)
    in_specs.append(any_spec)
    ins.append(bias)
    in_specs.append(pl.BlockSpec((2, seq_len, seq_len), lambda p: (p, 0, 0)))
    tall = jax.ShapeDtypeStruct((seq_len, width), bf16)
    outs = [
        tall,
        tall,
        tall,
        jax.ShapeDtypeStruct((width, seq_len), bf16),
        jax.ShapeDtypeStruct((heads // 2, 2, seq_len), f32),
        jax.ShapeDtypeStruct((seq_len, width), f32),
        jax.ShapeDtypeStruct((seq_len, experts), f32),
        jax.ShapeDtypeStruct((slots, width), bf16),
    ]
    if last:
        outs.append(jax.ShapeDtypeStruct((experts, 8, max(128, slots // experts)), f32))
    out_specs = whole_of(outs)
    out_specs[4] = pl.BlockSpec((1, 2, seq_len), lambda p: (p, 0, 0))
    if blocked:
        more = [
            jax.ShapeDtypeStruct((4, width, width), bf16),
            jax.ShapeDtypeStruct((experts, width), bf16),
        ]
        outs = more + outs
        out_specs = whole_of(more) + out_specs
    outs.append(jax.ShapeDtypeStruct(spread.shape, bf16))
    out_specs.append(any_spec)
    sems = pltpu.SemaphoreType.DMA((experts,))
    scratch = [sems, sems, pltpu.SemaphoreType.DMA]
    got = pl.pallas_call(
        partial(forward_kernel, head_dim, grid_shape, blocked, last),
        grid=(heads // 2,),
        in_specs=in_specs,
        out_specs=out_specs,
        out_shape=outs,
        scratch_shapes=scratch,
        compiler_params=params(identifier),
        cost_estimate=lasting(25),
        name="attention_forward",
    )(*ins)
    return tuple(got) if blocked else tuple(mats) + tuple(got)


def diagonal_fold(values, seq_len):
    rows, wide = seq_len, 2 * seq_len
    folded = None
    tile = 128
    count = seq_len // tile
    for row_tile in range(count):
        piece = values[row_tile * tile : (row_tile + 1) * tile].astype(f32)
        before = (count - 1 - row_tile) * tile
        after = wide - seq_len - before
        parts = []
        if before:
            parts.append(jnp.zeros((tile, before), f32))
        parts.append(piece)
        if after:
            parts.append(jnp.zeros((tile, after), f32))
        padded = jnp.concatenate(parts, axis=1)
        folded = padded if folded is None else folded + padded
    rows = tile
    while rows > 1:
        rows //= 2
        folded = pltpu.roll(folded[:rows], rows, 1) + folded[rows:]
    return folded


def reblock(grid_shape, blocks_ref, which, values):
    count_x, count_y = grid_shape
    tall = values.shape[0] // count_x
    wide = values.shape[1] // count_y
    for first in range(count_x):
        for second in range(count_y):
            spot = (first // 2, first % 2, second // 2, second % 2)
            lanes = slice(which * wide, (which + 1) * wide)
            blocks_ref[(*spot, slice(None), lanes)] = values[
                first * tall : (first + 1) * tall, second * wide : (second + 1) * wide
            ]


def d_logits_of(d_gate, logits, chosen):
    shares = jax.nn.softmax(logits, axis=-1)
    gate = jnp.sum(shares * chosen, axis=1, keepdims=True)
    return (d_gate * shares * (chosen - gate)).astype(bf16)


def spread_into(grad_now, comb_ref, slot_row_ref, chosen_ref, logits_ref, d_sent_ref, d_logits_ref):
    d_gate = jnp.sum(grad_now * comb_ref[...], axis=1, keepdims=True)
    logits, chosen = logits_ref[...], chosen_ref[...]
    d_logits_ref[...] = d_logits_of(d_gate, logits, chosen)
    gate = jnp.sum(jax.nn.softmax(logits, axis=-1) * chosen, axis=1, keepdims=True)
    placing = placing_rows(slot_row_ref[...], d_sent_ref.shape[0])
    d_sent_ref[...] = dot(placing, (gate * grad_now).astype(bf16)).astype(bf16)


def backward_kernel(
    head_dim,
    grid_shape,
    spreads,
    returns,
    unread,
    d_back_ref,
    slot_col_ref,
    d_logits_ref,
    grad_ref,
    middle_ref,
    hidden_ref,
    gain_attn_ref,
    gain_ffn_ref,
    mats_ref,
    router_ref,
    q_ref,
    k_ref,
    v_ref,
    att_ref,
    *refs,
):
    refs = list(refs)
    take = refs.pop
    spread_in = [take(0) for _ in range(4)] if spreads else []
    bias_ref, lse_ref = take(0), take(0)
    made_ref = take(0)
    del refs[:unread]
    grad_new_ref, blocks_ref, gwr_ref, gga_ref, ggf_ref, offsets_ref = (take(0) for _ in range(6))
    spread_out = [take(0) for _ in range(2)] if spreads else []
    returned_ref = take(0)
    d_att_s, d_middle_s, dqt_s, dk_s, dv_s, probs_s, scores_s = (take(0) for _ in range(7))
    own_sem, *sems = refs
    members = grid_shape[1]
    back = Exchange(members, made_ref.shape[0] // members, made_ref, returned_ref, *sems)
    mine = back.block(back.me)
    own = None
    if returns:
        own = pltpu.make_async_copy(made_ref.at[mine, :], returned_ref.at[mine, :], own_sem)
    aparts = part_of(members, returns)

    @pl.when(pl.program_id(0) == 0)
    def _():
        greet([back.peer(apart) for apart in aparts])
        start_all([back.copy(apart) for apart in aparts])
        if returns:
            own.start()

    pair, pairs = pl.program_id(0), pl.num_programs(0)
    seq_len = hidden_ref.shape[0]
    width = 2 * head_dim
    step = min(256, seq_len)
    scale = head_dim**-0.5

    @pl.when(pair == 0)
    def _():
        placing = placing_cols(slot_col_ref[...], d_back_ref.shape[0])
        d_logits = d_logits_ref[...]
        d_ffn = dot(placing, d_back_ref[...]) + dot(d_logits, router_ref[...])
        middle = middle_ref[...]
        gain_row = gain_ffn_ref[...]
        ffn_in = (middle * rms_factor(middle) * gain_row).astype(bf16)
        gwr_ref[...] = dot(d_logits, ffn_in, 0, 0)
        d_middle, d_gain = rms_pull(middle, gain_row, d_ffn)
        ggf_ref[...] = d_gain
        d_middle = d_middle + grad_ref[...].astype(f32)
        d_middle_s[...] = d_middle
        d_low = d_middle.astype(bf16)
        reblock(grid_shape, blocks_ref, 3, dot(att_ref[...], d_low).astype(bf16))
        d_att_s[...] = dot(d_low, mats_ref[3], 1, 1).astype(bf16)

    lanes = pl.ds(pl.multiple_of(pair * width, width), width)
    q2 = q_ref[:, lanes] * jnp.asarray(scale, bf16)
    k2 = k_ref[:, lanes]
    v2 = v_ref[:, lanes]
    da2 = d_att_s[:, lanes]
    k2t = k2.T
    first = half_masks(seq_len, width)
    d_key = jnp.zeros((seq_len, width), f32)
    d_value = jnp.zeros((seq_len, width), f32)
    for half in range(2):
        mask = first if half == 0 else ~first
        q_one = jnp.where(mask, q2, jnp.zeros_like(q2))
        da_one = jnp.where(mask, da2, jnp.zeros_like(da2))
        k_one = k2t[half * head_dim : (half + 1) * head_dim]
        rows = pl.ds(pl.multiple_of(pair * width + half * head_dim, head_dim), head_dim)
        for start in range(0, seq_len, step):
            cols = slice(start, start + step)
            scores = dot(k2, q_one[cols], 1, 1) + bias_ref[half, :, cols].astype(f32)
            probs = jnp.exp(scores - lse_ref[0, half : half + 1, cols])
            d_probs = dot(v2, da_one[cols], 1, 1)
            inner = jnp.sum(probs * d_probs, axis=0, keepdims=True)
            d_scores = (probs * (d_probs - inner)).astype(bf16)
            probs_s[:, cols] = probs.astype(bf16)
            scores_s[:, cols] = d_scores
            dqt_s[rows, cols] = (dot(k_one, d_scores) * scale).astype(bf16)
        d_key = d_key + dot(scores_s[...], q_one)
        d_value = d_value + dot(probs_s[...], da_one)
        offsets_ref[0, half : half + 1, :] = diagonal_fold(scores_s[...], seq_len)
    dk_s[:, lanes] = d_key.astype(bf16)
    dv_s[:, lanes] = d_value.astype(bf16)

    @pl.when(pair == pairs - 1)
    def _():
        hidden = hidden_ref[...].astype(f32)
        gain_row = gain_attn_ref[...]
        normed_t = (hidden * rms_factor(hidden) * gain_row).astype(bf16).T
        d_query = dqt_s[...].T
        d_normed = dot(d_query, mats_ref[0], 1, 1)
        reblock(grid_shape, blocks_ref, 0, dot(normed_t, d_query).astype(bf16))
        d_normed = d_normed + dot(dk_s[...], mats_ref[1], 1, 1)
        reblock(grid_shape, blocks_ref, 1, dot(normed_t, dk_s[...]).astype(bf16))
        d_normed = d_normed + dot(dv_s[...], mats_ref[2], 1, 1)
        reblock(grid_shape, blocks_ref, 2, dot(normed_t, dv_s[...]).astype(bf16))
        d_hidden, d_gain = rms_pull(hidden, gain_row, d_normed)
        gga_ref[...] = d_gain
        grad_new = d_hidden + d_middle_s[...]
        grad_new_ref[...] = grad_new
        if spreads:
            spread_into(grad_new, *spread_in, *spread_out)

    @pl.when(pair == pairs - 1)
    def _():
        wait_all([back.copy(apart) for apart in aparts])
        if returns:
            own.wait()


def attention_backward(
    d_back,
    slot_col,
    d_logits,
    grad_now,
    middle,
    hidden,
    gains,
    mats,
    q_k_v,
    attended,
    bias,
    lse,
    grid_shape,
    below=None,
    after=(),
    made=None,
    returns=False,
    identifier=None,
):
    seq_len, width = hidden.shape
    heads = bias.shape[0]
    head_dim = width // heads
    experts = mats[1].shape[0]
    count_x, count_y = grid_shape
    ins = (
        d_back,
        slot_col,
        d_logits,
        grad_now,
        middle,
        hidden,
        *gains,
        *mats,
        *q_k_v,
        attended,
    )
    spreads = below is not None
    if spreads:
        ins = ins + tuple(below)
    row = jax.ShapeDtypeStruct((1, width), f32)
    outs = (
        jax.ShapeDtypeStruct((seq_len, width), f32),
        jax.ShapeDtypeStruct(
            (count_x // 2, 2, count_y // 2, 2, width // count_x, 4 * (width // count_y)), bf16
        ),
        jax.ShapeDtypeStruct((experts, width), f32),
        row,
        row,
        jax.ShapeDtypeStruct((heads // 2, 2, 2 * seq_len), f32),
    )
    if spreads:
        outs = outs + (
            jax.ShapeDtypeStruct((2 * seq_len, width), bf16),
            jax.ShapeDtypeStruct(d_logits.shape, bf16),
        )
    outs = outs + (jax.ShapeDtypeStruct(made.shape, bf16),)
    out_specs = whole_of(outs)
    out_specs[-1] = any_spec
    out_specs[5] = pl.BlockSpec((1, 2, 2 * seq_len), lambda p: (p, 0, 0))
    return pl.pallas_call(
        partial(backward_kernel, head_dim, grid_shape, spreads, returns, len(after)),
        grid=(heads // 2,),
        in_specs=whole_of(ins)
        + [
            pl.BlockSpec((2, seq_len, seq_len), lambda p: (p, 0, 0)),
            pl.BlockSpec((1, 2, seq_len), lambda p: (p, 0, 0)),
        ]
        + [any_spec] * (len(after) + 1),
        out_specs=out_specs,
        out_shape=outs,
        scratch_shapes=[
            pltpu.VMEM((seq_len, width), bf16),
            pltpu.VMEM((seq_len, width), f32),
            pltpu.VMEM((width, seq_len), bf16),
            pltpu.VMEM((seq_len, width), bf16),
            pltpu.VMEM((seq_len, width), bf16),
            pltpu.VMEM((seq_len, seq_len), bf16),
            pltpu.VMEM((seq_len, seq_len), bf16),
        ]
        + [pltpu.SemaphoreType.DMA]
        + [pltpu.SemaphoreType.DMA((count_y,))] * 2,
        compiler_params=params(identifier),
        cost_estimate=lasting(32),
        name="attention_backward",
    )(*ins, bias, lse, made, *after)


class Exchange:
    def __init__(self, members, rows, src, dst, send_sems, recv_sems):
        self.me = lax.axis_index("gy")
        self.bits = members.bit_length() - 1
        self.rows, self.src, self.dst = rows, src, dst
        self.send_sems, self.recv_sems = send_sems, recv_sems

    def block(self, index):
        return pl.ds(pl.multiple_of(index * self.rows, self.rows), self.rows)

    def peer(self, apart):
        return {"gy": xor_of(self.me, apart, self.bits)}

    def copy(self, apart):
        peer = xor_of(self.me, apart, self.bits)
        return pltpu.make_async_remote_copy(
            src_ref=self.src.at[self.block(peer), :],
            dst_ref=self.dst.at[self.block(self.me), :],
            send_sem=self.send_sems.at[apart],
            recv_sem=self.recv_sems.at[apart],
            device_id={"gy": peer},
            device_id_type=MESH,
        )

    def keep_own(self):
        self.dst[self.block(self.me), :] = self.src[self.block(self.me), :]


class Leading(Exchange):
    def __init__(self, members, src, dst, send_sems, recv_sems):
        super().__init__(members, 1, src, dst, send_sems, recv_sems)

    def copy(self, apart):
        peer = xor_of(self.me, apart, self.bits)
        sems = (self.send_sems, self.recv_sems)
        return send(self.src.at[peer], self.dst.at[self.me], sems, apart, {"gy": peer})

    def keep_own(self):
        self.dst[self.me] = self.src[self.me]


def peers_along_gy(members):
    me = lax.axis_index("gy")
    bits = members.bit_length() - 1
    return [{"gy": xor_of(me, apart, bits)} for apart in range(1, members)]


def gelu_and_slope(pre):
    inner_scale = 0.7978845608028654
    square = pre * pre
    bent = jnp.tanh(inner_scale * pre * (1.0 + 0.044715 * square))
    act = 0.5 * pre * (1.0 + bent)
    slope = 0.5 * (1.0 + bent) + 0.5 * pre * (1.0 - bent * bent) * (
        inner_scale * (1.0 + 3 * 0.044715 * square)
    )
    return act, slope


def gelu_only(pre):
    inner_scale = 0.7978845608028654
    return 0.5 * pre * (1.0 + jnp.tanh(inner_scale * pre * (1.0 + 0.044715 * pre * pre)))


def send_order(members):
    return range(1, members)


def early(members):
    quarter = max(1, members // 4)
    return [apart for apart in range(members) if (apart // quarter) % 2 == 0]


def part_of(members, first):
    chosen = early(members)
    return [a for a in range(1, members) if (a in chosen) == first]


def collect(me, members, rows, first_ref, second_ref, dst, sems):
    copies = []
    for apart in range(members):
        start = xor_of(me, apart, bits_of(members)) * rows
        here = pl.ds(pl.multiple_of(start, rows), rows)
        ref = first_ref if apart in early(members) else second_ref
        copies.append(pltpu.make_async_copy(ref.at[here, :], dst.at[here, :], sems.at[apart]))
    return copies


def chunk_of(members, rows):
    return max(1, min(members, 256 // rows))


def expert_forward_kernel(
    grid_shape,
    gathers,
    sent_ref,
    slot_col_ref,
    chosen_ref,
    logits_ref,
    middle_ref,
    win_ref,
    wout_ref,
    *refs,
):
    refs = list(refs)
    take = refs.pop
    column_ref = take(0) if gathers else None
    arrived_ref, comb_ref, out_ref = (take(0) for _ in range(3))
    full_ref = take(0) if gathers else None
    win_s, wout_s, made_s, returned_s, w_sems = (take(0) for _ in range(5))
    send_sems, recv_sems, back_send_sems, back_recv_sems = (take(0) for _ in range(4))
    members = grid_shape[1]
    slots = sent_ref.shape[0]
    rows = slots // members
    group = chunk_of(members, rows)
    chunks = members // group
    chunk_bits = chunks.bit_length() - 1
    hidden_units = win_s.shape[1]
    tile = min(768, hidden_units)
    load_in = pltpu.make_async_copy(win_ref, win_s, w_sems.at[0])
    load_out = pltpu.make_async_copy(wout_ref, wout_s, w_sems.at[1])
    load_in.start()
    load_out.start()
    place = Place(grid_shape)
    more_peers = [place.core_peer()] + place.y_peers() if gathers else []
    greet(peers_along_gy(members) + more_peers)
    there = Exchange(members, rows, sent_ref, arrived_ref, send_sems, recv_sems)
    back = Exchange(members, rows, made_s, returned_s, back_send_sems, back_recv_sems)
    for apart in send_order(members):
        there.copy(apart).start()
    there.keep_own()
    if gathers:
        own_sem, *sems = refs
        split = (full_ref.shape[4] - tile_rows) // 2
        own = pltpu.make_async_copy(
            column_ref, full_ref.at[place.y, place.c, :, place.x], own_sem
        )
        own.start()
        second = gather_second(place, column_ref, full_ref, split, sems)
        third = gather_third(place, full_ref, split, sems)
        fourth = gather_core(place, full_ref, sems)
        start_all(second)
    load_in.wait()
    load_out.wait()
    my_chunk = there.me // group

    def chunk_rows(index):
        start = xor_of(my_chunk, index, chunk_bits) * (group * rows)
        return pl.ds(pl.multiple_of(start, group * rows), group * rows)

    def work(index, first):
        for member in range(first, group):
            there.copy(index * group + member).wait_recv()
        here = chunk_rows(index)
        taken = arrived_ref[here, :]
        total = jnp.zeros((group * rows, taken.shape[1]), f32)
        for start in range(0, hidden_units, tile):
            units = slice(start, start + tile)
            act = gelu_only(dot(taken, win_s[:, units])).astype(bf16)
            total = total + dot(act, wout_s[:, units], 1, 1)
        made_s[here, :] = total.astype(bf16)
        for member in range(first, group):
            back.copy(index * group + member).start()

    work(0, 1)
    back.keep_own()
    half = chunks // 2

    @pl.loop(1, half)
    def _(index):
        work(index, 0)

    if gathers:
        own.wait()
        wait_all(second)
        start_all(third)

    @pl.loop(half, chunks)
    def _(index):
        work(index, 0)

    if gathers:
        wait_all(third)
        start_all(fourth)
    slot_col = slot_col_ref[...]
    comb_ref[...] = jnp.zeros_like(comb_ref)

    def gather_back(index, first):
        for member in range(first, group):
            back.copy(index * group + member).wait_recv()
        begin = xor_of(my_chunk, index, chunk_bits) * (group * rows)
        places = lax.broadcasted_iota(jnp.int32, (slot_col.shape[0], group * rows), 1) + begin
        placing = (places == slot_col).astype(f32).astype(bf16)
        comb_ref[...] += dot(placing, returned_s[chunk_rows(index), :])

    gather_back(0, 1)

    @pl.loop(1, chunks)
    def _(index):
        gather_back(index, 0)

    gate = jnp.sum(jax.nn.softmax(logits_ref[...], axis=-1) * chosen_ref[...], axis=1, keepdims=True)
    out_ref[...] = middle_ref[...] + gate * comb_ref[...]
    if gathers:
        wait_all(fourth)

    @pl.loop(1, members)
    def _(apart):
        there.copy(apart).wait_send()
        back.copy(apart).wait_send()


def expert_forward(
    sent, slot_col, chosen_f, logits, middle, full_in, full_out, grid_shape, identifier, column=None
):
    members = grid_shape[1]
    gathers = column is not None
    ins = [sent, slot_col, chosen_f, logits, middle, full_in, full_out]
    in_specs = [vmem_spec] * 5 + [any_spec] * 2
    outs = [
        jax.ShapeDtypeStruct(sent.shape, bf16),
        jax.ShapeDtypeStruct(middle.shape, f32),
        jax.ShapeDtypeStruct(middle.shape, f32),
    ]
    out_specs = [vmem_spec] * 3
    sems = pltpu.SemaphoreType.DMA((members,))
    scratch = [
        pltpu.VMEM(full_in.shape, bf16),
        pltpu.VMEM(full_out.shape, bf16),
        pltpu.VMEM(sent.shape, bf16),
        pltpu.VMEM(sent.shape, bf16),
        pltpu.SemaphoreType.DMA((2,)),
        sems,
        sems,
        sems,
        sems,
    ]
    if gathers:
        ins.append(column)
        in_specs.append(any_spec)
        half = (grid_shape[0] // 2, 2, grid_shape[1] // 2, 2)
        outs.append(jax.ShapeDtypeStruct((*half, *column.shape[1:]), bf16))
        out_specs.append(any_spec)
        others = pltpu.SemaphoreType.DMA((gather_copies(grid_shape)[1],))
        scratch += [pltpu.SemaphoreType.DMA, others, others]
    return pl.pallas_call(
        partial(expert_forward_kernel, grid_shape, gathers),
        in_specs=in_specs,
        out_specs=out_specs,
        out_shape=outs,
        scratch_shapes=scratch,
        compiler_params=params(identifier),
        cost_estimate=lasting(75),
        name="expert_forward",
    )(*ins)


def expert_both_kernel(
    grid_shape,
    sent_ref,
    gates_ref,
    slot_col_ref,
    chosen_ref,
    logits_ref,
    first_ref,
    second_ref,
    win_ref,
    wout_ref,
    made_ref,
    d_back_ref,
    gin_ref,
    gout_ref,
    d_logits_ref,
    arrived_s,
    gates_s,
    win_s,
    wout_s,
    d_made_s,
    d_rows_s,
    act_s,
    d_pre_s,
    d_gates_s,
    d_gates_back_s,
    grads_ref,
    w_sems,
    *sems,
):
    members = grid_shape[1]
    slots = sent_ref.shape[0]
    rows = slots // members
    group = chunk_of(members, rows)
    chunks = members // group
    chunk_bits = bits_of(chunks)
    hidden_units = win_s.shape[1]
    tile = min(768, hidden_units)
    load_in = pltpu.make_async_copy(win_ref, win_s, w_sems.at[0])
    load_out = pltpu.make_async_copy(wout_ref, wout_s, w_sems.at[1])
    load_in.start()
    load_out.start()
    greet(peers_along_gy(members))
    there = Exchange(members, rows, sent_ref, arrived_s, *sems[0:2])
    back = Exchange(members, rows, d_rows_s, d_back_ref, *sems[2:4])
    gates_there = Leading(members, gates_ref, gates_s, *sems[4:6])
    gates_back = Leading(members, d_gates_s, d_gates_back_s, *sems[6:8])

    for apart in send_order(members):
        gates_there.copy(apart).start()
        there.copy(apart).start()

    collected = collect(there.me, members, rows, first_ref, second_ref, grads_ref, sems[8])
    start_all(collected)
    there.keep_own()
    gates_there.keep_own()
    load_in.wait()
    load_out.wait()
    wait_all(collected)
    my_chunk = there.me // group

    def work(index, first):
        for member in range(first, group):
            gates_there.copy(index * group + member).wait_recv()
            there.copy(index * group + member).wait_recv()
        chunk = xor_of(my_chunk, index, chunk_bits)
        here = pl.ds(pl.multiple_of(chunk * (group * rows), group * rows), group * rows)
        gate = jnp.concatenate(
            [gates_s[chunk * group + member].T[:rows, 0:1] for member in range(group)], axis=0
        )
        taken = arrived_s[here, :]
        grads = grads_ref[here, :].astype(f32)
        d_made = (gate * grads).astype(bf16)
        d_made_s[here, :] = d_made
        made = jnp.zeros((group * rows, taken.shape[1]), f32)
        d_rows = made
        for start in range(0, hidden_units, tile):
            units = slice(start, start + tile)
            act, slope = gelu_and_slope(dot(taken, win_s[:, units]))
            act = act.astype(bf16)
            act_s[here, units] = act
            d_pre = (dot(d_made, wout_s[:, units]) * slope).astype(bf16)
            d_pre_s[here, units] = d_pre
            d_rows = d_rows + dot(d_pre, win_s[:, units], 1, 1)
            made = made + dot(act, wout_s[:, units], 1, 1)
        d_rows_s[here, :] = d_rows.astype(bf16)
        made = made.astype(bf16)
        made_ref[here, :] = made
        d_gate = jnp.sum(grads * made.astype(f32), axis=1, keepdims=True)
        for member in range(group):
            part = jnp.broadcast_to(d_gate[member * rows : (member + 1) * rows], (rows, 128)).T
            d_gates_s[chunk * group + member, :, :rows] = part[: d_gates_s.shape[1]]
        for member in range(first, group):
            gates_back.copy(index * group + member).start()
            back.copy(index * group + member).start()

    work(0, 1)
    back.keep_own()
    gates_back.keep_own()

    @pl.loop(1, chunks)
    def _(index):
        work(index, 0)

    for lhs_ref, rhs_ref, out_ref in ((d_made_s, act_s, gout_ref), (arrived_s, d_pre_s, gin_ref)):
        lhs = lhs_ref[...].T

        @pl.loop(0, hidden_units // tile)
        def _(index, lhs=lhs, rhs_ref=rhs_ref, out_ref=out_ref):
            units = pl.ds(pl.multiple_of(index * tile, tile), tile)
            out_ref[:, units] = dot(lhs, rhs_ref[:, units]).astype(bf16)

    @pl.loop(1, members)
    def _(apart):
        gates_back.copy(apart).wait_recv()

    row = jnp.concatenate(
        [d_gates_back_s[expert, 0:1, :rows] for expert in range(members)], axis=1
    )
    slot_col = slot_col_ref[...]
    places = lax.broadcasted_iota(jnp.int32, (slot_col.shape[0], slots), 1)
    d_gate = jnp.sum(jnp.where(places == slot_col, row, 0.0), axis=1, keepdims=True)
    d_logits_ref[...] = d_logits_of(d_gate, logits_ref[...], chosen_ref[...])

    @pl.loop(1, members)
    def _(apart):
        back.copy(apart).wait_recv()
        there.copy(apart).wait_send()
        back.copy(apart).wait_send()
        gates_there.copy(apart).wait_send()
        gates_back.copy(apart).wait_send()


def expert_both(sent, gates, far_parts, slot_col, chosen_f, logits, full_in, full_out, grid_shape, identifier):
    members = grid_shape[1]
    slots = sent.shape[0]
    outs = (
        jax.ShapeDtypeStruct(sent.shape, bf16),
        jax.ShapeDtypeStruct(sent.shape, bf16),
        jax.ShapeDtypeStruct(full_in.shape, bf16),
        jax.ShapeDtypeStruct(full_out.shape, bf16),
        jax.ShapeDtypeStruct(logits.shape, bf16),
    )
    tall = pltpu.VMEM(sent.shape, bf16)
    wide = pltpu.VMEM((slots, full_in.shape[1]), bf16)
    small = pltpu.VMEM(gates.shape, f32)
    weights = pltpu.VMEM(full_in.shape, bf16)
    return pl.pallas_call(
        partial(expert_both_kernel, grid_shape),
        in_specs=[vmem_spec] * 5 + [any_spec] * 4,
        out_specs=[vmem_spec] * len(outs),
        out_shape=outs,
        scratch_shapes=[
            tall,
            small,
            weights,
            weights,
            tall,
            tall,
            wide,
            wide,
            small,
            small,
            tall,
            pltpu.SemaphoreType.DMA((2,)),
        ]
        + [pltpu.SemaphoreType.DMA((members,))] * 9,
        compiler_params=params(identifier),
        cost_estimate=lasting(85),
        name="expert_both",
    )(sent, gates, slot_col, chosen_f, logits, *far_parts, full_in, full_out)


def expert_backward_kernel(
    grid_shape,
    d_sent_ref,
    arrived_ref,
    blocks_ref,
    win_ref,
    wout_ref,
    d_back_ref,
    gin_ref,
    gout_ref,
    upper_ref,
    lower_ref,
    win_s,
    wout_s,
    d_arrived_s,
    d_rows_s,
    act_s,
    slope_s,
    first_s,
    up2_s,
    low2_s,
    w_sems,
    send_sems,
    recv_sems,
    back_send_sems,
    back_recv_sems,
    *sum_sems,
):
    members = grid_shape[1]
    place = Place(grid_shape)
    slots = d_sent_ref.shape[0]
    rows = slots // members
    group = chunk_of(members, rows)
    chunks = members // group
    chunk_bits = chunks.bit_length() - 1
    hidden_units = win_s.shape[1]
    tile = min(768, hidden_units)
    load_in = pltpu.make_async_copy(win_ref, win_s, w_sems.at[0])
    load_out = pltpu.make_async_copy(wout_ref, wout_s, w_sems.at[1])
    load_in.start()
    load_out.start()
    greet(peers_along_gy(members) + [place.core_peer()] + place.y_peers())
    landings = (first_s, up2_s, low2_s, upper_ref, lower_ref, None, None)
    sums = Scatter(place, blocks_ref, landings, sum_sems, upper_ref.shape[1])
    there = Exchange(members, rows, d_sent_ref, d_arrived_s, send_sems, recv_sems)
    back = Exchange(members, rows, d_rows_s, d_back_ref, back_send_sems, back_recv_sems)
    for apart in send_order(members):
        there.copy(apart).start()
    there.keep_own()
    my_chunk = there.me // group
    start_all(sums.copies(0))
    load_in.wait()

    @pl.loop(0, slots // 256)
    def _(index):
        here = pl.ds(pl.multiple_of(index * 256, 256), 256)
        taken = arrived_ref[here, :]
        for start in range(0, hidden_units, tile):
            units = slice(start, start + tile)
            act, slope = gelu_and_slope(dot(taken, win_s[:, units]))
            act_s[here, units] = act.astype(bf16)
            slope_s[here, units] = slope.astype(bf16)

    wait_all(sums.copies(0))
    sums.add(0)
    start_all(sums.copies(1))
    load_out.wait()

    def chunk_rows(index):
        start = xor_of(my_chunk, index, chunk_bits) * (group * rows)
        return pl.ds(pl.multiple_of(start, group * rows), group * rows)

    def work(index, first):
        for member in range(first, group):
            there.copy(index * group + member).wait_recv()
        here = chunk_rows(index)
        taken = d_arrived_s[here, :]
        total = jnp.zeros((group * rows, taken.shape[1]), f32)
        for start in range(0, hidden_units, tile):
            units = slice(start, start + tile)
            d_pre = (dot(taken, wout_s[:, units]) * slope_s[here, units].astype(f32)).astype(bf16)
            slope_s[here, units] = d_pre
            total = total + dot(d_pre, win_s[:, units], 1, 1)
        d_rows_s[here, :] = total.astype(bf16)
        for member in range(first, group):
            back.copy(index * group + member).start()

    work(0, 1)
    back.keep_own()

    @pl.loop(1, chunks)
    def _(index):
        work(index, 0)

    wait_all(sums.copies(1))
    sums.add(1)
    start_all(sums.copies(2))
    for lhs_ref, rhs_ref, out_ref in (
        (d_arrived_s, act_s, gout_ref),
        (arrived_ref, slope_s, gin_ref),
    ):
        lhs = lhs_ref[...].T

        @pl.loop(0, hidden_units // tile)
        def _(index, lhs=lhs, rhs_ref=rhs_ref, out_ref=out_ref):
            units = pl.ds(pl.multiple_of(index * tile, tile), tile)
            out_ref[:, units] = dot(lhs, rhs_ref[:, units]).astype(bf16)

    wait_all(sums.copies(2))
    sums.add(2)

    @pl.loop(1, members)
    def _(apart):
        back.copy(apart).wait_recv()
        there.copy(apart).wait_send()
        back.copy(apart).wait_send()


def expert_backward(d_sent, arrived, blocks, full_in, full_out, grid_shape, identifier):
    members = grid_shape[1]
    landings = whole_blocks(blocks.shape, blocks.shape[4] // 2)
    outs = (
        jax.ShapeDtypeStruct(d_sent.shape, bf16),
        jax.ShapeDtypeStruct(full_in.shape, bf16),
        jax.ShapeDtypeStruct(full_out.shape, bf16),
        *[jax.ShapeDtypeStruct(one, bf16) for one in landings[3:5]],
    )
    slots = d_sent.shape[0]
    sems = pltpu.SemaphoreType.DMA((members,))
    return pl.pallas_call(
        partial(expert_backward_kernel, grid_shape),
        in_specs=[vmem_spec] * 3 + [any_spec] * 2,
        out_specs=[vmem_spec] * len(outs),
        out_shape=outs,
        scratch_shapes=[
            pltpu.VMEM(full_in.shape, bf16),
            pltpu.VMEM(full_out.shape, bf16),
            pltpu.VMEM(d_sent.shape, bf16),
            pltpu.VMEM(d_sent.shape, bf16),
            pltpu.VMEM((slots, full_in.shape[1]), bf16),
            pltpu.VMEM((slots, full_in.shape[1]), bf16),
            *[pltpu.VMEM(one, bf16) for one in landings[:3]],
            pltpu.SemaphoreType.DMA((2,)),
            sems,
            sems,
            sems,
            sems,
            *[pltpu.SemaphoreType.DMA((scatter_copies(grid_shape),))] * 2,
        ],
        compiler_params=params(10 + identifier),
        cost_estimate=lasting(85),
        name="expert_backward",
    )(d_sent, arrived, blocks, full_in, full_out)


def body(
    hidden_in,
    route,
    piece_ids,
    buckets,
    rel_table,
    gain_attn,
    gain_ffn,
    w_query,
    w_key,
    w_value,
    w_output,
    w_router,
    w_in,
    w_out,
    cotangent,
):
    count_x = lax.axis_size("gx")
    count_y = lax.axis_size("gy")
    seq_len, width = hidden_in.shape
    layers = w_query.shape[0]
    heads = rel_table.shape[1]
    experts = w_router.shape[2] * count_y
    capacity = 2 * seq_len // experts
    wide_router = w_router.shape[2]
    tall, wide = w_query.shape[1], w_query.shape[2]
    grid_shape = (count_x, count_y)
    router_rows = jnp.pad(
        w_router.transpose(0, 2, 1), ((0, 0), (0, tile_rows - wide_router), (0, 4 * wide - tall))
    )
    buckets_row = jnp.pad(buckets, (0, 1), constant_values=-1)[None, :]
    mats, router, later, bias, slot_col, slot_row, chosen_f, spread = start(
        (w_query, w_key, w_value, w_output),
        router_rows,
        buckets_row,
        rel_table.T,
        piece_ids,
        route,
        cotangent,
        grid_shape,
    )
    gain_attn_f = gain_attn.astype(f32)
    gain_ffn_f = gain_ffn.astype(f32)

    hidden = hidden_in
    kept = []
    blocks = None
    far_parts = []
    for layer in range(layers):
        last = layer == layers - 1
        gains = (gain_attn_f[layer][None], gain_ffn_f[layer][None])
        mats, router, q, k, v, attended, lse, middle, logits, sent, *gates, far_part = attention_forward(
            hidden,
            gains[0],
            gains[1],
            (slot_row, slot_col, chosen_f),
            bias,
            grid_shape,
            1 + layer,
            spread,
            last,
            blocks=blocks,
            mats=(mats, router) if blocks is None else None,
        )
        far_parts.append(far_part)
        full_in = lax.all_gather(w_in[layer, 0], "gx", axis=1, tiled=True)
        full_out = lax.all_gather(w_out[layer, 0], "gx", axis=1, tiled=True)
        state = (hidden, gains, (mats, router), (q, k, v), attended, lse, middle, logits)
        if last:
            made, d_back, grad_in_full, grad_out_full, d_logits = expert_both(
                sent, gates[0], far_parts, slot_col, chosen_f, logits, full_in, full_out, grid_shape, 7
            )
            kept.append(state)
        else:
            arrived, combined, hidden, blocks = expert_forward(
                sent,
                slot_col,
                chosen_f,
                logits,
                middle,
                full_in,
                full_out,
                grid_shape,
                5 + layer,
                column=later[layer],
            )
            kept.append(state + (combined, arrived, full_in, full_out))

    grad_now = cotangent
    parts = []
    partials = []
    returned = []
    for layer in reversed(range(layers)):
        last = layer == layers - 1
        (prior, gains, mats, q_k_v, attended, lse, middle, logits) = kept[layer][:8]
        if not last:
            arrived, full_in, full_out = kept[layer][9:]
            d_back, grad_in_full, grad_out_full, upper, lower = expert_backward(
                d_sent, arrived, parts[-1][0], full_in, full_out, grid_shape, layer
            )
            partials.append((upper, lower[:1]))
        grad_out_part = lax.psum_scatter(grad_out_full, "gx", scatter_dimension=1, tiled=True)
        grad_in_part = lax.psum_scatter(grad_in_full, "gx", scatter_dimension=1, tiled=True)
        below = None
        if layer > 0:
            below = (kept[layer - 1][8], slot_row, chosen_f, kept[layer - 1][7])
        got = attention_backward(
            d_back,
            slot_col,
            d_logits,
            grad_now,
            middle,
            prior,
            gains,
            mats,
            q_k_v,
            attended,
            bias,
            lse,
            grid_shape,
            below=below,
            after=[array for part in parts for array in part[4:6]],
            made=made,
            returns=last,
            identifier=18 + layer,
        )
        grad_now, blocked, gwr, gga, ggf, offset_sums = got[:6]
        if layer > 0:
            d_sent, d_logits = got[6:8]
        returned.append(got[-1])
        offset_sums = offset_sums.reshape(heads, 2 * seq_len)
        parts.append((blocked, gwr, gga, ggf, grad_in_part, grad_out_part, offset_sums))
    parts = parts[::-1]
    buckets_count = rel_table.shape[0]
    smalls = [part[which] for which in (1, 2, 3, 6) for part in parts]
    top = kept[-1]
    *attn_grads, small, hidden_out = final_sums(
        parts[0][0],
        partials[::-1],
        smalls + [buckets_row],
        (slot_col, chosen_f, top[7], top[6]),
        returned,
        grid_shape,
        wide,
        buckets_count,
    )
    router_sum = small[: layers * experts].reshape(layers, experts, width)
    base = layers * experts
    gga_all, ggf_all = small[base : base + layers], small[base + layers : base + 2 * layers]
    base = base + 2 * layers
    d_table = small[base : base + heads, :buckets_count].T
    router_mine = lax.dynamic_slice(
        router_sum,
        (0, lax.axis_index("gy") * wide_router, lax.axis_index("gx") * tall),
        (layers, wide_router, tall),
    ).transpose(0, 2, 1)
    grad_in = jnp.stack([part[4] for part in parts]).astype(f32)[:, None]
    grad_out = jnp.stack([part[5] for part in parts]).astype(f32)[:, None]
    return (
        hidden_out,
        grad_now,
        d_table,
        gga_all,
        ggf_all,
        *attn_grads,
        router_mine,
        grad_in,
        grad_out,
    )


def solution(mesh):
    rows = P(("gx", "gy"), None)
    square = P(None, "gx", "gy")
    expert = P(None, "gy", None, "gx")
    return jax.shard_map(
        body,
        mesh=mesh,
        in_specs=(rows, rows, P(("gx", "gy")), P(), P(), P(), P())
        + (square,) * 5
        + (expert, expert, rows),
        out_specs=(rows, rows, P(), P(), P()) + (square,) * 5 + (expert, expert),
        check_vma=False,
    )
```

```python
from functools import partial

import jax
import jax.numpy as jnp
from jax import lax
from jax.experimental import pallas as pl
from jax.experimental.pallas import tpu as pltpu
from jax.sharding import PartitionSpec as P

eps_norm = 1e-06
highest = lax.Precision.HIGHEST
f32 = jnp.float32
bf16 = jnp.bfloat16
masked_out = -1e30
tile_rows = 16
MESH = pl.DeviceIdType.MESH
vmem_spec = pl.BlockSpec(memory_space=pltpu.VMEM)
any_spec = pl.BlockSpec(memory_space=pl.ANY)
vmem_bytes = 60 * 1024 * 1024


def whole(shape):
    zeros = (0,) * len(shape)
    return pl.BlockSpec(shape, lambda *_: zeros, pipeline_mode=pl.Buffered(1))


def whole_of(arrays):
    return [whole(array.shape) for array in arrays]


def params(identifier=None):
    if identifier is None:
        return pltpu.CompilerParams(vmem_limit_bytes=vmem_bytes)
    return pltpu.CompilerParams(
        vmem_limit_bytes=vmem_bytes, collective_id=identifier, has_side_effects=True
    )


def lasting(microseconds):
    return pl.CostEstimate(
        flops=int(microseconds * 1e9), bytes_accessed=1 << 20, transcendentals=0
    )


def dot(lhs, rhs, lhs_dim=1, rhs_dim=0):
    return lax.dot_general(
        lhs, rhs, (((lhs_dim,), (rhs_dim,)), ((), ())), preferred_element_type=f32
    )


def rms_factor(hidden):
    return lax.rsqrt(jnp.mean(hidden * hidden, axis=-1, keepdims=True) + eps_norm)


def rms_pull(hidden, gain_row, d_normed):
    factor = rms_factor(hidden)
    scaled = gain_row * d_normed
    inner = jnp.mean(hidden * scaled, axis=-1, keepdims=True)
    d_hidden = factor * scaled - hidden * (factor * factor * factor * inner)
    d_gain = jnp.sum(d_normed * hidden * factor, axis=0, keepdims=True)
    return d_hidden, d_gain


def xor_of(index, other, bits):
    total = 0
    for bit in range(bits):
        power = 1 << bit
        total = total + ((index // power + other // power) % 2) * power
    return total


def placing_rows(slot_row, slots):
    places = lax.broadcasted_iota(jnp.int32, (slots, slot_row.shape[1]), 0)
    return (places == slot_row).astype(f32).astype(bf16)


def placing_cols(slot_col, slots):
    places = lax.broadcasted_iota(jnp.int32, (slot_col.shape[0], slots), 1)
    return (places == slot_col).astype(f32).astype(bf16)


def greet(peers):
    barrier = pltpu.get_barrier_semaphore()
    for peer in peers:
        pl.semaphore_signal(barrier, inc=1, device_id=peer, device_id_type=MESH)
    pl.semaphore_wait(barrier, len(peers))


def bits_of(count):
    return count.bit_length() - 1


class Place:
    def __init__(self, grid_shape):
        self.count_y, self.count_z = grid_shape[0] // 2, grid_shape[1] // 2
        first, second = lax.axis_index("gx"), lax.axis_index("gy")
        self.c, self.y = first % 2, first // 2
        self.x, self.z = second % 2, second // 2

    def core_peer(self):
        return {"gx": self.y * 2 + 1 - self.c}

    def x_peer(self):
        return {"gy": self.z * 2 + 1 - self.x}

    def y_at(self, apart):
        return xor_of(self.y, apart, bits_of(self.count_y))

    def y_peer(self, apart):
        return {"gx": self.y_at(apart) * 2 + self.c}

    def y_peers(self):
        return [self.y_peer(apart) for apart in range(1, self.count_y)]

    def z_at(self, apart):
        return xor_of(self.z, apart, bits_of(self.count_z))

    def z_peer(self, apart):
        return {"gy": self.z_at(apart) * 2 + self.x}

    def z_peers(self):
        return [self.z_peer(apart) for apart in range(1, self.count_z)]


def send(src, dst, sems, index, peer):
    return pltpu.make_async_remote_copy(
        src_ref=src,
        dst_ref=dst,
        send_sem=sems[0].at[index],
        recv_sem=sems[1].at[index],
        device_id=peer,
        device_id_type=MESH,
    )


def start_all(copies):
    for copy in copies:
        copy.start()


def wait_all(copies):
    for copy in copies:
        copy.wait()


def gather_z(place, src, landing, sems):
    return [
        send(src, landing, sems, apart - 1, place.z_peer(apart)) for apart in range(1, place.count_z)
    ]


def gather_copies(grid_shape):
    return grid_shape[1] // 2 - 1, 2 * (grid_shape[0] // 2 - 1) + 3


def gather_second(place, column, full, split, sems):
    y, c, x = place.y, place.c, place.x
    upper, lower = pl.ds(0, split), pl.ds(split, full.shape[4] - split)
    copies = [
        send(column.at[:, upper], full.at[y, c, :, x, upper], sems, 0, place.x_peer())
    ]
    for apart in range(1, place.count_y):
        copies.append(
            send(column.at[:, lower], full.at[y, c, :, x, lower], sems, apart, place.y_peer(apart))
        )
    return copies


def gather_third(place, full, split, sems):
    y, c, x = place.y, place.c, place.x
    upper, lower = pl.ds(0, split), pl.ds(split, full.shape[4] - split)
    base = place.count_y
    ref = full.at[:, c, :, x, lower]
    copies = [send(ref, ref, sems, base, place.x_peer())]
    ref = full.at[y, c, :, :, upper]
    for apart in range(1, place.count_y):
        copies.append(send(ref, ref, sems, base + apart, place.y_peer(apart)))
    return copies


def gather_core(place, full, sems):
    ref = full.at[:, place.c]
    return [send(ref, ref, sems, 2 * place.count_y, place.core_peer())]


def whole_blocks(shape, split):
    count_y, _, count_z, _, tall, lanes = shape
    low = tall - split
    return [
        (count_y, count_z, 2, tall, lanes),
        (count_y - 1, count_z, 2, split, lanes),
        (count_y, count_z, low, lanes),
        (count_z, split, lanes),
        (count_y - 1, count_z, low, lanes),
        (count_z - 1, split, lanes),
        (count_z - 1, low, lanes),
    ]


def scatter_copies(grid_shape):
    return 1 + 2 * (grid_shape[0] // 2) + 2 * (grid_shape[1] // 2 - 1)


def add_low(dst, dst_at, *terms):
    total = terms[0].astype(f32)
    for term in terms[1:]:
        total = total + term.astype(f32)
    dst[dst_at] = total.astype(bf16)


class Scatter:
    def __init__(self, place, src, landings, sems, split):
        self.place, self.src, self.sems = place, src, sems
        self.first, self.up2, self.low2, self.up3, self.low3, self.up4, self.low4 = landings
        tall = src.shape[4]
        self.upper, self.lower = pl.ds(0, split), pl.ds(split, tall - split)

    def copies(self, stage):
        at, sems = self.place, self.sems
        count_y, count_z = at.count_y, at.count_z
        if stage == 0:
            return [send(self.src.at[:, 1 - at.c], self.first, sems, 0, at.core_peer())]
        if stage == 1:
            copies = [send(self.first.at[:, :, 1 - at.x, self.lower], self.low2, sems, 1, at.x_peer())]
            for apart in range(1, count_y):
                src = self.first.at[at.y_at(apart), :, :, self.upper]
                dst = self.up2.at[apart - 1]
                copies.append(send(src, dst, sems, 1 + apart, at.y_peer(apart)))
            return copies
        if stage == 2:
            base = 1 + count_y
            copies = [send(self.up2.at[0, :, 1 - at.x], self.up3, sems, base, at.x_peer())]
            for apart in range(1, count_y):
                src, dst = self.low2.at[at.y_at(apart)], self.low3.at[apart - 1]
                copies.append(send(src, dst, sems, base + apart, at.y_peer(apart)))
            return copies
        base = 2 * count_y
        copies = []
        for apart in range(1, count_z):
            there = at.z_at(apart)
            for src, dst, more in (
                (self.up3.at[there], self.up4.at[apart - 1], 0),
                (self.low3.at[0, there], self.low4.at[apart - 1], 1),
            ):
                index = base + 2 * apart - 1 + more
                copies.append(send(src, dst, sems, index, at.z_peer(apart)))
        return copies

    def add(self, stage):
        at = self.place
        count_y, count_z = at.count_y, at.count_z
        if stage == 0:

            @pl.loop(0, count_y * count_z)
            def _(index):
                y, z = index // count_z, index % count_z
                add_low(self.first, (y, z), self.first[y, z], self.src[y, at.c, z])

        elif stage == 1:

            @pl.loop(0, count_z)
            def _(z):
                for x in range(2):
                    terms = [self.up2[apart, z, x] for apart in range(count_y - 1)]
                    add_low(self.up2, (0, z, x), self.first[at.y, z, x, self.upper], *terms)

                @pl.loop(0, count_y)
                def _(y):
                    add_low(self.low2, (y, z), self.first[y, z, at.x, self.lower], self.low2[y, z])

        elif stage == 2:

            @pl.loop(0, count_z)
            def _(z):
                add_low(self.up3, (z,), self.up3[z], self.up2[0, z, at.x])
                terms = [self.low3[apart, z] for apart in range(count_y - 1)]
                add_low(self.low3, (0, z), self.low2[at.y, z], *terms)

    def result(self):
        at = self.place
        upper, lower = self.up3[at.z].astype(f32), self.low3[0, at.z].astype(f32)
        for apart in range(at.count_z - 1):
            upper = upper + self.up4[apart].astype(f32)
            lower = lower + self.low4[apart].astype(f32)
        return upper, lower


class SmallSum:
    def __init__(self, grid_shape, totals, landing, sems):
        self.totals, self.landing, self.sems = totals, landing, sems
        self.peers = []
        for name, count in (("gx", grid_shape[0]), ("gy", grid_shape[1])):
            me = lax.axis_index(name)
            for bit in range(bits_of(count)):
                self.peers.append({name: xor_of(me, 1 << bit, bits_of(count))})
        self.done = 0

    def copy(self):
        step = self.done
        return send(self.totals.at[step], self.landing.at[step], self.sems, step, self.peers[step])

    def begin(self):
        self.copy().start()

    def advance(self):
        if self.done == len(self.peers):
            return
        self.copy().wait()
        step = self.done
        self.totals[step + 1] = self.totals[step] + self.landing[step]
        self.done += 1
        if self.done < len(self.peers):
            self.begin()


def small_steps(grid_shape):
    return bits_of(grid_shape[0]) + bits_of(grid_shape[1])


def final_kernel(grid_shape, layers, buckets_count, *refs):
    refs = list(refs)
    take = refs.pop
    blocks_ref = take(0)
    partial_refs = [(take(0), take(0)) for _ in range(layers - 1)]
    router_refs, gga_refs, ggf_refs, offset_refs = ([take(0) for _ in range(layers)] for _ in range(4))
    buckets_ref, slot_col_ref, chosen_ref, logits_ref, middle_ref = (take(0) for _ in range(5))
    first_ref, second_ref, push_ref = take(0), take(0), take(0)
    packed_ref, small_out_ref, result_ref, landing_ref = (take(0) for _ in range(4))
    landings = [take(0) for _ in range(7)]
    z_landings = [(take(0), take(0)) for _ in range(layers - 1)]
    totals, landing, returned_s = take(0), take(0), take(0)
    sems = [(take(0), take(0)) for _ in range(layers)]
    small_sems, collect_sems, push_sems = (take(0), take(0)), take(0), (take(0), take(0))
    place = Place(grid_shape)
    tall = packed_ref.shape[1]
    split = tall // 2
    members = grid_shape[1]
    slots = returned_s.shape[0]
    upper_layers = []
    for layer in range(1, layers):
        upper, lower = partial_refs[layer - 1]
        places = (None, None, None, upper, lower, *z_landings[layer - 1])
        upper_layers.append(Scatter(place, blocks_ref, places, sems[layer], split))
    lowest = Scatter(place, blocks_ref, landings, sems[0], split)
    collected = collect(
        lax.axis_index("gy"),
        members,
        slots // members,
        (first_ref, second_ref),
        lambda apart: int(apart not in early(members)),
        returned_s,
        collect_sems,
    )
    start_all(collected)
    greet([place.core_peer(), place.x_peer()] + place.y_peers() + place.z_peers())
    start_all(lowest.copies(0))
    for one in upper_layers:
        start_all(one.copies(3))

    experts = router_refs[0].shape[0]
    totals[0] = jnp.zeros(totals.shape[1:], f32)
    row = 0
    for refs_of in (router_refs, gga_refs, ggf_refs):
        for ref in refs_of:
            totals[0, row : row + ref.shape[0], :] = ref[...]
            row += ref.shape[0]
    heads = offset_refs[0].shape[0]
    offsets = offset_refs[0][...]
    for ref in offset_refs[1:]:
        offsets = offsets + ref[...]
    in_bucket = (
        lax.broadcasted_iota(jnp.int32, (buckets_count, offsets.shape[1]), 0) == buckets_ref[...]
    ).astype(f32)
    totals[0, row : row + heads, :buckets_count] = lax.dot_general(
        offsets, in_bucket, (((1,), (1,)), ((), ())), precision=highest, preferred_element_type=f32
    )
    small = SmallSum(grid_shape, totals, landing, small_sems)
    small.begin()
    wait_all(lowest.copies(0))
    lowest.add(0)
    start_all(lowest.copies(1))
    small.advance()
    wait_all(collected)
    placing = placing_cols(slot_col_ref[...], slots)
    gate = jnp.sum(jax.nn.softmax(logits_ref[...], axis=-1) * chosen_ref[...], axis=1, keepdims=True)
    result_ref[...] = middle_ref[...] + gate * dot(placing, returned_s[...])
    small.advance()
    wait_all(lowest.copies(1))
    lowest.add(1)
    start_all(lowest.copies(2))
    pushed = push_blocks(
        place, push_ref, landing_ref, push_sems, push_ref.shape[1] - landing_ref.shape[1]
    )
    start_all(pushed)
    small.advance()

    def finish(layer, one):
        for part, rows in zip(one.result(), (slice(0, split), slice(split, tall))):
            packed_ref[layer, rows, :] = part

    for layer, one in enumerate(upper_layers):
        wait_all(one.copies(3))
        finish(layer + 1, one)
    wait_all(lowest.copies(2))
    lowest.add(2)
    start_all(lowest.copies(3))
    while small.done < len(small.peers):
        small.advance()
    small_out_ref[...] = totals[len(small.peers)]
    wait_all(lowest.copies(3))
    finish(0, lowest)
    wait_all(pushed)


def final_sums(blocks, partials, smalls, finishing, returned, push, grid_shape, buckets_count):
    layers = len(partials) + 1
    shape = blocks.shape
    tall = shape[4]
    width = finishing[-1].shape[1]
    landings = [pltpu.VMEM(one, bf16) for one in whole_blocks(shape, tall // 2)]
    steps = small_steps(grid_shape)
    rows = sum(one.shape[0] for one in smalls[: 3 * layers]) + smalls[3 * layers].shape[0]
    small_shape = (rows, width)
    sems = pltpu.SemaphoreType.DMA((scatter_copies(grid_shape),))
    small_sems = pltpu.SemaphoreType.DMA((steps,))
    outs = [jax.ShapeDtypeStruct((layers, tall, shape[5]), f32)]
    outs += [jax.ShapeDtypeStruct(small_shape, f32), jax.ShapeDtypeStruct(finishing[-1].shape, f32)]
    outs.append(landing_of(push, push.shape[1] - cut_of(push)))
    ins = [blocks, *[array for pair in partials for array in pair], *smalls, *finishing]
    return pl.pallas_call(
        partial(final_kernel, grid_shape, layers, buckets_count),
        in_specs=[vmem_spec] * len(ins) + [any_spec] * 3,
        out_specs=[vmem_spec] * (len(outs) - 1) + [any_spec],
        out_shape=outs,
        scratch_shapes=landings
        + landings[5:] * (layers - 1)
        + [pltpu.VMEM((steps + 1, *small_shape), f32), pltpu.VMEM((steps, *small_shape), f32)]
        + [pltpu.VMEM(returned[0].shape, bf16)]
        + [sems, sems] * layers
        + [small_sems, small_sems, pltpu.SemaphoreType.DMA((grid_shape[1],))]
        + [pltpu.SemaphoreType.DMA((grid_shape[0] // 2 - 1,))] * 2,
        compiler_params=params(24),
        cost_estimate=lasting(60),
        name="final_sums",
    )(*ins, *returned, push)


def unblock(grid_shape, blocks_ref, mats_ref, router_ref):
    count_x, count_y = grid_shape
    tall = mats_ref.shape[1] // count_x
    wide = mats_ref.shape[2] // count_y
    router_rows = []
    for first in range(count_x):
        spots = [(first // 2, first % 2, second // 2, second % 2) for second in range(count_y)]
        rows = slice(first * tall, (first + 1) * tall)
        for which in range(4):
            lanes = slice(which * wide, (which + 1) * wide)
            mats_ref[which, rows, :] = jnp.concatenate(
                [blocks_ref[(*spot, slice(0, tall), lanes)] for spot in spots], axis=1
            )
        router_rows.append(
            jnp.concatenate(
                [blocks_ref[(*spot, slice(tall, tall + 1), slice(0, tall))] for spot in spots],
                axis=0,
            )
        )
    router_ref[...] = jnp.concatenate(router_rows, axis=1)


def turned(row):
    return jnp.broadcast_to(row, (128, row.shape[1])).T[:, 0:1]


def start_kernel(
    grid_shape,
    wq_ref,
    wk_ref,
    wv_ref,
    wo_ref,
    router_rows_ref,
    buckets_ref,
    table_ref,
    piece_row_ref,
    route_row_ref,
    cotangent_ref,
    mats_ref,
    router_ref,
    later_ref,
    bias_ref,
    slot_col_ref,
    slot_row_ref,
    chosen_ref,
    spread_ref,
    far_ref,
    full_s,
    column_s,
    spread_send,
    spread_recv,
    later_send,
    later_recv,
    z_send,
    z_recv,
    send_sems,
    recv_sems,
):
    place = Place(grid_shape)
    layers, tall, wide = wq_ref.shape
    split = tall // 2
    y, c, z, x = place.y, place.c, place.z, place.x

    def packed(layer):
        return jnp.concatenate([ref[layer] for ref in (wq_ref, wk_ref, wv_ref, wo_ref)], axis=1)

    column_s[z, :tall] = packed(0)
    column_s[z, tall:] = router_rows_ref[0]
    members = grid_shape[1]
    spread = Exchange(
        members, spread_ref.shape[0] // members, spread_ref, far_ref, spread_send, spread_recv
    )
    spread_copies = [spread.copy(apart) for apart in in_third(members, 0)]
    greet(
        [place.core_peer(), place.x_peer()]
        + place.y_peers()
        + place.z_peers()
        + [spread.peer(apart) for apart in in_third(members, 0)]
    )
    first = gather_z(place, column_s.at[z], column_s.at[z], (z_send, z_recv))
    start_all(first)
    along_z = []
    for layer in range(1, layers):
        later_ref[layer - 1, z, :tall] = packed(layer)
        later_ref[layer - 1, z, tall:] = router_rows_ref[layer]
        mine = later_ref.at[layer - 1, z]
        along_z += gather_z(place, mine, mine, (later_send.at[layer - 1], later_recv.at[layer - 1]))

    seq_len, experts = chosen_ref.shape
    capacity = 2 * seq_len // experts
    heads = bias_ref.shape[0]
    buckets_count = table_ref.shape[1]
    in_bucket = (
        lax.broadcasted_iota(jnp.int32, (buckets_count, 2 * seq_len), 0) == buckets_ref[...]
    )
    offsets = dot(table_ref[...], in_bucket.astype(f32).astype(bf16))
    key_pos = lax.broadcasted_iota(jnp.int32, (seq_len, seq_len), 0)
    query_pos = lax.broadcasted_iota(jnp.int32, (seq_len, seq_len), 1)
    route_row, piece_row = route_row_ref[...], piece_row_ref[...]
    route_col, piece_col = turned(route_row), turned(piece_row)
    chosen = (lax.broadcasted_iota(jnp.int32, (seq_len, experts), 1) == route_col).astype(f32)
    chosen_t = (lax.broadcasted_iota(jnp.int32, (experts, seq_len), 0) == route_row).astype(f32)
    chosen_ref[...] = chosen
    earlier = (key_pos < query_pos).astype(f32).astype(bf16)
    before_t = dot(chosen_t.astype(bf16), earlier)
    rank_row = jnp.sum(before_t * chosen_t, axis=0, keepdims=True)
    slot_row_ref[...] = route_row * capacity + rank_row.astype(jnp.int32)
    later = (key_pos > query_pos).astype(f32).astype(bf16)
    before = dot(later, chosen.astype(bf16))
    rank_col = jnp.sum(before * chosen, axis=1, keepdims=True)
    slot_col_ref[...] = route_col * capacity + rank_col.astype(jnp.int32)
    placing = placing_rows(slot_row_ref[...], spread_ref.shape[0])
    spread_ref[...] = dot(placing, cotangent_ref[...]).astype(bf16)

    same = (piece_col == piece_row) & (piece_col > 0)
    allowed = (key_pos <= query_pos) | same

    def bias_for(head):
        row = jnp.broadcast_to(offsets[head : head + 1], (seq_len, 2 * seq_len))
        shifted = pltpu.roll(row, seq_len + 1, 1, stride=1, stride_axis=0)[:, :seq_len]
        bias_ref[head] = jnp.where(allowed, shifted, masked_out).astype(bf16)

    for head in range(heads // 2):
        bias_for(head)
    wait_all(first)
    sems = (send_sems, recv_sems)
    second = gather_second(place, column_s, full_s, split, sems)
    start_all(second)
    start_all(along_z)
    start_all(spread_copies)
    spread.keep_own()
    full_s[y, c, :, x] = column_s[...]
    for head in range(heads // 2, heads):
        bias_for(head)
    wait_all(second)
    third = gather_third(place, full_s, split, sems)
    start_all(third)

    wait_all(third)
    fourth = gather_core(place, full_s, sems)
    start_all(fourth)
    wait_all(fourth)
    unblock(grid_shape, full_s, mats_ref, router_ref)
    wait_all(along_z)
    wait_all(spread_copies)


def start(mats, router_rows, buckets, table_t, piece_ids, route, cotangent, grid_shape):
    layers, tall, wide = mats[0].shape
    seq_len = piece_ids.shape[0]
    heads = table_t.shape[0]
    width = tall * grid_shape[0]
    experts = grid_shape[1]
    block = (router_rows.shape[1] + tall, 4 * wide)
    half = (grid_shape[0] // 2, 2, grid_shape[1] // 2, 2)
    ins = (
        *mats,
        router_rows,
        buckets,
        table_t,
        piece_ids[None, :],
        route.reshape(1, seq_len),
        cotangent,
    )
    outs = (
        jax.ShapeDtypeStruct((4, width, width), bf16),
        jax.ShapeDtypeStruct((experts, width), bf16),
        jax.ShapeDtypeStruct((layers - 1, half[2], *block), bf16),
        jax.ShapeDtypeStruct((heads, seq_len, seq_len), bf16),
        jax.ShapeDtypeStruct((seq_len, 1), jnp.int32),
        jax.ShapeDtypeStruct((1, seq_len), jnp.int32),
        jax.ShapeDtypeStruct((seq_len, experts), f32),
        jax.ShapeDtypeStruct((2 * seq_len, width), bf16),
        jax.ShapeDtypeStruct((2 * seq_len, width), bf16),
    )
    along_z, others = gather_copies(grid_shape)
    return pl.pallas_call(
        partial(start_kernel, grid_shape),
        in_specs=[vmem_spec] * len(ins),
        out_specs=[vmem_spec] * len(outs),
        out_shape=outs,
        scratch_shapes=[
            pltpu.VMEM((*half, *block), bf16),
            pltpu.VMEM((half[2], *block), bf16),
            pltpu.SemaphoreType.DMA((experts,)),
            pltpu.SemaphoreType.DMA((experts,)),
            pltpu.SemaphoreType.DMA((layers - 1, along_z)),
            pltpu.SemaphoreType.DMA((layers - 1, along_z)),
            pltpu.SemaphoreType.DMA((along_z,)),
            pltpu.SemaphoreType.DMA((along_z,)),
            pltpu.SemaphoreType.DMA((others,)),
            pltpu.SemaphoreType.DMA((others,)),
        ],
        compiler_params=params(0),
        cost_estimate=lasting(45),
        name="start",
    )(*ins)


def half_masks(rows, width):
    lane = lax.broadcasted_iota(jnp.int32, (rows, width), 1)
    return lane < (width // 2)


def gates_of(logits, slot_col, chosen, gates_ref):
    experts = gates_ref.shape[0]
    seq_len = slot_col.shape[0]
    capacity = 2 * seq_len // experts
    gate = jnp.sum(jax.nn.softmax(logits, axis=-1) * chosen, axis=1, keepdims=True)
    places = lax.broadcasted_iota(jnp.int32, (seq_len, 2 * seq_len), 1)
    row = jnp.sum(jnp.where(places == slot_col, gate, 0.0), axis=0, keepdims=True)
    gates_ref[...] = jnp.zeros_like(gates_ref)
    for expert in range(experts):
        mine = row[:, expert * capacity : (expert + 1) * capacity]
        gates_ref[expert, :, :capacity] = jnp.broadcast_to(mine, (gates_ref.shape[1], capacity))


def forward_kernel(
    head_dim,
    grid_shape,
    blocked,
    last,
    hidden_ref,
    gain_attn_ref,
    gain_ffn_ref,
    slot_row_ref,
    slot_col_ref,
    chosen_ref,
    *refs,
):
    refs = list(refs)
    take = refs.pop
    blocks_ref = take(0) if blocked else None
    mats_ref, router_ref = (None, None) if blocked else (take(0), take(0))
    spread_ref = take(0)
    bias_ref = take(0)
    if blocked:
        mats_ref, router_ref = take(0), take(0)
    q_ref, k_ref, v_ref, att_ref, lse_ref, middle_ref, logits_ref, sent_ref = (
        take(0) for _ in range(8)
    )
    gates_ref = take(0) if last else None
    far_ref, send_sems, recv_sems = refs
    pair, pairs = pl.program_id(0), pl.num_programs(0)
    seq_len = hidden_ref.shape[0]
    width = 2 * head_dim
    step = min(512, seq_len)

    members = grid_shape[1]
    spread = Exchange(members, spread_ref.shape[0] // members, spread_ref, far_ref, send_sems, recv_sems)
    aparts = in_third(members, 2 if last else 1)

    @pl.when(pair == 0)
    def _():
        greet([spread.peer(apart) for apart in aparts])
        start_all([spread.copy(apart) for apart in aparts])

    @pl.when(pair == 0)
    def _():
        if blocked:
            unblock(grid_shape, blocks_ref, mats_ref, router_ref)
        hidden = hidden_ref[...].astype(f32)
        normed = (hidden * rms_factor(hidden) * gain_attn_ref[...]).astype(bf16)
        q_ref[...] = dot(normed, mats_ref[0]).astype(bf16)
        k_ref[...] = dot(normed, mats_ref[1]).astype(bf16)
        v_ref[...] = dot(normed, mats_ref[2]).astype(bf16)

    lanes = pl.ds(pl.multiple_of(pair * width, width), width)
    q2 = q_ref[:, lanes] * jnp.asarray(head_dim**-0.5, bf16)
    k2 = k_ref[:, lanes]
    v2t = v_ref[:, lanes].T
    first = half_masks(seq_len, width)
    for half in range(2):
        q_one = jnp.where(first if half == 0 else ~first, q2, jnp.zeros_like(q2))
        v_one = v2t[half * head_dim : (half + 1) * head_dim]
        for begin in range(0, seq_len, step):
            cols = slice(begin, begin + step)
            scores = dot(k2, q_one[cols], 1, 1) + bias_ref[half, :, cols].astype(f32)
            top = jnp.max(scores, axis=0, keepdims=True)
            raised = jnp.exp(scores - top)
            total = jnp.sum(raised, axis=0, keepdims=True)
            probs = raised.astype(bf16)
            rows = pl.ds(pl.multiple_of(pair * width + half * head_dim, head_dim), head_dim)
            att_ref[rows, cols] = (dot(v_one, probs) * (1.0 / total)).astype(bf16)
            lse_ref[0, half : half + 1, cols] = top + jnp.log(total)

    @pl.when(pair == pairs - 1)
    def _():
        middle = hidden_ref[...].astype(f32) + dot(att_ref[...].T, mats_ref[3])
        middle_ref[...] = middle
        ffn_in = (middle * rms_factor(middle) * gain_ffn_ref[...]).astype(bf16)
        logits = dot(ffn_in, router_ref[...], 1, 1)
        logits_ref[...] = logits
        if gates_ref is not None:
            gates_of(logits, slot_col_ref[...], chosen_ref[...], gates_ref)
        placing = placing_rows(slot_row_ref[...], sent_ref.shape[0])
        sent_ref[...] = dot(placing, ffn_in).astype(bf16)

    @pl.when(pair == pairs - 1)
    def _():
        wait_all([spread.copy(apart) for apart in aparts])


def attention_forward(
    hidden,
    gain_attn,
    gain_ffn,
    slots_and_chosen,
    bias,
    grid_shape,
    identifier,
    spread,
    last,
    blocks=None,
    mats=None,
):
    seq_len, width = hidden.shape
    heads = bias.shape[0]
    head_dim = width // heads
    slots = 2 * seq_len
    experts = grid_shape[1]
    blocked = blocks is not None
    ins = [hidden, gain_attn, gain_ffn, *slots_and_chosen] + ([blocks] if blocked else list(mats))
    in_specs = whole_of(ins)
    ins.append(spread)
    in_specs.append(any_spec)
    ins.append(bias)
    in_specs.append(pl.BlockSpec((2, seq_len, seq_len), lambda p: (p, 0, 0)))
    tall = jax.ShapeDtypeStruct((seq_len, width), bf16)
    outs = [
        tall,
        tall,
        tall,
        jax.ShapeDtypeStruct((width, seq_len), bf16),
        jax.ShapeDtypeStruct((heads // 2, 2, seq_len), f32),
        jax.ShapeDtypeStruct((seq_len, width), f32),
        jax.ShapeDtypeStruct((seq_len, experts), f32),
        jax.ShapeDtypeStruct((slots, width), bf16),
    ]
    if last:
        outs.append(jax.ShapeDtypeStruct((experts, 8, max(128, slots // experts)), f32))
    out_specs = whole_of(outs)
    out_specs[4] = pl.BlockSpec((1, 2, seq_len), lambda p: (p, 0, 0))
    if blocked:
        more = [
            jax.ShapeDtypeStruct((4, width, width), bf16),
            jax.ShapeDtypeStruct((experts, width), bf16),
        ]
        outs = more + outs
        out_specs = whole_of(more) + out_specs
    outs.append(jax.ShapeDtypeStruct(spread.shape, bf16))
    out_specs.append(any_spec)
    sems = pltpu.SemaphoreType.DMA((experts,))
    scratch = [sems, sems]
    got = pl.pallas_call(
        partial(forward_kernel, head_dim, grid_shape, blocked, last),
        grid=(heads // 2,),
        in_specs=in_specs,
        out_specs=out_specs,
        out_shape=outs,
        scratch_shapes=scratch,
        compiler_params=params(identifier),
        cost_estimate=lasting(25),
        name="attention_forward",
    )(*ins)
    return tuple(got) if blocked else tuple(mats) + tuple(got)


def diagonal_fold(values, seq_len):
    rows, wide = seq_len, 2 * seq_len
    folded = None
    tile = 128
    count = seq_len // tile
    for row_tile in range(count):
        piece = values[row_tile * tile : (row_tile + 1) * tile].astype(f32)
        before = (count - 1 - row_tile) * tile
        after = wide - seq_len - before
        parts = []
        if before:
            parts.append(jnp.zeros((tile, before), f32))
        parts.append(piece)
        if after:
            parts.append(jnp.zeros((tile, after), f32))
        padded = jnp.concatenate(parts, axis=1)
        folded = padded if folded is None else folded + padded
    rows = tile
    while rows > 1:
        rows //= 2
        folded = pltpu.roll(folded[:rows], rows, 1) + folded[rows:]
    return folded


def reblock(grid_shape, blocks_ref, which, values):
    count_x, count_y = grid_shape
    tall = values.shape[0] // count_x
    wide = values.shape[1] // count_y
    for first in range(count_x):
        for second in range(count_y):
            spot = (first // 2, first % 2, second // 2, second % 2)
            lanes = slice(which * wide, (which + 1) * wide)
            blocks_ref[(*spot, slice(None), lanes)] = values[
                first * tall : (first + 1) * tall, second * wide : (second + 1) * wide
            ]


def d_logits_of(d_gate, logits, chosen):
    shares = jax.nn.softmax(logits, axis=-1)
    gate = jnp.sum(shares * chosen, axis=1, keepdims=True)
    return (d_gate * shares * (chosen - gate)).astype(bf16)


def spread_into(grad_now, comb_ref, slot_row_ref, chosen_ref, logits_ref, d_sent_ref, d_logits_ref):
    d_gate = jnp.sum(grad_now * comb_ref[...], axis=1, keepdims=True)
    logits, chosen = logits_ref[...], chosen_ref[...]
    d_logits_ref[...] = d_logits_of(d_gate, logits, chosen)
    gate = jnp.sum(jax.nn.softmax(logits, axis=-1) * chosen, axis=1, keepdims=True)
    placing = placing_rows(slot_row_ref[...], d_sent_ref.shape[0])
    d_sent_ref[...] = dot(placing, (gate * grad_now).astype(bf16)).astype(bf16)


def backward_kernel(
    head_dim,
    grid_shape,
    spreads,
    returns,
    pushes,
    unread,
    d_back_ref,
    slot_col_ref,
    d_logits_ref,
    grad_ref,
    middle_ref,
    hidden_ref,
    gain_attn_ref,
    gain_ffn_ref,
    mats_ref,
    router_ref,
    q_ref,
    k_ref,
    v_ref,
    att_ref,
    *refs,
):
    refs = list(refs)
    take = refs.pop
    spread_in = [take(0) for _ in range(4)] if spreads else []
    bias_ref, lse_ref = take(0), take(0)
    made_ref = take(0)
    push_refs = (take(0), take(0)) if pushes else ()
    del refs[:unread]
    grad_new_ref, blocks_ref, gwr_ref, gga_ref, ggf_ref, offsets_ref = (take(0) for _ in range(6))
    spread_out = [take(0) for _ in range(2)] if spreads else []
    returned_ref = take(0)
    landing_refs = (take(0), take(0)) if pushes else ()
    d_att_s, d_middle_s, dqt_s, dk_s, dv_s, probs_s, scores_s = (take(0) for _ in range(7))
    own_sem, *sems = refs[:3]
    members = grid_shape[1]
    place = Place(grid_shape)
    pushed = []
    for src, landing, last_rows in zip(push_refs, landing_refs, (True, False)):
        begin = src.shape[1] - landing.shape[1] if last_rows else 0
        pushed += push_blocks(place, src, landing, refs[3:], begin, len(pushed))
    back = Exchange(members, made_ref.shape[0] // members, made_ref, returned_ref, *sems)
    mine = back.block(back.me)
    own = None
    if returns:
        own = pltpu.make_async_copy(made_ref.at[mine, :], returned_ref.at[mine, :], own_sem)
    aparts = part_of(members, returns)

    @pl.when(pl.program_id(0) == 0)
    def _():
        greet([back.peer(apart) for apart in aparts] + (place.y_peers() if pushes else []))
        start_all(pushed + [back.copy(apart) for apart in aparts])
        if returns:
            own.start()

    pair, pairs = pl.program_id(0), pl.num_programs(0)
    seq_len = hidden_ref.shape[0]
    width = 2 * head_dim
    step = min(512, seq_len)
    scale = head_dim**-0.5

    @pl.when(pair == 0)
    def _():
        placing = placing_cols(slot_col_ref[...], d_back_ref.shape[0])
        d_logits = d_logits_ref[...]
        d_ffn = dot(placing, d_back_ref[...]) + dot(d_logits, router_ref[...])
        middle = middle_ref[...]
        gain_row = gain_ffn_ref[...]
        ffn_in = (middle * rms_factor(middle) * gain_row).astype(bf16)
        gwr_ref[...] = dot(d_logits, ffn_in, 0, 0)
        d_middle, d_gain = rms_pull(middle, gain_row, d_ffn)
        ggf_ref[...] = d_gain
        d_middle = d_middle + grad_ref[...].astype(f32)
        d_middle_s[...] = d_middle
        d_low = d_middle.astype(bf16)
        reblock(grid_shape, blocks_ref, 3, dot(att_ref[...], d_low).astype(bf16))
        d_att_s[...] = dot(d_low, mats_ref[3], 1, 1).astype(bf16)

    lanes = pl.ds(pl.multiple_of(pair * width, width), width)
    q2 = q_ref[:, lanes] * jnp.asarray(scale, bf16)
    k2 = k_ref[:, lanes]
    v2 = v_ref[:, lanes]
    da2 = d_att_s[:, lanes]
    k2t = k2.T
    first = half_masks(seq_len, width)
    d_key = jnp.zeros((seq_len, width), f32)
    d_value = jnp.zeros((seq_len, width), f32)
    for half in range(2):
        mask = first if half == 0 else ~first
        q_one = jnp.where(mask, q2, jnp.zeros_like(q2))
        da_one = jnp.where(mask, da2, jnp.zeros_like(da2))
        k_one = k2t[half * head_dim : (half + 1) * head_dim]
        rows = pl.ds(pl.multiple_of(pair * width + half * head_dim, head_dim), head_dim)
        for start in range(0, seq_len, step):
            cols = slice(start, start + step)
            scores = dot(k2, q_one[cols], 1, 1) + bias_ref[half, :, cols].astype(f32)
            probs = jnp.exp(scores - lse_ref[0, half : half + 1, cols])
            d_probs = dot(v2, da_one[cols], 1, 1)
            inner = jnp.sum(probs * d_probs, axis=0, keepdims=True)
            d_scores = (probs * (d_probs - inner)).astype(bf16)
            probs_s[:, cols] = probs.astype(bf16)
            scores_s[:, cols] = d_scores
            dqt_s[rows, cols] = (dot(k_one, d_scores) * scale).astype(bf16)
        d_key = d_key + dot(scores_s[...], q_one)
        d_value = d_value + dot(probs_s[...], da_one)
        offsets_ref[pl.ds(2 * pair + half, 1), :] = diagonal_fold(scores_s[...], seq_len)
    dk_s[:, lanes] = d_key.astype(bf16)
    dv_s[:, lanes] = d_value.astype(bf16)

    @pl.when(pair == pairs - 1)
    def _():
        hidden = hidden_ref[...].astype(f32)
        gain_row = gain_attn_ref[...]
        normed_t = (hidden * rms_factor(hidden) * gain_row).astype(bf16).T
        d_query = dqt_s[...].T
        d_normed = dot(d_query, mats_ref[0], 1, 1)
        reblock(grid_shape, blocks_ref, 0, dot(normed_t, d_query).astype(bf16))
        d_normed = d_normed + dot(dk_s[...], mats_ref[1], 1, 1)
        reblock(grid_shape, blocks_ref, 1, dot(normed_t, dk_s[...]).astype(bf16))
        d_normed = d_normed + dot(dv_s[...], mats_ref[2], 1, 1)
        reblock(grid_shape, blocks_ref, 2, dot(normed_t, dv_s[...]).astype(bf16))
        d_hidden, d_gain = rms_pull(hidden, gain_row, d_normed)
        gga_ref[...] = d_gain
        grad_new = d_hidden + d_middle_s[...]
        grad_new_ref[...] = grad_new
        if spreads:
            spread_into(grad_new, *spread_in, *spread_out)

    @pl.when(pair == pairs - 1)
    def _():
        wait_all(pushed + [back.copy(apart) for apart in aparts])
        if returns:
            own.wait()


def attention_backward(
    d_back,
    slot_col,
    d_logits,
    grad_now,
    middle,
    hidden,
    gains,
    mats,
    q_k_v,
    attended,
    bias,
    lse,
    grid_shape,
    below=None,
    after=(),
    made=None,
    returns=False,
    push=None,
    identifier=None,
):
    seq_len, width = hidden.shape
    heads = bias.shape[0]
    head_dim = width // heads
    experts = mats[1].shape[0]
    count_x, count_y = grid_shape
    ins = (
        d_back,
        slot_col,
        d_logits,
        grad_now,
        middle,
        hidden,
        *gains,
        *mats,
        *q_k_v,
        attended,
    )
    spreads = below is not None
    if spreads:
        ins = ins + tuple(below)
    row = jax.ShapeDtypeStruct((1, width), f32)
    outs = (
        jax.ShapeDtypeStruct((seq_len, width), f32),
        jax.ShapeDtypeStruct(
            (count_x // 2, 2, count_y // 2, 2, width // count_x, 4 * (width // count_y)), bf16
        ),
        jax.ShapeDtypeStruct((experts, width), f32),
        row,
        row,
        jax.ShapeDtypeStruct((heads, 2 * seq_len), f32),
    )
    if spreads:
        outs = outs + (
            jax.ShapeDtypeStruct((2 * seq_len, width), bf16),
            jax.ShapeDtypeStruct(d_logits.shape, bf16),
        )
    outs = outs + (jax.ShapeDtypeStruct(made.shape, bf16),)
    pushes = push is not None
    out_specs = whole_of(outs)
    out_specs[-1] = any_spec
    if pushes:
        rows = [push[0].shape[1] - cut_of(push[0]), cut_of(push[1])]
        outs = outs + tuple(landing_of(one, many) for one, many in zip(push, rows))
        out_specs += [any_spec] * 2
    return pl.pallas_call(
        partial(backward_kernel, head_dim, grid_shape, spreads, returns, pushes, len(after)),
        grid=(heads // 2,),
        in_specs=whole_of(ins)
        + [
            pl.BlockSpec((2, seq_len, seq_len), lambda p: (p, 0, 0)),
            pl.BlockSpec((1, 2, seq_len), lambda p: (p, 0, 0)),
        ]
        + [any_spec] * (len(after) + 1 + 2 * pushes),
        out_specs=out_specs,
        out_shape=outs,
        scratch_shapes=[
            pltpu.VMEM((seq_len, width), bf16),
            pltpu.VMEM((seq_len, width), f32),
            pltpu.VMEM((width, seq_len), bf16),
            pltpu.VMEM((seq_len, width), bf16),
            pltpu.VMEM((seq_len, width), bf16),
            pltpu.VMEM((seq_len, seq_len), bf16),
            pltpu.VMEM((seq_len, seq_len), bf16),
        ]
        + [pltpu.SemaphoreType.DMA]
        + [pltpu.SemaphoreType.DMA((count_y,))] * 2
        + [pltpu.SemaphoreType.DMA((2 * (count_x // 2 - 1),))] * (2 * pushes),
        compiler_params=params(identifier),
        cost_estimate=lasting(32),
        name="attention_backward",
    )(*ins, bias, lse, made, *(push if pushes else ()), *after)


class Exchange:
    def __init__(self, members, rows, src, dst, send_sems, recv_sems):
        self.me = lax.axis_index("gy")
        self.bits = members.bit_length() - 1
        self.rows, self.src, self.dst = rows, src, dst
        self.send_sems, self.recv_sems = send_sems, recv_sems

    def block(self, index):
        return pl.ds(pl.multiple_of(index * self.rows, self.rows), self.rows)

    def peer(self, apart):
        return {"gy": xor_of(self.me, apart, self.bits)}

    def copy(self, apart):
        peer = xor_of(self.me, apart, self.bits)
        return pltpu.make_async_remote_copy(
            src_ref=self.src.at[self.block(peer), :],
            dst_ref=self.dst.at[self.block(self.me), :],
            send_sem=self.send_sems.at[apart],
            recv_sem=self.recv_sems.at[apart],
            device_id={"gy": peer},
            device_id_type=MESH,
        )

    def keep_own(self):
        self.dst[self.block(self.me), :] = self.src[self.block(self.me), :]


class Leading(Exchange):
    def __init__(self, members, src, dst, send_sems, recv_sems):
        super().__init__(members, 1, src, dst, send_sems, recv_sems)

    def copy(self, apart):
        peer = xor_of(self.me, apart, self.bits)
        sems = (self.send_sems, self.recv_sems)
        return send(self.src.at[peer], self.dst.at[self.me], sems, apart, {"gy": peer})

    def keep_own(self):
        self.dst[self.me] = self.src[self.me]


def peers_along_gy(members):
    me = lax.axis_index("gy")
    bits = members.bit_length() - 1
    return [{"gy": xor_of(me, apart, bits)} for apart in range(1, members)]


def gelu_and_slope(pre):
    inner_scale = 0.7978845608028654
    square = pre * pre
    bent = jnp.tanh(inner_scale * pre * (1.0 + 0.044715 * square))
    act = 0.5 * pre * (1.0 + bent)
    slope = 0.5 * (1.0 + bent) + 0.5 * pre * (1.0 - bent * bent) * (
        inner_scale * (1.0 + 3 * 0.044715 * square)
    )
    return act, slope


def gelu_only(pre):
    inner_scale = 0.7978845608028654
    return 0.5 * pre * (1.0 + jnp.tanh(inner_scale * pre * (1.0 + 0.044715 * pre * pre)))


def send_order(members):
    return range(1, members)


def early(members):
    quarter = max(1, members // 4)
    return [apart for apart in range(members) if (apart // quarter) % 2 == 0]


def part_of(members, first):
    chosen = early(members)
    return [a for a in range(1, members) if (a in chosen) == first]


def third_of(members, apart):
    quarter = max(1, members // 4)
    if (apart // quarter) % 2 == 0:
        return 0
    return 1 + (2 * (apart % quarter)) // quarter


def in_third(members, third):
    return [apart for apart in range(1, members) if third_of(members, apart) == third]


def collect(me, members, rows, refs, which_of, dst, sems):
    copies = []
    for apart in range(members):
        start = xor_of(me, apart, bits_of(members)) * rows
        here = pl.ds(pl.multiple_of(start, rows), rows)
        ref = refs[which_of(apart)]
        copies.append(pltpu.make_async_copy(ref.at[here, :], dst.at[here, :], sems.at[apart]))
    return copies


class Weights:
    def __init__(self, place, halves, whole_refs, local_sems, sems):
        blocks, _, units = halves[0].shape
        self.local, self.remote = [], []
        for which, (part, into) in enumerate(zip(halves, whole_refs)):
            for block in range(blocks):
                index = which * blocks + block
                begin = pl.multiple_of((place.c * blocks + block) * units, units)
                dst = into.at[:, pl.ds(begin, units)]
                src = part.at[block]
                self.local.append(pltpu.make_async_copy(src, dst, local_sems.at[index]))
                self.remote.append(send(src, dst, sems, index, place.core_peer()))
        self.blocks = blocks

    def start_local(self):
        start_all(self.local)

    def start_remote(self):
        start_all(self.remote)

    def wait(self, which):
        mine = slice(which * self.blocks, (which + 1) * self.blocks)
        for copy in self.local[mine] + self.remote[mine]:
            copy.wait()


def weight_gradients(place, products, sends, landings, outs, sems, after_first=()):
    blocks, _, units = outs[0].shape

    def product(lhs, rhs_ref, which, into_ref):
        @pl.loop(0, blocks)
        def _(block):
            begin = pl.multiple_of((which * blocks + block) * units, units)
            into_ref[block] = dot(lhs, rhs_ref[:, pl.ds(begin, units)]).astype(bf16)

    for index, (lhs_ref, rhs_ref) in enumerate(products):
        lhs = lhs_ref[...].T
        product(lhs, rhs_ref, 1 - place.c, sends[index])
        copy = send(sends[index], landings[index], sems, index, place.core_peer())
        copy.start()
        product(lhs, rhs_ref, place.c, outs[index])
        copy.wait()

        @pl.loop(0, blocks)
        def _(block, index=index):
            add_low(outs[index], (block,), outs[index][block], landings[index][block])

        if index == 0:
            start_all(after_first)


def push_blocks(place, src, landing, sems, begin, base=0):
    rows = pl.ds(begin, landing.shape[1])
    return [
        send(
            src.at[place.y_at(apart), rows],
            landing.at[apart - 1],
            sems,
            base + apart - 1,
            place.y_peer(apart),
        )
        for apart in range(1, place.count_y)
    ]


def cut_of(blocks):
    return blocks.shape[1] // 3 * 2


def landing_of(blocks, rows):
    return jax.ShapeDtypeStruct((blocks.shape[0] - 1, rows, blocks.shape[2]), bf16)


def chunk_of(members, rows):
    return max(1, min(members, 256 // rows))


def expert_forward_kernel(
    grid_shape,
    gathers,
    sent_ref,
    slot_col_ref,
    chosen_ref,
    logits_ref,
    middle_ref,
    win_ref,
    wout_ref,
    *refs,
):
    refs = list(refs)
    take = refs.pop
    column_ref = take(0) if gathers else None
    arrived_ref, comb_ref, out_ref = (take(0) for _ in range(3))
    full_ref = take(0) if gathers else None
    win_s, wout_s, made_s, returned_s, w_sems = (take(0) for _ in range(5))
    send_sems, recv_sems, back_send_sems, back_recv_sems = (take(0) for _ in range(4))
    weight_sems = (take(0), take(0))
    members = grid_shape[1]
    slots = sent_ref.shape[0]
    rows = slots // members
    group = chunk_of(members, rows)
    chunks = members // group
    chunk_bits = chunks.bit_length() - 1
    hidden_units = win_s.shape[1]
    tile = min(768, hidden_units)
    place = Place(grid_shape)
    weights = Weights(place, (win_ref, wout_ref), (win_s, wout_s), w_sems, weight_sems)
    weights.start_local()
    more_peers = place.y_peers() if gathers else []
    greet(peers_along_gy(members) + [place.core_peer()] + more_peers)
    weights.start_remote()
    there = Exchange(members, rows, sent_ref, arrived_ref, send_sems, recv_sems)
    back = Exchange(members, rows, made_s, returned_s, back_send_sems, back_recv_sems)
    for apart in send_order(members):
        there.copy(apart).start()
    there.keep_own()
    if gathers:
        own_sem, *sems = refs
        split = (full_ref.shape[4] - tile_rows) // 2
        own = pltpu.make_async_copy(
            column_ref, full_ref.at[place.y, place.c, :, place.x], own_sem
        )
        own.start()
        second = gather_second(place, column_ref, full_ref, split, sems)
        third = gather_third(place, full_ref, split, sems)
        fourth = gather_core(place, full_ref, sems)
        start_all(second)
    weights.wait(0)
    weights.wait(1)
    my_chunk = there.me // group

    def chunk_rows(index):
        start = xor_of(my_chunk, index, chunk_bits) * (group * rows)
        return pl.ds(pl.multiple_of(start, group * rows), group * rows)

    def work(index, first):
        for member in range(first, group):
            there.copy(index * group + member).wait_recv()
        here = chunk_rows(index)
        taken = arrived_ref[here, :]
        total = jnp.zeros((group * rows, taken.shape[1]), f32)
        for start in range(0, hidden_units, tile):
            units = slice(start, start + tile)
            act = gelu_only(dot(taken, win_s[:, units])).astype(bf16)
            total = total + dot(act, wout_s[:, units], 1, 1)
        made_s[here, :] = total.astype(bf16)
        for member in range(first, group):
            back.copy(index * group + member).start()

    work(0, 1)
    back.keep_own()
    half = chunks // 2

    @pl.loop(1, half)
    def _(index):
        work(index, 0)

    if gathers:
        own.wait()
        wait_all(second)
        start_all(third)

    @pl.loop(half, chunks)
    def _(index):
        work(index, 0)

    if gathers:
        wait_all(third)
        start_all(fourth)
    slot_col = slot_col_ref[...]
    comb_ref[...] = jnp.zeros_like(comb_ref)

    def gather_back(index, first):
        for member in range(first, group):
            back.copy(index * group + member).wait_recv()
        begin = xor_of(my_chunk, index, chunk_bits) * (group * rows)
        places = lax.broadcasted_iota(jnp.int32, (slot_col.shape[0], group * rows), 1) + begin
        placing = (places == slot_col).astype(f32).astype(bf16)
        comb_ref[...] += dot(placing, returned_s[chunk_rows(index), :])

    gather_back(0, 1)

    @pl.loop(1, chunks)
    def _(index):
        gather_back(index, 0)

    gate = jnp.sum(jax.nn.softmax(logits_ref[...], axis=-1) * chosen_ref[...], axis=1, keepdims=True)
    out_ref[...] = middle_ref[...] + gate * comb_ref[...]
    if gathers:
        wait_all(fourth)

    @pl.loop(1, members)
    def _(apart):
        there.copy(apart).wait_send()
        back.copy(apart).wait_send()


def doubled(half):
    return pltpu.VMEM((half.shape[1], 2 * half.shape[0] * half.shape[2]), bf16)


def expert_forward(
    sent, slot_col, chosen_f, logits, middle, full_in, full_out, grid_shape, identifier, column=None
):
    members = grid_shape[1]
    gathers = column is not None
    ins = [sent, slot_col, chosen_f, logits, middle, full_in, full_out]
    in_specs = [vmem_spec] * 5 + [any_spec] * 2
    outs = [
        jax.ShapeDtypeStruct(sent.shape, bf16),
        jax.ShapeDtypeStruct(middle.shape, f32),
        jax.ShapeDtypeStruct(middle.shape, f32),
    ]
    out_specs = [vmem_spec] * 3
    sems = pltpu.SemaphoreType.DMA((members,))
    scratch = [
        doubled(full_in),
        doubled(full_out),
        pltpu.VMEM(sent.shape, bf16),
        pltpu.VMEM(sent.shape, bf16),
        pltpu.SemaphoreType.DMA((2 * full_in.shape[0],)),
        sems,
        sems,
        sems,
        sems,
        pltpu.SemaphoreType.DMA((2 * full_in.shape[0],)),
        pltpu.SemaphoreType.DMA((2 * full_in.shape[0],)),
    ]
    if gathers:
        ins.append(column)
        in_specs.append(any_spec)
        half = (grid_shape[0] // 2, 2, grid_shape[1] // 2, 2)
        outs.append(jax.ShapeDtypeStruct((*half, *column.shape[1:]), bf16))
        out_specs.append(any_spec)
        others = pltpu.SemaphoreType.DMA((gather_copies(grid_shape)[1],))
        scratch += [pltpu.SemaphoreType.DMA, others, others]
    return pl.pallas_call(
        partial(expert_forward_kernel, grid_shape, gathers),
        in_specs=in_specs,
        out_specs=out_specs,
        out_shape=outs,
        scratch_shapes=scratch,
        compiler_params=params(identifier),
        cost_estimate=lasting(75),
        name="expert_forward",
    )(*ins)


def expert_both_kernel(
    grid_shape,
    sent_ref,
    gates_ref,
    slot_col_ref,
    chosen_ref,
    logits_ref,
    far_first_ref,
    far_second_ref,
    far_third_ref,
    win_ref,
    wout_ref,
    made_ref,
    d_back_ref,
    gin_ref,
    gout_ref,
    d_logits_ref,
    arrived_s,
    gates_s,
    win_s,
    wout_s,
    d_made_s,
    d_rows_s,
    act_s,
    d_pre_s,
    d_gates_s,
    d_gates_back_s,
    grads_ref,
    gin_send,
    gin_land,
    gout_send,
    gout_land,
    w_sems,
    *sems,
):
    far_refs = (far_first_ref, far_second_ref, far_third_ref)
    members = grid_shape[1]
    weight_sems, sum_sems = sems[9:11], sems[11:13]
    slots = sent_ref.shape[0]
    rows = slots // members
    group = chunk_of(members, rows)
    chunks = members // group
    chunk_bits = bits_of(chunks)
    hidden_units = win_s.shape[1]
    tile = min(768, hidden_units)
    place = Place(grid_shape)
    weights = Weights(place, (win_ref, wout_ref), (win_s, wout_s), w_sems, weight_sems)
    weights.start_local()
    greet(peers_along_gy(members) + [place.core_peer()])
    weights.start_remote()
    there = Exchange(members, rows, sent_ref, arrived_s, *sems[0:2])
    back = Exchange(members, rows, d_rows_s, d_back_ref, *sems[2:4])
    gates_there = Leading(members, gates_ref, gates_s, *sems[4:6])
    gates_back = Leading(members, d_gates_s, d_gates_back_s, *sems[6:8])

    for apart in send_order(members):
        gates_there.copy(apart).start()
        there.copy(apart).start()

    collected = collect(
        there.me, members, rows, far_refs, partial(third_of, members), grads_ref, sems[8]
    )
    start_all(collected)
    there.keep_own()
    gates_there.keep_own()
    weights.wait(0)
    weights.wait(1)
    wait_all(collected)
    my_chunk = there.me // group

    def work(index, first):
        for member in range(first, group):
            gates_there.copy(index * group + member).wait_recv()
            there.copy(index * group + member).wait_recv()
        chunk = xor_of(my_chunk, index, chunk_bits)
        here = pl.ds(pl.multiple_of(chunk * (group * rows), group * rows), group * rows)
        gate = jnp.concatenate(
            [gates_s[chunk * group + member].T[:rows, 0:1] for member in range(group)], axis=0
        )
        taken = arrived_s[here, :]
        grads = grads_ref[here, :].astype(f32)
        d_made = (gate * grads).astype(bf16)
        d_made_s[here, :] = d_made
        made = jnp.zeros((group * rows, taken.shape[1]), f32)
        d_rows = made
        for start in range(0, hidden_units, tile):
            units = slice(start, start + tile)
            act, slope = gelu_and_slope(dot(taken, win_s[:, units]))
            act = act.astype(bf16)
            act_s[here, units] = act
            d_pre = (dot(d_made, wout_s[:, units]) * slope).astype(bf16)
            d_pre_s[here, units] = d_pre
            d_rows = d_rows + dot(d_pre, win_s[:, units], 1, 1)
            made = made + dot(act, wout_s[:, units], 1, 1)
        d_rows_s[here, :] = d_rows.astype(bf16)
        made = made.astype(bf16)
        made_ref[here, :] = made
        d_gate = jnp.sum(grads * made.astype(f32), axis=1, keepdims=True)
        for member in range(group):
            part = jnp.broadcast_to(d_gate[member * rows : (member + 1) * rows], (rows, 128)).T
            d_gates_s[chunk * group + member, :, :rows] = part[: d_gates_s.shape[1]]
        for member in range(first, group):
            gates_back.copy(index * group + member).start()
            back.copy(index * group + member).start()

    work(0, 1)
    back.keep_own()
    gates_back.keep_own()

    @pl.loop(1, chunks)
    def _(index):
        work(index, 0)

    weight_gradients(
        place,
        ((d_made_s, act_s), (arrived_s, d_pre_s)),
        (gout_send, gin_send),
        (gout_land, gin_land),
        (gout_ref, gin_ref),
        sum_sems,
    )

    @pl.loop(1, members)
    def _(apart):
        gates_back.copy(apart).wait_recv()

    row = jnp.concatenate(
        [d_gates_back_s[expert, 0:1, :rows] for expert in range(members)], axis=1
    )
    slot_col = slot_col_ref[...]
    places = lax.broadcasted_iota(jnp.int32, (slot_col.shape[0], slots), 1)
    d_gate = jnp.sum(jnp.where(places == slot_col, row, 0.0), axis=1, keepdims=True)
    d_logits_ref[...] = d_logits_of(d_gate, logits_ref[...], chosen_ref[...])

    @pl.loop(1, members)
    def _(apart):
        back.copy(apart).wait_recv()
        there.copy(apart).wait_send()
        back.copy(apart).wait_send()
        gates_there.copy(apart).wait_send()
        gates_back.copy(apart).wait_send()


def expert_both(sent, gates, far_parts, slot_col, chosen_f, logits, full_in, full_out, grid_shape, identifier):
    members = grid_shape[1]
    slots = sent.shape[0]
    outs = (
        jax.ShapeDtypeStruct(sent.shape, bf16),
        jax.ShapeDtypeStruct(sent.shape, bf16),
        jax.ShapeDtypeStruct(full_in.shape, bf16),
        jax.ShapeDtypeStruct(full_out.shape, bf16),
        jax.ShapeDtypeStruct(logits.shape, bf16),
    )
    tall = pltpu.VMEM(sent.shape, bf16)
    wide = pltpu.VMEM((slots, 2 * full_in.shape[0] * full_in.shape[2]), bf16)
    half = pltpu.VMEM(full_in.shape, bf16)
    small = pltpu.VMEM(gates.shape, f32)
    weights = doubled(full_in)
    return pl.pallas_call(
        partial(expert_both_kernel, grid_shape),
        in_specs=[vmem_spec] * 5 + [any_spec] * 5,
        out_specs=[vmem_spec] * len(outs),
        out_shape=outs,
        scratch_shapes=[
            tall,
            small,
            weights,
            weights,
            tall,
            tall,
            wide,
            wide,
            small,
            small,
            tall,
            half,
            half,
            half,
            half,
            pltpu.SemaphoreType.DMA((2 * full_in.shape[0],)),
        ]
        + [pltpu.SemaphoreType.DMA((members,))] * 9
        + [pltpu.SemaphoreType.DMA((2 * full_in.shape[0],))] * 4,
        compiler_params=params(identifier),
        cost_estimate=lasting(85),
        name="expert_both",
    )(sent, gates, slot_col, chosen_f, logits, *far_parts, full_in, full_out)


def expert_backward_kernel(
    grid_shape,
    d_sent_ref,
    arrived_ref,
    blocks_ref,
    win_ref,
    wout_ref,
    d_back_ref,
    gin_ref,
    gout_ref,
    upper_ref,
    lower_ref,
    landing_ref,
    win_s,
    wout_s,
    d_arrived_s,
    d_rows_s,
    act_s,
    slope_s,
    first_s,
    up2_s,
    low2_s,
    gin_send,
    gin_land,
    gout_send,
    gout_land,
    w_sems,
    send_sems,
    recv_sems,
    back_send_sems,
    back_recv_sems,
    *more_sems,
):
    members = grid_shape[1]
    sum_sems, weight_sems, gradient_sems = more_sems[0:2], more_sems[2:4], more_sems[4:6]
    push_sems = more_sems[6:8]
    slots = d_sent_ref.shape[0]
    rows = slots // members
    group = chunk_of(members, rows)
    chunks = members // group
    chunk_bits = chunks.bit_length() - 1
    hidden_units = win_s.shape[1]
    tile = min(768, hidden_units)
    place = Place(grid_shape)
    weights = Weights(place, (win_ref, wout_ref), (win_s, wout_s), w_sems, weight_sems)
    weights.start_local()
    greet(peers_along_gy(members) + [place.core_peer()] + place.y_peers())
    weights.start_remote()
    landings = (first_s, up2_s, low2_s, upper_ref, lower_ref, None, None)
    sums = Scatter(place, blocks_ref, landings, sum_sems, upper_ref.shape[1])
    there = Exchange(members, rows, d_sent_ref, d_arrived_s, send_sems, recv_sems)
    back = Exchange(members, rows, d_rows_s, d_back_ref, back_send_sems, back_recv_sems)
    for apart in send_order(members):
        there.copy(apart).start()
    there.keep_own()
    my_chunk = there.me // group
    start_all(sums.copies(0))
    weights.wait(0)

    @pl.loop(0, slots // 256)
    def _(index):
        here = pl.ds(pl.multiple_of(index * 256, 256), 256)
        taken = arrived_ref[here, :]
        for start in range(0, hidden_units, tile):
            units = slice(start, start + tile)
            act, slope = gelu_and_slope(dot(taken, win_s[:, units]))
            act_s[here, units] = act.astype(bf16)
            slope_s[here, units] = slope.astype(bf16)

    wait_all(sums.copies(0))
    sums.add(0)
    start_all(sums.copies(1))
    weights.wait(1)

    def chunk_rows(index):
        start = xor_of(my_chunk, index, chunk_bits) * (group * rows)
        return pl.ds(pl.multiple_of(start, group * rows), group * rows)

    def work(index, first):
        for member in range(first, group):
            there.copy(index * group + member).wait_recv()
        here = chunk_rows(index)
        taken = d_arrived_s[here, :]
        total = jnp.zeros((group * rows, taken.shape[1]), f32)
        for start in range(0, hidden_units, tile):
            units = slice(start, start + tile)
            d_pre = (dot(taken, wout_s[:, units]) * slope_s[here, units].astype(f32)).astype(bf16)
            slope_s[here, units] = d_pre
            total = total + dot(d_pre, win_s[:, units], 1, 1)
        d_rows_s[here, :] = total.astype(bf16)
        for member in range(first, group):
            back.copy(index * group + member).start()

    work(0, 1)
    back.keep_own()

    @pl.loop(1, chunks)
    def _(index):
        work(index, 0)

    wait_all(sums.copies(1))
    sums.add(1)
    start_all(sums.copies(2))
    pushed = push_blocks(place, gout_ref, landing_ref, push_sems, 0)
    weight_gradients(
        place,
        ((d_arrived_s, act_s), (arrived_ref, slope_s)),
        (gout_send, gin_send),
        (gout_land, gin_land),
        (gout_ref, gin_ref),
        gradient_sems,
        pushed,
    )
    wait_all(sums.copies(2))
    sums.add(2)

    @pl.loop(1, members)
    def _(apart):
        back.copy(apart).wait_recv()
        there.copy(apart).wait_send()
        back.copy(apart).wait_send()

    wait_all(pushed)


def expert_backward(d_sent, arrived, blocks, full_in, full_out, grid_shape, identifier):
    members = grid_shape[1]
    landings = whole_blocks(blocks.shape, blocks.shape[4] // 2)
    outs = (
        jax.ShapeDtypeStruct(d_sent.shape, bf16),
        jax.ShapeDtypeStruct(full_in.shape, bf16),
        jax.ShapeDtypeStruct(full_out.shape, bf16),
        *[jax.ShapeDtypeStruct(one, bf16) for one in landings[3:5]],
        landing_of(full_out, cut_of(full_out)),
    )
    slots = d_sent.shape[0]
    sems = pltpu.SemaphoreType.DMA((members,))
    return pl.pallas_call(
        partial(expert_backward_kernel, grid_shape),
        in_specs=[vmem_spec] * 3 + [any_spec] * 2,
        out_specs=[vmem_spec] * (len(outs) - 1) + [any_spec],
        out_shape=outs,
        scratch_shapes=[
            doubled(full_in),
            doubled(full_out),
            pltpu.VMEM(d_sent.shape, bf16),
            pltpu.VMEM(d_sent.shape, bf16),
            pltpu.VMEM((slots, 2 * full_in.shape[0] * full_in.shape[2]), bf16),
            pltpu.VMEM((slots, 2 * full_in.shape[0] * full_in.shape[2]), bf16),
            *[pltpu.VMEM(one, bf16) for one in landings[:3]],
            *[pltpu.VMEM(full_in.shape, bf16)] * 4,
            pltpu.SemaphoreType.DMA((2 * full_in.shape[0],)),
            sems,
            sems,
            sems,
            sems,
            *[pltpu.SemaphoreType.DMA((scatter_copies(grid_shape),))] * 2,
            *[pltpu.SemaphoreType.DMA((2 * full_in.shape[0],))] * 4,
            *[pltpu.SemaphoreType.DMA((full_in.shape[0] - 1,))] * 2,
        ],
        compiler_params=params(10 + identifier),
        cost_estimate=lasting(85),
        name="expert_backward",
    )(d_sent, arrived, blocks, full_in, full_out)


def emit_kernel(
    table_shape,
    at_ref,
    gin_ref,
    gin_first_ref,
    gin_second_ref,
    gin_up_ref,
    gout_ref,
    gout_first_ref,
    gout_second_ref,
    gout_up_ref,
    result_ref,
    grad_ref,
    packed_ref,
    small_ref,
    gin_out_ref,
    gout_out_ref,
    result_out_ref,
    grad_out_ref,
    wq_ref,
    wk_ref,
    wv_ref,
    wo_ref,
    router_out_ref,
    gga_ref,
    ggf_ref,
    table_ref,
):
    step = pl.program_id(0)

    def landed(ref):
        total = ref[0].astype(f32)
        for index in range(1, ref.shape[0]):
            total = total + ref[index].astype(f32)
        return total

    begins = step < pl.num_programs(0) // 3 * 2
    for own, first, second, up, out in (
        (gin_ref, gin_first_ref, gin_second_ref, gin_up_ref, gin_out_ref),
        (gout_ref, gout_first_ref, gout_second_ref, gout_up_ref, gout_out_ref),
    ):
        out[0, 0] = own[0].astype(f32) + jnp.where(begins, landed(first), landed(second))
        out[1, 0] = up[...].astype(f32)

    @pl.when(step == 0)
    def _():
        result_out_ref[...] = result_ref[...]
        grad_out_ref[...] = grad_ref[...]
        layers, tall, wide = wq_ref.shape
        for which, ref in enumerate((wq_ref, wk_ref, wv_ref, wo_ref)):
            ref[...] = packed_ref[:, :, which * wide : (which + 1) * wide]
        buckets_count, heads = table_shape
        width = small_ref.shape[1]
        experts = (small_ref.shape[0] - 2 * layers - heads) // layers
        base = layers * experts
        gga_ref[...] = small_ref[base : base + layers, :]
        ggf_ref[...] = small_ref[base + layers : base + 2 * layers, :]
        base = base + 2 * layers
        table_ref[...] = small_ref[base : base + heads, :buckets_count]
        for layer in range(layers):
            row = small_ref[pl.ds(layer * experts + at_ref[1], 1), :]
            row = jnp.broadcast_to(row, (8, width))
            mine = pltpu.roll(row, lax.rem(width - at_ref[0] * tall, width), 1)
            router_out_ref[layer] = mine[0:1, :tall]


def emit(at, grads_in, grads_out, result, grad_now, packed, small, table_shape):
    layers, tall, lanes = packed.shape
    gin, gin_first, gin_second, gin_up = grads_in
    gout, gout_first, gout_second, gout_up = grads_out
    _, rows, units = gin.shape
    steps = 6
    early_steps = steps // 3 * 2
    tile = rows // steps
    wide = lanes // 4
    whole_in = [result, grad_now, packed, small]
    own = pl.BlockSpec((1, tile, units), lambda i, at: (at[2], i, 0))
    up = pl.BlockSpec((tile, units), lambda i, at: (i, 0))

    def land(array, index):
        return pl.BlockSpec((array.shape[0], tile, units), lambda i, at: (0, index(i), 0))

    out = pl.BlockSpec((layers, 1, tile, units), lambda i, at: (0, 0, i, 0))
    expert = jax.ShapeDtypeStruct((layers, 1, rows, units), f32)
    square = jax.ShapeDtypeStruct((layers, tall, wide), f32)
    gain = jax.ShapeDtypeStruct((layers, small.shape[1]), f32)
    rest = [jax.ShapeDtypeStruct(result.shape, f32)] * 2 + [square] * 4
    rest += [jax.ShapeDtypeStruct((layers, 1, tall), f32), gain, gain]
    rest.append(jax.ShapeDtypeStruct(table_shape[::-1], f32))

    def first_index(i):
        return jnp.minimum(i, early_steps - 1)

    def second_index(i):
        return jnp.maximum(i - early_steps, 0)

    def expert_specs(first_land, second_land):
        return [own, land(first_land, first_index), land(second_land, second_index), up]

    return pl.pallas_call(
        partial(emit_kernel, table_shape),
        grid_spec=pltpu.PrefetchScalarGridSpec(
            num_scalar_prefetch=1,
            grid=(steps,),
            in_specs=expert_specs(gin_first, gin_second)
            + expert_specs(gout_first, gout_second)
            + whole_of(whole_in),
            out_specs=[out, out] + whole_of(rest),
        ),
        out_shape=[expert, expert] + rest,
        compiler_params=params(),
        cost_estimate=lasting(7),
        name="emit",
    )(at, *grads_in, *grads_out, *whole_in)


def body(
    hidden_in,
    route,
    piece_ids,
    buckets,
    rel_table,
    gain_attn,
    gain_ffn,
    w_query,
    w_key,
    w_value,
    w_output,
    w_router,
    w_in,
    w_out,
    cotangent,
):
    count_x = lax.axis_size("gx")
    count_y = lax.axis_size("gy")
    seq_len, width = hidden_in.shape
    layers = w_query.shape[0]
    heads = rel_table.shape[1]
    experts = w_router.shape[2] * count_y
    capacity = 2 * seq_len // experts
    wide_router = w_router.shape[2]
    tall, wide = w_query.shape[1], w_query.shape[2]
    grid_shape = (count_x, count_y)
    same_core = [list(range(core, count_x, 2)) for core in range(2)]
    router_rows = jnp.pad(
        w_router.transpose(0, 2, 1), ((0, 0), (0, tile_rows - wide_router), (0, 4 * wide - tall))
    )
    buckets_row = jnp.pad(buckets, (0, 1), constant_values=-1)[None, :]
    mats, router, later, bias, slot_col, slot_row, chosen_f, spread, far_part = start(
        (w_query, w_key, w_value, w_output),
        router_rows,
        buckets_row,
        rel_table.T,
        piece_ids,
        route,
        cotangent,
        grid_shape,
    )
    gain_attn_f = gain_attn.astype(f32)
    gain_ffn_f = gain_ffn.astype(f32)

    hidden = hidden_in
    kept = []
    blocks = None
    far_parts = [far_part]
    for layer in range(layers):
        last = layer == layers - 1
        gains = (gain_attn_f[layer][None], gain_ffn_f[layer][None])
        mats, router, q, k, v, attended, lse, middle, logits, sent, *gates, far_part = attention_forward(
            hidden,
            gains[0],
            gains[1],
            (slot_row, slot_col, chosen_f),
            bias,
            grid_shape,
            1 + layer,
            spread,
            last,
            blocks=blocks,
            mats=(mats, router) if blocks is None else None,
        )
        far_parts.append(far_part)
        full_in, full_out = (
            lax.all_gather(one[layer, 0], "gx", axis=0, tiled=False, axis_index_groups=same_core)
            for one in (w_in, w_out)
        )
        state = (hidden, gains, (mats, router), (q, k, v), attended, lse, middle, logits)
        if last:
            made, d_back, grad_in_full, grad_out_full, d_logits = expert_both(
                sent, gates[0], far_parts, slot_col, chosen_f, logits, full_in, full_out, grid_shape, 7
            )
            kept.append(state)
        else:
            arrived, combined, hidden, blocks = expert_forward(
                sent,
                slot_col,
                chosen_f,
                logits,
                middle,
                full_in,
                full_out,
                grid_shape,
                5 + layer,
                column=later[layer],
            )
            kept.append(state + (combined, arrived, full_in, full_out))

    grad_now = cotangent
    parts = []
    partials = []
    returned = []
    for layer in reversed(range(layers)):
        last = layer == layers - 1
        (prior, gains, mats, q_k_v, attended, lse, middle, logits) = kept[layer][:8]
        if not last:
            arrived, full_in, full_out = kept[layer][9:]
            d_back, grad_in_full, grad_out_full, upper, lower, out_first = expert_backward(
                d_sent, arrived, parts[-1][0], full_in, full_out, grid_shape, layer
            )
            partials.append((upper, lower[:1]))
        experts_parts = []
        if layer > 0:
            experts_parts = [
                lax.psum_scatter(
                    one, "gx", scatter_dimension=0, tiled=False, axis_index_groups=same_core
                )
                for one in (grad_in_full, grad_out_full)
            ]
        below = None
        if layer > 0:
            below = (kept[layer - 1][8], slot_row, chosen_f, kept[layer - 1][7])
        got = attention_backward(
            d_back,
            slot_col,
            d_logits,
            grad_now,
            middle,
            prior,
            gains,
            mats,
            q_k_v,
            attended,
            bias,
            lse,
            grid_shape,
            below=below,
            after=[array for part in parts for array in part[4]],
            made=made,
            returns=last,
            push=(grad_out_full, grad_in_full) if layer == 0 else None,
            identifier=18 + layer,
        )
        grad_now, blocked, gwr, gga, ggf, offset_sums = got[:6]
        if layer > 0:
            d_sent, d_logits = got[6:8]
        if layer == 0:
            *got, out_second, in_first = got
        returned.append(got[-1])
        parts.append((blocked, gwr, gga, ggf, experts_parts, offset_sums))
    parts = parts[::-1]
    buckets_count = rel_table.shape[0]
    smalls = [part[which] for which in (1, 2, 3, 5) for part in parts]
    top = kept[-1]
    packed, small, hidden_out, in_second = final_sums(
        parts[0][0],
        partials[::-1],
        smalls + [buckets_row],
        (slot_col, chosen_f, top[7], top[6]),
        returned,
        grad_in_full,
        grid_shape,
        buckets_count,
    )
    first, second = lax.axis_index("gx"), lax.axis_index("gy")
    grad_in, grad_out, hidden_out, grad_now, gwq, gwk, gwv, gwo, gwr, gga_all, ggf_all, d_table = emit(
        jnp.stack([first, second, first // 2]).astype(jnp.int32),
        (grad_in_full, in_first, in_second, parts[1][4][0]),
        (grad_out_full, out_first, out_second, parts[1][4][1]),
        hidden_out,
        grad_now,
        packed,
        small,
        rel_table.shape,
    )
    return (
        hidden_out,
        grad_now,
        d_table.T,
        gga_all,
        ggf_all,
        gwq,
        gwk,
        gwv,
        gwo,
        gwr.transpose(0, 2, 1),
        grad_in,
        grad_out,
    )


def solution(mesh):
    rows = P(("gx", "gy"), None)
    square = P(None, "gx", "gy")
    expert = P(None, "gy", None, "gx")
    return jax.shard_map(
        body,
        mesh=mesh,
        in_specs=(rows, rows, P(("gx", "gy")), P(), P(), P(), P())
        + (square,) * 5
        + (expert, expert, rows),
        out_specs=(rows, rows, P(), P(), P()) + (square,) * 5 + (expert, expert),
        check_vma=False,
    )
```

```python
from functools import partial

import jax
import jax.numpy as jnp
from jax import lax
from jax.experimental import pallas as pl
from jax.experimental.pallas import tpu as pltpu
from jax.sharding import PartitionSpec as P

eps_norm = 1e-06
highest = lax.Precision.HIGHEST
f32 = jnp.float32
bf16 = jnp.bfloat16
masked_out = -1e30
tile_rows = 16
MESH = pl.DeviceIdType.MESH
vmem_spec = pl.BlockSpec(memory_space=pltpu.VMEM)
any_spec = pl.BlockSpec(memory_space=pl.ANY)
vmem_bytes = 60 * 1024 * 1024


def whole(shape):
    zeros = (0,) * len(shape)
    return pl.BlockSpec(shape, lambda *_: zeros, pipeline_mode=pl.Buffered(1))


def whole_of(arrays):
    return [whole(array.shape) for array in arrays]


def params(identifier=None):
    if identifier is None:
        return pltpu.CompilerParams(vmem_limit_bytes=vmem_bytes)
    return pltpu.CompilerParams(
        vmem_limit_bytes=vmem_bytes, collective_id=identifier, has_side_effects=True
    )


def lasting(microseconds):
    return pl.CostEstimate(
        flops=int(microseconds * 1e9), bytes_accessed=1 << 20, transcendentals=0
    )


def dot(lhs, rhs, lhs_dim=1, rhs_dim=0):
    return lax.dot_general(
        lhs, rhs, (((lhs_dim,), (rhs_dim,)), ((), ())), preferred_element_type=f32
    )


def rms_factor(hidden):
    return lax.rsqrt(jnp.mean(hidden * hidden, axis=-1, keepdims=True) + eps_norm)


def rms_pull(hidden, gain_row, d_normed):
    factor = rms_factor(hidden)
    scaled = gain_row * d_normed
    inner = jnp.mean(hidden * scaled, axis=-1, keepdims=True)
    d_hidden = factor * scaled - hidden * (factor * factor * factor * inner)
    d_gain = jnp.sum(d_normed * hidden * factor, axis=0, keepdims=True)
    return d_hidden, d_gain


def xor_of(index, other, bits):
    total = 0
    for bit in range(bits):
        power = 1 << bit
        total = total + ((index // power + other // power) % 2) * power
    return total


def placing_rows(slot_row, slots):
    places = lax.broadcasted_iota(jnp.int32, (slots, slot_row.shape[1]), 0)
    return (places == slot_row).astype(f32).astype(bf16)


def placing_cols(slot_col, slots):
    places = lax.broadcasted_iota(jnp.int32, (slot_col.shape[0], slots), 1)
    return (places == slot_col).astype(f32).astype(bf16)


def greet(peers):
    barrier = pltpu.get_barrier_semaphore()
    for peer in peers:
        pl.semaphore_signal(barrier, inc=1, device_id=peer, device_id_type=MESH)
    pl.semaphore_wait(barrier, len(peers))


def bits_of(count):
    return count.bit_length() - 1


class Place:
    def __init__(self, grid_shape):
        self.count_y, self.count_z = grid_shape[0] // 2, grid_shape[1] // 2
        first, second = lax.axis_index("gx"), lax.axis_index("gy")
        self.c, self.y = first % 2, first // 2
        self.x, self.z = second % 2, second // 2

    def core_peer(self):
        return {"gx": self.y * 2 + 1 - self.c}

    def x_peer(self):
        return {"gy": self.z * 2 + 1 - self.x}

    def y_at(self, apart):
        return xor_of(self.y, apart, bits_of(self.count_y))

    def y_peer(self, apart):
        return {"gx": self.y_at(apart) * 2 + self.c}

    def y_peers(self):
        return [self.y_peer(apart) for apart in range(1, self.count_y)]

    def z_at(self, apart):
        return xor_of(self.z, apart, bits_of(self.count_z))

    def z_peer(self, apart):
        return {"gy": self.z_at(apart) * 2 + self.x}

    def z_peers(self):
        return [self.z_peer(apart) for apart in range(1, self.count_z)]


def send(src, dst, sems, index, peer):
    return pltpu.make_async_remote_copy(
        src_ref=src,
        dst_ref=dst,
        send_sem=sems[0].at[index],
        recv_sem=sems[1].at[index],
        device_id=peer,
        device_id_type=MESH,
    )


def start_all(copies):
    for copy in copies:
        copy.start()


def wait_all(copies):
    for copy in copies:
        copy.wait()


def local_copies(pairs, sems, base=0):
    return [
        pltpu.make_async_copy(src, dst, sems.at[base + index])
        for index, (src, dst) in enumerate(pairs)
    ]


def scratch_of(arrays):
    return [pltpu.VMEM(array.shape, array.dtype) for array in arrays]


def gather_z(place, src, landing, sems):
    return [
        send(src, landing, sems, apart - 1, place.z_peer(apart)) for apart in range(1, place.count_z)
    ]


def gather_copies(grid_shape):
    return grid_shape[1] // 2 - 1, 2 * (grid_shape[0] // 2 - 1) + 3


def gather_second(place, column, full, split, sems):
    y, c, x = place.y, place.c, place.x
    upper, lower = pl.ds(0, split), pl.ds(split, full.shape[4] - split)
    copies = [
        send(column.at[:, upper], full.at[y, c, :, x, upper], sems, 0, place.x_peer())
    ]
    for apart in range(1, place.count_y):
        copies.append(
            send(column.at[:, lower], full.at[y, c, :, x, lower], sems, apart, place.y_peer(apart))
        )
    return copies


def gather_third(place, full, split, sems):
    y, c, x = place.y, place.c, place.x
    upper, lower = pl.ds(0, split), pl.ds(split, full.shape[4] - split)
    base = place.count_y
    ref = full.at[:, c, :, x, lower]
    copies = [send(ref, ref, sems, base, place.x_peer())]
    ref = full.at[y, c, :, :, upper]
    for apart in range(1, place.count_y):
        copies.append(send(ref, ref, sems, base + apart, place.y_peer(apart)))
    return copies


def gather_core(place, full, sems):
    ref = full.at[:, place.c]
    return [send(ref, ref, sems, 2 * place.count_y, place.core_peer())]


def whole_blocks(shape, split):
    count_y, _, count_z, _, tall, lanes = shape
    low = tall - split
    return [
        (count_y, count_z, 2, tall, lanes),
        (count_y - 1, count_z, 2, split, lanes),
        (count_y, count_z, low, lanes),
        (count_z, split, lanes),
        (count_y - 1, count_z, low, lanes),
        (count_z - 1, split, lanes),
        (count_z - 1, low, lanes),
    ]


def scatter_copies(grid_shape):
    return 1 + 2 * (grid_shape[0] // 2) + 2 * (grid_shape[1] // 2 - 1)


def add_low(dst, dst_at, *terms):
    total = terms[0].astype(f32)
    for term in terms[1:]:
        total = total + term.astype(f32)
    dst[dst_at] = total.astype(bf16)


class Scatter:
    def __init__(self, place, src, landings, sems, split, source=None):
        self.place, self.src, self.sems = place, src, sems
        self.source = src if source is None else source
        self.first, self.up2, self.low2, self.up3, self.low3, self.up4, self.low4 = landings
        tall = src.shape[4]
        self.upper, self.lower = pl.ds(0, split), pl.ds(split, tall - split)

    def copies(self, stage):
        at, sems = self.place, self.sems
        count_y, count_z = at.count_y, at.count_z
        if stage == 0:
            return [send(self.source.at[:, 1 - at.c], self.first, sems, 0, at.core_peer())]
        if stage == 1:
            copies = [send(self.first.at[:, :, 1 - at.x, self.lower], self.low2, sems, 1, at.x_peer())]
            for apart in range(1, count_y):
                src = self.first.at[at.y_at(apart), :, :, self.upper]
                dst = self.up2.at[apart - 1]
                copies.append(send(src, dst, sems, 1 + apart, at.y_peer(apart)))
            return copies
        if stage == 2:
            base = 1 + count_y
            copies = [send(self.up2.at[0, :, 1 - at.x], self.up3, sems, base, at.x_peer())]
            for apart in range(1, count_y):
                src, dst = self.low2.at[at.y_at(apart)], self.low3.at[apart - 1]
                copies.append(send(src, dst, sems, base + apart, at.y_peer(apart)))
            return copies
        base = 2 * count_y
        copies = []
        for apart in range(1, count_z):
            there = at.z_at(apart)
            for src, dst, more in (
                (self.up3.at[there], self.up4.at[apart - 1], 0),
                (self.low3.at[0, there], self.low4.at[apart - 1], 1),
            ):
                index = base + 2 * apart - 1 + more
                copies.append(send(src, dst, sems, index, at.z_peer(apart)))
        return copies

    def add(self, stage):
        at = self.place
        count_y, count_z = at.count_y, at.count_z
        if stage == 0:

            @pl.loop(0, count_y * count_z)
            def _(index):
                y, z = index // count_z, index % count_z
                add_low(self.first, (y, z), self.first[y, z], self.src[y, at.c, z])

        elif stage == 1:

            @pl.loop(0, count_z)
            def _(z):
                for x in range(2):
                    terms = [self.up2[apart, z, x] for apart in range(count_y - 1)]
                    add_low(self.up2, (0, z, x), self.first[at.y, z, x, self.upper], *terms)

                @pl.loop(0, count_y)
                def _(y):
                    add_low(self.low2, (y, z), self.first[y, z, at.x, self.lower], self.low2[y, z])

        elif stage == 2:

            @pl.loop(0, count_z)
            def _(z):
                add_low(self.up3, (z,), self.up3[z], self.up2[0, z, at.x])
                terms = [self.low3[apart, z] for apart in range(count_y - 1)]
                add_low(self.low3, (0, z), self.low2[at.y, z], *terms)

    def result(self):
        at = self.place
        upper, lower = self.up3[at.z].astype(f32), self.low3[0, at.z].astype(f32)
        for apart in range(at.count_z - 1):
            upper = upper + self.up4[apart].astype(f32)
            lower = lower + self.low4[apart].astype(f32)
        return upper, lower


class SmallSum:
    def __init__(self, grid_shape, totals, landing, sems):
        self.totals, self.landing, self.sems = totals, landing, sems
        self.peers = []
        for name, count in (("gx", grid_shape[0]), ("gy", grid_shape[1])):
            me = lax.axis_index(name)
            for bit in range(bits_of(count)):
                self.peers.append({name: xor_of(me, 1 << bit, bits_of(count))})
        self.done = 0

    def copy(self):
        step = self.done
        return send(self.totals.at[step], self.landing.at[step], self.sems, step, self.peers[step])

    def begin(self):
        self.copy().start()

    def advance(self):
        if self.done == len(self.peers):
            return
        self.copy().wait()
        step = self.done
        self.totals[step + 1] = self.totals[step] + self.landing[step]
        self.done += 1
        if self.done < len(self.peers):
            self.begin()


def small_steps(grid_shape):
    return bits_of(grid_shape[0]) + bits_of(grid_shape[1])


def final_kernel(grid_shape, layers, buckets_count, *refs):
    refs = list(refs)
    take = refs.pop
    partial_refs = [(take(0), take(0)) for _ in range(layers - 1)]
    router_refs, gga_refs, ggf_refs, offset_refs = ([take(0) for _ in range(layers)] for _ in range(4))
    buckets_ref, slot_col_ref, chosen_ref, logits_ref = (take(0) for _ in range(4))
    blocks_in_ref, middle_in_ref = take(0), take(0)
    first_ref, second_ref, push_ref = take(0), take(0), take(0)
    packed_ref, small_out_ref, result_ref, landing_ref = (take(0) for _ in range(4))
    blocks_ref, middle_ref, move_sems = (take(0) for _ in range(3))
    landings = [take(0) for _ in range(7)]
    z_landings = [(take(0), take(0)) for _ in range(layers - 1)]
    totals, landing, returned_s = take(0), take(0), take(0)
    sems = [(take(0), take(0)) for _ in range(layers)]
    small_sems, collect_sems, push_sems = (take(0), take(0)), take(0), (take(0), take(0))
    place = Place(grid_shape)
    tall = packed_ref.shape[1]
    split = tall // 2
    members = grid_shape[1]
    slots = returned_s.shape[0]
    upper_layers = []
    for layer in range(1, layers):
        upper, lower = partial_refs[layer - 1]
        places = (None, None, None, upper, lower, *z_landings[layer - 1])
        upper_layers.append(Scatter(place, blocks_ref, places, sems[layer], split))
    lowest = Scatter(place, blocks_ref, landings, sems[0], split, blocks_in_ref)
    c = place.c
    moves = local_copies(
        [(blocks_in_ref.at[:, c], blocks_ref.at[:, c]), (middle_in_ref, middle_ref)], move_sems
    )
    start_all(moves)
    collected = collect(
        lax.axis_index("gy"),
        members,
        slots // members,
        (first_ref, second_ref),
        lambda apart: int(apart not in early(members)),
        returned_s,
        collect_sems,
    )
    start_all(collected)
    greet([place.core_peer(), place.x_peer()] + place.y_peers() + place.z_peers())
    start_all(lowest.copies(0))
    for one in upper_layers:
        start_all(one.copies(3))

    experts = router_refs[0].shape[0]
    totals[0] = jnp.zeros(totals.shape[1:], f32)
    row = 0
    for refs_of in (router_refs, gga_refs, ggf_refs):
        for ref in refs_of:
            totals[0, row : row + ref.shape[0], :] = ref[...]
            row += ref.shape[0]
    heads = offset_refs[0].shape[0]
    offsets = offset_refs[0][...]
    for ref in offset_refs[1:]:
        offsets = offsets + ref[...]
    in_bucket = (
        lax.broadcasted_iota(jnp.int32, (buckets_count, offsets.shape[1]), 0) == buckets_ref[...]
    ).astype(f32)
    totals[0, row : row + heads, :buckets_count] = lax.dot_general(
        offsets, in_bucket, (((1,), (1,)), ((), ())), precision=highest, preferred_element_type=f32
    )
    small = SmallSum(grid_shape, totals, landing, small_sems)
    small.begin()
    wait_all(moves + lowest.copies(0))
    lowest.add(0)
    start_all(lowest.copies(1))
    small.advance()
    wait_all(collected)
    placing = placing_cols(slot_col_ref[...], slots)
    gate = jnp.sum(jax.nn.softmax(logits_ref[...], axis=-1) * chosen_ref[...], axis=1, keepdims=True)
    result_ref[...] = middle_ref[...] + gate * dot(placing, returned_s[...])
    small.advance()
    wait_all(lowest.copies(1))
    lowest.add(1)
    start_all(lowest.copies(2))
    pushed = push_blocks(
        place, push_ref, landing_ref, push_sems, push_ref.shape[1] - landing_ref.shape[1]
    )
    start_all(pushed)
    small.advance()

    def finish(layer, one):
        for part, rows in zip(one.result(), (slice(0, split), slice(split, tall))):
            packed_ref[layer, rows, :] = part

    for layer, one in enumerate(upper_layers):
        wait_all(one.copies(3))
        finish(layer + 1, one)
    wait_all(lowest.copies(2))
    lowest.add(2)
    start_all(lowest.copies(3))
    while small.done < len(small.peers):
        small.advance()
    small_out_ref[...] = totals[len(small.peers)]
    wait_all(lowest.copies(3))
    finish(0, lowest)
    wait_all(pushed)


def final_sums(blocks, partials, smalls, finishing, returned, push, grid_shape, buckets_count):
    layers = len(partials) + 1
    shape = blocks.shape
    tall = shape[4]
    width = finishing[-1].shape[1]
    landings = [pltpu.VMEM(one, bf16) for one in whole_blocks(shape, tall // 2)]
    steps = small_steps(grid_shape)
    rows = sum(one.shape[0] for one in smalls[: 3 * layers]) + smalls[3 * layers].shape[0]
    small_shape = (rows, width)
    sems = pltpu.SemaphoreType.DMA((scatter_copies(grid_shape),))
    small_sems = pltpu.SemaphoreType.DMA((steps,))
    outs = [jax.ShapeDtypeStruct((layers, tall, shape[5]), f32)]
    outs += [jax.ShapeDtypeStruct(small_shape, f32), jax.ShapeDtypeStruct(finishing[-1].shape, f32)]
    outs.append(landing_of(push, push.shape[1] - push.shape[1] // 2))
    ins = [*[array for pair in partials for array in pair], *smalls, *finishing[:3]]
    moved = [blocks, finishing[-1]]
    return pl.pallas_call(
        partial(final_kernel, grid_shape, layers, buckets_count),
        in_specs=[vmem_spec] * len(ins) + [any_spec] * 5,
        out_specs=[vmem_spec] * (len(outs) - 1) + [any_spec],
        out_shape=outs,
        scratch_shapes=scratch_of(moved)
        + [pltpu.SemaphoreType.DMA((2,))]
        + landings
        + landings[5:] * (layers - 1)
        + [pltpu.VMEM((steps + 1, *small_shape), f32), pltpu.VMEM((steps, *small_shape), f32)]
        + [pltpu.VMEM(returned[0].shape, bf16)]
        + [sems, sems] * layers
        + [small_sems, small_sems, pltpu.SemaphoreType.DMA((grid_shape[1],))]
        + [pltpu.SemaphoreType.DMA((grid_shape[0] // 2 - 1,))] * 2,
        compiler_params=params(24),
        cost_estimate=lasting(60),
        name="final_sums",
    )(*ins, *moved, *returned, push)


def unblock(grid_shape, blocks_ref, mats_ref, router_ref):
    count_x, count_y = grid_shape
    tall = mats_ref.shape[1] // count_x
    wide = mats_ref.shape[2] // count_y
    router_rows = []
    for first in range(count_x):
        spots = [(first // 2, first % 2, second // 2, second % 2) for second in range(count_y)]
        rows = slice(first * tall, (first + 1) * tall)
        for which in range(4):
            lanes = slice(which * wide, (which + 1) * wide)
            mats_ref[which, rows, :] = jnp.concatenate(
                [blocks_ref[(*spot, slice(0, tall), lanes)] for spot in spots], axis=1
            )
        router_rows.append(
            jnp.concatenate(
                [blocks_ref[(*spot, slice(tall, tall + 1), slice(0, tall))] for spot in spots],
                axis=0,
            )
        )
    router_ref[...] = jnp.concatenate(router_rows, axis=1)


def turned(row):
    return jnp.broadcast_to(row, (128, row.shape[1])).T[:, 0:1]


def start_kernel(
    grid_shape,
    wq_ref,
    wk_ref,
    wv_ref,
    wo_ref,
    router_rows_ref,
    buckets_ref,
    table_ref,
    piece_row_ref,
    route_row_ref,
    cotangent_ref,
    mats_ref,
    router_ref,
    later_ref,
    bias_out_ref,
    slot_col_ref,
    slot_row_ref,
    chosen_ref,
    spread_out_ref,
    far_ref,
    bias_ref,
    spread_ref,
    write_sems,
    full_s,
    column_s,
    spread_send,
    spread_recv,
    later_send,
    later_recv,
    z_send,
    z_recv,
    send_sems,
    recv_sems,
):
    place = Place(grid_shape)
    layers, tall, wide = wq_ref.shape
    split = tall // 2
    y, c, z, x = place.y, place.c, place.z, place.x

    def packed(layer):
        return jnp.concatenate([ref[layer] for ref in (wq_ref, wk_ref, wv_ref, wo_ref)], axis=1)

    column_s[z, :tall] = packed(0)
    column_s[z, tall:] = router_rows_ref[0]
    members = grid_shape[1]
    spread = Exchange(
        members, spread_ref.shape[0] // members, spread_ref, far_ref, spread_send, spread_recv
    )
    spread_copies = [spread.copy(apart) for apart in in_third(members, 0)]
    mine_here = spread.block(spread.me)
    half_heads = bias_ref.shape[0] // 2
    parts = [pl.ds(0, half_heads), pl.ds(half_heads, half_heads)]
    write_spread, write_own, *write_bias = local_copies(
        [(spread_ref, spread_out_ref), (spread_ref.at[mine_here, :], far_ref.at[mine_here, :])]
        + [(bias_ref.at[part], bias_out_ref.at[part]) for part in parts],
        write_sems,
    )
    greet(
        [place.core_peer(), place.x_peer()]
        + place.y_peers()
        + place.z_peers()
        + [spread.peer(apart) for apart in in_third(members, 0)]
    )
    first = gather_z(place, column_s.at[z], column_s.at[z], (z_send, z_recv))
    start_all(first)
    along_z = []
    for layer in range(1, layers):
        later_ref[layer - 1, z, :tall] = packed(layer)
        later_ref[layer - 1, z, tall:] = router_rows_ref[layer]
        mine = later_ref.at[layer - 1, z]
        along_z += gather_z(place, mine, mine, (later_send.at[layer - 1], later_recv.at[layer - 1]))

    seq_len, experts = chosen_ref.shape
    capacity = 2 * seq_len // experts
    heads = bias_ref.shape[0]
    buckets_count = table_ref.shape[1]
    in_bucket = (
        lax.broadcasted_iota(jnp.int32, (buckets_count, 2 * seq_len), 0) == buckets_ref[...]
    )
    offsets = dot(table_ref[...], in_bucket.astype(f32).astype(bf16))
    key_pos = lax.broadcasted_iota(jnp.int32, (seq_len, seq_len), 0)
    query_pos = lax.broadcasted_iota(jnp.int32, (seq_len, seq_len), 1)
    route_row, piece_row = route_row_ref[...], piece_row_ref[...]
    route_col, piece_col = turned(route_row), turned(piece_row)
    chosen = (lax.broadcasted_iota(jnp.int32, (seq_len, experts), 1) == route_col).astype(f32)
    chosen_t = (lax.broadcasted_iota(jnp.int32, (experts, seq_len), 0) == route_row).astype(f32)
    chosen_ref[...] = chosen
    earlier = (key_pos < query_pos).astype(f32).astype(bf16)
    before_t = dot(chosen_t.astype(bf16), earlier)
    rank_row = jnp.sum(before_t * chosen_t, axis=0, keepdims=True)
    slot_row_ref[...] = route_row * capacity + rank_row.astype(jnp.int32)
    later = (key_pos > query_pos).astype(f32).astype(bf16)
    before = dot(later, chosen.astype(bf16))
    rank_col = jnp.sum(before * chosen, axis=1, keepdims=True)
    slot_col_ref[...] = route_col * capacity + rank_col.astype(jnp.int32)
    placing = placing_rows(slot_row_ref[...], spread_ref.shape[0])
    spread_ref[...] = dot(placing, cotangent_ref[...]).astype(bf16)
    start_all([write_spread, write_own])

    same = (piece_col == piece_row) & (piece_col > 0)
    allowed = (key_pos <= query_pos) | same

    def bias_for(head):
        row = jnp.broadcast_to(offsets[head : head + 1], (seq_len, 2 * seq_len))
        shifted = pltpu.roll(row, seq_len + 1, 1, stride=1, stride_axis=0)[:, :seq_len]
        bias_ref[head] = jnp.where(allowed, shifted, masked_out).astype(bf16)

    for head in range(heads // 2):
        bias_for(head)
    wait_all(first)
    sems = (send_sems, recv_sems)
    second = gather_second(place, column_s, full_s, split, sems)
    start_all(second)
    start_all(along_z)
    start_all(spread_copies)
    write_bias[0].start()
    full_s[y, c, :, x] = column_s[...]
    for head in range(heads // 2, heads):
        bias_for(head)
    write_bias[1].start()
    wait_all(second)
    third = gather_third(place, full_s, split, sems)
    start_all(third)

    wait_all(third)
    fourth = gather_core(place, full_s, sems)
    start_all(fourth)
    wait_all(fourth)
    unblock(grid_shape, full_s, mats_ref, router_ref)
    wait_all(along_z)
    wait_all(spread_copies)
    wait_all([write_spread, write_own, *write_bias])


def start(mats, router_rows, buckets, table_t, piece_ids, route, cotangent, grid_shape):
    layers, tall, wide = mats[0].shape
    seq_len = piece_ids.shape[0]
    heads = table_t.shape[0]
    width = tall * grid_shape[0]
    experts = grid_shape[1]
    block = (router_rows.shape[1] + tall, 4 * wide)
    half = (grid_shape[0] // 2, 2, grid_shape[1] // 2, 2)
    ins = (
        *mats,
        router_rows,
        buckets,
        table_t,
        piece_ids[None, :],
        route.reshape(1, seq_len),
        cotangent,
    )
    outs = (
        jax.ShapeDtypeStruct((4, width, width), bf16),
        jax.ShapeDtypeStruct((experts, width), bf16),
        jax.ShapeDtypeStruct((layers - 1, half[2], *block), bf16),
        jax.ShapeDtypeStruct((heads, seq_len, seq_len), bf16),
        jax.ShapeDtypeStruct((seq_len, 1), jnp.int32),
        jax.ShapeDtypeStruct((1, seq_len), jnp.int32),
        jax.ShapeDtypeStruct((seq_len, experts), f32),
        jax.ShapeDtypeStruct((2 * seq_len, width), bf16),
        jax.ShapeDtypeStruct((2 * seq_len, width), bf16),
    )
    along_z, others = gather_copies(grid_shape)
    return pl.pallas_call(
        partial(start_kernel, grid_shape),
        in_specs=[vmem_spec] * len(ins),
        out_specs=[vmem_spec] * 3 + [any_spec] + [vmem_spec] * 3 + [any_spec] * 2,
        out_shape=outs,
        scratch_shapes=[
            *scratch_of([outs[3], outs[7]]),
            pltpu.SemaphoreType.DMA((4,)),
            pltpu.VMEM((*half, *block), bf16),
            pltpu.VMEM((half[2], *block), bf16),
            pltpu.SemaphoreType.DMA((experts,)),
            pltpu.SemaphoreType.DMA((experts,)),
            pltpu.SemaphoreType.DMA((layers - 1, along_z)),
            pltpu.SemaphoreType.DMA((layers - 1, along_z)),
            pltpu.SemaphoreType.DMA((along_z,)),
            pltpu.SemaphoreType.DMA((along_z,)),
            pltpu.SemaphoreType.DMA((others,)),
            pltpu.SemaphoreType.DMA((others,)),
        ],
        compiler_params=params(0),
        cost_estimate=lasting(45),
        name="start",
    )(*ins)


def half_masks(rows, width):
    lane = lax.broadcasted_iota(jnp.int32, (rows, width), 1)
    return lane < (width // 2)


def gates_of(logits, slot_col, chosen, gates_ref):
    experts = gates_ref.shape[0]
    seq_len = slot_col.shape[0]
    capacity = 2 * seq_len // experts
    gate = jnp.sum(jax.nn.softmax(logits, axis=-1) * chosen, axis=1, keepdims=True)
    places = lax.broadcasted_iota(jnp.int32, (seq_len, 2 * seq_len), 1)
    row = jnp.sum(jnp.where(places == slot_col, gate, 0.0), axis=0, keepdims=True)
    gates_ref[...] = jnp.zeros_like(gates_ref)
    for expert in range(experts):
        mine = row[:, expert * capacity : (expert + 1) * capacity]
        gates_ref[expert, :, :capacity] = jnp.broadcast_to(mine, (gates_ref.shape[1], capacity))


def forward_kernel(
    head_dim,
    grid_shape,
    blocked,
    last,
    hidden_ref,
    gain_attn_ref,
    gain_ffn_ref,
    slot_row_ref,
    slot_col_ref,
    chosen_ref,
    *refs,
):
    refs = list(refs)
    take = refs.pop
    blocks_ref = take(0) if blocked else None
    mats_ref, router_ref = (None, None) if blocked else (take(0), take(0))
    spread_ref = take(0)
    bias_ref = take(0)
    outs = []
    if blocked:
        outs.append(take(0))
        router_ref = take(0)
    outs += [take(0) for _ in range(3)]
    att_ref, lse_ref, middle_ref, logits_ref, sent_ref = (take(0) for _ in range(5))
    gates_ref = take(0) if last else None
    far_ref, send_sems, recv_sems, write_sems, *made_here = refs
    q_ref, k_ref, v_ref = made_here[-3:]
    if blocked:
        mats_ref = made_here[0]
    writes = local_copies(list(zip(made_here, outs)), write_sems)
    pair, pairs = pl.program_id(0), pl.num_programs(0)
    seq_len = hidden_ref.shape[0]
    width = 2 * head_dim
    step = min(512, seq_len)

    members = grid_shape[1]
    spread = Exchange(members, spread_ref.shape[0] // members, spread_ref, far_ref, send_sems, recv_sems)
    aparts = in_third(members, 2 if last else 1)

    @pl.when(pair == 0)
    def _():
        greet([spread.peer(apart) for apart in aparts])
        start_all([spread.copy(apart) for apart in aparts])

    @pl.when(pair == 0)
    def _():
        if blocked:
            unblock(grid_shape, blocks_ref, mats_ref, router_ref)
        hidden = hidden_ref[...].astype(f32)
        normed = (hidden * rms_factor(hidden) * gain_attn_ref[...]).astype(bf16)
        q_ref[...] = dot(normed, mats_ref[0]).astype(bf16)
        k_ref[...] = dot(normed, mats_ref[1]).astype(bf16)
        v_ref[...] = dot(normed, mats_ref[2]).astype(bf16)
        start_all(writes)

    lanes = pl.ds(pl.multiple_of(pair * width, width), width)
    q2 = q_ref[:, lanes] * jnp.asarray(head_dim**-0.5, bf16)
    k2 = k_ref[:, lanes]
    v2t = v_ref[:, lanes].T
    first = half_masks(seq_len, width)
    for half in range(2):
        q_one = jnp.where(first if half == 0 else ~first, q2, jnp.zeros_like(q2))
        v_one = v2t[half * head_dim : (half + 1) * head_dim]
        for begin in range(0, seq_len, step):
            cols = slice(begin, begin + step)
            scores = dot(k2, q_one[cols], 1, 1) + bias_ref[half, :, cols].astype(f32)
            top = jnp.max(scores, axis=0, keepdims=True)
            raised = jnp.exp(scores - top)
            total = jnp.sum(raised, axis=0, keepdims=True)
            probs = raised.astype(bf16)
            rows = pl.ds(pl.multiple_of(pair * width + half * head_dim, head_dim), head_dim)
            att_ref[rows, cols] = (dot(v_one, probs) * (1.0 / total)).astype(bf16)
            lse_ref[0, half : half + 1, cols] = top + jnp.log(total)

    @pl.when(pair == pairs - 1)
    def _():
        middle = hidden_ref[...].astype(f32) + dot(att_ref[...].T, mats_ref[3])
        middle_ref[...] = middle
        ffn_in = (middle * rms_factor(middle) * gain_ffn_ref[...]).astype(bf16)
        logits = dot(ffn_in, router_ref[...], 1, 1)
        logits_ref[...] = logits
        if gates_ref is not None:
            gates_of(logits, slot_col_ref[...], chosen_ref[...], gates_ref)
        placing = placing_rows(slot_row_ref[...], sent_ref.shape[0])
        sent_ref[...] = dot(placing, ffn_in).astype(bf16)

    @pl.when(pair == pairs - 1)
    def _():
        wait_all([spread.copy(apart) for apart in aparts])
        wait_all(writes)


def attention_forward(
    hidden,
    gain_attn,
    gain_ffn,
    slots_and_chosen,
    bias,
    grid_shape,
    identifier,
    spread,
    last,
    blocks=None,
    mats=None,
):
    seq_len, width = hidden.shape
    heads = bias.shape[0]
    head_dim = width // heads
    slots = 2 * seq_len
    experts = grid_shape[1]
    blocked = blocks is not None
    ins = [hidden, gain_attn, gain_ffn, *slots_and_chosen] + ([blocks] if blocked else list(mats))
    in_specs = whole_of(ins)
    ins.append(spread)
    in_specs.append(any_spec)
    ins.append(bias)
    in_specs.append(pl.BlockSpec((2, seq_len, seq_len), lambda p: (p, 0, 0)))
    tall = jax.ShapeDtypeStruct((seq_len, width), bf16)
    outs = [
        tall,
        tall,
        tall,
        jax.ShapeDtypeStruct((width, seq_len), bf16),
        jax.ShapeDtypeStruct((heads // 2, 2, seq_len), f32),
        jax.ShapeDtypeStruct((seq_len, width), f32),
        jax.ShapeDtypeStruct((seq_len, experts), f32),
        jax.ShapeDtypeStruct((slots, width), bf16),
    ]
    if last:
        outs.append(jax.ShapeDtypeStruct((experts, 8, max(128, slots // experts)), f32))
    out_specs = whole_of(outs)
    out_specs[:3] = [any_spec] * 3
    written = outs[:3]
    out_specs[4] = pl.BlockSpec((1, 2, seq_len), lambda p: (p, 0, 0))
    if blocked:
        more = [
            jax.ShapeDtypeStruct((4, width, width), bf16),
            jax.ShapeDtypeStruct((experts, width), bf16),
        ]
        outs = more + outs
        out_specs = [any_spec] + whole_of(more[1:]) + out_specs
        written = more[:1] + written
    outs.append(jax.ShapeDtypeStruct(spread.shape, bf16))
    out_specs.append(any_spec)
    sems = pltpu.SemaphoreType.DMA((experts,))
    scratch = [sems, sems, pltpu.SemaphoreType.DMA((len(written),)), *scratch_of(written)]
    got = pl.pallas_call(
        partial(forward_kernel, head_dim, grid_shape, blocked, last),
        grid=(heads // 2,),
        in_specs=in_specs,
        out_specs=out_specs,
        out_shape=outs,
        scratch_shapes=scratch,
        compiler_params=params(identifier),
        cost_estimate=lasting(25),
        name="attention_forward",
    )(*ins)
    return tuple(got) if blocked else tuple(mats) + tuple(got)


def diagonal_fold(values, seq_len):
    rows, wide = seq_len, 2 * seq_len
    folded = None
    tile = 128
    count = seq_len // tile
    for row_tile in range(count):
        piece = values[row_tile * tile : (row_tile + 1) * tile].astype(f32)
        before = (count - 1 - row_tile) * tile
        after = wide - seq_len - before
        parts = []
        if before:
            parts.append(jnp.zeros((tile, before), f32))
        parts.append(piece)
        if after:
            parts.append(jnp.zeros((tile, after), f32))
        padded = jnp.concatenate(parts, axis=1)
        folded = padded if folded is None else folded + padded
    rows = tile
    while rows > 1:
        rows //= 2
        folded = pltpu.roll(folded[:rows], rows, 1) + folded[rows:]
    return folded


def reblock(grid_shape, blocks_ref, which, values):
    count_x, count_y = grid_shape
    tall = values.shape[0] // count_x
    wide = values.shape[1] // count_y
    for first in range(count_x):
        for second in range(count_y):
            spot = (first // 2, first % 2, second // 2, second % 2)
            lanes = slice(which * wide, (which + 1) * wide)
            blocks_ref[(*spot, slice(None), lanes)] = values[
                first * tall : (first + 1) * tall, second * wide : (second + 1) * wide
            ]


def d_logits_of(d_gate, logits, chosen):
    shares = jax.nn.softmax(logits, axis=-1)
    gate = jnp.sum(shares * chosen, axis=1, keepdims=True)
    return (d_gate * shares * (chosen - gate)).astype(bf16)


def spread_into(grad_now, comb_ref, slot_row_ref, chosen_ref, logits_ref, d_sent_ref, d_logits_ref):
    d_gate = jnp.sum(grad_now * comb_ref[...], axis=1, keepdims=True)
    logits, chosen = logits_ref[...], chosen_ref[...]
    d_logits_ref[...] = d_logits_of(d_gate, logits, chosen)
    gate = jnp.sum(jax.nn.softmax(logits, axis=-1) * chosen, axis=1, keepdims=True)
    placing = placing_rows(slot_row_ref[...], d_sent_ref.shape[0])
    d_sent_ref[...] = dot(placing, (gate * grad_now).astype(bf16)).astype(bf16)


def backward_kernel(
    head_dim,
    grid_shape,
    spreads,
    returns,
    pushes,
    unread,
    d_back_ref,
    slot_col_ref,
    d_logits_ref,
    grad_ref,
    middle_ref,
    gain_attn_ref,
    gain_ffn_ref,
    router_ref,
    att_ref,
    *refs,
):
    refs = list(refs)
    take = refs.pop
    spread_in = [take(0) for _ in range(4)] if spreads else []
    bias_ref, lse_ref = take(0), take(0)
    made_ref = take(0)
    push_refs = (take(0), take(0)) if pushes else ()
    later = [take(0) for _ in range(5)]
    del refs[:unread]
    grad_new_ref, blocks_ref, gwr_ref, gga_ref, ggf_ref, offsets_ref = (take(0) for _ in range(6))
    spread_out = [take(0) for _ in range(2)] if spreads else []
    returned_ref = take(0)
    landing_refs = (take(0), take(0)) if pushes else ()
    d_att_s, d_middle_s, dqt_s, dk_s, dv_s, probs_s, scores_s = (take(0) for _ in range(7))
    loaded = [take(0) for _ in range(5)]
    load_sems = take(0)
    mats_ref, q_ref, k_ref, v_ref, hidden_ref = loaded
    mats_later = later[0]
    load_output = local_copies([(mats_later.at[3], mats_ref.at[3])], load_sems)
    load_heads = local_copies(list(zip(later[1:4], loaded[1:4])), load_sems, 1)
    first_three = pl.ds(0, 3)
    load_rest = local_copies(
        [(mats_later.at[first_three], mats_ref.at[first_three]), (later[4], hidden_ref)], load_sems, 4
    )
    own_sem, *sems = refs[:3]
    members = grid_shape[1]
    place = Place(grid_shape)
    pushed = []
    for src, landing, last_rows in zip(push_refs, landing_refs, (True, False)):
        begin = src.shape[1] - landing.shape[1] if last_rows else 0
        pushed += push_blocks(place, src, landing, refs[3:], begin, len(pushed))
    back = Exchange(members, made_ref.shape[0] // members, made_ref, returned_ref, *sems)
    mine = back.block(back.me)
    own = None
    if returns:
        own = pltpu.make_async_copy(made_ref.at[mine, :], returned_ref.at[mine, :], own_sem)
    aparts = part_of(members, returns)

    @pl.when(pl.program_id(0) == 0)
    def _():
        start_all(load_output + load_heads + load_rest)
        greet([back.peer(apart) for apart in aparts] + (place.y_peers() if pushes else []))
        start_all(pushed + [back.copy(apart) for apart in aparts])
        if returns:
            own.start()

    pair, pairs = pl.program_id(0), pl.num_programs(0)
    seq_len = att_ref.shape[1]
    width = 2 * head_dim
    step = min(512, seq_len)
    scale = head_dim**-0.5

    @pl.when(pair == 0)
    def _():
        placing = placing_cols(slot_col_ref[...], d_back_ref.shape[0])
        d_logits = d_logits_ref[...]
        d_ffn = dot(placing, d_back_ref[...]) + dot(d_logits, router_ref[...])
        middle = middle_ref[...]
        gain_row = gain_ffn_ref[...]
        ffn_in = (middle * rms_factor(middle) * gain_row).astype(bf16)
        gwr_ref[...] = dot(d_logits, ffn_in, 0, 0)
        d_middle, d_gain = rms_pull(middle, gain_row, d_ffn)
        ggf_ref[...] = d_gain
        d_middle = d_middle + grad_ref[...].astype(f32)
        d_middle_s[...] = d_middle
        d_low = d_middle.astype(bf16)
        wait_all(load_output)
        reblock(grid_shape, blocks_ref, 3, dot(att_ref[...], d_low).astype(bf16))
        d_att_s[...] = dot(d_low, mats_ref[3], 1, 1).astype(bf16)
        wait_all(load_heads)

    lanes = pl.ds(pl.multiple_of(pair * width, width), width)
    q2 = q_ref[:, lanes] * jnp.asarray(scale, bf16)
    k2 = k_ref[:, lanes]
    v2 = v_ref[:, lanes]
    da2 = d_att_s[:, lanes]
    k2t = k2.T
    first = half_masks(seq_len, width)
    d_key = jnp.zeros((seq_len, width), f32)
    d_value = jnp.zeros((seq_len, width), f32)
    for half in range(2):
        mask = first if half == 0 else ~first
        q_one = jnp.where(mask, q2, jnp.zeros_like(q2))
        da_one = jnp.where(mask, da2, jnp.zeros_like(da2))
        k_one = k2t[half * head_dim : (half + 1) * head_dim]
        rows = pl.ds(pl.multiple_of(pair * width + half * head_dim, head_dim), head_dim)
        for start in range(0, seq_len, step):
            cols = slice(start, start + step)
            scores = dot(k2, q_one[cols], 1, 1) + bias_ref[half, :, cols].astype(f32)
            probs = jnp.exp(scores - lse_ref[0, half : half + 1, cols])
            d_probs = dot(v2, da_one[cols], 1, 1)
            inner = jnp.sum(probs * d_probs, axis=0, keepdims=True)
            d_scores = (probs * (d_probs - inner)).astype(bf16)
            probs_s[:, cols] = probs.astype(bf16)
            scores_s[:, cols] = d_scores
            dqt_s[rows, cols] = (dot(k_one, d_scores) * scale).astype(bf16)
        d_key = d_key + dot(scores_s[...], q_one)
        d_value = d_value + dot(probs_s[...], da_one)
        offsets_ref[pl.ds(2 * pair + half, 1), :] = diagonal_fold(scores_s[...], seq_len)
    dk_s[:, lanes] = d_key.astype(bf16)
    dv_s[:, lanes] = d_value.astype(bf16)

    @pl.when(pair == pairs - 1)
    def _():
        wait_all(load_rest)
        hidden = hidden_ref[...].astype(f32)
        gain_row = gain_attn_ref[...]
        normed_t = (hidden * rms_factor(hidden) * gain_row).astype(bf16).T
        d_query = dqt_s[...].T
        d_normed = dot(d_query, mats_ref[0], 1, 1)
        reblock(grid_shape, blocks_ref, 0, dot(normed_t, d_query).astype(bf16))
        d_normed = d_normed + dot(dk_s[...], mats_ref[1], 1, 1)
        reblock(grid_shape, blocks_ref, 1, dot(normed_t, dk_s[...]).astype(bf16))
        d_normed = d_normed + dot(dv_s[...], mats_ref[2], 1, 1)
        reblock(grid_shape, blocks_ref, 2, dot(normed_t, dv_s[...]).astype(bf16))
        d_hidden, d_gain = rms_pull(hidden, gain_row, d_normed)
        gga_ref[...] = d_gain
        grad_new = d_hidden + d_middle_s[...]
        grad_new_ref[...] = grad_new
        if spreads:
            spread_into(grad_new, *spread_in, *spread_out)

    @pl.when(pair == pairs - 1)
    def _():
        wait_all(pushed + [back.copy(apart) for apart in aparts])
        if returns:
            own.wait()


def attention_backward(
    d_back,
    slot_col,
    d_logits,
    grad_now,
    middle,
    hidden,
    gains,
    mats,
    q_k_v,
    attended,
    bias,
    lse,
    grid_shape,
    below=None,
    after=(),
    made=None,
    returns=False,
    push=None,
    identifier=None,
):
    seq_len, width = hidden.shape
    heads = bias.shape[0]
    head_dim = width // heads
    experts = mats[1].shape[0]
    count_x, count_y = grid_shape
    ins = (
        d_back,
        slot_col,
        d_logits,
        grad_now,
        middle,
        *gains,
        mats[1],
        attended,
    )
    later = [mats[0], *q_k_v, hidden]
    spreads = below is not None
    if spreads:
        ins = ins + tuple(below)
    row = jax.ShapeDtypeStruct((1, width), f32)
    outs = (
        jax.ShapeDtypeStruct((seq_len, width), f32),
        jax.ShapeDtypeStruct(
            (count_x // 2, 2, count_y // 2, 2, width // count_x, 4 * (width // count_y)), bf16
        ),
        jax.ShapeDtypeStruct((experts, width), f32),
        row,
        row,
        jax.ShapeDtypeStruct((heads, 2 * seq_len), f32),
    )
    if spreads:
        outs = outs + (
            jax.ShapeDtypeStruct((2 * seq_len, width), bf16),
            jax.ShapeDtypeStruct(d_logits.shape, bf16),
        )
    outs = outs + (jax.ShapeDtypeStruct(made.shape, bf16),)
    pushes = push is not None
    out_specs = whole_of(outs)
    out_specs[-1] = any_spec
    if pushes:
        rows = [push[0].shape[1] - cut_of(push[0]), push[1].shape[1] // 2]
        outs = outs + tuple(landing_of(one, many) for one, many in zip(push, rows))
        out_specs += [any_spec] * 2
    return pl.pallas_call(
        partial(backward_kernel, head_dim, grid_shape, spreads, returns, pushes, len(after)),
        grid=(heads // 2,),
        in_specs=whole_of(ins)
        + [
            pl.BlockSpec((2, seq_len, seq_len), lambda p: (p, 0, 0)),
            pl.BlockSpec((1, 2, seq_len), lambda p: (p, 0, 0)),
        ]
        + [any_spec] * (len(after) + 6 + 2 * pushes),
        out_specs=out_specs,
        out_shape=outs,
        scratch_shapes=[
            pltpu.VMEM((seq_len, width), bf16),
            pltpu.VMEM((seq_len, width), f32),
            pltpu.VMEM((width, seq_len), bf16),
            pltpu.VMEM((seq_len, width), bf16),
            pltpu.VMEM((seq_len, width), bf16),
            pltpu.VMEM((seq_len, seq_len), bf16),
            pltpu.VMEM((seq_len, seq_len), bf16),
        ]
        + scratch_of(later)
        + [pltpu.SemaphoreType.DMA((6,)), pltpu.SemaphoreType.DMA]
        + [pltpu.SemaphoreType.DMA((count_y,))] * 2
        + [pltpu.SemaphoreType.DMA((2 * (count_x // 2 - 1),))] * (2 * pushes),
        compiler_params=params(identifier),
        cost_estimate=lasting(32),
        name="attention_backward",
    )(*ins, bias, lse, made, *(push if pushes else ()), *later, *after)


class Exchange:
    def __init__(self, members, rows, src, dst, send_sems, recv_sems):
        self.me = lax.axis_index("gy")
        self.bits = members.bit_length() - 1
        self.rows, self.src, self.dst = rows, src, dst
        self.send_sems, self.recv_sems = send_sems, recv_sems

    def block(self, index):
        return pl.ds(pl.multiple_of(index * self.rows, self.rows), self.rows)

    def peer(self, apart):
        return {"gy": xor_of(self.me, apart, self.bits)}

    def copy(self, apart):
        peer = xor_of(self.me, apart, self.bits)
        return pltpu.make_async_remote_copy(
            src_ref=self.src.at[self.block(peer), :],
            dst_ref=self.dst.at[self.block(self.me), :],
            send_sem=self.send_sems.at[apart],
            recv_sem=self.recv_sems.at[apart],
            device_id={"gy": peer},
            device_id_type=MESH,
        )

    def keep_own(self):
        self.dst[self.block(self.me), :] = self.src[self.block(self.me), :]


class Leading(Exchange):
    def __init__(self, members, src, dst, send_sems, recv_sems):
        super().__init__(members, 1, src, dst, send_sems, recv_sems)

    def copy(self, apart):
        peer = xor_of(self.me, apart, self.bits)
        sems = (self.send_sems, self.recv_sems)
        return send(self.src.at[peer], self.dst.at[self.me], sems, apart, {"gy": peer})

    def keep_own(self):
        self.dst[self.me] = self.src[self.me]


def peers_along_gy(members):
    me = lax.axis_index("gy")
    bits = members.bit_length() - 1
    return [{"gy": xor_of(me, apart, bits)} for apart in range(1, members)]


def gelu_and_slope(pre):
    inner_scale = 0.7978845608028654
    square = pre * pre
    bent = jnp.tanh(inner_scale * pre * (1.0 + 0.044715 * square))
    act = 0.5 * pre * (1.0 + bent)
    slope = 0.5 * (1.0 + bent) + 0.5 * pre * (1.0 - bent * bent) * (
        inner_scale * (1.0 + 3 * 0.044715 * square)
    )
    return act, slope


def gelu_only(pre):
    inner_scale = 0.7978845608028654
    return 0.5 * pre * (1.0 + jnp.tanh(inner_scale * pre * (1.0 + 0.044715 * pre * pre)))


def send_order(members):
    return range(1, members)


def early(members):
    quarter = max(1, members // 4)
    return [apart for apart in range(members) if (apart // quarter) % 2 == 0]


def part_of(members, first):
    chosen = early(members)
    return [a for a in range(1, members) if (a in chosen) == first]


def third_of(members, apart):
    quarter = max(1, members // 4)
    if (apart // quarter) % 2 == 0:
        return 0
    return 1 + (2 * (apart % quarter)) // quarter


def in_third(members, third):
    return [apart for apart in range(1, members) if third_of(members, apart) == third]


def collect(me, members, rows, refs, which_of, dst, sems):
    copies = []
    for apart in range(members):
        start = xor_of(me, apart, bits_of(members)) * rows
        here = pl.ds(pl.multiple_of(start, rows), rows)
        ref = refs[which_of(apart)]
        copies.append(pltpu.make_async_copy(ref.at[here, :], dst.at[here, :], sems.at[apart]))
    return copies


class Weights:
    def __init__(self, place, halves, whole_refs, local_sems, sems):
        blocks, _, units = halves[0].shape
        self.local, self.remote = [], []
        for which, (part, into) in enumerate(zip(halves, whole_refs)):
            for block in range(blocks):
                index = which * blocks + block
                begin = pl.multiple_of((place.c * blocks + block) * units, units)
                dst = into.at[:, pl.ds(begin, units)]
                src = part.at[block]
                self.local.append(pltpu.make_async_copy(src, dst, local_sems.at[index]))
                self.remote.append(send(src, dst, sems, index, place.core_peer()))
        self.blocks = blocks

    def start_local(self):
        start_all(self.local)

    def start_remote(self):
        start_all(self.remote)

    def wait(self, which):
        mine = slice(which * self.blocks, (which + 1) * self.blocks)
        for copy in self.local[mine] + self.remote[mine]:
            copy.wait()


def weight_gradients(place, products, sends, landings, outs, sems, after):
    blocks, _, units = outs[0].shape

    def product(lhs, rhs_ref, which, into_ref):
        @pl.loop(0, blocks)
        def _(block):
            begin = pl.multiple_of((which * blocks + block) * units, units)
            into_ref[block] = dot(lhs, rhs_ref[:, pl.ds(begin, units)]).astype(bf16)

    for index, (lhs_ref, rhs_ref) in enumerate(products):
        lhs = lhs_ref[...].T
        product(lhs, rhs_ref, 1 - place.c, sends[index])
        copy = send(sends[index], landings[index], sems, index, place.core_peer())
        copy.start()
        product(lhs, rhs_ref, place.c, outs[index])
        copy.wait()

        @pl.loop(0, blocks)
        def _(block, index=index):
            add_low(outs[index], (block,), outs[index][block], landings[index][block])

        start_all(after[index])


def push_blocks(place, src, landing, sems, begin, base=0):
    rows = pl.ds(begin, landing.shape[1])
    return [
        send(
            src.at[place.y_at(apart), rows],
            landing.at[apart - 1],
            sems,
            base + apart - 1,
            place.y_peer(apart),
        )
        for apart in range(1, place.count_y)
    ]


def cut_of(blocks):
    return blocks.shape[1] // 3 * 2


def landing_of(blocks, rows):
    return jax.ShapeDtypeStruct((blocks.shape[0] - 1, rows, blocks.shape[2]), bf16)


def chunk_of(members, rows):
    return max(1, min(members, 256 // rows))


def expert_forward_kernel(
    grid_shape,
    gathers,
    sent_ref,
    slot_col_ref,
    chosen_ref,
    logits_ref,
    middle_in_ref,
    win_ref,
    wout_ref,
    *refs,
):
    refs = list(refs)
    take = refs.pop
    column_ref = take(0) if gathers else None
    arrived_out_ref, comb_ref, out_ref = (take(0) for _ in range(3))
    full_ref = take(0) if gathers else None
    arrived_ref, middle_ref, move_sems = (take(0) for _ in range(3))
    load_middle, write_arrived = local_copies(
        [(middle_in_ref, middle_ref), (arrived_ref, arrived_out_ref)], move_sems
    )
    win_s, wout_s, made_s, returned_s, w_sems = (take(0) for _ in range(5))
    send_sems, recv_sems, back_send_sems, back_recv_sems = (take(0) for _ in range(4))
    weight_sems = (take(0), take(0))
    members = grid_shape[1]
    slots = sent_ref.shape[0]
    rows = slots // members
    group = chunk_of(members, rows)
    chunks = members // group
    chunk_bits = chunks.bit_length() - 1
    hidden_units = win_s.shape[1]
    tile = min(768, hidden_units)
    place = Place(grid_shape)
    weights = Weights(place, (win_ref, wout_ref), (win_s, wout_s), w_sems, weight_sems)
    weights.start_local()
    load_middle.start()
    more_peers = place.y_peers() if gathers else []
    greet(peers_along_gy(members) + [place.core_peer()] + more_peers)
    weights.start_remote()
    there = Exchange(members, rows, sent_ref, arrived_ref, send_sems, recv_sems)
    back = Exchange(members, rows, made_s, returned_s, back_send_sems, back_recv_sems)
    for apart in send_order(members):
        there.copy(apart).start()
    there.keep_own()
    if gathers:
        own_sem, *sems = refs
        split = (full_ref.shape[4] - tile_rows) // 2
        own = pltpu.make_async_copy(
            column_ref, full_ref.at[place.y, place.c, :, place.x], own_sem
        )
        own.start()
        second = gather_second(place, column_ref, full_ref, split, sems)
        third = gather_third(place, full_ref, split, sems)
        fourth = gather_core(place, full_ref, sems)
        start_all(second)
    weights.wait(0)
    weights.wait(1)
    my_chunk = there.me // group

    def chunk_rows(index):
        start = xor_of(my_chunk, index, chunk_bits) * (group * rows)
        return pl.ds(pl.multiple_of(start, group * rows), group * rows)

    def work(index, first):
        for member in range(first, group):
            there.copy(index * group + member).wait_recv()
        here = chunk_rows(index)
        taken = arrived_ref[here, :]
        total = jnp.zeros((group * rows, taken.shape[1]), f32)
        for start in range(0, hidden_units, tile):
            units = slice(start, start + tile)
            act = gelu_only(dot(taken, win_s[:, units])).astype(bf16)
            total = total + dot(act, wout_s[:, units], 1, 1)
        made_s[here, :] = total.astype(bf16)
        for member in range(first, group):
            back.copy(index * group + member).start()

    work(0, 1)
    back.keep_own()
    half = chunks // 2

    @pl.loop(1, half)
    def _(index):
        work(index, 0)

    if gathers:
        own.wait()
        wait_all(second)
        start_all(third)

    @pl.loop(half, chunks)
    def _(index):
        work(index, 0)

    if gathers:
        wait_all(third)
        start_all(fourth)
    write_arrived.start()
    slot_col = slot_col_ref[...]
    comb_ref[...] = jnp.zeros_like(comb_ref)

    def gather_back(index, first):
        for member in range(first, group):
            back.copy(index * group + member).wait_recv()
        begin = xor_of(my_chunk, index, chunk_bits) * (group * rows)
        places = lax.broadcasted_iota(jnp.int32, (slot_col.shape[0], group * rows), 1) + begin
        placing = (places == slot_col).astype(f32).astype(bf16)
        comb_ref[...] += dot(placing, returned_s[chunk_rows(index), :])

    gather_back(0, 1)

    @pl.loop(1, chunks)
    def _(index):
        gather_back(index, 0)

    load_middle.wait()
    gate = jnp.sum(jax.nn.softmax(logits_ref[...], axis=-1) * chosen_ref[...], axis=1, keepdims=True)
    out_ref[...] = middle_ref[...] + gate * comb_ref[...]
    if gathers:
        wait_all(fourth)

    @pl.loop(1, members)
    def _(apart):
        there.copy(apart).wait_send()
        back.copy(apart).wait_send()

    write_arrived.wait()


def doubled(half):
    return pltpu.VMEM((half.shape[1], 2 * half.shape[0] * half.shape[2]), bf16)


def expert_forward(
    sent, slot_col, chosen_f, logits, middle, full_in, full_out, grid_shape, identifier, column=None
):
    members = grid_shape[1]
    gathers = column is not None
    ins = [sent, slot_col, chosen_f, logits, middle, full_in, full_out]
    in_specs = [vmem_spec] * 4 + [any_spec] * 3
    outs = [
        jax.ShapeDtypeStruct(sent.shape, bf16),
        jax.ShapeDtypeStruct(middle.shape, f32),
        jax.ShapeDtypeStruct(middle.shape, f32),
    ]
    out_specs = [any_spec] + [vmem_spec] * 2
    sems = pltpu.SemaphoreType.DMA((members,))
    scratch = [
        *scratch_of([sent, middle]),
        pltpu.SemaphoreType.DMA((2,)),
        doubled(full_in),
        doubled(full_out),
        pltpu.VMEM(sent.shape, bf16),
        pltpu.VMEM(sent.shape, bf16),
        pltpu.SemaphoreType.DMA((2 * full_in.shape[0],)),
        sems,
        sems,
        sems,
        sems,
        pltpu.SemaphoreType.DMA((2 * full_in.shape[0],)),
        pltpu.SemaphoreType.DMA((2 * full_in.shape[0],)),
    ]
    if gathers:
        ins.append(column)
        in_specs.append(any_spec)
        half = (grid_shape[0] // 2, 2, grid_shape[1] // 2, 2)
        outs.append(jax.ShapeDtypeStruct((*half, *column.shape[1:]), bf16))
        out_specs.append(any_spec)
        others = pltpu.SemaphoreType.DMA((gather_copies(grid_shape)[1],))
        scratch += [pltpu.SemaphoreType.DMA, others, others]
    return pl.pallas_call(
        partial(expert_forward_kernel, grid_shape, gathers),
        in_specs=in_specs,
        out_specs=out_specs,
        out_shape=outs,
        scratch_shapes=scratch,
        compiler_params=params(identifier),
        cost_estimate=lasting(75),
        name="expert_forward",
    )(*ins)


def expert_both_kernel(
    grid_shape,
    sent_ref,
    gates_ref,
    slot_col_ref,
    chosen_ref,
    logits_ref,
    far_first_ref,
    far_second_ref,
    far_third_ref,
    win_ref,
    wout_ref,
    made_out_ref,
    d_back_ref,
    gin_out_ref,
    gout_out_ref,
    d_logits_ref,
    arrived_s,
    gates_s,
    win_s,
    wout_s,
    d_made_s,
    d_rows_s,
    act_s,
    d_pre_s,
    d_gates_s,
    d_gates_back_s,
    grads_ref,
    gin_send,
    gin_land,
    gout_send,
    gout_land,
    made_ref,
    gin_ref,
    gout_ref,
    write_sems,
    w_sems,
    *sems,
):
    far_refs = (far_first_ref, far_second_ref, far_third_ref)
    members = grid_shape[1]
    weight_sems, sum_sems = sems[9:11], sems[11:13]
    slots = sent_ref.shape[0]
    rows = slots // members
    group = chunk_of(members, rows)
    chunks = members // group
    chunk_bits = bits_of(chunks)
    hidden_units = win_s.shape[1]
    tile = min(768, hidden_units)
    place = Place(grid_shape)
    weights = Weights(place, (win_ref, wout_ref), (win_s, wout_s), w_sems, weight_sems)
    weights.start_local()
    greet(peers_along_gy(members) + [place.core_peer()])
    weights.start_remote()
    there = Exchange(members, rows, sent_ref, arrived_s, *sems[0:2])
    back = Exchange(members, rows, d_rows_s, d_back_ref, *sems[2:4])
    gates_there = Leading(members, gates_ref, gates_s, *sems[4:6])
    gates_back = Leading(members, d_gates_s, d_gates_back_s, *sems[6:8])

    for apart in send_order(members):
        gates_there.copy(apart).start()
        there.copy(apart).start()

    collected = collect(
        there.me, members, rows, far_refs, partial(third_of, members), grads_ref, sems[8]
    )
    start_all(collected)
    there.keep_own()
    gates_there.keep_own()
    weights.wait(0)
    weights.wait(1)
    wait_all(collected)
    my_chunk = there.me // group

    def work(index, first):
        for member in range(first, group):
            gates_there.copy(index * group + member).wait_recv()
            there.copy(index * group + member).wait_recv()
        chunk = xor_of(my_chunk, index, chunk_bits)
        here = pl.ds(pl.multiple_of(chunk * (group * rows), group * rows), group * rows)
        gate = jnp.concatenate(
            [gates_s[chunk * group + member].T[:rows, 0:1] for member in range(group)], axis=0
        )
        taken = arrived_s[here, :]
        grads = grads_ref[here, :].astype(f32)
        d_made = (gate * grads).astype(bf16)
        d_made_s[here, :] = d_made
        made = jnp.zeros((group * rows, taken.shape[1]), f32)
        d_rows = made
        for start in range(0, hidden_units, tile):
            units = slice(start, start + tile)
            act, slope = gelu_and_slope(dot(taken, win_s[:, units]))
            act = act.astype(bf16)
            act_s[here, units] = act
            d_pre = (dot(d_made, wout_s[:, units]) * slope).astype(bf16)
            d_pre_s[here, units] = d_pre
            d_rows = d_rows + dot(d_pre, win_s[:, units], 1, 1)
            made = made + dot(act, wout_s[:, units], 1, 1)
        d_rows_s[here, :] = d_rows.astype(bf16)
        made = made.astype(bf16)
        made_ref[here, :] = made
        d_gate = jnp.sum(grads * made.astype(f32), axis=1, keepdims=True)
        for member in range(group):
            part = jnp.broadcast_to(d_gate[member * rows : (member + 1) * rows], (rows, 128)).T
            d_gates_s[chunk * group + member, :, :rows] = part[: d_gates_s.shape[1]]
        for member in range(first, group):
            gates_back.copy(index * group + member).start()
            back.copy(index * group + member).start()

    work(0, 1)
    back.keep_own()
    gates_back.keep_own()

    @pl.loop(1, chunks)
    def _(index):
        work(index, 0)

    write_made, write_out, write_in = local_copies(
        [(made_ref, made_out_ref), (gout_ref, gout_out_ref), (gin_ref, gin_out_ref)], write_sems
    )
    write_made.start()
    weight_gradients(
        place,
        ((d_made_s, act_s), (arrived_s, d_pre_s)),
        (gout_send, gin_send),
        (gout_land, gin_land),
        (gout_ref, gin_ref),
        sum_sems,
        ([write_out], [write_in]),
    )

    @pl.loop(1, members)
    def _(apart):
        gates_back.copy(apart).wait_recv()

    row = jnp.concatenate(
        [d_gates_back_s[expert, 0:1, :rows] for expert in range(members)], axis=1
    )
    slot_col = slot_col_ref[...]
    places = lax.broadcasted_iota(jnp.int32, (slot_col.shape[0], slots), 1)
    d_gate = jnp.sum(jnp.where(places == slot_col, row, 0.0), axis=1, keepdims=True)
    d_logits_ref[...] = d_logits_of(d_gate, logits_ref[...], chosen_ref[...])

    @pl.loop(1, members)
    def _(apart):
        back.copy(apart).wait_recv()
        there.copy(apart).wait_send()
        back.copy(apart).wait_send()
        gates_there.copy(apart).wait_send()
        gates_back.copy(apart).wait_send()

    wait_all([write_made, write_out, write_in])


def expert_both(sent, gates, far_parts, slot_col, chosen_f, logits, full_in, full_out, grid_shape, identifier):
    members = grid_shape[1]
    slots = sent.shape[0]
    outs = (
        jax.ShapeDtypeStruct(sent.shape, bf16),
        jax.ShapeDtypeStruct(sent.shape, bf16),
        jax.ShapeDtypeStruct(full_in.shape, bf16),
        jax.ShapeDtypeStruct(full_out.shape, bf16),
        jax.ShapeDtypeStruct(logits.shape, bf16),
    )
    tall = pltpu.VMEM(sent.shape, bf16)
    wide = pltpu.VMEM((slots, 2 * full_in.shape[0] * full_in.shape[2]), bf16)
    half = pltpu.VMEM(full_in.shape, bf16)
    small = pltpu.VMEM(gates.shape, f32)
    weights = doubled(full_in)
    return pl.pallas_call(
        partial(expert_both_kernel, grid_shape),
        in_specs=[vmem_spec] * 5 + [any_spec] * 5,
        out_specs=[any_spec, vmem_spec, any_spec, any_spec, vmem_spec],
        out_shape=outs,
        scratch_shapes=[
            tall,
            small,
            weights,
            weights,
            tall,
            tall,
            wide,
            wide,
            small,
            small,
            tall,
            half,
            half,
            half,
            half,
            tall,
            half,
            half,
            pltpu.SemaphoreType.DMA((3,)),
            pltpu.SemaphoreType.DMA((2 * full_in.shape[0],)),
        ]
        + [pltpu.SemaphoreType.DMA((members,))] * 9
        + [pltpu.SemaphoreType.DMA((2 * full_in.shape[0],))] * 4,
        compiler_params=params(identifier),
        cost_estimate=lasting(85),
        name="expert_both",
    )(sent, gates, slot_col, chosen_f, logits, *far_parts, full_in, full_out)


def expert_backward_kernel(
    grid_shape,
    d_sent_ref,
    arrived_in_ref,
    blocks_in_ref,
    win_ref,
    wout_ref,
    d_back_ref,
    gin_out_ref,
    gout_out_ref,
    upper_ref,
    lower_ref,
    landing_ref,
    win_s,
    wout_s,
    d_arrived_s,
    d_rows_s,
    act_s,
    slope_s,
    first_s,
    up2_s,
    low2_s,
    gin_send,
    gin_land,
    gout_send,
    gout_land,
    arrived_ref,
    blocks_ref,
    gin_ref,
    gout_ref,
    move_sems,
    w_sems,
    send_sems,
    recv_sems,
    back_send_sems,
    back_recv_sems,
    *more_sems,
):
    members = grid_shape[1]
    sum_sems, weight_sems, gradient_sems = more_sems[0:2], more_sems[2:4], more_sems[4:6]
    push_sems = more_sems[6:8]
    slots = d_sent_ref.shape[0]
    rows = slots // members
    group = chunk_of(members, rows)
    chunks = members // group
    chunk_bits = chunks.bit_length() - 1
    hidden_units = win_s.shape[1]
    tile = min(768, hidden_units)
    place = Place(grid_shape)
    weights = Weights(place, (win_ref, wout_ref), (win_s, wout_s), w_sems, weight_sems)
    weights.start_local()
    moves = local_copies(
        [
            (arrived_in_ref, arrived_ref),
            (blocks_in_ref.at[:, place.c], blocks_ref.at[:, place.c]),
            (gout_ref, gout_out_ref),
            (gin_ref, gin_out_ref),
        ],
        move_sems,
    )
    start_all(moves[:2])
    greet(peers_along_gy(members) + [place.core_peer()] + place.y_peers())
    weights.start_remote()
    landings = (first_s, up2_s, low2_s, upper_ref, lower_ref, None, None)
    sums = Scatter(place, blocks_ref, landings, sum_sems, upper_ref.shape[1], blocks_in_ref)
    there = Exchange(members, rows, d_sent_ref, d_arrived_s, send_sems, recv_sems)
    back = Exchange(members, rows, d_rows_s, d_back_ref, back_send_sems, back_recv_sems)
    for apart in send_order(members):
        there.copy(apart).start()
    there.keep_own()
    my_chunk = there.me // group
    start_all(sums.copies(0))
    wait_all(moves[:2])
    weights.wait(0)

    @pl.loop(0, slots // 256)
    def _(index):
        here = pl.ds(pl.multiple_of(index * 256, 256), 256)
        taken = arrived_ref[here, :]
        for start in range(0, hidden_units, tile):
            units = slice(start, start + tile)
            act, slope = gelu_and_slope(dot(taken, win_s[:, units]))
            act_s[here, units] = act.astype(bf16)
            slope_s[here, units] = slope.astype(bf16)

    wait_all(sums.copies(0))
    sums.add(0)
    start_all(sums.copies(1))
    weights.wait(1)

    def chunk_rows(index):
        start = xor_of(my_chunk, index, chunk_bits) * (group * rows)
        return pl.ds(pl.multiple_of(start, group * rows), group * rows)

    def work(index, first):
        for member in range(first, group):
            there.copy(index * group + member).wait_recv()
        here = chunk_rows(index)
        taken = d_arrived_s[here, :]
        total = jnp.zeros((group * rows, taken.shape[1]), f32)
        for start in range(0, hidden_units, tile):
            units = slice(start, start + tile)
            d_pre = (dot(taken, wout_s[:, units]) * slope_s[here, units].astype(f32)).astype(bf16)
            slope_s[here, units] = d_pre
            total = total + dot(d_pre, win_s[:, units], 1, 1)
        d_rows_s[here, :] = total.astype(bf16)
        for member in range(first, group):
            back.copy(index * group + member).start()

    work(0, 1)
    back.keep_own()

    @pl.loop(1, chunks)
    def _(index):
        work(index, 0)

    wait_all(sums.copies(1))
    sums.add(1)
    start_all(sums.copies(2))
    pushed = push_blocks(place, gout_ref, landing_ref, push_sems, 0)
    weight_gradients(
        place,
        ((d_arrived_s, act_s), (arrived_ref, slope_s)),
        (gout_send, gin_send),
        (gout_land, gin_land),
        (gout_ref, gin_ref),
        gradient_sems,
        ([*pushed, moves[2]], [moves[3]]),
    )
    wait_all(sums.copies(2))
    sums.add(2)

    @pl.loop(1, members)
    def _(apart):
        back.copy(apart).wait_recv()
        there.copy(apart).wait_send()
        back.copy(apart).wait_send()

    wait_all(pushed + moves[2:])


def expert_backward(d_sent, arrived, blocks, full_in, full_out, grid_shape, identifier):
    members = grid_shape[1]
    landings = whole_blocks(blocks.shape, blocks.shape[4] // 2)
    outs = (
        jax.ShapeDtypeStruct(d_sent.shape, bf16),
        jax.ShapeDtypeStruct(full_in.shape, bf16),
        jax.ShapeDtypeStruct(full_out.shape, bf16),
        *[jax.ShapeDtypeStruct(one, bf16) for one in landings[3:5]],
        landing_of(full_out, cut_of(full_out)),
    )
    slots = d_sent.shape[0]
    sems = pltpu.SemaphoreType.DMA((members,))
    return pl.pallas_call(
        partial(expert_backward_kernel, grid_shape),
        in_specs=[vmem_spec] + [any_spec] * 4,
        out_specs=[vmem_spec] + [any_spec] * 2 + [vmem_spec] * 2 + [any_spec],
        out_shape=outs,
        scratch_shapes=[
            doubled(full_in),
            doubled(full_out),
            pltpu.VMEM(d_sent.shape, bf16),
            pltpu.VMEM(d_sent.shape, bf16),
            pltpu.VMEM((slots, 2 * full_in.shape[0] * full_in.shape[2]), bf16),
            pltpu.VMEM((slots, 2 * full_in.shape[0] * full_in.shape[2]), bf16),
            *[pltpu.VMEM(one, bf16) for one in landings[:3]],
            *[pltpu.VMEM(full_in.shape, bf16)] * 4,
            *scratch_of([arrived, blocks, full_in, full_out]),
            pltpu.SemaphoreType.DMA((4,)),
            pltpu.SemaphoreType.DMA((2 * full_in.shape[0],)),
            sems,
            sems,
            sems,
            sems,
            *[pltpu.SemaphoreType.DMA((scatter_copies(grid_shape),))] * 2,
            *[pltpu.SemaphoreType.DMA((2 * full_in.shape[0],))] * 4,
            *[pltpu.SemaphoreType.DMA((full_in.shape[0] - 1,))] * 2,
        ],
        compiler_params=params(10 + identifier),
        cost_estimate=lasting(85),
        name="expert_backward",
    )(d_sent, arrived, blocks, full_in, full_out)


def emit_kernel(
    table_shape,
    at_ref,
    gin_ref,
    gin_first_ref,
    gin_second_ref,
    gin_up_ref,
    gout_ref,
    gout_first_ref,
    gout_second_ref,
    gout_up_ref,
    result_ref,
    grad_ref,
    packed_ref,
    small_ref,
    gin_out_ref,
    gout_out_ref,
    result_out_ref,
    grad_out_ref,
    wq_ref,
    wk_ref,
    wv_ref,
    wo_ref,
    router_out_ref,
    gga_ref,
    ggf_ref,
    table_ref,
):
    step = pl.program_id(0)

    def landed(ref):
        total = ref[0].astype(f32)
        for index in range(1, ref.shape[0]):
            total = total + ref[index].astype(f32)
        return total

    steps = pl.num_programs(0)
    for own, first, second, up, out, early_steps in (
        (gin_ref, gin_first_ref, gin_second_ref, gin_up_ref, gin_out_ref, steps // 2),
        (gout_ref, gout_first_ref, gout_second_ref, gout_up_ref, gout_out_ref, steps // 3 * 2),
    ):
        out[0, 0] = own[0].astype(f32) + jnp.where(step < early_steps, landed(first), landed(second))
        out[1, 0] = up[...].astype(f32)

    @pl.when(step < 4)
    def _():
        result_out_ref[...] = result_ref[...]
        grad_out_ref[...] = grad_ref[...]

    @pl.when(step == 0)
    def _():
        layers, tall, wide = wq_ref.shape
        for which, ref in enumerate((wq_ref, wk_ref, wv_ref, wo_ref)):
            ref[...] = packed_ref[:, :, which * wide : (which + 1) * wide]
        buckets_count, heads = table_shape
        width = small_ref.shape[1]
        experts = (small_ref.shape[0] - 2 * layers - heads) // layers
        base = layers * experts
        gga_ref[...] = small_ref[base : base + layers, :]
        ggf_ref[...] = small_ref[base + layers : base + 2 * layers, :]
        base = base + 2 * layers
        table_ref[...] = small_ref[base : base + heads, :buckets_count]
        for layer in range(layers):
            row = small_ref[pl.ds(layer * experts + at_ref[1], 1), :]
            row = jnp.broadcast_to(row, (8, width))
            mine = pltpu.roll(row, lax.rem(width - at_ref[0] * tall, width), 1)
            router_out_ref[layer] = mine[0:1, :tall]


def emit(at, grads_in, grads_out, result, grad_now, packed, small, table_shape):
    layers, tall, lanes = packed.shape
    gin, gin_first, gin_second, gin_up = grads_in
    gout, gout_first, gout_second, gout_up = grads_out
    _, rows, units = gin.shape
    steps = 6
    tile = rows // steps
    wide = lanes // 4
    whole_in = [packed, small]
    passed = pl.BlockSpec((result.shape[0] // 4, result.shape[1]), lambda i, at: (jnp.minimum(i, 3), 0))
    own = pl.BlockSpec((1, tile, units), lambda i, at: (at[2], i, 0))
    up = pl.BlockSpec((tile, units), lambda i, at: (i, 0))

    def land(array, index):
        return pl.BlockSpec((array.shape[0], tile, units), lambda i, at: (0, index(i), 0))

    out = pl.BlockSpec((layers, 1, tile, units), lambda i, at: (0, 0, i, 0))
    expert = jax.ShapeDtypeStruct((layers, 1, rows, units), f32)
    square = jax.ShapeDtypeStruct((layers, tall, wide), f32)
    gain = jax.ShapeDtypeStruct((layers, small.shape[1]), f32)
    rest = [square] * 4
    rest += [jax.ShapeDtypeStruct((layers, 1, tall), f32), gain, gain]
    rest.append(jax.ShapeDtypeStruct(table_shape[::-1], f32))

    def expert_specs(first_land, second_land):
        early_steps = first_land.shape[1] // tile
        return [
            own,
            land(first_land, lambda i: jnp.minimum(i, early_steps - 1)),
            land(second_land, lambda i: jnp.maximum(i - early_steps, 0)),
            up,
        ]

    return pl.pallas_call(
        partial(emit_kernel, table_shape),
        grid_spec=pltpu.PrefetchScalarGridSpec(
            num_scalar_prefetch=1,
            grid=(steps,),
            in_specs=expert_specs(gin_first, gin_second)
            + expert_specs(gout_first, gout_second)
            + [passed, passed]
            + whole_of(whole_in),
            out_specs=[out, out, passed, passed] + whole_of(rest),
        ),
        out_shape=[expert, expert] + [jax.ShapeDtypeStruct(result.shape, f32)] * 2 + rest,
        compiler_params=params(),
        cost_estimate=lasting(7),
        name="emit",
    )(at, *grads_in, *grads_out, result, grad_now, *whole_in)


def body(
    hidden_in,
    route,
    piece_ids,
    buckets,
    rel_table,
    gain_attn,
    gain_ffn,
    w_query,
    w_key,
    w_value,
    w_output,
    w_router,
    w_in,
    w_out,
    cotangent,
):
    count_x = lax.axis_size("gx")
    count_y = lax.axis_size("gy")
    seq_len, width = hidden_in.shape
    layers = w_query.shape[0]
    heads = rel_table.shape[1]
    experts = w_router.shape[2] * count_y
    capacity = 2 * seq_len // experts
    wide_router = w_router.shape[2]
    tall, wide = w_query.shape[1], w_query.shape[2]
    grid_shape = (count_x, count_y)
    same_core = [list(range(core, count_x, 2)) for core in range(2)]
    router_rows = jnp.pad(
        w_router.transpose(0, 2, 1), ((0, 0), (0, tile_rows - wide_router), (0, 4 * wide - tall))
    )
    buckets_row = jnp.pad(buckets, (0, 1), constant_values=-1)[None, :]
    mats, router, later, bias, slot_col, slot_row, chosen_f, spread, far_part = start(
        (w_query, w_key, w_value, w_output),
        router_rows,
        buckets_row,
        rel_table.T,
        piece_ids,
        route,
        cotangent,
        grid_shape,
    )
    gain_attn_f = gain_attn.astype(f32)
    gain_ffn_f = gain_ffn.astype(f32)

    hidden = hidden_in
    kept = []
    blocks = None
    far_parts = [far_part]
    for layer in range(layers):
        last = layer == layers - 1
        gains = (gain_attn_f[layer][None], gain_ffn_f[layer][None])
        mats, router, q, k, v, attended, lse, middle, logits, sent, *gates, far_part = attention_forward(
            hidden,
            gains[0],
            gains[1],
            (slot_row, slot_col, chosen_f),
            bias,
            grid_shape,
            1 + layer,
            spread,
            last,
            blocks=blocks,
            mats=(mats, router) if blocks is None else None,
        )
        far_parts.append(far_part)
        full_in, full_out = (
            lax.all_gather(one[layer, 0], "gx", axis=0, tiled=False, axis_index_groups=same_core)
            for one in (w_in, w_out)
        )
        state = (hidden, gains, (mats, router), (q, k, v), attended, lse, middle, logits)
        if last:
            made, d_back, grad_in_full, grad_out_full, d_logits = expert_both(
                sent, gates[0], far_parts, slot_col, chosen_f, logits, full_in, full_out, grid_shape, 7
            )
            kept.append(state)
        else:
            arrived, combined, hidden, blocks = expert_forward(
                sent,
                slot_col,
                chosen_f,
                logits,
                middle,
                full_in,
                full_out,
                grid_shape,
                5 + layer,
                column=later[layer],
            )
            kept.append(state + (combined, arrived, full_in, full_out))

    grad_now = cotangent
    parts = []
    partials = []
    returned = []
    for layer in reversed(range(layers)):
        last = layer == layers - 1
        (prior, gains, mats, q_k_v, attended, lse, middle, logits) = kept[layer][:8]
        if not last:
            arrived, full_in, full_out = kept[layer][9:]
            d_back, grad_in_full, grad_out_full, upper, lower, out_first = expert_backward(
                d_sent, arrived, parts[-1][0], full_in, full_out, grid_shape, layer
            )
            partials.append((upper, lower[:1]))
        experts_parts = []
        if layer > 0:
            experts_parts = [
                lax.psum_scatter(
                    one, "gx", scatter_dimension=0, tiled=False, axis_index_groups=same_core
                )
                for one in (grad_in_full, grad_out_full)
            ]
        below = None
        if layer > 0:
            below = (kept[layer - 1][8], slot_row, chosen_f, kept[layer - 1][7])
        got = attention_backward(
            d_back,
            slot_col,
            d_logits,
            grad_now,
            middle,
            prior,
            gains,
            mats,
            q_k_v,
            attended,
            bias,
            lse,
            grid_shape,
            below=below,
            after=[array for part in parts for array in part[4]],
            made=made,
            returns=last,
            push=(grad_out_full, grad_in_full) if layer == 0 else None,
            identifier=18 + layer,
        )
        grad_now, blocked, gwr, gga, ggf, offset_sums = got[:6]
        if layer > 0:
            d_sent, d_logits = got[6:8]
        if layer == 0:
            *got, out_second, in_first = got
        returned.append(got[-1])
        parts.append((blocked, gwr, gga, ggf, experts_parts, offset_sums))
    parts = parts[::-1]
    buckets_count = rel_table.shape[0]
    smalls = [part[which] for which in (1, 2, 3, 5) for part in parts]
    top = kept[-1]
    packed, small, hidden_out, in_second = final_sums(
        parts[0][0],
        partials[::-1],
        smalls + [buckets_row],
        (slot_col, chosen_f, top[7], top[6]),
        returned,
        grad_in_full,
        grid_shape,
        buckets_count,
    )
    first, second = lax.axis_index("gx"), lax.axis_index("gy")
    grad_in, grad_out, hidden_out, grad_now, gwq, gwk, gwv, gwo, gwr, gga_all, ggf_all, d_table = emit(
        jnp.stack([first, second, first // 2]).astype(jnp.int32),
        (grad_in_full, in_first, in_second, parts[1][4][0]),
        (grad_out_full, out_first, out_second, parts[1][4][1]),
        hidden_out,
        grad_now,
        packed,
        small,
        rel_table.shape,
    )
    return (
        hidden_out,
        grad_now,
        d_table.T,
        gga_all,
        ggf_all,
        gwq,
        gwk,
        gwv,
        gwo,
        gwr.transpose(0, 2, 1),
        grad_in,
        grad_out,
    )


def solution(mesh):
    rows = P(("gx", "gy"), None)
    square = P(None, "gx", "gy")
    expert = P(None, "gy", None, "gx")
    return jax.shard_map(
        body,
        mesh=mesh,
        in_specs=(rows, rows, P(("gx", "gy")), P(), P(), P(), P())
        + (square,) * 5
        + (expert, expert, rows),
        out_specs=(rows, rows, P(), P(), P()) + (square,) * 5 + (expert, expert),
        check_vma=False,
    )
```

```python
from functools import partial

import jax
import jax.numpy as jnp
from jax import lax
from jax.experimental import pallas as pl
from jax.experimental.pallas import tpu as pltpu
from jax.sharding import PartitionSpec as P

eps_norm = 1e-06
highest = lax.Precision.HIGHEST
f32 = jnp.float32
bf16 = jnp.bfloat16
masked_out = -1e30
tile_rows = 16
MESH = pl.DeviceIdType.MESH
vmem_spec = pl.BlockSpec(memory_space=pltpu.VMEM)
any_spec = pl.BlockSpec(memory_space=pl.ANY)
vmem_bytes = 60 * 1024 * 1024


def whole(shape):
    zeros = (0,) * len(shape)
    return pl.BlockSpec(shape, lambda *_: zeros, pipeline_mode=pl.Buffered(1))


def whole_of(arrays):
    return [whole(array.shape) for array in arrays]


def params(identifier=None):
    if identifier is None:
        return pltpu.CompilerParams(vmem_limit_bytes=vmem_bytes)
    return pltpu.CompilerParams(
        vmem_limit_bytes=vmem_bytes, collective_id=identifier, has_side_effects=True
    )


def lasting(microseconds):
    return pl.CostEstimate(
        flops=int(microseconds * 1e9), bytes_accessed=1 << 20, transcendentals=0
    )


def dot(lhs, rhs, lhs_dim=1, rhs_dim=0):
    return lax.dot_general(
        lhs, rhs, (((lhs_dim,), (rhs_dim,)), ((), ())), preferred_element_type=f32
    )


def rms_factor(hidden):
    return lax.rsqrt(jnp.mean(hidden * hidden, axis=-1, keepdims=True) + eps_norm)


def rms_pull(hidden, gain_row, d_normed):
    factor = rms_factor(hidden)
    scaled = gain_row * d_normed
    inner = jnp.mean(hidden * scaled, axis=-1, keepdims=True)
    d_hidden = factor * scaled - hidden * (factor * factor * factor * inner)
    d_gain = jnp.sum(d_normed * hidden * factor, axis=0, keepdims=True)
    return d_hidden, d_gain


def xor_of(index, other, bits):
    total = 0
    for bit in range(bits):
        power = 1 << bit
        total = total + ((index // power + other // power) % 2) * power
    return total


def placing_rows(slot_row, slots):
    places = lax.broadcasted_iota(jnp.int32, (slots, slot_row.shape[1]), 0)
    return (places == slot_row).astype(f32).astype(bf16)


def placing_cols(slot_col, slots):
    places = lax.broadcasted_iota(jnp.int32, (slot_col.shape[0], slots), 1)
    return (places == slot_col).astype(f32).astype(bf16)


def greet(peers):
    barrier = pltpu.get_barrier_semaphore()
    for peer in peers:
        pl.semaphore_signal(barrier, inc=1, device_id=peer, device_id_type=MESH)
    pl.semaphore_wait(barrier, len(peers))


def bits_of(count):
    return count.bit_length() - 1


class Place:
    def __init__(self, grid_shape):
        self.count_y, self.count_z = grid_shape[0] // 2, grid_shape[1] // 2
        first, second = lax.axis_index("gx"), lax.axis_index("gy")
        self.c, self.y = first % 2, first // 2
        self.x, self.z = second % 2, second // 2

    def core_peer(self):
        return {"gx": self.y * 2 + 1 - self.c}

    def x_peer(self):
        return {"gy": self.z * 2 + 1 - self.x}

    def y_at(self, apart):
        return xor_of(self.y, apart, bits_of(self.count_y))

    def y_peer(self, apart):
        return {"gx": self.y_at(apart) * 2 + self.c}

    def y_peers(self):
        return [self.y_peer(apart) for apart in range(1, self.count_y)]

    def z_at(self, apart):
        return xor_of(self.z, apart, bits_of(self.count_z))

    def z_peer(self, apart):
        return {"gy": self.z_at(apart) * 2 + self.x}

    def z_peers(self):
        return [self.z_peer(apart) for apart in range(1, self.count_z)]


def send(src, dst, sems, index, peer):
    return pltpu.make_async_remote_copy(
        src_ref=src,
        dst_ref=dst,
        send_sem=sems[0].at[index],
        recv_sem=sems[1].at[index],
        device_id=peer,
        device_id_type=MESH,
    )


def start_all(copies):
    for copy in copies:
        copy.start()


def wait_all(copies):
    for copy in copies:
        copy.wait()


def local_copies(pairs, sems, base=0):
    return [
        pltpu.make_async_copy(src, dst, sems.at[base + index])
        for index, (src, dst) in enumerate(pairs)
    ]


def scratch_of(arrays):
    return [pltpu.VMEM(array.shape, array.dtype) for array in arrays]


def gather_z(place, src, landing, sems):
    return [
        send(src, landing, sems, apart - 1, place.z_peer(apart)) for apart in range(1, place.count_z)
    ]


def gather_copies(grid_shape):
    return grid_shape[1] // 2 - 1, 2 * (grid_shape[0] // 2 - 1) + 3


def gather_second(place, column, full, split, sems):
    y, c, x = place.y, place.c, place.x
    upper, lower = pl.ds(0, split), pl.ds(split, full.shape[4] - split)
    copies = [
        send(column.at[:, upper], full.at[y, c, :, x, upper], sems, 0, place.x_peer())
    ]
    for apart in range(1, place.count_y):
        copies.append(
            send(column.at[:, lower], full.at[y, c, :, x, lower], sems, apart, place.y_peer(apart))
        )
    return copies


def gather_third(place, full, split, sems):
    y, c, x = place.y, place.c, place.x
    upper, lower = pl.ds(0, split), pl.ds(split, full.shape[4] - split)
    base = place.count_y
    ref = full.at[:, c, :, x, lower]
    copies = [send(ref, ref, sems, base, place.x_peer())]
    ref = full.at[y, c, :, :, upper]
    for apart in range(1, place.count_y):
        copies.append(send(ref, ref, sems, base + apart, place.y_peer(apart)))
    return copies


def gather_core(place, full, sems):
    ref = full.at[:, place.c]
    return [send(ref, ref, sems, 2 * place.count_y, place.core_peer())]


def whole_blocks(shape, split):
    count_y, _, count_z, _, tall, lanes = shape
    low = tall - split
    return [
        (count_y, count_z, 2, tall, lanes),
        (count_y - 1, count_z, 2, split, lanes),
        (count_y, count_z, low, lanes),
        (count_z, split, lanes),
        (count_y - 1, count_z, low, lanes),
        (count_z - 1, split, lanes),
        (count_z - 1, low, lanes),
    ]


def scatter_copies(grid_shape):
    return 1 + 2 * (grid_shape[0] // 2) + 2 * (grid_shape[1] // 2 - 1)


def add_low(dst, dst_at, *terms):
    total = terms[0].astype(f32)
    for term in terms[1:]:
        total = total + term.astype(f32)
    dst[dst_at] = total.astype(bf16)


class Scatter:
    def __init__(self, place, src, landings, sems, split, source=None):
        self.place, self.src, self.sems = place, src, sems
        self.source = src if source is None else source
        self.first, self.up2, self.low2, self.up3, self.low3, self.up4, self.low4 = landings
        tall = src.shape[4]
        self.upper, self.lower = pl.ds(0, split), pl.ds(split, tall - split)

    def copies(self, stage):
        at, sems = self.place, self.sems
        count_y, count_z = at.count_y, at.count_z
        if stage == 0:
            return [send(self.source.at[:, 1 - at.c], self.first, sems, 0, at.core_peer())]
        if stage == 1:
            copies = [send(self.first.at[:, :, 1 - at.x, self.lower], self.low2, sems, 1, at.x_peer())]
            for apart in range(1, count_y):
                src = self.first.at[at.y_at(apart), :, :, self.upper]
                dst = self.up2.at[apart - 1]
                copies.append(send(src, dst, sems, 1 + apart, at.y_peer(apart)))
            return copies
        if stage == 2:
            base = 1 + count_y
            copies = [send(self.up2.at[0, :, 1 - at.x], self.up3, sems, base, at.x_peer())]
            for apart in range(1, count_y):
                src, dst = self.low2.at[at.y_at(apart)], self.low3.at[apart - 1]
                copies.append(send(src, dst, sems, base + apart, at.y_peer(apart)))
            return copies
        base = 2 * count_y
        copies = []
        for apart in range(1, count_z):
            there = at.z_at(apart)
            for src, dst, more in (
                (self.up3.at[there], self.up4.at[apart - 1], 0),
                (self.low3.at[0, there], self.low4.at[apart - 1], 1),
            ):
                index = base + 2 * apart - 1 + more
                copies.append(send(src, dst, sems, index, at.z_peer(apart)))
        return copies

    def add(self, stage):
        at = self.place
        count_y, count_z = at.count_y, at.count_z
        if stage == 0:

            @pl.loop(0, count_y * count_z)
            def _(index):
                y, z = index // count_z, index % count_z
                add_low(self.first, (y, z), self.first[y, z], self.src[y, at.c, z])

        elif stage == 1:

            @pl.loop(0, count_z)
            def _(z):
                for x in range(2):
                    terms = [self.up2[apart, z, x] for apart in range(count_y - 1)]
                    add_low(self.up2, (0, z, x), self.first[at.y, z, x, self.upper], *terms)

                @pl.loop(0, count_y)
                def _(y):
                    add_low(self.low2, (y, z), self.first[y, z, at.x, self.lower], self.low2[y, z])

        elif stage == 2:

            @pl.loop(0, count_z)
            def _(z):
                add_low(self.up3, (z,), self.up3[z], self.up2[0, z, at.x])
                terms = [self.low3[apart, z] for apart in range(count_y - 1)]
                add_low(self.low3, (0, z), self.low2[at.y, z], *terms)

    def result(self):
        at = self.place
        upper, lower = self.up3[at.z].astype(f32), self.low3[0, at.z].astype(f32)
        for apart in range(at.count_z - 1):
            upper = upper + self.up4[apart].astype(f32)
            lower = lower + self.low4[apart].astype(f32)
        return upper, lower


class SmallSum:
    def __init__(self, grid_shape, totals, landing, sems):
        self.totals, self.landing, self.sems = totals, landing, sems
        self.peers = []
        for name, count in (("gx", grid_shape[0]), ("gy", grid_shape[1])):
            me = lax.axis_index(name)
            for bit in range(bits_of(count)):
                self.peers.append({name: xor_of(me, 1 << bit, bits_of(count))})
        self.done = 0

    def copy(self):
        step = self.done
        return send(self.totals.at[step], self.landing.at[step], self.sems, step, self.peers[step])

    def begin(self):
        self.copy().start()

    def advance(self):
        if self.done == len(self.peers):
            return
        self.copy().wait()
        step = self.done
        self.totals[step + 1] = self.totals[step] + self.landing[step]
        self.done += 1
        if self.done < len(self.peers):
            self.begin()


def small_steps(grid_shape):
    return bits_of(grid_shape[0]) + bits_of(grid_shape[1])


def lane_parts(lanes):
    return lanes // 128 if lanes % 128 == 0 else 1


def lane_part(ref, part, parts):
    if parts == 1:
        return ref
    lanes = ref.shape[-1] // parts
    return ref.at[..., pl.ds(part * lanes, lanes)]


def final_kernel(grid_shape, layers, buckets_count, *refs):
    refs = list(refs)
    take = refs.pop
    partial_refs = [(take(0), take(0)) for _ in range(layers - 1)]
    router_refs, gga_refs, ggf_refs, offset_refs = ([take(0) for _ in range(layers)] for _ in range(4))
    buckets_ref, slot_col_ref, chosen_ref, logits_ref = (take(0) for _ in range(4))
    blocks_in_ref, middle_in_ref = take(0), take(0)
    first_ref, second_ref, push_ref = take(0), take(0), take(0)
    packed_ref, small_out_ref, result_ref, landing_ref = (take(0) for _ in range(4))
    blocks_ref, middle_ref, move_sems = (take(0) for _ in range(3))
    landings = [take(0) for _ in range(7)]
    z_landings = [(take(0), take(0)) for _ in range(layers - 1)]
    totals, landing, returned_s = take(0), take(0), take(0)
    sems = [(take(0), take(0)) for _ in range(layers)]
    small_sems, collect_sems, push_sems = (take(0), take(0)), take(0), (take(0), take(0))
    place = Place(grid_shape)
    tall = packed_ref.shape[1]
    split = tall // 2
    members = grid_shape[1]
    slots = returned_s.shape[0]
    upper_layers = []
    for layer in range(1, layers):
        upper, lower = partial_refs[layer - 1]
        places = (None, None, None, upper, lower, *z_landings[layer - 1])
        upper_layers.append(Scatter(place, blocks_ref, places, sems[layer], split))
    parts = lane_parts(packed_ref.shape[2])
    lowest = [
        Scatter(
            place,
            lane_part(blocks_ref, part, parts),
            [lane_part(landing_part, part, parts) for landing_part in landings],
            (sems[0][0].at[part], sems[0][1].at[part]),
            split,
            lane_part(blocks_in_ref, part, parts),
        )
        for part in range(parts)
    ]

    def step(stage):
        for one in lowest:
            wait_all(one.copies(stage))
            one.add(stage)
            start_all(one.copies(stage + 1))

    c = place.c
    moves = local_copies(
        [(blocks_in_ref.at[:, c], blocks_ref.at[:, c]), (middle_in_ref, middle_ref)], move_sems
    )
    start_all(moves)
    collected = collect(
        lax.axis_index("gy"),
        members,
        slots // members,
        (first_ref, second_ref),
        lambda apart: int(apart not in early(members)),
        returned_s,
        collect_sems,
    )
    start_all(collected)
    greet([place.core_peer(), place.x_peer()] + place.y_peers() + place.z_peers())
    for one in lowest:
        start_all(one.copies(0))
    for one in upper_layers:
        start_all(one.copies(3))

    experts = router_refs[0].shape[0]
    totals[0] = jnp.zeros(totals.shape[1:], f32)
    row = 0
    for refs_of in (router_refs, gga_refs, ggf_refs):
        for ref in refs_of:
            totals[0, row : row + ref.shape[0], :] = ref[...]
            row += ref.shape[0]
    heads = offset_refs[0].shape[0]
    offsets = offset_refs[0][...]
    for ref in offset_refs[1:]:
        offsets = offsets + ref[...]
    in_bucket = (
        lax.broadcasted_iota(jnp.int32, (buckets_count, offsets.shape[1]), 0) == buckets_ref[...]
    ).astype(f32)
    totals[0, row : row + heads, :buckets_count] = lax.dot_general(
        offsets, in_bucket, (((1,), (1,)), ((), ())), precision=highest, preferred_element_type=f32
    )
    small = SmallSum(grid_shape, totals, landing, small_sems)
    small.begin()
    wait_all(moves)
    step(0)
    small.advance()
    wait_all(collected)
    placing = placing_cols(slot_col_ref[...], slots)
    gate = jnp.sum(jax.nn.softmax(logits_ref[...], axis=-1) * chosen_ref[...], axis=1, keepdims=True)
    result_ref[...] = middle_ref[...] + gate * dot(placing, returned_s[...])
    small.advance()
    step(1)
    small.advance()

    def finish(layer, one, lanes=slice(None)):
        for part, rows in zip(one.result(), (slice(0, split), slice(split, tall))):
            packed_ref[layer, rows, lanes] = part

    for layer, one in enumerate(upper_layers):
        wait_all(one.copies(3))
        finish(layer + 1, one)
    step(2)
    pushed = push_blocks(
        place, push_ref, landing_ref, push_sems, push_ref.shape[1] - landing_ref.shape[1]
    )
    start_all(pushed)
    while small.done < len(small.peers):
        small.advance()
    small_out_ref[...] = totals[len(small.peers)]
    each = packed_ref.shape[2] // parts
    for part, one in enumerate(lowest):
        wait_all(one.copies(3))
        finish(0, one, slice(part * each, (part + 1) * each))
    wait_all(pushed)


def final_sums(blocks, partials, smalls, finishing, returned, push, grid_shape, buckets_count):
    layers = len(partials) + 1
    shape = blocks.shape
    tall = shape[4]
    width = finishing[-1].shape[1]
    landings = [pltpu.VMEM(one, bf16) for one in whole_blocks(shape, tall // 2)]
    steps = small_steps(grid_shape)
    rows = sum(one.shape[0] for one in smalls[: 3 * layers]) + smalls[3 * layers].shape[0]
    small_shape = (rows, width)
    sems = pltpu.SemaphoreType.DMA((scatter_copies(grid_shape),))
    first_sems = pltpu.SemaphoreType.DMA((lane_parts(shape[5]), scatter_copies(grid_shape)))
    small_sems = pltpu.SemaphoreType.DMA((steps,))
    outs = [jax.ShapeDtypeStruct((layers, tall, shape[5]), f32)]
    outs += [jax.ShapeDtypeStruct(small_shape, f32), jax.ShapeDtypeStruct(finishing[-1].shape, f32)]
    outs.append(landing_of(push, push.shape[1] - push.shape[1] // 2))
    ins = [*[array for pair in partials for array in pair], *smalls, *finishing[:3]]
    moved = [blocks, finishing[-1]]
    return pl.pallas_call(
        partial(final_kernel, grid_shape, layers, buckets_count),
        in_specs=[vmem_spec] * len(ins) + [any_spec] * 5,
        out_specs=[vmem_spec] * (len(outs) - 1) + [any_spec],
        out_shape=outs,
        scratch_shapes=scratch_of(moved)
        + [pltpu.SemaphoreType.DMA((2,))]
        + landings
        + landings[5:] * (layers - 1)
        + [pltpu.VMEM((steps + 1, *small_shape), f32), pltpu.VMEM((steps, *small_shape), f32)]
        + [pltpu.VMEM(returned[0].shape, bf16)]
        + [first_sems, first_sems]
        + [sems, sems] * (layers - 1)
        + [small_sems, small_sems, pltpu.SemaphoreType.DMA((grid_shape[1],))]
        + [pltpu.SemaphoreType.DMA((grid_shape[0] // 2 - 1,))] * 2,
        compiler_params=params(24),
        cost_estimate=lasting(60),
        name="final_sums",
    )(*ins, *moved, *returned, push)


def unblock(grid_shape, blocks_ref, mats_ref, router_ref):
    count_x, count_y = grid_shape
    tall = mats_ref.shape[1] // count_x
    wide = mats_ref.shape[2] // count_y
    router_rows = []
    for first in range(count_x):
        spots = [(first // 2, first % 2, second // 2, second % 2) for second in range(count_y)]
        rows = slice(first * tall, (first + 1) * tall)
        for which in range(4):
            lanes = slice(which * wide, (which + 1) * wide)
            mats_ref[which, rows, :] = jnp.concatenate(
                [blocks_ref[(*spot, slice(0, tall), lanes)] for spot in spots], axis=1
            )
        router_rows.append(
            jnp.concatenate(
                [blocks_ref[(*spot, slice(tall, tall + 1), slice(0, tall))] for spot in spots],
                axis=0,
            )
        )
    router_ref[...] = jnp.concatenate(router_rows, axis=1)


def turned(row):
    return jnp.broadcast_to(row, (128, row.shape[1])).T[:, 0:1]


def start_kernel(
    grid_shape,
    wq_ref,
    wk_ref,
    wv_ref,
    wo_ref,
    router_rows_ref,
    buckets_ref,
    table_ref,
    piece_row_ref,
    route_row_ref,
    cotangent_ref,
    mats_ref,
    router_ref,
    later_ref,
    bias_out_ref,
    slot_col_ref,
    slot_row_ref,
    chosen_ref,
    spread_out_ref,
    far_ref,
    bias_ref,
    spread_ref,
    write_sems,
    full_s,
    column_s,
    spread_send,
    spread_recv,
    later_send,
    later_recv,
    z_send,
    z_recv,
    send_sems,
    recv_sems,
):
    place = Place(grid_shape)
    layers, tall, wide = wq_ref.shape
    split = tall // 2
    y, c, z, x = place.y, place.c, place.z, place.x

    def packed(layer):
        return jnp.concatenate([ref[layer] for ref in (wq_ref, wk_ref, wv_ref, wo_ref)], axis=1)

    column_s[z, :tall] = packed(0)
    column_s[z, tall:] = router_rows_ref[0]
    members = grid_shape[1]
    spread = Exchange(
        members, spread_ref.shape[0] // members, spread_ref, far_ref, spread_send, spread_recv
    )
    spread_copies = [spread.copy(apart) for apart in in_third(members, 0)]
    mine_here = spread.block(spread.me)
    half_heads = bias_ref.shape[0] // 2
    parts = [pl.ds(0, half_heads), pl.ds(half_heads, half_heads)]
    write_spread, write_own, *write_bias = local_copies(
        [(spread_ref, spread_out_ref), (spread_ref.at[mine_here, :], far_ref.at[mine_here, :])]
        + [(bias_ref.at[part], bias_out_ref.at[part]) for part in parts],
        write_sems,
    )
    greet(
        [place.core_peer(), place.x_peer()]
        + place.y_peers()
        + place.z_peers()
        + [spread.peer(apart) for apart in in_third(members, 0)]
    )
    first = gather_z(place, column_s.at[z], column_s.at[z], (z_send, z_recv))
    start_all(first)
    along_z = []
    for layer in range(1, layers):
        later_ref[layer - 1, z, :tall] = packed(layer)
        later_ref[layer - 1, z, tall:] = router_rows_ref[layer]
        mine = later_ref.at[layer - 1, z]
        along_z += gather_z(place, mine, mine, (later_send.at[layer - 1], later_recv.at[layer - 1]))

    seq_len, experts = chosen_ref.shape
    capacity = 2 * seq_len // experts
    heads = bias_ref.shape[0]
    buckets_count = table_ref.shape[1]
    in_bucket = (
        lax.broadcasted_iota(jnp.int32, (buckets_count, 2 * seq_len), 0) == buckets_ref[...]
    )
    offsets = dot(table_ref[...], in_bucket.astype(f32).astype(bf16))
    key_pos = lax.broadcasted_iota(jnp.int32, (seq_len, seq_len), 0)
    query_pos = lax.broadcasted_iota(jnp.int32, (seq_len, seq_len), 1)
    route_row, piece_row = route_row_ref[...], piece_row_ref[...]
    route_col, piece_col = turned(route_row), turned(piece_row)
    chosen = (lax.broadcasted_iota(jnp.int32, (seq_len, experts), 1) == route_col).astype(f32)
    chosen_t = (lax.broadcasted_iota(jnp.int32, (experts, seq_len), 0) == route_row).astype(f32)
    chosen_ref[...] = chosen
    earlier = (key_pos < query_pos).astype(f32).astype(bf16)
    before_t = dot(chosen_t.astype(bf16), earlier)
    rank_row = jnp.sum(before_t * chosen_t, axis=0, keepdims=True)
    slot_row_ref[...] = route_row * capacity + rank_row.astype(jnp.int32)
    later = (key_pos > query_pos).astype(f32).astype(bf16)
    before = dot(later, chosen.astype(bf16))
    rank_col = jnp.sum(before * chosen, axis=1, keepdims=True)
    slot_col_ref[...] = route_col * capacity + rank_col.astype(jnp.int32)
    placing = placing_rows(slot_row_ref[...], spread_ref.shape[0])
    spread_ref[...] = dot(placing, cotangent_ref[...]).astype(bf16)
    start_all([write_spread, write_own])

    same = (piece_col == piece_row) & (piece_col > 0)
    allowed = (key_pos <= query_pos) | same

    def bias_for(head):
        row = jnp.broadcast_to(offsets[head : head + 1], (seq_len, 2 * seq_len))
        shifted = pltpu.roll(row, seq_len + 1, 1, stride=1, stride_axis=0)[:, :seq_len]
        bias_ref[head] = jnp.where(allowed, shifted, masked_out).astype(bf16)

    for head in range(heads // 2):
        bias_for(head)
    wait_all(first)
    sems = (send_sems, recv_sems)
    second = gather_second(place, column_s, full_s, split, sems)
    start_all(second)
    start_all(along_z)
    start_all(spread_copies)
    write_bias[0].start()
    full_s[y, c, :, x] = column_s[...]
    for head in range(heads // 2, heads):
        bias_for(head)
    write_bias[1].start()
    wait_all(second)
    third = gather_third(place, full_s, split, sems)
    start_all(third)

    wait_all(third)
    fourth = gather_core(place, full_s, sems)
    start_all(fourth)
    wait_all(fourth)
    unblock(grid_shape, full_s, mats_ref, router_ref)
    wait_all(along_z)
    wait_all(spread_copies)
    wait_all([write_spread, write_own, *write_bias])


def start(mats, router_rows, buckets, table_t, piece_ids, route, cotangent, grid_shape):
    layers, tall, wide = mats[0].shape
    seq_len = piece_ids.shape[0]
    heads = table_t.shape[0]
    width = tall * grid_shape[0]
    experts = grid_shape[1]
    block = (router_rows.shape[1] + tall, 4 * wide)
    half = (grid_shape[0] // 2, 2, grid_shape[1] // 2, 2)
    ins = (
        *mats,
        router_rows,
        buckets,
        table_t,
        piece_ids[None, :],
        route.reshape(1, seq_len),
        cotangent,
    )
    outs = (
        jax.ShapeDtypeStruct((4, width, width), bf16),
        jax.ShapeDtypeStruct((experts, width), bf16),
        jax.ShapeDtypeStruct((layers - 1, half[2], *block), bf16),
        jax.ShapeDtypeStruct((heads, seq_len, seq_len), bf16),
        jax.ShapeDtypeStruct((seq_len, 1), jnp.int32),
        jax.ShapeDtypeStruct((1, seq_len), jnp.int32),
        jax.ShapeDtypeStruct((seq_len, experts), f32),
        jax.ShapeDtypeStruct((2 * seq_len, width), bf16),
        jax.ShapeDtypeStruct((2 * seq_len, width), bf16),
    )
    along_z, others = gather_copies(grid_shape)
    return pl.pallas_call(
        partial(start_kernel, grid_shape),
        in_specs=[vmem_spec] * len(ins),
        out_specs=[vmem_spec] * 3 + [any_spec] + [vmem_spec] * 3 + [any_spec] * 2,
        out_shape=outs,
        scratch_shapes=[
            *scratch_of([outs[3], outs[7]]),
            pltpu.SemaphoreType.DMA((4,)),
            pltpu.VMEM((*half, *block), bf16),
            pltpu.VMEM((half[2], *block), bf16),
            pltpu.SemaphoreType.DMA((experts,)),
            pltpu.SemaphoreType.DMA((experts,)),
            pltpu.SemaphoreType.DMA((layers - 1, along_z)),
            pltpu.SemaphoreType.DMA((layers - 1, along_z)),
            pltpu.SemaphoreType.DMA((along_z,)),
            pltpu.SemaphoreType.DMA((along_z,)),
            pltpu.SemaphoreType.DMA((others,)),
            pltpu.SemaphoreType.DMA((others,)),
        ],
        compiler_params=params(0),
        cost_estimate=lasting(45),
        name="start",
    )(*ins)


def half_masks(rows, width):
    lane = lax.broadcasted_iota(jnp.int32, (rows, width), 1)
    return lane < (width // 2)


def gates_of(logits, slot_col, chosen, gates_ref):
    experts = gates_ref.shape[0]
    seq_len = slot_col.shape[0]
    capacity = 2 * seq_len // experts
    gate = jnp.sum(jax.nn.softmax(logits, axis=-1) * chosen, axis=1, keepdims=True)
    places = lax.broadcasted_iota(jnp.int32, (seq_len, 2 * seq_len), 1)
    row = jnp.sum(jnp.where(places == slot_col, gate, 0.0), axis=0, keepdims=True)
    gates_ref[...] = jnp.zeros_like(gates_ref)
    for expert in range(experts):
        mine = row[:, expert * capacity : (expert + 1) * capacity]
        gates_ref[expert, :, :capacity] = jnp.broadcast_to(mine, (gates_ref.shape[1], capacity))


def forward_kernel(
    head_dim,
    grid_shape,
    blocked,
    last,
    hidden_ref,
    gain_attn_ref,
    gain_ffn_ref,
    slot_row_ref,
    slot_col_ref,
    chosen_ref,
    *refs,
):
    refs = list(refs)
    take = refs.pop
    blocks_ref = take(0) if blocked else None
    mats_ref, router_ref = (None, None) if blocked else (take(0), take(0))
    spread_ref = take(0)
    bias_ref = take(0)
    outs = []
    if blocked:
        outs.append(take(0))
        router_ref = take(0)
    outs += [take(0) for _ in range(3)]
    att_ref, lse_ref, middle_ref, logits_ref, sent_ref = (take(0) for _ in range(5))
    gates_ref = take(0) if last else None
    far_ref, send_sems, recv_sems, write_sems, *made_here = refs
    q_ref, k_ref, v_ref = made_here[-3:]
    if blocked:
        mats_ref = made_here[0]
    writes = local_copies(list(zip(made_here, outs)), write_sems)
    pair, pairs = pl.program_id(0), pl.num_programs(0)
    seq_len = hidden_ref.shape[0]
    width = 2 * head_dim
    step = min(512, seq_len)

    members = grid_shape[1]
    spread = Exchange(members, spread_ref.shape[0] // members, spread_ref, far_ref, send_sems, recv_sems)
    aparts = in_third(members, 2 if last else 1)

    @pl.when(pair == 0)
    def _():
        greet([spread.peer(apart) for apart in aparts])
        start_all([spread.copy(apart) for apart in aparts])

    @pl.when(pair == 0)
    def _():
        if blocked:
            unblock(grid_shape, blocks_ref, mats_ref, router_ref)
        hidden = hidden_ref[...].astype(f32)
        normed = (hidden * rms_factor(hidden) * gain_attn_ref[...]).astype(bf16)
        q_ref[...] = dot(normed, mats_ref[0]).astype(bf16)
        k_ref[...] = dot(normed, mats_ref[1]).astype(bf16)
        v_ref[...] = dot(normed, mats_ref[2]).astype(bf16)
        start_all(writes)

    lanes = pl.ds(pl.multiple_of(pair * width, width), width)
    q2 = q_ref[:, lanes] * jnp.asarray(head_dim**-0.5, bf16)
    k2 = k_ref[:, lanes]
    v2t = v_ref[:, lanes].T
    first = half_masks(seq_len, width)
    for half in range(2):
        q_one = jnp.where(first if half == 0 else ~first, q2, jnp.zeros_like(q2))
        v_one = v2t[half * head_dim : (half + 1) * head_dim]
        for begin in range(0, seq_len, step):
            cols = slice(begin, begin + step)
            scores = dot(k2, q_one[cols], 1, 1) + bias_ref[half, :, cols].astype(f32)
            top = jnp.max(scores, axis=0, keepdims=True)
            raised = jnp.exp(scores - top)
            total = jnp.sum(raised, axis=0, keepdims=True)
            probs = raised.astype(bf16)
            rows = pl.ds(pl.multiple_of(pair * width + half * head_dim, head_dim), head_dim)
            att_ref[rows, cols] = (dot(v_one, probs) * (1.0 / total)).astype(bf16)
            lse_ref[0, half : half + 1, cols] = top + jnp.log(total)

    @pl.when(pair == pairs - 1)
    def _():
        middle = hidden_ref[...].astype(f32) + dot(att_ref[...].T, mats_ref[3])
        middle_ref[...] = middle
        ffn_in = (middle * rms_factor(middle) * gain_ffn_ref[...]).astype(bf16)
        logits = dot(ffn_in, router_ref[...], 1, 1)
        logits_ref[...] = logits
        if gates_ref is not None:
            gates_of(logits, slot_col_ref[...], chosen_ref[...], gates_ref)
        placing = placing_rows(slot_row_ref[...], sent_ref.shape[0])
        sent_ref[...] = dot(placing, ffn_in).astype(bf16)

    @pl.when(pair == pairs - 1)
    def _():
        wait_all([spread.copy(apart) for apart in aparts])
        wait_all(writes)


def attention_forward(
    hidden,
    gain_attn,
    gain_ffn,
    slots_and_chosen,
    bias,
    grid_shape,
    identifier,
    spread,
    last,
    blocks=None,
    mats=None,
):
    seq_len, width = hidden.shape
    heads = bias.shape[0]
    head_dim = width // heads
    slots = 2 * seq_len
    experts = grid_shape[1]
    blocked = blocks is not None
    ins = [hidden, gain_attn, gain_ffn, *slots_and_chosen] + ([blocks] if blocked else list(mats))
    in_specs = whole_of(ins)
    ins.append(spread)
    in_specs.append(any_spec)
    ins.append(bias)
    in_specs.append(pl.BlockSpec((2, seq_len, seq_len), lambda p: (p, 0, 0)))
    tall = jax.ShapeDtypeStruct((seq_len, width), bf16)
    outs = [
        tall,
        tall,
        tall,
        jax.ShapeDtypeStruct((width, seq_len), bf16),
        jax.ShapeDtypeStruct((heads // 2, 2, seq_len), f32),
        jax.ShapeDtypeStruct((seq_len, width), f32),
        jax.ShapeDtypeStruct((seq_len, experts), f32),
        jax.ShapeDtypeStruct((slots, width), bf16),
    ]
    if last:
        outs.append(jax.ShapeDtypeStruct((experts, 8, max(128, slots // experts)), f32))
    out_specs = whole_of(outs)
    out_specs[:3] = [any_spec] * 3
    written = outs[:3]
    out_specs[4] = pl.BlockSpec((1, 2, seq_len), lambda p: (p, 0, 0))
    if blocked:
        more = [
            jax.ShapeDtypeStruct((4, width, width), bf16),
            jax.ShapeDtypeStruct((experts, width), bf16),
        ]
        outs = more + outs
        out_specs = [any_spec] + whole_of(more[1:]) + out_specs
        written = more[:1] + written
    outs.append(jax.ShapeDtypeStruct(spread.shape, bf16))
    out_specs.append(any_spec)
    sems = pltpu.SemaphoreType.DMA((experts,))
    scratch = [sems, sems, pltpu.SemaphoreType.DMA((len(written),)), *scratch_of(written)]
    got = pl.pallas_call(
        partial(forward_kernel, head_dim, grid_shape, blocked, last),
        grid=(heads // 2,),
        in_specs=in_specs,
        out_specs=out_specs,
        out_shape=outs,
        scratch_shapes=scratch,
        compiler_params=params(identifier),
        cost_estimate=lasting(25),
        name="attention_forward",
    )(*ins)
    return tuple(got) if blocked else tuple(mats) + tuple(got)


def diagonal_fold(values, seq_len):
    rows, wide = seq_len, 2 * seq_len
    folded = None
    tile = 128
    count = seq_len // tile
    for row_tile in range(count):
        piece = values[row_tile * tile : (row_tile + 1) * tile].astype(f32)
        before = (count - 1 - row_tile) * tile
        after = wide - seq_len - before
        parts = []
        if before:
            parts.append(jnp.zeros((tile, before), f32))
        parts.append(piece)
        if after:
            parts.append(jnp.zeros((tile, after), f32))
        padded = jnp.concatenate(parts, axis=1)
        folded = padded if folded is None else folded + padded
    rows = tile
    while rows > 1:
        rows //= 2
        folded = pltpu.roll(folded[:rows], rows, 1) + folded[rows:]
    return folded


def reblock(grid_shape, blocks_ref, which, values):
    count_x, count_y = grid_shape
    tall = values.shape[0] // count_x
    wide = values.shape[1] // count_y
    for first in range(count_x):
        for second in range(count_y):
            spot = (first // 2, first % 2, second // 2, second % 2)
            lanes = slice(which * wide, (which + 1) * wide)
            blocks_ref[(*spot, slice(None), lanes)] = values[
                first * tall : (first + 1) * tall, second * wide : (second + 1) * wide
            ]


def d_logits_of(d_gate, logits, chosen):
    shares = jax.nn.softmax(logits, axis=-1)
    gate = jnp.sum(shares * chosen, axis=1, keepdims=True)
    return (d_gate * shares * (chosen - gate)).astype(bf16)


def spread_into(grad_now, comb_ref, slot_row_ref, chosen_ref, logits_ref, d_sent_ref, d_logits_ref):
    d_gate = jnp.sum(grad_now * comb_ref[...], axis=1, keepdims=True)
    logits, chosen = logits_ref[...], chosen_ref[...]
    d_logits_ref[...] = d_logits_of(d_gate, logits, chosen)
    gate = jnp.sum(jax.nn.softmax(logits, axis=-1) * chosen, axis=1, keepdims=True)
    placing = placing_rows(slot_row_ref[...], d_sent_ref.shape[0])
    d_sent_ref[...] = dot(placing, (gate * grad_now).astype(bf16)).astype(bf16)


def backward_kernel(
    head_dim,
    grid_shape,
    spreads,
    returns,
    pushes,
    unread,
    d_back_ref,
    slot_col_ref,
    d_logits_ref,
    grad_ref,
    middle_ref,
    gain_attn_ref,
    gain_ffn_ref,
    router_ref,
    att_ref,
    *refs,
):
    refs = list(refs)
    take = refs.pop
    spread_in = [take(0) for _ in range(4)] if spreads else []
    bias_ref, lse_ref = take(0), take(0)
    made_ref = take(0)
    push_refs = (take(0), take(0)) if pushes else ()
    later = [take(0) for _ in range(5)]
    del refs[:unread]
    grad_new_ref, blocks_ref, gwr_ref, gga_ref, ggf_ref, offsets_ref = (take(0) for _ in range(6))
    spread_out = [take(0) for _ in range(2)] if spreads else []
    returned_ref = take(0)
    landing_refs = (take(0), take(0)) if pushes else ()
    d_att_s, d_middle_s, dqt_s, dk_s, dv_s, probs_s, scores_s = (take(0) for _ in range(7))
    loaded = [take(0) for _ in range(5)]
    load_sems = take(0)
    mats_ref, q_ref, k_ref, v_ref, hidden_ref = loaded
    mats_later = later[0]
    load_output = local_copies([(mats_later.at[3], mats_ref.at[3])], load_sems)
    load_heads = local_copies(list(zip(later[1:4], loaded[1:4])), load_sems, 1)
    first_three = pl.ds(0, 3)
    load_rest = local_copies(
        [(mats_later.at[first_three], mats_ref.at[first_three]), (later[4], hidden_ref)], load_sems, 4
    )
    own_sem, *sems = refs[:3]
    members = grid_shape[1]
    place = Place(grid_shape)
    pushed = []
    for src, landing, last_rows in zip(push_refs, landing_refs, (True, False)):
        begin = src.shape[1] - landing.shape[1] if last_rows else 0
        pushed += push_blocks(place, src, landing, refs[3:], begin, len(pushed))
    back = Exchange(members, made_ref.shape[0] // members, made_ref, returned_ref, *sems)
    mine = back.block(back.me)
    own = None
    if returns:
        own = pltpu.make_async_copy(made_ref.at[mine, :], returned_ref.at[mine, :], own_sem)
    aparts = part_of(members, returns)

    @pl.when(pl.program_id(0) == 0)
    def _():
        start_all(load_output + load_heads + load_rest)
        greet([back.peer(apart) for apart in aparts] + (place.y_peers() if pushes else []))
        start_all(pushed + [back.copy(apart) for apart in aparts])
        if returns:
            own.start()

    pair, pairs = pl.program_id(0), pl.num_programs(0)
    seq_len = att_ref.shape[1]
    width = 2 * head_dim
    step = min(512, seq_len)
    scale = head_dim**-0.5

    @pl.when(pair == 0)
    def _():
        placing = placing_cols(slot_col_ref[...], d_back_ref.shape[0])
        d_logits = d_logits_ref[...]
        d_ffn = dot(placing, d_back_ref[...]) + dot(d_logits, router_ref[...])
        middle = middle_ref[...]
        gain_row = gain_ffn_ref[...]
        ffn_in = (middle * rms_factor(middle) * gain_row).astype(bf16)
        gwr_ref[...] = dot(d_logits, ffn_in, 0, 0)
        d_middle, d_gain = rms_pull(middle, gain_row, d_ffn)
        ggf_ref[...] = d_gain
        d_middle = d_middle + grad_ref[...].astype(f32)
        d_middle_s[...] = d_middle
        d_low = d_middle.astype(bf16)
        wait_all(load_output)
        reblock(grid_shape, blocks_ref, 3, dot(att_ref[...], d_low).astype(bf16))
        d_att_s[...] = dot(d_low, mats_ref[3], 1, 1).astype(bf16)
        wait_all(load_heads)

    lanes = pl.ds(pl.multiple_of(pair * width, width), width)
    q2 = q_ref[:, lanes] * jnp.asarray(scale, bf16)
    k2 = k_ref[:, lanes]
    v2 = v_ref[:, lanes]
    da2 = d_att_s[:, lanes]
    k2t = k2.T
    first = half_masks(seq_len, width)
    d_key = jnp.zeros((seq_len, width), f32)
    d_value = jnp.zeros((seq_len, width), f32)
    for half in range(2):
        mask = first if half == 0 else ~first
        q_one = jnp.where(mask, q2, jnp.zeros_like(q2))
        da_one = jnp.where(mask, da2, jnp.zeros_like(da2))
        k_one = k2t[half * head_dim : (half + 1) * head_dim]
        rows = pl.ds(pl.multiple_of(pair * width + half * head_dim, head_dim), head_dim)
        for start in range(0, seq_len, step):
            cols = slice(start, start + step)
            scores = dot(k2, q_one[cols], 1, 1) + bias_ref[half, :, cols].astype(f32)
            probs = jnp.exp(scores - lse_ref[0, half : half + 1, cols])
            d_probs = dot(v2, da_one[cols], 1, 1)
            inner = jnp.sum(probs * d_probs, axis=0, keepdims=True)
            d_scores = (probs * (d_probs - inner)).astype(bf16)
            probs_s[:, cols] = probs.astype(bf16)
            scores_s[:, cols] = d_scores
            dqt_s[rows, cols] = (dot(k_one, d_scores) * scale).astype(bf16)
        d_key = d_key + dot(scores_s[...], q_one)
        d_value = d_value + dot(probs_s[...], da_one)
        offsets_ref[pl.ds(2 * pair + half, 1), :] = diagonal_fold(scores_s[...], seq_len)
    dk_s[:, lanes] = d_key.astype(bf16)
    dv_s[:, lanes] = d_value.astype(bf16)

    @pl.when(pair == pairs - 1)
    def _():
        wait_all(load_rest)
        hidden = hidden_ref[...].astype(f32)
        gain_row = gain_attn_ref[...]
        normed_t = (hidden * rms_factor(hidden) * gain_row).astype(bf16).T
        d_query = dqt_s[...].T
        d_normed = dot(d_query, mats_ref[0], 1, 1)
        reblock(grid_shape, blocks_ref, 0, dot(normed_t, d_query).astype(bf16))
        d_normed = d_normed + dot(dk_s[...], mats_ref[1], 1, 1)
        reblock(grid_shape, blocks_ref, 1, dot(normed_t, dk_s[...]).astype(bf16))
        d_normed = d_normed + dot(dv_s[...], mats_ref[2], 1, 1)
        reblock(grid_shape, blocks_ref, 2, dot(normed_t, dv_s[...]).astype(bf16))
        d_hidden, d_gain = rms_pull(hidden, gain_row, d_normed)
        gga_ref[...] = d_gain
        grad_new = d_hidden + d_middle_s[...]
        grad_new_ref[...] = grad_new
        if spreads:
            spread_into(grad_new, *spread_in, *spread_out)

    @pl.when(pair == pairs - 1)
    def _():
        wait_all(pushed + [back.copy(apart) for apart in aparts])
        if returns:
            own.wait()


def attention_backward(
    d_back,
    slot_col,
    d_logits,
    grad_now,
    middle,
    hidden,
    gains,
    mats,
    q_k_v,
    attended,
    bias,
    lse,
    grid_shape,
    below=None,
    after=(),
    made=None,
    returns=False,
    push=None,
    identifier=None,
):
    seq_len, width = hidden.shape
    heads = bias.shape[0]
    head_dim = width // heads
    experts = mats[1].shape[0]
    count_x, count_y = grid_shape
    ins = (
        d_back,
        slot_col,
        d_logits,
        grad_now,
        middle,
        *gains,
        mats[1],
        attended,
    )
    later = [mats[0], *q_k_v, hidden]
    spreads = below is not None
    if spreads:
        ins = ins + tuple(below)
    row = jax.ShapeDtypeStruct((1, width), f32)
    outs = (
        jax.ShapeDtypeStruct((seq_len, width), f32),
        jax.ShapeDtypeStruct(
            (count_x // 2, 2, count_y // 2, 2, width // count_x, 4 * (width // count_y)), bf16
        ),
        jax.ShapeDtypeStruct((experts, width), f32),
        row,
        row,
        jax.ShapeDtypeStruct((heads, 2 * seq_len), f32),
    )
    if spreads:
        outs = outs + (
            jax.ShapeDtypeStruct((2 * seq_len, width), bf16),
            jax.ShapeDtypeStruct(d_logits.shape, bf16),
        )
    outs = outs + (jax.ShapeDtypeStruct(made.shape, bf16),)
    pushes = push is not None
    out_specs = whole_of(outs)
    out_specs[-1] = any_spec
    if pushes:
        rows = [push[0].shape[1] - cut_of(push[0]), push[1].shape[1] // 2]
        outs = outs + tuple(landing_of(one, many) for one, many in zip(push, rows))
        out_specs += [any_spec] * 2
    return pl.pallas_call(
        partial(backward_kernel, head_dim, grid_shape, spreads, returns, pushes, len(after)),
        grid=(heads // 2,),
        in_specs=whole_of(ins)
        + [
            pl.BlockSpec((2, seq_len, seq_len), lambda p: (p, 0, 0)),
            pl.BlockSpec((1, 2, seq_len), lambda p: (p, 0, 0)),
        ]
        + [any_spec] * (len(after) + 6 + 2 * pushes),
        out_specs=out_specs,
        out_shape=outs,
        scratch_shapes=[
            pltpu.VMEM((seq_len, width), bf16),
            pltpu.VMEM((seq_len, width), f32),
            pltpu.VMEM((width, seq_len), bf16),
            pltpu.VMEM((seq_len, width), bf16),
            pltpu.VMEM((seq_len, width), bf16),
            pltpu.VMEM((seq_len, seq_len), bf16),
            pltpu.VMEM((seq_len, seq_len), bf16),
        ]
        + scratch_of(later)
        + [pltpu.SemaphoreType.DMA((6,)), pltpu.SemaphoreType.DMA]
        + [pltpu.SemaphoreType.DMA((count_y,))] * 2
        + [pltpu.SemaphoreType.DMA((2 * (count_x // 2 - 1),))] * (2 * pushes),
        compiler_params=params(identifier),
        cost_estimate=lasting(32),
        name="attention_backward",
    )(*ins, bias, lse, made, *(push if pushes else ()), *later, *after)


class Exchange:
    def __init__(self, members, rows, src, dst, send_sems, recv_sems):
        self.me = lax.axis_index("gy")
        self.bits = members.bit_length() - 1
        self.rows, self.src, self.dst = rows, src, dst
        self.send_sems, self.recv_sems = send_sems, recv_sems

    def block(self, index):
        return pl.ds(pl.multiple_of(index * self.rows, self.rows), self.rows)

    def peer(self, apart):
        return {"gy": xor_of(self.me, apart, self.bits)}

    def copy(self, apart):
        peer = xor_of(self.me, apart, self.bits)
        return pltpu.make_async_remote_copy(
            src_ref=self.src.at[self.block(peer), :],
            dst_ref=self.dst.at[self.block(self.me), :],
            send_sem=self.send_sems.at[apart],
            recv_sem=self.recv_sems.at[apart],
            device_id={"gy": peer},
            device_id_type=MESH,
        )

    def keep_own(self):
        self.dst[self.block(self.me), :] = self.src[self.block(self.me), :]


class Leading(Exchange):
    def __init__(self, members, src, dst, send_sems, recv_sems):
        super().__init__(members, 1, src, dst, send_sems, recv_sems)

    def copy(self, apart):
        peer = xor_of(self.me, apart, self.bits)
        sems = (self.send_sems, self.recv_sems)
        return send(self.src.at[peer], self.dst.at[self.me], sems, apart, {"gy": peer})

    def keep_own(self):
        self.dst[self.me] = self.src[self.me]


def peers_along_gy(members):
    me = lax.axis_index("gy")
    bits = members.bit_length() - 1
    return [{"gy": xor_of(me, apart, bits)} for apart in range(1, members)]


def gelu_and_slope(pre):
    inner_scale = 0.7978845608028654
    square = pre * pre
    bent = jnp.tanh(inner_scale * pre * (1.0 + 0.044715 * square))
    act = 0.5 * pre * (1.0 + bent)
    slope = 0.5 * (1.0 + bent) + 0.5 * pre * (1.0 - bent * bent) * (
        inner_scale * (1.0 + 3 * 0.044715 * square)
    )
    return act, slope


def gelu_only(pre):
    inner_scale = 0.7978845608028654
    return 0.5 * pre * (1.0 + jnp.tanh(inner_scale * pre * (1.0 + 0.044715 * pre * pre)))


def send_order(members):
    return range(1, members)


def early(members):
    quarter = max(1, members // 4)
    return [apart for apart in range(members) if (apart // quarter) % 2 == 0]


def part_of(members, first):
    chosen = early(members)
    return [a for a in range(1, members) if (a in chosen) == first]


def third_of(members, apart):
    quarter = max(1, members // 4)
    if (apart // quarter) % 2 == 0:
        return 0
    return 1 + (2 * (apart % quarter)) // quarter


def in_third(members, third):
    return [apart for apart in range(1, members) if third_of(members, apart) == third]


def collect(me, members, rows, refs, which_of, dst, sems):
    copies = []
    for apart in range(members):
        start = xor_of(me, apart, bits_of(members)) * rows
        here = pl.ds(pl.multiple_of(start, rows), rows)
        ref = refs[which_of(apart)]
        copies.append(pltpu.make_async_copy(ref.at[here, :], dst.at[here, :], sems.at[apart]))
    return copies


class Weights:
    def __init__(self, place, halves, whole_refs, local_sems, sems):
        blocks, _, units = halves[0].shape
        self.local, self.remote = [], []
        for which, (part, into) in enumerate(zip(halves, whole_refs)):
            for block in range(blocks):
                index = which * blocks + block
                begin = pl.multiple_of((place.c * blocks + block) * units, units)
                dst = into.at[:, pl.ds(begin, units)]
                src = part.at[block]
                self.local.append(pltpu.make_async_copy(src, dst, local_sems.at[index]))
                self.remote.append(send(src, dst, sems, index, place.core_peer()))
        self.blocks = blocks

    def start_local(self):
        start_all(self.local)

    def start_remote(self):
        start_all(self.remote)

    def wait(self, which):
        mine = slice(which * self.blocks, (which + 1) * self.blocks)
        for copy in self.local[mine] + self.remote[mine]:
            copy.wait()


def weight_gradients(place, products, sends, landings, outs, sems, after):
    blocks, _, units = outs[0].shape

    def product(lhs, rhs_ref, which, into_ref):
        @pl.loop(0, blocks)
        def _(block):
            begin = pl.multiple_of((which * blocks + block) * units, units)
            into_ref[block] = dot(lhs, rhs_ref[:, pl.ds(begin, units)]).astype(bf16)

    for index, (lhs_ref, rhs_ref) in enumerate(products):
        lhs = lhs_ref[...].T
        product(lhs, rhs_ref, 1 - place.c, sends[index])
        copy = send(sends[index], landings[index], sems, index, place.core_peer())
        copy.start()
        product(lhs, rhs_ref, place.c, outs[index])
        copy.wait()

        @pl.loop(0, blocks)
        def _(block, index=index):
            add_low(outs[index], (block,), outs[index][block], landings[index][block])

        start_all(after[index])


def push_blocks(place, src, landing, sems, begin, base=0):
    rows = pl.ds(begin, landing.shape[1])
    return [
        send(
            src.at[place.y_at(apart), rows],
            landing.at[apart - 1],
            sems,
            base + apart - 1,
            place.y_peer(apart),
        )
        for apart in range(1, place.count_y)
    ]


def cut_of(blocks):
    return blocks.shape[1] // 3 * 2


def landing_of(blocks, rows):
    return jax.ShapeDtypeStruct((blocks.shape[0] - 1, rows, blocks.shape[2]), bf16)


def chunk_of(members, rows):
    return max(1, min(members, 256 // rows))


def expert_forward_kernel(
    grid_shape,
    gathers,
    sent_ref,
    slot_col_ref,
    chosen_ref,
    logits_ref,
    middle_in_ref,
    win_ref,
    wout_ref,
    *refs,
):
    refs = list(refs)
    take = refs.pop
    column_ref = take(0) if gathers else None
    arrived_out_ref, comb_ref, out_ref = (take(0) for _ in range(3))
    full_ref = take(0) if gathers else None
    arrived_ref, middle_ref, move_sems = (take(0) for _ in range(3))
    load_middle, write_arrived = local_copies(
        [(middle_in_ref, middle_ref), (arrived_ref, arrived_out_ref)], move_sems
    )
    win_s, wout_s, made_s, returned_s, w_sems = (take(0) for _ in range(5))
    send_sems, recv_sems, back_send_sems, back_recv_sems = (take(0) for _ in range(4))
    weight_sems = (take(0), take(0))
    members = grid_shape[1]
    slots = sent_ref.shape[0]
    rows = slots // members
    group = chunk_of(members, rows)
    chunks = members // group
    chunk_bits = chunks.bit_length() - 1
    hidden_units = win_s.shape[1]
    tile = min(768, hidden_units)
    place = Place(grid_shape)
    weights = Weights(place, (win_ref, wout_ref), (win_s, wout_s), w_sems, weight_sems)
    weights.start_local()
    load_middle.start()
    more_peers = place.y_peers() if gathers else []
    greet(peers_along_gy(members) + [place.core_peer()] + more_peers)
    weights.start_remote()
    there = Exchange(members, rows, sent_ref, arrived_ref, send_sems, recv_sems)
    back = Exchange(members, rows, made_s, returned_s, back_send_sems, back_recv_sems)
    for apart in send_order(members):
        there.copy(apart).start()
    there.keep_own()
    if gathers:
        own_sem, *sems = refs
        split = (full_ref.shape[4] - tile_rows) // 2
        own = pltpu.make_async_copy(
            column_ref, full_ref.at[place.y, place.c, :, place.x], own_sem
        )
        own.start()
        second = gather_second(place, column_ref, full_ref, split, sems)
        third = gather_third(place, full_ref, split, sems)
        fourth = gather_core(place, full_ref, sems)
        start_all(second)
    weights.wait(0)
    weights.wait(1)
    my_chunk = there.me // group

    def chunk_rows(index):
        start = xor_of(my_chunk, index, chunk_bits) * (group * rows)
        return pl.ds(pl.multiple_of(start, group * rows), group * rows)

    def work(index, first):
        for member in range(first, group):
            there.copy(index * group + member).wait_recv()
        here = chunk_rows(index)
        taken = arrived_ref[here, :]
        total = jnp.zeros((group * rows, taken.shape[1]), f32)
        for start in range(0, hidden_units, tile):
            units = slice(start, start + tile)
            act = gelu_only(dot(taken, win_s[:, units])).astype(bf16)
            total = total + dot(act, wout_s[:, units], 1, 1)
        made_s[here, :] = total.astype(bf16)
        for member in range(first, group):
            back.copy(index * group + member).start()

    work(0, 1)
    back.keep_own()
    half = chunks // 2

    @pl.loop(1, half)
    def _(index):
        work(index, 0)

    if gathers:
        own.wait()
        wait_all(second)
        start_all(third)

    @pl.loop(half, chunks)
    def _(index):
        work(index, 0)

    if gathers:
        wait_all(third)
        start_all(fourth)
    write_arrived.start()
    slot_col = slot_col_ref[...]
    comb_ref[...] = jnp.zeros_like(comb_ref)

    def gather_back(index, first):
        for member in range(first, group):
            back.copy(index * group + member).wait_recv()
        begin = xor_of(my_chunk, index, chunk_bits) * (group * rows)
        places = lax.broadcasted_iota(jnp.int32, (slot_col.shape[0], group * rows), 1) + begin
        placing = (places == slot_col).astype(f32).astype(bf16)
        comb_ref[...] += dot(placing, returned_s[chunk_rows(index), :])

    gather_back(0, 1)

    @pl.loop(1, chunks)
    def _(index):
        gather_back(index, 0)

    load_middle.wait()
    gate = jnp.sum(jax.nn.softmax(logits_ref[...], axis=-1) * chosen_ref[...], axis=1, keepdims=True)
    out_ref[...] = middle_ref[...] + gate * comb_ref[...]
    if gathers:
        wait_all(fourth)

    @pl.loop(1, members)
    def _(apart):
        there.copy(apart).wait_send()
        back.copy(apart).wait_send()

    write_arrived.wait()


def doubled(half):
    return pltpu.VMEM((half.shape[1], 2 * half.shape[0] * half.shape[2]), bf16)


def expert_forward(
    sent, slot_col, chosen_f, logits, middle, full_in, full_out, grid_shape, identifier, column=None
):
    members = grid_shape[1]
    gathers = column is not None
    ins = [sent, slot_col, chosen_f, logits, middle, full_in, full_out]
    in_specs = [vmem_spec] * 4 + [any_spec] * 3
    outs = [
        jax.ShapeDtypeStruct(sent.shape, bf16),
        jax.ShapeDtypeStruct(middle.shape, f32),
        jax.ShapeDtypeStruct(middle.shape, f32),
    ]
    out_specs = [any_spec] + [vmem_spec] * 2
    sems = pltpu.SemaphoreType.DMA((members,))
    scratch = [
        *scratch_of([sent, middle]),
        pltpu.SemaphoreType.DMA((2,)),
        doubled(full_in),
        doubled(full_out),
        pltpu.VMEM(sent.shape, bf16),
        pltpu.VMEM(sent.shape, bf16),
        pltpu.SemaphoreType.DMA((2 * full_in.shape[0],)),
        sems,
        sems,
        sems,
        sems,
        pltpu.SemaphoreType.DMA((2 * full_in.shape[0],)),
        pltpu.SemaphoreType.DMA((2 * full_in.shape[0],)),
    ]
    if gathers:
        ins.append(column)
        in_specs.append(any_spec)
        half = (grid_shape[0] // 2, 2, grid_shape[1] // 2, 2)
        outs.append(jax.ShapeDtypeStruct((*half, *column.shape[1:]), bf16))
        out_specs.append(any_spec)
        others = pltpu.SemaphoreType.DMA((gather_copies(grid_shape)[1],))
        scratch += [pltpu.SemaphoreType.DMA, others, others]
    return pl.pallas_call(
        partial(expert_forward_kernel, grid_shape, gathers),
        in_specs=in_specs,
        out_specs=out_specs,
        out_shape=outs,
        scratch_shapes=scratch,
        compiler_params=params(identifier),
        cost_estimate=lasting(75),
        name="expert_forward",
    )(*ins)


def expert_both_kernel(
    grid_shape,
    sent_ref,
    gates_ref,
    slot_col_ref,
    chosen_ref,
    logits_ref,
    far_first_ref,
    far_second_ref,
    far_third_ref,
    win_ref,
    wout_ref,
    made_out_ref,
    d_back_ref,
    gin_out_ref,
    gout_out_ref,
    d_logits_ref,
    arrived_s,
    gates_s,
    win_s,
    wout_s,
    d_made_s,
    d_rows_s,
    act_s,
    d_pre_s,
    d_gates_s,
    d_gates_back_s,
    grads_ref,
    gin_send,
    gin_land,
    gout_send,
    gout_land,
    made_ref,
    gin_ref,
    gout_ref,
    write_sems,
    w_sems,
    *sems,
):
    far_refs = (far_first_ref, far_second_ref, far_third_ref)
    members = grid_shape[1]
    weight_sems, sum_sems = sems[9:11], sems[11:13]
    slots = sent_ref.shape[0]
    rows = slots // members
    group = chunk_of(members, rows)
    chunks = members // group
    chunk_bits = bits_of(chunks)
    hidden_units = win_s.shape[1]
    tile = min(768, hidden_units)
    place = Place(grid_shape)
    weights = Weights(place, (win_ref, wout_ref), (win_s, wout_s), w_sems, weight_sems)
    weights.start_local()
    greet(peers_along_gy(members) + [place.core_peer()])
    weights.start_remote()
    there = Exchange(members, rows, sent_ref, arrived_s, *sems[0:2])
    back = Exchange(members, rows, d_rows_s, d_back_ref, *sems[2:4])
    gates_there = Leading(members, gates_ref, gates_s, *sems[4:6])
    gates_back = Leading(members, d_gates_s, d_gates_back_s, *sems[6:8])

    for apart in send_order(members):
        gates_there.copy(apart).start()
        there.copy(apart).start()

    collected = collect(
        there.me, members, rows, far_refs, partial(third_of, members), grads_ref, sems[8]
    )
    start_all(collected)
    there.keep_own()
    gates_there.keep_own()
    weights.wait(0)
    weights.wait(1)
    wait_all(collected)
    my_chunk = there.me // group

    def work(index, first):
        for member in range(first, group):
            gates_there.copy(index * group + member).wait_recv()
            there.copy(index * group + member).wait_recv()
        chunk = xor_of(my_chunk, index, chunk_bits)
        here = pl.ds(pl.multiple_of(chunk * (group * rows), group * rows), group * rows)
        gate = jnp.concatenate(
            [gates_s[chunk * group + member].T[:rows, 0:1] for member in range(group)], axis=0
        )
        taken = arrived_s[here, :]
        grads = grads_ref[here, :].astype(f32)
        d_made = (gate * grads).astype(bf16)
        d_made_s[here, :] = d_made
        made = jnp.zeros((group * rows, taken.shape[1]), f32)
        d_rows = made
        for start in range(0, hidden_units, tile):
            units = slice(start, start + tile)
            act, slope = gelu_and_slope(dot(taken, win_s[:, units]))
            act = act.astype(bf16)
            act_s[here, units] = act
            d_pre = (dot(d_made, wout_s[:, units]) * slope).astype(bf16)
            d_pre_s[here, units] = d_pre
            d_rows = d_rows + dot(d_pre, win_s[:, units], 1, 1)
            made = made + dot(act, wout_s[:, units], 1, 1)
        d_rows_s[here, :] = d_rows.astype(bf16)
        made = made.astype(bf16)
        made_ref[here, :] = made
        d_gate = jnp.sum(grads * made.astype(f32), axis=1, keepdims=True)
        for member in range(group):
            part = jnp.broadcast_to(d_gate[member * rows : (member + 1) * rows], (rows, 128)).T
            d_gates_s[chunk * group + member, :, :rows] = part[: d_gates_s.shape[1]]
        for member in range(first, group):
            gates_back.copy(index * group + member).start()
            back.copy(index * group + member).start()

    work(0, 1)
    back.keep_own()
    gates_back.keep_own()

    @pl.loop(1, chunks)
    def _(index):
        work(index, 0)

    write_made, write_out, write_in = local_copies(
        [(made_ref, made_out_ref), (gout_ref, gout_out_ref), (gin_ref, gin_out_ref)], write_sems
    )
    write_made.start()
    weight_gradients(
        place,
        ((d_made_s, act_s), (arrived_s, d_pre_s)),
        (gout_send, gin_send),
        (gout_land, gin_land),
        (gout_ref, gin_ref),
        sum_sems,
        ([write_out], [write_in]),
    )

    @pl.loop(1, members)
    def _(apart):
        gates_back.copy(apart).wait_recv()

    row = jnp.concatenate(
        [d_gates_back_s[expert, 0:1, :rows] for expert in range(members)], axis=1
    )
    slot_col = slot_col_ref[...]
    places = lax.broadcasted_iota(jnp.int32, (slot_col.shape[0], slots), 1)
    d_gate = jnp.sum(jnp.where(places == slot_col, row, 0.0), axis=1, keepdims=True)
    d_logits_ref[...] = d_logits_of(d_gate, logits_ref[...], chosen_ref[...])

    @pl.loop(1, members)
    def _(apart):
        back.copy(apart).wait_recv()
        there.copy(apart).wait_send()
        back.copy(apart).wait_send()
        gates_there.copy(apart).wait_send()
        gates_back.copy(apart).wait_send()

    wait_all([write_made, write_out, write_in])


def expert_both(sent, gates, far_parts, slot_col, chosen_f, logits, full_in, full_out, grid_shape, identifier):
    members = grid_shape[1]
    slots = sent.shape[0]
    outs = (
        jax.ShapeDtypeStruct(sent.shape, bf16),
        jax.ShapeDtypeStruct(sent.shape, bf16),
        jax.ShapeDtypeStruct(full_in.shape, bf16),
        jax.ShapeDtypeStruct(full_out.shape, bf16),
        jax.ShapeDtypeStruct(logits.shape, bf16),
    )
    tall = pltpu.VMEM(sent.shape, bf16)
    wide = pltpu.VMEM((slots, 2 * full_in.shape[0] * full_in.shape[2]), bf16)
    half = pltpu.VMEM(full_in.shape, bf16)
    small = pltpu.VMEM(gates.shape, f32)
    weights = doubled(full_in)
    return pl.pallas_call(
        partial(expert_both_kernel, grid_shape),
        in_specs=[vmem_spec] * 5 + [any_spec] * 5,
        out_specs=[any_spec, vmem_spec, any_spec, any_spec, vmem_spec],
        out_shape=outs,
        scratch_shapes=[
            tall,
            small,
            weights,
            weights,
            tall,
            tall,
            wide,
            wide,
            small,
            small,
            tall,
            half,
            half,
            half,
            half,
            tall,
            half,
            half,
            pltpu.SemaphoreType.DMA((3,)),
            pltpu.SemaphoreType.DMA((2 * full_in.shape[0],)),
        ]
        + [pltpu.SemaphoreType.DMA((members,))] * 9
        + [pltpu.SemaphoreType.DMA((2 * full_in.shape[0],))] * 4,
        compiler_params=params(identifier),
        cost_estimate=lasting(85),
        name="expert_both",
    )(sent, gates, slot_col, chosen_f, logits, *far_parts, full_in, full_out)


def expert_backward_kernel(
    grid_shape,
    d_sent_ref,
    arrived_in_ref,
    blocks_in_ref,
    win_ref,
    wout_ref,
    d_back_ref,
    gin_out_ref,
    gout_out_ref,
    upper_ref,
    lower_ref,
    landing_ref,
    win_s,
    wout_s,
    d_arrived_s,
    d_rows_s,
    act_s,
    slope_s,
    first_s,
    up2_s,
    low2_s,
    gin_send,
    gin_land,
    gout_send,
    gout_land,
    arrived_ref,
    blocks_ref,
    gin_ref,
    gout_ref,
    move_sems,
    w_sems,
    send_sems,
    recv_sems,
    back_send_sems,
    back_recv_sems,
    *more_sems,
):
    members = grid_shape[1]
    sum_sems, weight_sems, gradient_sems = more_sems[0:2], more_sems[2:4], more_sems[4:6]
    push_sems = more_sems[6:8]
    slots = d_sent_ref.shape[0]
    rows = slots // members
    group = chunk_of(members, rows)
    chunks = members // group
    chunk_bits = chunks.bit_length() - 1
    hidden_units = win_s.shape[1]
    tile = min(768, hidden_units)
    place = Place(grid_shape)
    weights = Weights(place, (win_ref, wout_ref), (win_s, wout_s), w_sems, weight_sems)
    weights.start_local()
    moves = local_copies(
        [
            (arrived_in_ref, arrived_ref),
            (blocks_in_ref.at[:, place.c], blocks_ref.at[:, place.c]),
            (gout_ref, gout_out_ref),
            (gin_ref, gin_out_ref),
        ],
        move_sems,
    )
    start_all(moves[:2])
    greet(peers_along_gy(members) + [place.core_peer()] + place.y_peers())
    weights.start_remote()
    landings = (first_s, up2_s, low2_s, upper_ref, lower_ref, None, None)
    sums = Scatter(place, blocks_ref, landings, sum_sems, upper_ref.shape[1], blocks_in_ref)
    there = Exchange(members, rows, d_sent_ref, d_arrived_s, send_sems, recv_sems)
    back = Exchange(members, rows, d_rows_s, d_back_ref, back_send_sems, back_recv_sems)
    for apart in send_order(members):
        there.copy(apart).start()
    there.keep_own()
    my_chunk = there.me // group
    start_all(sums.copies(0))
    wait_all(moves[:2])
    weights.wait(0)

    @pl.loop(0, slots // 256)
    def _(index):
        here = pl.ds(pl.multiple_of(index * 256, 256), 256)
        taken = arrived_ref[here, :]
        for start in range(0, hidden_units, tile):
            units = slice(start, start + tile)
            act, slope = gelu_and_slope(dot(taken, win_s[:, units]))
            act_s[here, units] = act.astype(bf16)
            slope_s[here, units] = slope.astype(bf16)

    wait_all(sums.copies(0))
    sums.add(0)
    start_all(sums.copies(1))
    weights.wait(1)

    def chunk_rows(index):
        start = xor_of(my_chunk, index, chunk_bits) * (group * rows)
        return pl.ds(pl.multiple_of(start, group * rows), group * rows)

    def work(index, first):
        for member in range(first, group):
            there.copy(index * group + member).wait_recv()
        here = chunk_rows(index)
        taken = d_arrived_s[here, :]
        total = jnp.zeros((group * rows, taken.shape[1]), f32)
        for start in range(0, hidden_units, tile):
            units = slice(start, start + tile)
            d_pre = (dot(taken, wout_s[:, units]) * slope_s[here, units].astype(f32)).astype(bf16)
            slope_s[here, units] = d_pre
            total = total + dot(d_pre, win_s[:, units], 1, 1)
        d_rows_s[here, :] = total.astype(bf16)
        for member in range(first, group):
            back.copy(index * group + member).start()

    work(0, 1)
    back.keep_own()

    @pl.loop(1, chunks)
    def _(index):
        work(index, 0)

    wait_all(sums.copies(1))
    sums.add(1)
    start_all(sums.copies(2))
    pushed = push_blocks(place, gout_ref, landing_ref, push_sems, 0)
    weight_gradients(
        place,
        ((d_arrived_s, act_s), (arrived_ref, slope_s)),
        (gout_send, gin_send),
        (gout_land, gin_land),
        (gout_ref, gin_ref),
        gradient_sems,
        ([*pushed, moves[2]], [moves[3]]),
    )
    wait_all(sums.copies(2))
    sums.add(2)

    @pl.loop(1, members)
    def _(apart):
        back.copy(apart).wait_recv()
        there.copy(apart).wait_send()
        back.copy(apart).wait_send()

    wait_all(pushed + moves[2:])


def expert_backward(d_sent, arrived, blocks, full_in, full_out, grid_shape, identifier):
    members = grid_shape[1]
    landings = whole_blocks(blocks.shape, blocks.shape[4] // 2)
    outs = (
        jax.ShapeDtypeStruct(d_sent.shape, bf16),
        jax.ShapeDtypeStruct(full_in.shape, bf16),
        jax.ShapeDtypeStruct(full_out.shape, bf16),
        *[jax.ShapeDtypeStruct(one, bf16) for one in landings[3:5]],
        landing_of(full_out, cut_of(full_out)),
    )
    slots = d_sent.shape[0]
    sems = pltpu.SemaphoreType.DMA((members,))
    return pl.pallas_call(
        partial(expert_backward_kernel, grid_shape),
        in_specs=[vmem_spec] + [any_spec] * 4,
        out_specs=[vmem_spec] + [any_spec] * 2 + [vmem_spec] * 2 + [any_spec],
        out_shape=outs,
        scratch_shapes=[
            doubled(full_in),
            doubled(full_out),
            pltpu.VMEM(d_sent.shape, bf16),
            pltpu.VMEM(d_sent.shape, bf16),
            pltpu.VMEM((slots, 2 * full_in.shape[0] * full_in.shape[2]), bf16),
            pltpu.VMEM((slots, 2 * full_in.shape[0] * full_in.shape[2]), bf16),
            *[pltpu.VMEM(one, bf16) for one in landings[:3]],
            *[pltpu.VMEM(full_in.shape, bf16)] * 4,
            *scratch_of([arrived, blocks, full_in, full_out]),
            pltpu.SemaphoreType.DMA((4,)),
            pltpu.SemaphoreType.DMA((2 * full_in.shape[0],)),
            sems,
            sems,
            sems,
            sems,
            *[pltpu.SemaphoreType.DMA((scatter_copies(grid_shape),))] * 2,
            *[pltpu.SemaphoreType.DMA((2 * full_in.shape[0],))] * 4,
            *[pltpu.SemaphoreType.DMA((full_in.shape[0] - 1,))] * 2,
        ],
        compiler_params=params(10 + identifier),
        cost_estimate=lasting(85),
        name="expert_backward",
    )(d_sent, arrived, blocks, full_in, full_out)


def emit_kernel(
    table_shape,
    at_ref,
    gin_ref,
    gin_first_ref,
    gin_second_ref,
    gin_up_ref,
    gout_ref,
    gout_first_ref,
    gout_second_ref,
    gout_up_ref,
    result_ref,
    grad_ref,
    packed_ref,
    small_ref,
    gin_out_ref,
    gout_out_ref,
    result_out_ref,
    grad_out_ref,
    wq_ref,
    wk_ref,
    wv_ref,
    wo_ref,
    router_out_ref,
    gga_ref,
    ggf_ref,
    table_ref,
):
    step = pl.program_id(0)

    def landed(ref):
        total = ref[0].astype(f32)
        for index in range(1, ref.shape[0]):
            total = total + ref[index].astype(f32)
        return total

    steps = pl.num_programs(0)
    for own, first, second, up, out, early_steps in (
        (gin_ref, gin_first_ref, gin_second_ref, gin_up_ref, gin_out_ref, steps // 2),
        (gout_ref, gout_first_ref, gout_second_ref, gout_up_ref, gout_out_ref, steps // 3 * 2),
    ):
        out[0, 0] = own[0].astype(f32) + jnp.where(step < early_steps, landed(first), landed(second))
        out[1, 0] = up[...].astype(f32)

    @pl.when(step < 4)
    def _():
        result_out_ref[...] = result_ref[...]
        grad_out_ref[...] = grad_ref[...]

    @pl.when(step == 0)
    def _():
        layers, tall, wide = wq_ref.shape
        for which, ref in enumerate((wq_ref, wk_ref, wv_ref, wo_ref)):
            ref[...] = packed_ref[:, :, which * wide : (which + 1) * wide]
        buckets_count, heads = table_shape
        width = small_ref.shape[1]
        experts = (small_ref.shape[0] - 2 * layers - heads) // layers
        base = layers * experts
        gga_ref[...] = small_ref[base : base + layers, :]
        ggf_ref[...] = small_ref[base + layers : base + 2 * layers, :]
        base = base + 2 * layers
        table_ref[...] = small_ref[base : base + heads, :buckets_count]
        for layer in range(layers):
            row = small_ref[pl.ds(layer * experts + at_ref[1], 1), :]
            row = jnp.broadcast_to(row, (8, width))
            mine = pltpu.roll(row, lax.rem(width - at_ref[0] * tall, width), 1)
            router_out_ref[layer] = mine[0:1, :tall]


def emit(at, grads_in, grads_out, result, grad_now, packed, small, table_shape):
    layers, tall, lanes = packed.shape
    gin, gin_first, gin_second, gin_up = grads_in
    gout, gout_first, gout_second, gout_up = grads_out
    _, rows, units = gin.shape
    steps = 6
    tile = rows // steps
    wide = lanes // 4
    whole_in = [packed, small]
    passed = pl.BlockSpec((result.shape[0] // 4, result.shape[1]), lambda i, at: (jnp.minimum(i, 3), 0))
    own = pl.BlockSpec((1, tile, units), lambda i, at: (at[2], i, 0))
    up = pl.BlockSpec((tile, units), lambda i, at: (i, 0))

    def land(array, index):
        return pl.BlockSpec((array.shape[0], tile, units), lambda i, at: (0, index(i), 0))

    out = pl.BlockSpec((layers, 1, tile, units), lambda i, at: (0, 0, i, 0))
    expert = jax.ShapeDtypeStruct((layers, 1, rows, units), f32)
    square = jax.ShapeDtypeStruct((layers, tall, wide), f32)
    gain = jax.ShapeDtypeStruct((layers, small.shape[1]), f32)
    rest = [square] * 4
    rest += [jax.ShapeDtypeStruct((layers, 1, tall), f32), gain, gain]
    rest.append(jax.ShapeDtypeStruct(table_shape[::-1], f32))

    def expert_specs(first_land, second_land):
        early_steps = first_land.shape[1] // tile
        return [
            own,
            land(first_land, lambda i: jnp.minimum(i, early_steps - 1)),
            land(second_land, lambda i: jnp.maximum(i - early_steps, 0)),
            up,
        ]

    return pl.pallas_call(
        partial(emit_kernel, table_shape),
        grid_spec=pltpu.PrefetchScalarGridSpec(
            num_scalar_prefetch=1,
            grid=(steps,),
            in_specs=expert_specs(gin_first, gin_second)
            + expert_specs(gout_first, gout_second)
            + [passed, passed]
            + whole_of(whole_in),
            out_specs=[out, out, passed, passed] + whole_of(rest),
        ),
        out_shape=[expert, expert] + [jax.ShapeDtypeStruct(result.shape, f32)] * 2 + rest,
        compiler_params=params(),
        cost_estimate=lasting(7),
        name="emit",
    )(at, *grads_in, *grads_out, result, grad_now, *whole_in)


def body(
    hidden_in,
    route,
    piece_ids,
    buckets,
    rel_table,
    gain_attn,
    gain_ffn,
    w_query,
    w_key,
    w_value,
    w_output,
    w_router,
    w_in,
    w_out,
    cotangent,
):
    count_x = lax.axis_size("gx")
    count_y = lax.axis_size("gy")
    seq_len, width = hidden_in.shape
    layers = w_query.shape[0]
    heads = rel_table.shape[1]
    experts = w_router.shape[2] * count_y
    capacity = 2 * seq_len // experts
    wide_router = w_router.shape[2]
    tall, wide = w_query.shape[1], w_query.shape[2]
    grid_shape = (count_x, count_y)
    same_core = [list(range(core, count_x, 2)) for core in range(2)]
    router_rows = jnp.pad(
        w_router.transpose(0, 2, 1), ((0, 0), (0, tile_rows - wide_router), (0, 4 * wide - tall))
    )
    buckets_row = jnp.pad(buckets, (0, 1), constant_values=-1)[None, :]
    mats, router, later, bias, slot_col, slot_row, chosen_f, spread, far_part = start(
        (w_query, w_key, w_value, w_output),
        router_rows,
        buckets_row,
        rel_table.T,
        piece_ids,
        route,
        cotangent,
        grid_shape,
    )
    gain_attn_f = gain_attn.astype(f32)
    gain_ffn_f = gain_ffn.astype(f32)

    hidden = hidden_in
    kept = []
    blocks = None
    far_parts = [far_part]
    for layer in range(layers):
        last = layer == layers - 1
        gains = (gain_attn_f[layer][None], gain_ffn_f[layer][None])
        mats, router, q, k, v, attended, lse, middle, logits, sent, *gates, far_part = attention_forward(
            hidden,
            gains[0],
            gains[1],
            (slot_row, slot_col, chosen_f),
            bias,
            grid_shape,
            1 + layer,
            spread,
            last,
            blocks=blocks,
            mats=(mats, router) if blocks is None else None,
        )
        far_parts.append(far_part)
        full_in, full_out = (
            lax.all_gather(one[layer, 0], "gx", axis=0, tiled=False, axis_index_groups=same_core)
            for one in (w_in, w_out)
        )
        state = (hidden, gains, (mats, router), (q, k, v), attended, lse, middle, logits)
        if last:
            made, d_back, grad_in_full, grad_out_full, d_logits = expert_both(
                sent, gates[0], far_parts, slot_col, chosen_f, logits, full_in, full_out, grid_shape, 7
            )
            kept.append(state)
        else:
            arrived, combined, hidden, blocks = expert_forward(
                sent,
                slot_col,
                chosen_f,
                logits,
                middle,
                full_in,
                full_out,
                grid_shape,
                5 + layer,
                column=later[layer],
            )
            kept.append(state + (combined, arrived, full_in, full_out))

    grad_now = cotangent
    parts = []
    partials = []
    returned = []
    for layer in reversed(range(layers)):
        last = layer == layers - 1
        (prior, gains, mats, q_k_v, attended, lse, middle, logits) = kept[layer][:8]
        if not last:
            arrived, full_in, full_out = kept[layer][9:]
            d_back, grad_in_full, grad_out_full, upper, lower, out_first = expert_backward(
                d_sent, arrived, parts[-1][0], full_in, full_out, grid_shape, layer
            )
            partials.append((upper, lower[:1]))
        experts_parts = []
        if layer > 0:
            experts_parts = [
                lax.psum_scatter(
                    one, "gx", scatter_dimension=0, tiled=False, axis_index_groups=same_core
                )
                for one in (grad_in_full, grad_out_full)
            ]
        below = None
        if layer > 0:
            below = (kept[layer - 1][8], slot_row, chosen_f, kept[layer - 1][7])
        got = attention_backward(
            d_back,
            slot_col,
            d_logits,
            grad_now,
            middle,
            prior,
            gains,
            mats,
            q_k_v,
            attended,
            bias,
            lse,
            grid_shape,
            below=below,
            after=[array for part in parts for array in part[4]],
            made=made,
            returns=last,
            push=(grad_out_full, grad_in_full) if layer == 0 else None,
            identifier=18 + layer,
        )
        grad_now, blocked, gwr, gga, ggf, offset_sums = got[:6]
        if layer > 0:
            d_sent, d_logits = got[6:8]
        if layer == 0:
            *got, out_second, in_first = got
        returned.append(got[-1])
        parts.append((blocked, gwr, gga, ggf, experts_parts, offset_sums))
    parts = parts[::-1]
    buckets_count = rel_table.shape[0]
    smalls = [part[which] for which in (1, 2, 3, 5) for part in parts]
    top = kept[-1]
    packed, small, hidden_out, in_second = final_sums(
        parts[0][0],
        partials[::-1],
        smalls + [buckets_row],
        (slot_col, chosen_f, top[7], top[6]),
        returned,
        grad_in_full,
        grid_shape,
        buckets_count,
    )
    first, second = lax.axis_index("gx"), lax.axis_index("gy")
    grad_in, grad_out, hidden_out, grad_now, gwq, gwk, gwv, gwo, gwr, gga_all, ggf_all, d_table = emit(
        jnp.stack([first, second, first // 2]).astype(jnp.int32),
        (grad_in_full, in_first, in_second, parts[1][4][0]),
        (grad_out_full, out_first, out_second, parts[1][4][1]),
        hidden_out,
        grad_now,
        packed,
        small,
        rel_table.shape,
    )
    return (
        hidden_out,
        grad_now,
        d_table.T,
        gga_all,
        ggf_all,
        gwq,
        gwk,
        gwv,
        gwo,
        gwr.transpose(0, 2, 1),
        grad_in,
        grad_out,
    )


def solution(mesh):
    rows = P(("gx", "gy"), None)
    square = P(None, "gx", "gy")
    expert = P(None, "gy", None, "gx")
    return jax.shard_map(
        body,
        mesh=mesh,
        in_specs=(rows, rows, P(("gx", "gy")), P(), P(), P(), P())
        + (square,) * 5
        + (expert, expert, rows),
        out_specs=(rows, rows, P(), P(), P()) + (square,) * 5 + (expert, expert),
        check_vma=False,
    )
```

```python
from functools import partial

import jax
import jax.numpy as jnp
from jax import lax
from jax.experimental import pallas as pl
from jax.experimental.pallas import tpu as pltpu
from jax.sharding import PartitionSpec as P

eps_norm = 1e-06
highest = lax.Precision.HIGHEST
f32 = jnp.float32
bf16 = jnp.bfloat16
masked_out = -1e30
tile_rows = 16
MESH = pl.DeviceIdType.MESH
vmem_spec = pl.BlockSpec(memory_space=pltpu.VMEM)
any_spec = pl.BlockSpec(memory_space=pl.ANY)
vmem_bytes = 60 * 1024 * 1024


def whole(shape):
    zeros = (0,) * len(shape)
    return pl.BlockSpec(shape, lambda *_: zeros, pipeline_mode=pl.Buffered(1))


def whole_of(arrays):
    return [whole(array.shape) for array in arrays]


def params(identifier=None):
    if identifier is None:
        return pltpu.CompilerParams(vmem_limit_bytes=vmem_bytes)
    return pltpu.CompilerParams(
        vmem_limit_bytes=vmem_bytes, collective_id=identifier, has_side_effects=True
    )


def lasting(microseconds):
    return pl.CostEstimate(
        flops=int(microseconds * 1e9), bytes_accessed=1 << 20, transcendentals=0
    )


def dot(lhs, rhs, lhs_dim=1, rhs_dim=0):
    return lax.dot_general(
        lhs, rhs, (((lhs_dim,), (rhs_dim,)), ((), ())), preferred_element_type=f32
    )


def rms_factor(hidden):
    return lax.rsqrt(jnp.mean(hidden * hidden, axis=-1, keepdims=True) + eps_norm)


def rms_pull(hidden, gain_row, d_normed):
    factor = rms_factor(hidden)
    scaled = gain_row * d_normed
    inner = jnp.mean(hidden * scaled, axis=-1, keepdims=True)
    d_hidden = factor * scaled - hidden * (factor * factor * factor * inner)
    d_gain = jnp.sum(d_normed * hidden * factor, axis=0, keepdims=True)
    return d_hidden, d_gain


def xor_of(index, other, bits):
    total = 0
    for bit in range(bits):
        power = 1 << bit
        total = total + ((index // power + other // power) % 2) * power
    return total


def placing_rows(slot_row, slots):
    places = lax.broadcasted_iota(jnp.int32, (slots, slot_row.shape[1]), 0)
    return (places == slot_row).astype(f32).astype(bf16)


def placing_cols(slot_col, slots):
    places = lax.broadcasted_iota(jnp.int32, (slot_col.shape[0], slots), 1)
    return (places == slot_col).astype(f32).astype(bf16)


def greet(peers):
    barrier = pltpu.get_barrier_semaphore()
    for peer in peers:
        pl.semaphore_signal(barrier, inc=1, device_id=peer, device_id_type=MESH)
    pl.semaphore_wait(barrier, len(peers))


def bits_of(count):
    return count.bit_length() - 1


class Place:
    def __init__(self, grid_shape):
        self.count_y, self.count_z = grid_shape[0] // 2, grid_shape[1] // 2
        first, second = lax.axis_index("gx"), lax.axis_index("gy")
        self.c, self.y = first % 2, first // 2
        self.x, self.z = second % 2, second // 2

    def core_peer(self):
        return {"gx": self.y * 2 + 1 - self.c}

    def x_peer(self):
        return {"gy": self.z * 2 + 1 - self.x}

    def y_at(self, apart):
        return xor_of(self.y, apart, bits_of(self.count_y))

    def y_peer(self, apart):
        return {"gx": self.y_at(apart) * 2 + self.c}

    def y_peers(self):
        return [self.y_peer(apart) for apart in range(1, self.count_y)]

    def z_at(self, apart):
        return xor_of(self.z, apart, bits_of(self.count_z))

    def z_peer(self, apart):
        return {"gy": self.z_at(apart) * 2 + self.x}

    def z_peers(self):
        return [self.z_peer(apart) for apart in range(1, self.count_z)]


def send(src, dst, sems, index, peer):
    return pltpu.make_async_remote_copy(
        src_ref=src,
        dst_ref=dst,
        send_sem=sems[0].at[index],
        recv_sem=sems[1].at[index],
        device_id=peer,
        device_id_type=MESH,
    )


def start_all(copies):
    for copy in copies:
        copy.start()


def wait_all(copies):
    for copy in copies:
        copy.wait()


def local_copies(pairs, sems, base=0):
    return [
        pltpu.make_async_copy(src, dst, sems.at[base + index])
        for index, (src, dst) in enumerate(pairs)
    ]


def scratch_of(arrays):
    return [pltpu.VMEM(array.shape, array.dtype) for array in arrays]


def gather_z(place, src, landing, sems):
    return [
        send(src, landing, sems, apart - 1, place.z_peer(apart)) for apart in range(1, place.count_z)
    ]


def gather_copies(grid_shape):
    return grid_shape[1] // 2 - 1, 2 * (grid_shape[0] // 2 - 1) + 3


def gather_second(place, column, full, split, sems):
    y, c, x = place.y, place.c, place.x
    upper, lower = pl.ds(0, split), pl.ds(split, full.shape[4] - split)
    copies = [
        send(column.at[:, upper], full.at[y, c, :, x, upper], sems, 0, place.x_peer())
    ]
    for apart in range(1, place.count_y):
        copies.append(
            send(column.at[:, lower], full.at[y, c, :, x, lower], sems, apart, place.y_peer(apart))
        )
    return copies


def gather_third(place, full, split, sems):
    y, c, x = place.y, place.c, place.x
    upper, lower = pl.ds(0, split), pl.ds(split, full.shape[4] - split)
    base = place.count_y
    ref = full.at[:, c, :, x, lower]
    copies = [send(ref, ref, sems, base, place.x_peer())]
    ref = full.at[y, c, :, :, upper]
    for apart in range(1, place.count_y):
        copies.append(send(ref, ref, sems, base + apart, place.y_peer(apart)))
    return copies


def gather_core(place, full, sems):
    ref = full.at[:, place.c]
    return [send(ref, ref, sems, 2 * place.count_y, place.core_peer())]


def whole_blocks(shape, split):
    count_y, _, count_z, _, tall, lanes = shape
    low = tall - split
    return [
        (count_y, count_z, 2, tall, lanes),
        (count_y - 1, count_z, 2, split, lanes),
        (count_y, count_z, low, lanes),
        (count_z, split, lanes),
        (count_y - 1, count_z, low, lanes),
        (count_z - 1, split, lanes),
        (count_z - 1, low, lanes),
    ]


def scatter_copies(grid_shape):
    return 1 + 2 * (grid_shape[0] // 2) + 2 * (grid_shape[1] // 2 - 1)


def add_low(dst, dst_at, *terms):
    total = terms[0].astype(f32)
    for term in terms[1:]:
        total = total + term.astype(f32)
    dst[dst_at] = total.astype(bf16)


class Scatter:
    def __init__(self, place, src, landings, sems, split, source=None):
        self.place, self.src, self.sems = place, src, sems
        self.source = src if source is None else source
        self.first, self.up2, self.low2, self.up3, self.low3, self.up4, self.low4 = landings
        tall = src.shape[4]
        self.upper, self.lower = pl.ds(0, split), pl.ds(split, tall - split)

    def copies(self, stage):
        at, sems = self.place, self.sems
        count_y, count_z = at.count_y, at.count_z
        if stage == 0:
            return [send(self.source.at[:, 1 - at.c], self.first, sems, 0, at.core_peer())]
        if stage == 1:
            copies = [send(self.first.at[:, :, 1 - at.x, self.lower], self.low2, sems, 1, at.x_peer())]
            for apart in range(1, count_y):
                src = self.first.at[at.y_at(apart), :, :, self.upper]
                dst = self.up2.at[apart - 1]
                copies.append(send(src, dst, sems, 1 + apart, at.y_peer(apart)))
            return copies
        if stage == 2:
            base = 1 + count_y
            copies = [send(self.up2.at[0, :, 1 - at.x], self.up3, sems, base, at.x_peer())]
            for apart in range(1, count_y):
                src, dst = self.low2.at[at.y_at(apart)], self.low3.at[apart - 1]
                copies.append(send(src, dst, sems, base + apart, at.y_peer(apart)))
            return copies
        base = 2 * count_y
        copies = []
        for apart in range(1, count_z):
            there = at.z_at(apart)
            for src, dst, more in (
                (self.up3.at[there], self.up4.at[apart - 1], 0),
                (self.low3.at[0, there], self.low4.at[apart - 1], 1),
            ):
                index = base + 2 * apart - 1 + more
                copies.append(send(src, dst, sems, index, at.z_peer(apart)))
        return copies

    def add(self, stage):
        at = self.place
        count_y, count_z = at.count_y, at.count_z
        if stage == 0:

            @pl.loop(0, count_y * count_z)
            def _(index):
                y, z = index // count_z, index % count_z
                add_low(self.first, (y, z), self.first[y, z], self.src[y, at.c, z])

        elif stage == 1:

            @pl.loop(0, count_z)
            def _(z):
                for x in range(2):
                    terms = [self.up2[apart, z, x] for apart in range(count_y - 1)]
                    add_low(self.up2, (0, z, x), self.first[at.y, z, x, self.upper], *terms)

                @pl.loop(0, count_y)
                def _(y):
                    add_low(self.low2, (y, z), self.first[y, z, at.x, self.lower], self.low2[y, z])

        elif stage == 2:

            @pl.loop(0, count_z)
            def _(z):
                add_low(self.up3, (z,), self.up3[z], self.up2[0, z, at.x])
                terms = [self.low3[apart, z] for apart in range(count_y - 1)]
                add_low(self.low3, (0, z), self.low2[at.y, z], *terms)

    def result(self):
        at = self.place
        upper, lower = self.up3[at.z].astype(f32), self.low3[0, at.z].astype(f32)
        for apart in range(at.count_z - 1):
            upper = upper + self.up4[apart].astype(f32)
            lower = lower + self.low4[apart].astype(f32)
        return upper, lower


class SmallSum:
    def __init__(self, grid_shape, totals, landing, sems):
        self.totals, self.landing, self.sems = totals, landing, sems
        self.peers = []
        for name, count in (("gx", grid_shape[0]), ("gy", grid_shape[1])):
            me = lax.axis_index(name)
            for bit in range(bits_of(count)):
                self.peers.append({name: xor_of(me, 1 << bit, bits_of(count))})
        self.done = 0

    def copy(self):
        step = self.done
        return send(self.totals.at[step], self.landing.at[step], self.sems, step, self.peers[step])

    def begin(self):
        self.copy().start()

    def advance(self):
        if self.done == len(self.peers):
            return
        self.copy().wait()
        step = self.done
        self.totals[step + 1] = self.totals[step] + self.landing[step]
        self.done += 1
        if self.done < len(self.peers):
            self.begin()


def small_steps(grid_shape):
    return bits_of(grid_shape[0]) + bits_of(grid_shape[1])


def lane_parts(lanes):
    return lanes // 128 if lanes % 128 == 0 else 1


def lane_part(ref, part, parts):
    if parts == 1:
        return ref
    lanes = ref.shape[-1] // parts
    return ref.at[..., pl.ds(part * lanes, lanes)]


def final_kernel(grid_shape, layers, buckets_count, *refs):
    refs = list(refs)
    take = refs.pop
    partial_refs = [(take(0), take(0)) for _ in range(layers - 1)]
    router_refs, gga_refs, ggf_refs, offset_refs = ([take(0) for _ in range(layers)] for _ in range(4))
    buckets_ref, slot_col_ref, chosen_ref, logits_ref = (take(0) for _ in range(4))
    blocks_in_ref, middle_in_ref = take(0), take(0)
    first_ref, second_ref, push_ref = take(0), take(0), take(0)
    packed_ref, small_out_ref, result_ref, landing_ref = (take(0) for _ in range(4))
    blocks_ref, middle_ref, move_sems = (take(0) for _ in range(3))
    landings = [take(0) for _ in range(7)]
    z_landings = [(take(0), take(0)) for _ in range(layers - 1)]
    totals, landing, returned_s = take(0), take(0), take(0)
    sems = [(take(0), take(0)) for _ in range(layers)]
    small_sems, collect_sems, push_sems = (take(0), take(0)), take(0), (take(0), take(0))
    place = Place(grid_shape)
    tall = packed_ref.shape[1]
    split = tall // 2
    members = grid_shape[1]
    slots = returned_s.shape[0]
    upper_layers = []
    for layer in range(1, layers):
        upper, lower = partial_refs[layer - 1]
        places = (None, None, None, upper, lower, *z_landings[layer - 1])
        upper_layers.append(Scatter(place, blocks_ref, places, sems[layer], split))
    parts = lane_parts(packed_ref.shape[2])
    lowest = [
        Scatter(
            place,
            lane_part(blocks_ref, part, parts),
            [lane_part(landing_part, part, parts) for landing_part in landings],
            (sems[0][0].at[part], sems[0][1].at[part]),
            split,
            lane_part(blocks_in_ref, part, parts),
        )
        for part in range(parts)
    ]

    def step(stage):
        for one in lowest:
            wait_all(one.copies(stage))
            one.add(stage)
            start_all(one.copies(stage + 1))

    c = place.c
    moves = local_copies(
        [(blocks_in_ref.at[:, c], blocks_ref.at[:, c]), (middle_in_ref, middle_ref)], move_sems
    )
    start_all(moves)
    collected = collect(
        lax.axis_index("gy"),
        members,
        slots // members,
        (first_ref, second_ref),
        lambda apart: int(apart not in early(members)),
        returned_s,
        collect_sems,
    )
    start_all(collected)
    greet([place.core_peer(), place.x_peer()] + place.y_peers() + place.z_peers())
    for one in lowest:
        start_all(one.copies(0))
    for one in upper_layers:
        start_all(one.copies(3))

    experts = router_refs[0].shape[0]
    totals[0] = jnp.zeros(totals.shape[1:], f32)
    row = 0
    for refs_of in (router_refs, gga_refs, ggf_refs):
        for ref in refs_of:
            totals[0, row : row + ref.shape[0], :] = ref[...]
            row += ref.shape[0]
    heads = offset_refs[0].shape[0]
    offsets = offset_refs[0][...]
    for ref in offset_refs[1:]:
        offsets = offsets + ref[...]
    in_bucket = (
        lax.broadcasted_iota(jnp.int32, (buckets_count, offsets.shape[1]), 0) == buckets_ref[...]
    ).astype(f32)
    totals[0, row : row + heads, :buckets_count] = lax.dot_general(
        offsets, in_bucket, (((1,), (1,)), ((), ())), precision=highest, preferred_element_type=f32
    )
    small = SmallSum(grid_shape, totals, landing, small_sems)
    small.begin()
    wait_all(moves)
    step(0)
    small.advance()
    wait_all(collected)
    placing = placing_cols(slot_col_ref[...], slots)
    gate = jnp.sum(jax.nn.softmax(logits_ref[...], axis=-1) * chosen_ref[...], axis=1, keepdims=True)
    result_ref[...] = middle_ref[...] + gate * dot(placing, returned_s[...])
    small.advance()
    step(1)
    small.advance()

    def finish(layer, one, lanes=slice(None)):
        for part, rows in zip(one.result(), (slice(0, split), slice(split, tall))):
            packed_ref[layer, rows, lanes] = part

    for layer, one in enumerate(upper_layers):
        wait_all(one.copies(3))
        finish(layer + 1, one)
    step(2)
    pushed = push_blocks(
        place, push_ref, landing_ref, push_sems, push_ref.shape[1] - landing_ref.shape[1]
    )
    start_all(pushed)
    while small.done < len(small.peers):
        small.advance()
    small_out_ref[...] = totals[len(small.peers)]
    each = packed_ref.shape[2] // parts
    for part, one in enumerate(lowest):
        wait_all(one.copies(3))
        finish(0, one, slice(part * each, (part + 1) * each))
    wait_all(pushed)


def final_sums(blocks, partials, smalls, finishing, returned, push, grid_shape, buckets_count):
    layers = len(partials) + 1
    shape = blocks.shape
    tall = shape[4]
    width = finishing[-1].shape[1]
    landings = [pltpu.VMEM(one, bf16) for one in whole_blocks(shape, tall // 2)]
    steps = small_steps(grid_shape)
    rows = sum(one.shape[0] for one in smalls[: 3 * layers]) + smalls[3 * layers].shape[0]
    small_shape = (rows, width)
    sems = pltpu.SemaphoreType.DMA((scatter_copies(grid_shape),))
    first_sems = pltpu.SemaphoreType.DMA((lane_parts(shape[5]), scatter_copies(grid_shape)))
    small_sems = pltpu.SemaphoreType.DMA((steps,))
    outs = [jax.ShapeDtypeStruct((layers, tall, shape[5]), f32)]
    outs += [jax.ShapeDtypeStruct(small_shape, f32), jax.ShapeDtypeStruct(finishing[-1].shape, f32)]
    outs.append(landing_of(push, push.shape[1] - push.shape[1] // 2))
    ins = [*[array for pair in partials for array in pair], *smalls, *finishing[:3]]
    moved = [blocks, finishing[-1]]
    return pl.pallas_call(
        partial(final_kernel, grid_shape, layers, buckets_count),
        in_specs=[vmem_spec] * len(ins) + [any_spec] * 5,
        out_specs=[vmem_spec] * (len(outs) - 1) + [any_spec],
        out_shape=outs,
        scratch_shapes=scratch_of(moved)
        + [pltpu.SemaphoreType.DMA((2,))]
        + landings
        + landings[5:] * (layers - 1)
        + [pltpu.VMEM((steps + 1, *small_shape), f32), pltpu.VMEM((steps, *small_shape), f32)]
        + [pltpu.VMEM(returned[0].shape, bf16)]
        + [first_sems, first_sems]
        + [sems, sems] * (layers - 1)
        + [small_sems, small_sems, pltpu.SemaphoreType.DMA((grid_shape[1],))]
        + [pltpu.SemaphoreType.DMA((grid_shape[0] // 2 - 1,))] * 2,
        compiler_params=params(24),
        cost_estimate=lasting(60),
        name="final_sums",
    )(*ins, *moved, *returned, push)


def unblock(grid_shape, blocks_ref, mats_ref, router_ref):
    count_x, count_y = grid_shape
    tall = mats_ref.shape[1] // count_x
    wide = mats_ref.shape[2] // count_y
    router_rows = []
    for first in range(count_x):
        spots = [(first // 2, first % 2, second // 2, second % 2) for second in range(count_y)]
        rows = slice(first * tall, (first + 1) * tall)
        for which in range(4):
            lanes = slice(which * wide, (which + 1) * wide)
            mats_ref[which, rows, :] = jnp.concatenate(
                [blocks_ref[(*spot, slice(0, tall), lanes)] for spot in spots], axis=1
            )
        router_rows.append(
            jnp.concatenate(
                [blocks_ref[(*spot, slice(tall, tall + 1), slice(0, tall))] for spot in spots],
                axis=0,
            )
        )
    router_ref[...] = jnp.concatenate(router_rows, axis=1)


def turned(row):
    return jnp.broadcast_to(row, (128, row.shape[1])).T[:, 0:1]


def start_kernel(
    grid_shape,
    wq_ref,
    wk_ref,
    wv_ref,
    wo_ref,
    router_rows_ref,
    buckets_ref,
    table_ref,
    piece_row_ref,
    route_row_ref,
    cotangent_ref,
    mats_ref,
    router_ref,
    later_ref,
    bias_out_ref,
    slot_col_ref,
    slot_row_ref,
    chosen_ref,
    spread_out_ref,
    far_ref,
    bias_ref,
    spread_ref,
    write_sems,
    full_s,
    column_s,
    spread_send,
    spread_recv,
    later_send,
    later_recv,
    z_send,
    z_recv,
    send_sems,
    recv_sems,
):
    place = Place(grid_shape)
    layers, tall, wide = wq_ref.shape
    split = tall // 2
    y, c, z, x = place.y, place.c, place.z, place.x

    def packed(layer):
        return jnp.concatenate([ref[layer] for ref in (wq_ref, wk_ref, wv_ref, wo_ref)], axis=1)

    column_s[z, :tall] = packed(0)
    column_s[z, tall:] = router_rows_ref[0]
    members = grid_shape[1]
    spread = Exchange(
        members, spread_ref.shape[0] // members, spread_ref, far_ref, spread_send, spread_recv
    )
    spread_copies = [spread.copy(apart) for apart in in_third(members, 0)]
    mine_here = spread.block(spread.me)
    half_heads = bias_ref.shape[0] // 2
    parts = [pl.ds(0, half_heads), pl.ds(half_heads, half_heads)]
    write_spread, write_own, *write_bias = local_copies(
        [(spread_ref, spread_out_ref), (spread_ref.at[mine_here, :], far_ref.at[mine_here, :])]
        + [(bias_ref.at[part], bias_out_ref.at[part]) for part in parts],
        write_sems,
    )
    greet(
        [place.core_peer(), place.x_peer()]
        + place.y_peers()
        + place.z_peers()
        + [spread.peer(apart) for apart in in_third(members, 0)]
    )
    first = gather_z(place, column_s.at[z], column_s.at[z], (z_send, z_recv))
    start_all(first)
    along_z = []
    for layer in range(1, layers):
        later_ref[layer - 1, z, :tall] = packed(layer)
        later_ref[layer - 1, z, tall:] = router_rows_ref[layer]
        mine = later_ref.at[layer - 1, z]
        along_z += gather_z(place, mine, mine, (later_send.at[layer - 1], later_recv.at[layer - 1]))

    seq_len, experts = chosen_ref.shape
    capacity = 2 * seq_len // experts
    heads = bias_ref.shape[0]
    buckets_count = table_ref.shape[1]
    in_bucket = (
        lax.broadcasted_iota(jnp.int32, (buckets_count, 2 * seq_len), 0) == buckets_ref[...]
    )
    offsets = dot(table_ref[...], in_bucket.astype(f32).astype(bf16))
    key_pos = lax.broadcasted_iota(jnp.int32, (seq_len, seq_len), 0)
    query_pos = lax.broadcasted_iota(jnp.int32, (seq_len, seq_len), 1)
    route_row, piece_row = route_row_ref[...], piece_row_ref[...]
    route_col, piece_col = turned(route_row), turned(piece_row)
    chosen = (lax.broadcasted_iota(jnp.int32, (seq_len, experts), 1) == route_col).astype(f32)
    chosen_t = (lax.broadcasted_iota(jnp.int32, (experts, seq_len), 0) == route_row).astype(f32)
    chosen_ref[...] = chosen
    earlier = (key_pos < query_pos).astype(f32).astype(bf16)
    before_t = dot(chosen_t.astype(bf16), earlier)
    rank_row = jnp.sum(before_t * chosen_t, axis=0, keepdims=True)
    slot_row_ref[...] = route_row * capacity + rank_row.astype(jnp.int32)
    later = (key_pos > query_pos).astype(f32).astype(bf16)
    before = dot(later, chosen.astype(bf16))
    rank_col = jnp.sum(before * chosen, axis=1, keepdims=True)
    slot_col_ref[...] = route_col * capacity + rank_col.astype(jnp.int32)
    placing = placing_rows(slot_row_ref[...], spread_ref.shape[0])
    spread_ref[...] = dot(placing, cotangent_ref[...]).astype(bf16)
    start_all([write_spread, write_own])

    same = (piece_col == piece_row) & (piece_col > 0)
    allowed = (key_pos <= query_pos) | same

    def bias_for(head):
        row = jnp.broadcast_to(offsets[head : head + 1], (seq_len, 2 * seq_len))
        shifted = pltpu.roll(row, seq_len + 1, 1, stride=1, stride_axis=0)[:, :seq_len]
        bias_ref[head] = jnp.where(allowed, shifted, masked_out).astype(bf16)

    for head in range(heads // 2):
        bias_for(head)
    wait_all(first)
    sems = (send_sems, recv_sems)
    second = gather_second(place, column_s, full_s, split, sems)
    start_all(second)
    start_all(along_z)
    start_all(spread_copies)
    write_bias[0].start()
    full_s[y, c, :, x] = column_s[...]
    for head in range(heads // 2, heads):
        bias_for(head)
    write_bias[1].start()
    wait_all(second)
    third = gather_third(place, full_s, split, sems)
    start_all(third)

    wait_all(third)
    fourth = gather_core(place, full_s, sems)
    start_all(fourth)
    wait_all(fourth)
    unblock(grid_shape, full_s, mats_ref, router_ref)
    wait_all(along_z)
    wait_all(spread_copies)
    wait_all([write_spread, write_own, *write_bias])


def start(mats, router_rows, buckets, table_t, piece_ids, route, cotangent, grid_shape):
    layers, tall, wide = mats[0].shape
    seq_len = piece_ids.shape[0]
    heads = table_t.shape[0]
    width = tall * grid_shape[0]
    experts = grid_shape[1]
    block = (router_rows.shape[1] + tall, 4 * wide)
    half = (grid_shape[0] // 2, 2, grid_shape[1] // 2, 2)
    ins = (
        *mats,
        router_rows,
        buckets,
        table_t,
        piece_ids[None, :],
        route.reshape(1, seq_len),
        cotangent,
    )
    outs = (
        jax.ShapeDtypeStruct((4, width, width), bf16),
        jax.ShapeDtypeStruct((experts, width), bf16),
        jax.ShapeDtypeStruct((layers - 1, half[2], *block), bf16),
        jax.ShapeDtypeStruct((heads, seq_len, seq_len), bf16),
        jax.ShapeDtypeStruct((seq_len, 1), jnp.int32),
        jax.ShapeDtypeStruct((1, seq_len), jnp.int32),
        jax.ShapeDtypeStruct((seq_len, experts), f32),
        jax.ShapeDtypeStruct((2 * seq_len, width), bf16),
        jax.ShapeDtypeStruct((2 * seq_len, width), bf16),
    )
    along_z, others = gather_copies(grid_shape)
    return pl.pallas_call(
        partial(start_kernel, grid_shape),
        in_specs=[vmem_spec] * len(ins),
        out_specs=[vmem_spec] * 3 + [any_spec] + [vmem_spec] * 3 + [any_spec] * 2,
        out_shape=outs,
        scratch_shapes=[
            *scratch_of([outs[3], outs[7]]),
            pltpu.SemaphoreType.DMA((4,)),
            pltpu.VMEM((*half, *block), bf16),
            pltpu.VMEM((half[2], *block), bf16),
            pltpu.SemaphoreType.DMA((experts,)),
            pltpu.SemaphoreType.DMA((experts,)),
            pltpu.SemaphoreType.DMA((layers - 1, along_z)),
            pltpu.SemaphoreType.DMA((layers - 1, along_z)),
            pltpu.SemaphoreType.DMA((along_z,)),
            pltpu.SemaphoreType.DMA((along_z,)),
            pltpu.SemaphoreType.DMA((others,)),
            pltpu.SemaphoreType.DMA((others,)),
        ],
        compiler_params=params(0),
        cost_estimate=lasting(45),
        name="start",
    )(*ins)


def half_masks(rows, width):
    lane = lax.broadcasted_iota(jnp.int32, (rows, width), 1)
    return lane < (width // 2)


def gates_of(logits, slot_col, chosen, gates_ref):
    experts = gates_ref.shape[0]
    seq_len = slot_col.shape[0]
    capacity = 2 * seq_len // experts
    gate = jnp.sum(jax.nn.softmax(logits, axis=-1) * chosen, axis=1, keepdims=True)
    places = lax.broadcasted_iota(jnp.int32, (seq_len, 2 * seq_len), 1)
    row = jnp.sum(jnp.where(places == slot_col, gate, 0.0), axis=0, keepdims=True)
    gates_ref[...] = jnp.zeros_like(gates_ref)
    for expert in range(experts):
        mine = row[:, expert * capacity : (expert + 1) * capacity]
        gates_ref[expert, :, :capacity] = jnp.broadcast_to(mine, (gates_ref.shape[1], capacity))


def forward_kernel(
    head_dim,
    grid_shape,
    blocked,
    last,
    hidden_ref,
    gain_attn_ref,
    gain_ffn_ref,
    slot_row_ref,
    slot_col_ref,
    chosen_ref,
    *refs,
):
    refs = list(refs)
    take = refs.pop
    blocks_ref = take(0) if blocked else None
    mats_ref, router_ref = (None, None) if blocked else (take(0), take(0))
    spread_ref = take(0)
    bias_ref = take(0)
    outs = []
    if blocked:
        outs.append(take(0))
        router_ref = take(0)
    outs += [take(0) for _ in range(3)]
    att_ref, lse_ref, middle_ref, logits_ref, sent_ref = (take(0) for _ in range(5))
    gates_ref = take(0) if last else None
    far_ref, send_sems, recv_sems, write_sems, *made_here = refs
    q_ref, k_ref, v_ref = made_here[-3:]
    if blocked:
        mats_ref = made_here[0]
    writes = local_copies(list(zip(made_here, outs)), write_sems)
    pair, pairs = pl.program_id(0), pl.num_programs(0)
    seq_len = hidden_ref.shape[0]
    width = 2 * head_dim
    step = min(512, seq_len)

    members = grid_shape[1]
    spread = Exchange(members, spread_ref.shape[0] // members, spread_ref, far_ref, send_sems, recv_sems)
    aparts = in_third(members, 2 if last else 1)

    @pl.when(pair == 0)
    def _():
        greet([spread.peer(apart) for apart in aparts])
        start_all([spread.copy(apart) for apart in aparts])

    @pl.when(pair == 0)
    def _():
        if blocked:
            unblock(grid_shape, blocks_ref, mats_ref, router_ref)
        hidden = hidden_ref[...].astype(f32)
        normed = (hidden * rms_factor(hidden) * gain_attn_ref[...]).astype(bf16)
        q_ref[...] = dot(normed, mats_ref[0]).astype(bf16)
        k_ref[...] = dot(normed, mats_ref[1]).astype(bf16)
        v_ref[...] = dot(normed, mats_ref[2]).astype(bf16)
        start_all(writes)

    lanes = pl.ds(pl.multiple_of(pair * width, width), width)
    q2 = q_ref[:, lanes] * jnp.asarray(head_dim**-0.5, bf16)
    k2 = k_ref[:, lanes]
    v2t = v_ref[:, lanes].T
    first = half_masks(seq_len, width)
    for half in range(2):
        q_one = jnp.where(first if half == 0 else ~first, q2, jnp.zeros_like(q2))
        v_one = v2t[half * head_dim : (half + 1) * head_dim]
        for begin in range(0, seq_len, step):
            cols = slice(begin, begin + step)
            scores = dot(k2, q_one[cols], 1, 1) + bias_ref[half, :, cols].astype(f32)
            top = jnp.max(scores, axis=0, keepdims=True)
            raised = jnp.exp(scores - top)
            total = jnp.sum(raised, axis=0, keepdims=True)
            probs = raised.astype(bf16)
            rows = pl.ds(pl.multiple_of(pair * width + half * head_dim, head_dim), head_dim)
            att_ref[rows, cols] = (dot(v_one, probs) * (1.0 / total)).astype(bf16)
            lse_ref[0, half : half + 1, cols] = top + jnp.log(total)

    @pl.when(pair == pairs - 1)
    def _():
        middle = hidden_ref[...].astype(f32) + dot(att_ref[...].T, mats_ref[3])
        middle_ref[...] = middle
        ffn_in = (middle * rms_factor(middle) * gain_ffn_ref[...]).astype(bf16)
        logits = dot(ffn_in, router_ref[...], 1, 1)
        logits_ref[...] = logits
        if gates_ref is not None:
            gates_of(logits, slot_col_ref[...], chosen_ref[...], gates_ref)
        placing = placing_rows(slot_row_ref[...], sent_ref.shape[0])
        sent_ref[...] = dot(placing, ffn_in).astype(bf16)

    @pl.when(pair == pairs - 1)
    def _():
        wait_all([spread.copy(apart) for apart in aparts])
        wait_all(writes)


def attention_forward(
    hidden,
    gain_attn,
    gain_ffn,
    slots_and_chosen,
    bias,
    grid_shape,
    identifier,
    spread,
    last,
    blocks=None,
    mats=None,
):
    seq_len, width = hidden.shape
    heads = bias.shape[0]
    head_dim = width // heads
    slots = 2 * seq_len
    experts = grid_shape[1]
    blocked = blocks is not None
    ins = [hidden, gain_attn, gain_ffn, *slots_and_chosen] + ([blocks] if blocked else list(mats))
    in_specs = whole_of(ins)
    ins.append(spread)
    in_specs.append(any_spec)
    ins.append(bias)
    in_specs.append(pl.BlockSpec((2, seq_len, seq_len), lambda p: (p, 0, 0)))
    tall = jax.ShapeDtypeStruct((seq_len, width), bf16)
    outs = [
        tall,
        tall,
        tall,
        jax.ShapeDtypeStruct((width, seq_len), bf16),
        jax.ShapeDtypeStruct((heads // 2, 2, seq_len), f32),
        jax.ShapeDtypeStruct((seq_len, width), f32),
        jax.ShapeDtypeStruct((seq_len, experts), f32),
        jax.ShapeDtypeStruct((slots, width), bf16),
    ]
    if last:
        outs.append(jax.ShapeDtypeStruct((experts, 8, max(128, slots // experts)), f32))
    out_specs = whole_of(outs)
    out_specs[:3] = [any_spec] * 3
    written = outs[:3]
    out_specs[4] = pl.BlockSpec((1, 2, seq_len), lambda p: (p, 0, 0))
    if blocked:
        more = [
            jax.ShapeDtypeStruct((4, width, width), bf16),
            jax.ShapeDtypeStruct((experts, width), bf16),
        ]
        outs = more + outs
        out_specs = [any_spec] + whole_of(more[1:]) + out_specs
        written = more[:1] + written
    outs.append(jax.ShapeDtypeStruct(spread.shape, bf16))
    out_specs.append(any_spec)
    sems = pltpu.SemaphoreType.DMA((experts,))
    scratch = [sems, sems, pltpu.SemaphoreType.DMA((len(written),)), *scratch_of(written)]
    got = pl.pallas_call(
        partial(forward_kernel, head_dim, grid_shape, blocked, last),
        grid=(heads // 2,),
        in_specs=in_specs,
        out_specs=out_specs,
        out_shape=outs,
        scratch_shapes=scratch,
        compiler_params=params(identifier),
        cost_estimate=lasting(25),
        name="attention_forward",
    )(*ins)
    return tuple(got) if blocked else tuple(mats) + tuple(got)


def diagonal_fold(values, seq_len):
    rows, wide = seq_len, 2 * seq_len
    folded = None
    tile = 128
    count = seq_len // tile
    for row_tile in range(count):
        piece = values[row_tile * tile : (row_tile + 1) * tile].astype(f32)
        before = (count - 1 - row_tile) * tile
        after = wide - seq_len - before
        parts = []
        if before:
            parts.append(jnp.zeros((tile, before), f32))
        parts.append(piece)
        if after:
            parts.append(jnp.zeros((tile, after), f32))
        padded = jnp.concatenate(parts, axis=1)
        folded = padded if folded is None else folded + padded
    rows = tile
    while rows > 1:
        rows //= 2
        folded = pltpu.roll(folded[:rows], rows, 1) + folded[rows:]
    return folded


def reblock(grid_shape, blocks_ref, which, values):
    count_x, count_y = grid_shape
    tall = values.shape[0] // count_x
    wide = values.shape[1] // count_y
    for first in range(count_x):
        for second in range(count_y):
            spot = (first // 2, first % 2, second // 2, second % 2)
            lanes = slice(which * wide, (which + 1) * wide)
            blocks_ref[(*spot, slice(None), lanes)] = values[
                first * tall : (first + 1) * tall, second * wide : (second + 1) * wide
            ]


def d_logits_of(d_gate, logits, chosen):
    shares = jax.nn.softmax(logits, axis=-1)
    gate = jnp.sum(shares * chosen, axis=1, keepdims=True)
    return (d_gate * shares * (chosen - gate)).astype(bf16)


def spread_into(grad_now, comb_ref, slot_row_ref, chosen_ref, logits_ref, d_sent_ref, d_logits_ref):
    d_gate = jnp.sum(grad_now * comb_ref[...], axis=1, keepdims=True)
    logits, chosen = logits_ref[...], chosen_ref[...]
    d_logits_ref[...] = d_logits_of(d_gate, logits, chosen)
    gate = jnp.sum(jax.nn.softmax(logits, axis=-1) * chosen, axis=1, keepdims=True)
    placing = placing_rows(slot_row_ref[...], d_sent_ref.shape[0])
    d_sent_ref[...] = dot(placing, (gate * grad_now).astype(bf16)).astype(bf16)


def backward_kernel(
    head_dim,
    grid_shape,
    spreads,
    returns,
    pushes,
    unread,
    d_back_ref,
    slot_col_ref,
    d_logits_ref,
    grad_ref,
    middle_ref,
    gain_attn_ref,
    gain_ffn_ref,
    router_ref,
    att_ref,
    *refs,
):
    refs = list(refs)
    take = refs.pop
    spread_in = [take(0) for _ in range(4)] if spreads else []
    bias_ref, lse_ref = take(0), take(0)
    made_ref = take(0)
    push_refs = (take(0), take(0)) if pushes else ()
    later = [take(0) for _ in range(5)]
    del refs[:unread]
    grad_new_ref, blocks_ref, gwr_ref, gga_ref, ggf_ref, offsets_ref = (take(0) for _ in range(6))
    spread_out = [take(0) for _ in range(2)] if spreads else []
    returned_ref = take(0)
    landing_refs = (take(0), take(0)) if pushes else ()
    d_att_s, d_middle_s, dqt_s, dk_s, dv_s, probs_s, scores_s = (take(0) for _ in range(7))
    loaded = [take(0) for _ in range(5)]
    load_sems = take(0)
    mats_ref, q_ref, k_ref, v_ref, hidden_ref = loaded
    mats_later = later[0]
    load_output = local_copies([(mats_later.at[3], mats_ref.at[3])], load_sems)
    load_heads = local_copies(list(zip(later[1:4], loaded[1:4])), load_sems, 1)
    first_three = pl.ds(0, 3)
    load_rest = local_copies(
        [(mats_later.at[first_three], mats_ref.at[first_three]), (later[4], hidden_ref)], load_sems, 4
    )
    own_sem, *sems = refs[:3]
    members = grid_shape[1]
    place = Place(grid_shape)
    pushed = []
    for src, landing, last_rows in zip(push_refs, landing_refs, (True, False)):
        begin = src.shape[1] - landing.shape[1] if last_rows else 0
        pushed += push_blocks(place, src, landing, refs[3:], begin, len(pushed))
    back = Exchange(members, made_ref.shape[0] // members, made_ref, returned_ref, *sems)
    mine = back.block(back.me)
    own = None
    if returns:
        own = pltpu.make_async_copy(made_ref.at[mine, :], returned_ref.at[mine, :], own_sem)
    aparts = part_of(members, returns)

    @pl.when(pl.program_id(0) == 0)
    def _():
        start_all(load_output + load_heads + load_rest)
        greet([back.peer(apart) for apart in aparts] + (place.y_peers() if pushes else []))
        start_all(pushed + [back.copy(apart) for apart in aparts])
        if returns:
            own.start()

    pair, pairs = pl.program_id(0), pl.num_programs(0)
    seq_len = att_ref.shape[1]
    width = 2 * head_dim
    step = min(512, seq_len)
    scale = head_dim**-0.5

    @pl.when(pair == 0)
    def _():
        placing = placing_cols(slot_col_ref[...], d_back_ref.shape[0])
        d_logits = d_logits_ref[...]
        d_ffn = dot(placing, d_back_ref[...]) + dot(d_logits, router_ref[...])
        middle = middle_ref[...]
        gain_row = gain_ffn_ref[...]
        ffn_in = (middle * rms_factor(middle) * gain_row).astype(bf16)
        gwr_ref[...] = dot(d_logits, ffn_in, 0, 0)
        d_middle, d_gain = rms_pull(middle, gain_row, d_ffn)
        ggf_ref[...] = d_gain
        d_middle = d_middle + grad_ref[...].astype(f32)
        d_middle_s[...] = d_middle
        d_low = d_middle.astype(bf16)
        wait_all(load_output)
        reblock(grid_shape, blocks_ref, 3, dot(att_ref[...], d_low).astype(bf16))
        d_att_s[...] = dot(d_low, mats_ref[3], 1, 1).astype(bf16)
        wait_all(load_heads)

    lanes = pl.ds(pl.multiple_of(pair * width, width), width)
    q2 = q_ref[:, lanes] * jnp.asarray(scale, bf16)
    k2 = k_ref[:, lanes]
    v2 = v_ref[:, lanes]
    da2 = d_att_s[:, lanes]
    k2t = k2.T
    first = half_masks(seq_len, width)
    d_key = jnp.zeros((seq_len, width), f32)
    d_value = jnp.zeros((seq_len, width), f32)
    for half in range(2):
        mask = first if half == 0 else ~first
        q_one = jnp.where(mask, q2, jnp.zeros_like(q2))
        da_one = jnp.where(mask, da2, jnp.zeros_like(da2))
        k_one = k2t[half * head_dim : (half + 1) * head_dim]
        rows = pl.ds(pl.multiple_of(pair * width + half * head_dim, head_dim), head_dim)
        for start in range(0, seq_len, step):
            cols = slice(start, start + step)
            scores = dot(k2, q_one[cols], 1, 1) + bias_ref[half, :, cols].astype(f32)
            probs = jnp.exp(scores - lse_ref[0, half : half + 1, cols])
            d_probs = dot(v2, da_one[cols], 1, 1)
            inner = jnp.sum(probs * d_probs, axis=0, keepdims=True)
            d_scores = (probs * (d_probs - inner)).astype(bf16)
            probs_s[:, cols] = probs.astype(bf16)
            scores_s[:, cols] = d_scores
            dqt_s[rows, cols] = (dot(k_one, d_scores) * scale).astype(bf16)
        d_key = d_key + dot(scores_s[...], q_one)
        d_value = d_value + dot(probs_s[...], da_one)
        offsets_ref[pl.ds(2 * pair + half, 1), :] = diagonal_fold(scores_s[...], seq_len)
    dk_s[:, lanes] = d_key.astype(bf16)
    dv_s[:, lanes] = d_value.astype(bf16)

    @pl.when(pair == pairs - 1)
    def _():
        wait_all(load_rest)
        hidden = hidden_ref[...].astype(f32)
        gain_row = gain_attn_ref[...]
        normed_t = (hidden * rms_factor(hidden) * gain_row).astype(bf16).T
        d_query = dqt_s[...].T
        d_normed = dot(d_query, mats_ref[0], 1, 1)
        reblock(grid_shape, blocks_ref, 0, dot(normed_t, d_query).astype(bf16))
        d_normed = d_normed + dot(dk_s[...], mats_ref[1], 1, 1)
        reblock(grid_shape, blocks_ref, 1, dot(normed_t, dk_s[...]).astype(bf16))
        d_normed = d_normed + dot(dv_s[...], mats_ref[2], 1, 1)
        reblock(grid_shape, blocks_ref, 2, dot(normed_t, dv_s[...]).astype(bf16))
        d_hidden, d_gain = rms_pull(hidden, gain_row, d_normed)
        gga_ref[...] = d_gain
        grad_new = d_hidden + d_middle_s[...]
        grad_new_ref[...] = grad_new
        if spreads:
            spread_into(grad_new, *spread_in, *spread_out)

    @pl.when(pair == pairs - 1)
    def _():
        wait_all(pushed + [back.copy(apart) for apart in aparts])
        if returns:
            own.wait()


def attention_backward(
    d_back,
    slot_col,
    d_logits,
    grad_now,
    middle,
    hidden,
    gains,
    mats,
    q_k_v,
    attended,
    bias,
    lse,
    grid_shape,
    below=None,
    after=(),
    made=None,
    returns=False,
    push=None,
    identifier=None,
):
    seq_len, width = hidden.shape
    heads = bias.shape[0]
    head_dim = width // heads
    experts = mats[1].shape[0]
    count_x, count_y = grid_shape
    ins = (
        d_back,
        slot_col,
        d_logits,
        grad_now,
        middle,
        *gains,
        mats[1],
        attended,
    )
    later = [mats[0], *q_k_v, hidden]
    spreads = below is not None
    if spreads:
        ins = ins + tuple(below)
    row = jax.ShapeDtypeStruct((1, width), f32)
    outs = (
        jax.ShapeDtypeStruct((seq_len, width), f32),
        jax.ShapeDtypeStruct(
            (count_x // 2, 2, count_y // 2, 2, width // count_x, 4 * (width // count_y)), bf16
        ),
        jax.ShapeDtypeStruct((experts, width), f32),
        row,
        row,
        jax.ShapeDtypeStruct((heads, 2 * seq_len), f32),
    )
    if spreads:
        outs = outs + (
            jax.ShapeDtypeStruct((2 * seq_len, width), bf16),
            jax.ShapeDtypeStruct(d_logits.shape, bf16),
        )
    outs = outs + (jax.ShapeDtypeStruct(made.shape, bf16),)
    pushes = push is not None
    out_specs = whole_of(outs)
    out_specs[-1] = any_spec
    if pushes:
        rows = [push[0].shape[1] - cut_of(push[0]), push[1].shape[1] // 2]
        outs = outs + tuple(landing_of(one, many) for one, many in zip(push, rows))
        out_specs += [any_spec] * 2
    return pl.pallas_call(
        partial(backward_kernel, head_dim, grid_shape, spreads, returns, pushes, len(after)),
        grid=(heads // 2,),
        in_specs=whole_of(ins)
        + [
            pl.BlockSpec((2, seq_len, seq_len), lambda p: (p, 0, 0)),
            pl.BlockSpec((1, 2, seq_len), lambda p: (p, 0, 0)),
        ]
        + [any_spec] * (len(after) + 6 + 2 * pushes),
        out_specs=out_specs,
        out_shape=outs,
        scratch_shapes=[
            pltpu.VMEM((seq_len, width), bf16),
            pltpu.VMEM((seq_len, width), f32),
            pltpu.VMEM((width, seq_len), bf16),
            pltpu.VMEM((seq_len, width), bf16),
            pltpu.VMEM((seq_len, width), bf16),
            pltpu.VMEM((seq_len, seq_len), bf16),
            pltpu.VMEM((seq_len, seq_len), bf16),
        ]
        + scratch_of(later)
        + [pltpu.SemaphoreType.DMA((6,)), pltpu.SemaphoreType.DMA]
        + [pltpu.SemaphoreType.DMA((count_y,))] * 2
        + [pltpu.SemaphoreType.DMA((2 * (count_x // 2 - 1),))] * (2 * pushes),
        compiler_params=params(identifier),
        cost_estimate=lasting(32),
        name="attention_backward",
    )(*ins, bias, lse, made, *(push if pushes else ()), *later, *after)


class Exchange:
    def __init__(self, members, rows, src, dst, send_sems, recv_sems):
        self.me = lax.axis_index("gy")
        self.bits = members.bit_length() - 1
        self.rows, self.src, self.dst = rows, src, dst
        self.send_sems, self.recv_sems = send_sems, recv_sems

    def block(self, index):
        return pl.ds(pl.multiple_of(index * self.rows, self.rows), self.rows)

    def peer(self, apart):
        return {"gy": xor_of(self.me, apart, self.bits)}

    def copy(self, apart):
        peer = xor_of(self.me, apart, self.bits)
        return pltpu.make_async_remote_copy(
            src_ref=self.src.at[self.block(peer), :],
            dst_ref=self.dst.at[self.block(self.me), :],
            send_sem=self.send_sems.at[apart],
            recv_sem=self.recv_sems.at[apart],
            device_id={"gy": peer},
            device_id_type=MESH,
        )

    def keep_own(self):
        self.dst[self.block(self.me), :] = self.src[self.block(self.me), :]


class Leading(Exchange):
    def __init__(self, members, src, dst, send_sems, recv_sems):
        super().__init__(members, 1, src, dst, send_sems, recv_sems)

    def copy(self, apart):
        peer = xor_of(self.me, apart, self.bits)
        sems = (self.send_sems, self.recv_sems)
        return send(self.src.at[peer], self.dst.at[self.me], sems, apart, {"gy": peer})

    def keep_own(self):
        self.dst[self.me] = self.src[self.me]


def peers_along_gy(members):
    me = lax.axis_index("gy")
    bits = members.bit_length() - 1
    return [{"gy": xor_of(me, apart, bits)} for apart in range(1, members)]


def gelu_and_slope(pre):
    inner_scale = 0.7978845608028654
    square = pre * pre
    bent = jnp.tanh(inner_scale * pre * (1.0 + 0.044715 * square))
    act = 0.5 * pre * (1.0 + bent)
    slope = 0.5 * (1.0 + bent) + 0.5 * pre * (1.0 - bent * bent) * (
        inner_scale * (1.0 + 3 * 0.044715 * square)
    )
    return act, slope


def gelu_only(pre):
    inner_scale = 0.7978845608028654
    return 0.5 * pre * (1.0 + jnp.tanh(inner_scale * pre * (1.0 + 0.044715 * pre * pre)))


def send_order(members):
    return range(1, members)


def early(members):
    quarter = max(1, members // 4)
    return [apart for apart in range(members) if (apart // quarter) % 2 == 0]


def part_of(members, first):
    chosen = early(members)
    return [a for a in range(1, members) if (a in chosen) == first]


def third_of(members, apart):
    quarter = max(1, members // 4)
    if (apart // quarter) % 2 == 0:
        return 0
    return 1 + (2 * (apart % quarter)) // quarter


def in_third(members, third):
    return [apart for apart in range(1, members) if third_of(members, apart) == third]


def collect(me, members, rows, refs, which_of, dst, sems):
    copies = []
    for apart in range(members):
        start = xor_of(me, apart, bits_of(members)) * rows
        here = pl.ds(pl.multiple_of(start, rows), rows)
        ref = refs[which_of(apart)]
        copies.append(pltpu.make_async_copy(ref.at[here, :], dst.at[here, :], sems.at[apart]))
    return copies


class Weights:
    def __init__(self, place, halves, whole_refs, local_sems, sems):
        blocks, _, units = halves[0].shape
        self.local, self.remote = [], []
        for which, (part, into) in enumerate(zip(halves, whole_refs)):
            for block in range(blocks):
                index = which * blocks + block
                begin = pl.multiple_of((place.c * blocks + block) * units, units)
                dst = into.at[:, pl.ds(begin, units)]
                src = part.at[block]
                self.local.append(pltpu.make_async_copy(src, dst, local_sems.at[index]))
                self.remote.append(send(src, dst, sems, index, place.core_peer()))
        self.blocks = blocks

    def start_local(self):
        start_all(self.local)

    def start_remote(self):
        start_all(self.remote)

    def wait(self, which):
        mine = slice(which * self.blocks, (which + 1) * self.blocks)
        for copy in self.local[mine] + self.remote[mine]:
            copy.wait()


def weight_gradients(place, products, sends, landings, outs, sems, after):
    blocks, _, units = outs[0].shape

    def product(lhs, rhs_ref, which, into_ref):
        @pl.loop(0, blocks)
        def _(block):
            begin = pl.multiple_of((which * blocks + block) * units, units)
            into_ref[block] = dot(lhs, rhs_ref[:, pl.ds(begin, units)]).astype(bf16)

    for index, (lhs_ref, rhs_ref) in enumerate(products):
        lhs = lhs_ref[...].T
        product(lhs, rhs_ref, 1 - place.c, sends[index])
        copy = send(sends[index], landings[index], sems, index, place.core_peer())
        copy.start()
        product(lhs, rhs_ref, place.c, outs[index])
        copy.wait()

        @pl.loop(0, blocks)
        def _(block, index=index):
            add_low(outs[index], (block,), outs[index][block], landings[index][block])

        start_all(after[index])


def push_blocks(place, src, landing, sems, begin, base=0):
    rows = pl.ds(begin, landing.shape[1])
    return [
        send(
            src.at[place.y_at(apart), rows],
            landing.at[apart - 1],
            sems,
            base + apart - 1,
            place.y_peer(apart),
        )
        for apart in range(1, place.count_y)
    ]


def cut_of(blocks):
    return blocks.shape[1] // 3 * 2


def landing_of(blocks, rows):
    return jax.ShapeDtypeStruct((blocks.shape[0] - 1, rows, blocks.shape[2]), bf16)


def chunk_of(members, rows):
    return max(1, min(members, 256 // rows))


def expert_forward_kernel(
    grid_shape,
    gathers,
    sent_ref,
    slot_col_ref,
    chosen_ref,
    logits_ref,
    middle_in_ref,
    win_ref,
    wout_ref,
    *refs,
):
    refs = list(refs)
    take = refs.pop
    column_ref = take(0) if gathers else None
    arrived_out_ref, comb_ref, out_ref = (take(0) for _ in range(3))
    full_ref = take(0) if gathers else None
    arrived_ref, middle_ref, move_sems = (take(0) for _ in range(3))
    load_middle, write_arrived = local_copies(
        [(middle_in_ref, middle_ref), (arrived_ref, arrived_out_ref)], move_sems
    )
    win_s, wout_s, made_s, returned_s, w_sems = (take(0) for _ in range(5))
    send_sems, recv_sems, back_send_sems, back_recv_sems = (take(0) for _ in range(4))
    weight_sems = (take(0), take(0))
    members = grid_shape[1]
    slots = sent_ref.shape[0]
    rows = slots // members
    group = chunk_of(members, rows)
    chunks = members // group
    chunk_bits = chunks.bit_length() - 1
    hidden_units = win_s.shape[1]
    tile = min(768, hidden_units)
    place = Place(grid_shape)
    weights = Weights(place, (win_ref, wout_ref), (win_s, wout_s), w_sems, weight_sems)
    weights.start_local()
    load_middle.start()
    more_peers = place.y_peers() if gathers else []
    greet(peers_along_gy(members) + [place.core_peer()] + more_peers)
    weights.start_remote()
    there = Exchange(members, rows, sent_ref, arrived_ref, send_sems, recv_sems)
    back = Exchange(members, rows, made_s, returned_s, back_send_sems, back_recv_sems)
    for apart in send_order(members):
        there.copy(apart).start()
    there.keep_own()
    if gathers:
        own_sem, *sems = refs
        split = (full_ref.shape[4] - tile_rows) // 2
        own = pltpu.make_async_copy(
            column_ref, full_ref.at[place.y, place.c, :, place.x], own_sem
        )
        own.start()
        second = gather_second(place, column_ref, full_ref, split, sems)
        third = gather_third(place, full_ref, split, sems)
        fourth = gather_core(place, full_ref, sems)
        start_all(second)
    weights.wait(0)
    weights.wait(1)
    my_chunk = there.me // group

    def chunk_rows(index):
        start = xor_of(my_chunk, index, chunk_bits) * (group * rows)
        return pl.ds(pl.multiple_of(start, group * rows), group * rows)

    def work(index, first):
        for member in range(first, group):
            there.copy(index * group + member).wait_recv()
        here = chunk_rows(index)
        taken = arrived_ref[here, :]
        total = jnp.zeros((group * rows, taken.shape[1]), f32)
        for start in range(0, hidden_units, tile):
            units = slice(start, start + tile)
            act = gelu_only(dot(taken, win_s[:, units])).astype(bf16)
            total = total + dot(act, wout_s[:, units], 1, 1)
        made_s[here, :] = total.astype(bf16)
        for member in range(first, group):
            back.copy(index * group + member).start()

    work(0, 1)
    back.keep_own()
    half = chunks // 2

    @pl.loop(1, half)
    def _(index):
        work(index, 0)

    if gathers:
        own.wait()
        wait_all(second)
        start_all(third)

    @pl.loop(half, chunks)
    def _(index):
        work(index, 0)

    if gathers:
        wait_all(third)
        start_all(fourth)
    write_arrived.start()
    slot_col = slot_col_ref[...]
    comb_ref[...] = jnp.zeros_like(comb_ref)

    def gather_back(index, first):
        for member in range(first, group):
            back.copy(index * group + member).wait_recv()
        begin = xor_of(my_chunk, index, chunk_bits) * (group * rows)
        places = lax.broadcasted_iota(jnp.int32, (slot_col.shape[0], group * rows), 1) + begin
        placing = (places == slot_col).astype(f32).astype(bf16)
        comb_ref[...] += dot(placing, returned_s[chunk_rows(index), :])

    gather_back(0, 1)

    @pl.loop(1, chunks)
    def _(index):
        gather_back(index, 0)

    load_middle.wait()
    gate = jnp.sum(jax.nn.softmax(logits_ref[...], axis=-1) * chosen_ref[...], axis=1, keepdims=True)
    out_ref[...] = middle_ref[...] + gate * comb_ref[...]
    if gathers:
        wait_all(fourth)

    @pl.loop(1, members)
    def _(apart):
        there.copy(apart).wait_send()
        back.copy(apart).wait_send()

    write_arrived.wait()


def doubled(half):
    return pltpu.VMEM((half.shape[1], 2 * half.shape[0] * half.shape[2]), bf16)


def expert_forward(
    sent, slot_col, chosen_f, logits, middle, full_in, full_out, grid_shape, identifier, column=None
):
    members = grid_shape[1]
    gathers = column is not None
    ins = [sent, slot_col, chosen_f, logits, middle, full_in, full_out]
    in_specs = [vmem_spec] * 4 + [any_spec] * 3
    outs = [
        jax.ShapeDtypeStruct(sent.shape, bf16),
        jax.ShapeDtypeStruct(middle.shape, f32),
        jax.ShapeDtypeStruct(middle.shape, f32),
    ]
    out_specs = [any_spec] + [vmem_spec] * 2
    sems = pltpu.SemaphoreType.DMA((members,))
    scratch = [
        *scratch_of([sent, middle]),
        pltpu.SemaphoreType.DMA((2,)),
        doubled(full_in),
        doubled(full_out),
        pltpu.VMEM(sent.shape, bf16),
        pltpu.VMEM(sent.shape, bf16),
        pltpu.SemaphoreType.DMA((2 * full_in.shape[0],)),
        sems,
        sems,
        sems,
        sems,
        pltpu.SemaphoreType.DMA((2 * full_in.shape[0],)),
        pltpu.SemaphoreType.DMA((2 * full_in.shape[0],)),
    ]
    if gathers:
        ins.append(column)
        in_specs.append(any_spec)
        half = (grid_shape[0] // 2, 2, grid_shape[1] // 2, 2)
        outs.append(jax.ShapeDtypeStruct((*half, *column.shape[1:]), bf16))
        out_specs.append(any_spec)
        others = pltpu.SemaphoreType.DMA((gather_copies(grid_shape)[1],))
        scratch += [pltpu.SemaphoreType.DMA, others, others]
    return pl.pallas_call(
        partial(expert_forward_kernel, grid_shape, gathers),
        in_specs=in_specs,
        out_specs=out_specs,
        out_shape=outs,
        scratch_shapes=scratch,
        compiler_params=params(identifier),
        cost_estimate=lasting(75),
        name="expert_forward",
    )(*ins)


def expert_both_kernel(
    grid_shape,
    sent_ref,
    gates_ref,
    slot_col_ref,
    chosen_ref,
    logits_ref,
    far_first_ref,
    far_second_ref,
    far_third_ref,
    win_ref,
    wout_ref,
    made_out_ref,
    d_back_ref,
    gin_out_ref,
    gout_out_ref,
    d_logits_ref,
    arrived_s,
    gates_s,
    win_s,
    wout_s,
    d_made_s,
    d_rows_s,
    act_s,
    d_pre_s,
    d_gates_s,
    d_gates_back_s,
    grads_ref,
    gin_send,
    gin_land,
    gout_send,
    gout_land,
    made_ref,
    gin_ref,
    gout_ref,
    write_sems,
    w_sems,
    *sems,
):
    far_refs = (far_first_ref, far_second_ref, far_third_ref)
    members = grid_shape[1]
    weight_sems, sum_sems = sems[9:11], sems[11:13]
    slots = sent_ref.shape[0]
    rows = slots // members
    group = chunk_of(members, rows)
    chunks = members // group
    chunk_bits = bits_of(chunks)
    hidden_units = win_s.shape[1]
    tile = min(384, hidden_units)
    place = Place(grid_shape)
    weights = Weights(place, (win_ref, wout_ref), (win_s, wout_s), w_sems, weight_sems)
    weights.start_local()
    greet(peers_along_gy(members) + [place.core_peer()])
    weights.start_remote()
    there = Exchange(members, rows, sent_ref, arrived_s, *sems[0:2])
    back = Exchange(members, rows, d_rows_s, d_back_ref, *sems[2:4])
    gates_there = Leading(members, gates_ref, gates_s, *sems[4:6])
    gates_back = Leading(members, d_gates_s, d_gates_back_s, *sems[6:8])

    for apart in send_order(members):
        gates_there.copy(apart).start()
        there.copy(apart).start()

    collected = collect(
        there.me, members, rows, far_refs, partial(third_of, members), grads_ref, sems[8]
    )
    start_all(collected)
    there.keep_own()
    gates_there.keep_own()
    weights.wait(0)
    weights.wait(1)
    wait_all(collected)
    my_chunk = there.me // group

    def work(index, first):
        for member in range(first, group):
            gates_there.copy(index * group + member).wait_recv()
            there.copy(index * group + member).wait_recv()
        chunk = xor_of(my_chunk, index, chunk_bits)
        here = pl.ds(pl.multiple_of(chunk * (group * rows), group * rows), group * rows)
        gate = jnp.concatenate(
            [gates_s[chunk * group + member].T[:rows, 0:1] for member in range(group)], axis=0
        )
        taken = arrived_s[here, :]
        grads = grads_ref[here, :].astype(f32)
        d_made = (gate * grads).astype(bf16)
        d_made_s[here, :] = d_made
        made = jnp.zeros((group * rows, taken.shape[1]), f32)
        d_rows = made
        for start in range(0, hidden_units, tile):
            units = slice(start, start + tile)
            act, slope = gelu_and_slope(dot(taken, win_s[:, units]))
            act = act.astype(bf16)
            act_s[here, units] = act
            d_pre = (dot(d_made, wout_s[:, units]) * slope).astype(bf16)
            d_pre_s[here, units] = d_pre
            d_rows = d_rows + dot(d_pre, win_s[:, units], 1, 1)
            made = made + dot(act, wout_s[:, units], 1, 1)
        d_rows_s[here, :] = d_rows.astype(bf16)
        made = made.astype(bf16)
        made_ref[here, :] = made
        d_gate = jnp.sum(grads * made.astype(f32), axis=1, keepdims=True)
        for member in range(group):
            part = jnp.broadcast_to(d_gate[member * rows : (member + 1) * rows], (rows, 128)).T
            d_gates_s[chunk * group + member, :, :rows] = part[: d_gates_s.shape[1]]
        for member in range(first, group):
            gates_back.copy(index * group + member).start()
            back.copy(index * group + member).start()

    work(0, 1)
    back.keep_own()
    gates_back.keep_own()

    @pl.loop(1, chunks)
    def _(index):
        work(index, 0)

    write_made, write_out, write_in = local_copies(
        [(made_ref, made_out_ref), (gout_ref, gout_out_ref), (gin_ref, gin_out_ref)], write_sems
    )
    write_made.start()
    weight_gradients(
        place,
        ((d_made_s, act_s), (arrived_s, d_pre_s)),
        (gout_send, gin_send),
        (gout_land, gin_land),
        (gout_ref, gin_ref),
        sum_sems,
        ([write_out], [write_in]),
    )

    @pl.loop(1, members)
    def _(apart):
        gates_back.copy(apart).wait_recv()

    row = jnp.concatenate(
        [d_gates_back_s[expert, 0:1, :rows] for expert in range(members)], axis=1
    )
    slot_col = slot_col_ref[...]
    places = lax.broadcasted_iota(jnp.int32, (slot_col.shape[0], slots), 1)
    d_gate = jnp.sum(jnp.where(places == slot_col, row, 0.0), axis=1, keepdims=True)
    d_logits_ref[...] = d_logits_of(d_gate, logits_ref[...], chosen_ref[...])

    @pl.loop(1, members)
    def _(apart):
        back.copy(apart).wait_recv()
        there.copy(apart).wait_send()
        back.copy(apart).wait_send()
        gates_there.copy(apart).wait_send()
        gates_back.copy(apart).wait_send()

    wait_all([write_made, write_out, write_in])


def expert_both(sent, gates, far_parts, slot_col, chosen_f, logits, full_in, full_out, grid_shape, identifier):
    members = grid_shape[1]
    slots = sent.shape[0]
    outs = (
        jax.ShapeDtypeStruct(sent.shape, bf16),
        jax.ShapeDtypeStruct(sent.shape, bf16),
        jax.ShapeDtypeStruct(full_in.shape, bf16),
        jax.ShapeDtypeStruct(full_out.shape, bf16),
        jax.ShapeDtypeStruct(logits.shape, bf16),
    )
    tall = pltpu.VMEM(sent.shape, bf16)
    wide = pltpu.VMEM((slots, 2 * full_in.shape[0] * full_in.shape[2]), bf16)
    half = pltpu.VMEM(full_in.shape, bf16)
    small = pltpu.VMEM(gates.shape, f32)
    weights = doubled(full_in)
    return pl.pallas_call(
        partial(expert_both_kernel, grid_shape),
        in_specs=[vmem_spec] * 5 + [any_spec] * 5,
        out_specs=[any_spec, vmem_spec, any_spec, any_spec, vmem_spec],
        out_shape=outs,
        scratch_shapes=[
            tall,
            small,
            weights,
            weights,
            tall,
            tall,
            wide,
            wide,
            small,
            small,
            tall,
            half,
            half,
            half,
            half,
            tall,
            half,
            half,
            pltpu.SemaphoreType.DMA((3,)),
            pltpu.SemaphoreType.DMA((2 * full_in.shape[0],)),
        ]
        + [pltpu.SemaphoreType.DMA((members,))] * 9
        + [pltpu.SemaphoreType.DMA((2 * full_in.shape[0],))] * 4,
        compiler_params=params(identifier),
        cost_estimate=lasting(85),
        name="expert_both",
    )(sent, gates, slot_col, chosen_f, logits, *far_parts, full_in, full_out)


def expert_backward_kernel(
    grid_shape,
    d_sent_ref,
    arrived_in_ref,
    blocks_in_ref,
    win_ref,
    wout_ref,
    d_back_ref,
    gin_out_ref,
    gout_out_ref,
    upper_ref,
    lower_ref,
    landing_ref,
    win_s,
    wout_s,
    d_arrived_s,
    d_rows_s,
    act_s,
    slope_s,
    first_s,
    up2_s,
    low2_s,
    gin_send,
    gin_land,
    gout_send,
    gout_land,
    arrived_ref,
    blocks_ref,
    gin_ref,
    gout_ref,
    move_sems,
    w_sems,
    send_sems,
    recv_sems,
    back_send_sems,
    back_recv_sems,
    *more_sems,
):
    members = grid_shape[1]
    sum_sems, weight_sems, gradient_sems = more_sems[0:2], more_sems[2:4], more_sems[4:6]
    push_sems = more_sems[6:8]
    slots = d_sent_ref.shape[0]
    rows = slots // members
    group = chunk_of(members, rows)
    chunks = members // group
    chunk_bits = chunks.bit_length() - 1
    hidden_units = win_s.shape[1]
    tile = min(768, hidden_units)
    place = Place(grid_shape)
    weights = Weights(place, (win_ref, wout_ref), (win_s, wout_s), w_sems, weight_sems)
    weights.start_local()
    moves = local_copies(
        [
            (arrived_in_ref, arrived_ref),
            (blocks_in_ref.at[:, place.c], blocks_ref.at[:, place.c]),
            (gout_ref, gout_out_ref),
            (gin_ref, gin_out_ref),
        ],
        move_sems,
    )
    start_all(moves[:2])
    greet(peers_along_gy(members) + [place.core_peer()] + place.y_peers())
    weights.start_remote()
    landings = (first_s, up2_s, low2_s, upper_ref, lower_ref, None, None)
    sums = Scatter(place, blocks_ref, landings, sum_sems, upper_ref.shape[1], blocks_in_ref)
    there = Exchange(members, rows, d_sent_ref, d_arrived_s, send_sems, recv_sems)
    back = Exchange(members, rows, d_rows_s, d_back_ref, back_send_sems, back_recv_sems)
    for apart in send_order(members):
        there.copy(apart).start()
    there.keep_own()
    my_chunk = there.me // group
    start_all(sums.copies(0))
    wait_all(moves[:2])
    weights.wait(0)

    @pl.loop(0, slots // 256)
    def _(index):
        here = pl.ds(pl.multiple_of(index * 256, 256), 256)
        taken = arrived_ref[here, :]
        for start in range(0, hidden_units, tile):
            units = slice(start, start + tile)
            act, slope = gelu_and_slope(dot(taken, win_s[:, units]))
            act_s[here, units] = act.astype(bf16)
            slope_s[here, units] = slope.astype(bf16)

    wait_all(sums.copies(0))
    sums.add(0)
    start_all(sums.copies(1))
    weights.wait(1)

    def chunk_rows(index):
        start = xor_of(my_chunk, index, chunk_bits) * (group * rows)
        return pl.ds(pl.multiple_of(start, group * rows), group * rows)

    def work(index, first):
        for member in range(first, group):
            there.copy(index * group + member).wait_recv()
        here = chunk_rows(index)
        taken = d_arrived_s[here, :]
        total = jnp.zeros((group * rows, taken.shape[1]), f32)
        for start in range(0, hidden_units, tile):
            units = slice(start, start + tile)
            d_pre = (dot(taken, wout_s[:, units]) * slope_s[here, units].astype(f32)).astype(bf16)
            slope_s[here, units] = d_pre
            total = total + dot(d_pre, win_s[:, units], 1, 1)
        d_rows_s[here, :] = total.astype(bf16)
        for member in range(first, group):
            back.copy(index * group + member).start()

    work(0, 1)
    back.keep_own()

    @pl.loop(1, chunks)
    def _(index):
        work(index, 0)

    wait_all(sums.copies(1))
    sums.add(1)
    start_all(sums.copies(2))
    pushed = push_blocks(place, gout_ref, landing_ref, push_sems, 0)
    weight_gradients(
        place,
        ((d_arrived_s, act_s), (arrived_ref, slope_s)),
        (gout_send, gin_send),
        (gout_land, gin_land),
        (gout_ref, gin_ref),
        gradient_sems,
        ([*pushed, moves[2]], [moves[3]]),
    )
    wait_all(sums.copies(2))
    sums.add(2)

    @pl.loop(1, members)
    def _(apart):
        back.copy(apart).wait_recv()
        there.copy(apart).wait_send()
        back.copy(apart).wait_send()

    wait_all(pushed + moves[2:])


def expert_backward(d_sent, arrived, blocks, full_in, full_out, grid_shape, identifier):
    members = grid_shape[1]
    landings = whole_blocks(blocks.shape, blocks.shape[4] // 2)
    outs = (
        jax.ShapeDtypeStruct(d_sent.shape, bf16),
        jax.ShapeDtypeStruct(full_in.shape, bf16),
        jax.ShapeDtypeStruct(full_out.shape, bf16),
        *[jax.ShapeDtypeStruct(one, bf16) for one in landings[3:5]],
        landing_of(full_out, cut_of(full_out)),
    )
    slots = d_sent.shape[0]
    sems = pltpu.SemaphoreType.DMA((members,))
    return pl.pallas_call(
        partial(expert_backward_kernel, grid_shape),
        in_specs=[vmem_spec] + [any_spec] * 4,
        out_specs=[vmem_spec] + [any_spec] * 2 + [vmem_spec] * 2 + [any_spec],
        out_shape=outs,
        scratch_shapes=[
            doubled(full_in),
            doubled(full_out),
            pltpu.VMEM(d_sent.shape, bf16),
            pltpu.VMEM(d_sent.shape, bf16),
            pltpu.VMEM((slots, 2 * full_in.shape[0] * full_in.shape[2]), bf16),
            pltpu.VMEM((slots, 2 * full_in.shape[0] * full_in.shape[2]), bf16),
            *[pltpu.VMEM(one, bf16) for one in landings[:3]],
            *[pltpu.VMEM(full_in.shape, bf16)] * 4,
            *scratch_of([arrived, blocks, full_in, full_out]),
            pltpu.SemaphoreType.DMA((4,)),
            pltpu.SemaphoreType.DMA((2 * full_in.shape[0],)),
            sems,
            sems,
            sems,
            sems,
            *[pltpu.SemaphoreType.DMA((scatter_copies(grid_shape),))] * 2,
            *[pltpu.SemaphoreType.DMA((2 * full_in.shape[0],))] * 4,
            *[pltpu.SemaphoreType.DMA((full_in.shape[0] - 1,))] * 2,
        ],
        compiler_params=params(10 + identifier),
        cost_estimate=lasting(85),
        name="expert_backward",
    )(d_sent, arrived, blocks, full_in, full_out)


def emit_kernel(
    table_shape,
    at_ref,
    gin_ref,
    gin_first_ref,
    gin_second_ref,
    gin_up_ref,
    gout_ref,
    gout_first_ref,
    gout_second_ref,
    gout_up_ref,
    result_ref,
    grad_ref,
    packed_ref,
    small_ref,
    gin_out_ref,
    gout_out_ref,
    result_out_ref,
    grad_out_ref,
    wq_ref,
    wk_ref,
    wv_ref,
    wo_ref,
    router_out_ref,
    gga_ref,
    ggf_ref,
    table_ref,
):
    step = pl.program_id(0)

    def landed(ref):
        total = ref[0].astype(f32)
        for index in range(1, ref.shape[0]):
            total = total + ref[index].astype(f32)
        return total

    steps = pl.num_programs(0)
    for own, first, second, up, out, early_steps in (
        (gin_ref, gin_first_ref, gin_second_ref, gin_up_ref, gin_out_ref, steps // 2),
        (gout_ref, gout_first_ref, gout_second_ref, gout_up_ref, gout_out_ref, steps // 3 * 2),
    ):
        out[0, 0] = own[0].astype(f32) + jnp.where(step < early_steps, landed(first), landed(second))
        out[1, 0] = up[...].astype(f32)

    @pl.when(step < 4)
    def _():
        result_out_ref[...] = result_ref[...]
        grad_out_ref[...] = grad_ref[...]

    @pl.when(step == 0)
    def _():
        layers, tall, wide = wq_ref.shape
        for which, ref in enumerate((wq_ref, wk_ref, wv_ref, wo_ref)):
            ref[...] = packed_ref[:, :, which * wide : (which + 1) * wide]
        buckets_count, heads = table_shape
        width = small_ref.shape[1]
        experts = (small_ref.shape[0] - 2 * layers - heads) // layers
        base = layers * experts
        gga_ref[...] = small_ref[base : base + layers, :]
        ggf_ref[...] = small_ref[base + layers : base + 2 * layers, :]
        base = base + 2 * layers
        table_ref[...] = small_ref[base : base + heads, :buckets_count]
        for layer in range(layers):
            row = small_ref[pl.ds(layer * experts + at_ref[1], 1), :]
            row = jnp.broadcast_to(row, (8, width))
            mine = pltpu.roll(row, lax.rem(width - at_ref[0] * tall, width), 1)
            router_out_ref[layer] = mine[0:1, :tall]


def emit(at, grads_in, grads_out, result, grad_now, packed, small, table_shape):
    layers, tall, lanes = packed.shape
    gin, gin_first, gin_second, gin_up = grads_in
    gout, gout_first, gout_second, gout_up = grads_out
    _, rows, units = gin.shape
    steps = 6
    tile = rows // steps
    wide = lanes // 4
    whole_in = [packed, small]
    passed = pl.BlockSpec((result.shape[0] // 4, result.shape[1]), lambda i, at: (jnp.minimum(i, 3), 0))
    own = pl.BlockSpec((1, tile, units), lambda i, at: (at[2], i, 0))
    up = pl.BlockSpec((tile, units), lambda i, at: (i, 0))

    def land(array, index):
        return pl.BlockSpec((array.shape[0], tile, units), lambda i, at: (0, index(i), 0))

    out = pl.BlockSpec((layers, 1, tile, units), lambda i, at: (0, 0, i, 0))
    expert = jax.ShapeDtypeStruct((layers, 1, rows, units), f32)
    square = jax.ShapeDtypeStruct((layers, tall, wide), f32)
    gain = jax.ShapeDtypeStruct((layers, small.shape[1]), f32)
    rest = [square] * 4
    rest += [jax.ShapeDtypeStruct((layers, 1, tall), f32), gain, gain]
    rest.append(jax.ShapeDtypeStruct(table_shape[::-1], f32))

    def expert_specs(first_land, second_land):
        early_steps = first_land.shape[1] // tile
        return [
            own,
            land(first_land, lambda i: jnp.minimum(i, early_steps - 1)),
            land(second_land, lambda i: jnp.maximum(i - early_steps, 0)),
            up,
        ]

    return pl.pallas_call(
        partial(emit_kernel, table_shape),
        grid_spec=pltpu.PrefetchScalarGridSpec(
            num_scalar_prefetch=1,
            grid=(steps,),
            in_specs=expert_specs(gin_first, gin_second)
            + expert_specs(gout_first, gout_second)
            + [passed, passed]
            + whole_of(whole_in),
            out_specs=[out, out, passed, passed] + whole_of(rest),
        ),
        out_shape=[expert, expert] + [jax.ShapeDtypeStruct(result.shape, f32)] * 2 + rest,
        compiler_params=params(),
        cost_estimate=lasting(7),
        name="emit",
    )(at, *grads_in, *grads_out, result, grad_now, *whole_in)


def body(
    hidden_in,
    route,
    piece_ids,
    buckets,
    rel_table,
    gain_attn,
    gain_ffn,
    w_query,
    w_key,
    w_value,
    w_output,
    w_router,
    w_in,
    w_out,
    cotangent,
):
    count_x = lax.axis_size("gx")
    count_y = lax.axis_size("gy")
    seq_len, width = hidden_in.shape
    layers = w_query.shape[0]
    heads = rel_table.shape[1]
    experts = w_router.shape[2] * count_y
    capacity = 2 * seq_len // experts
    wide_router = w_router.shape[2]
    tall, wide = w_query.shape[1], w_query.shape[2]
    grid_shape = (count_x, count_y)
    same_core = [list(range(core, count_x, 2)) for core in range(2)]
    router_rows = jnp.pad(
        w_router.transpose(0, 2, 1), ((0, 0), (0, tile_rows - wide_router), (0, 4 * wide - tall))
    )
    buckets_row = jnp.pad(buckets, (0, 1), constant_values=-1)[None, :]
    mats, router, later, bias, slot_col, slot_row, chosen_f, spread, far_part = start(
        (w_query, w_key, w_value, w_output),
        router_rows,
        buckets_row,
        rel_table.T,
        piece_ids,
        route,
        cotangent,
        grid_shape,
    )
    gain_attn_f = gain_attn.astype(f32)
    gain_ffn_f = gain_ffn.astype(f32)

    hidden = hidden_in
    kept = []
    blocks = None
    far_parts = [far_part]
    for layer in range(layers):
        last = layer == layers - 1
        gains = (gain_attn_f[layer][None], gain_ffn_f[layer][None])
        mats, router, q, k, v, attended, lse, middle, logits, sent, *gates, far_part = attention_forward(
            hidden,
            gains[0],
            gains[1],
            (slot_row, slot_col, chosen_f),
            bias,
            grid_shape,
            1 + layer,
            spread,
            last,
            blocks=blocks,
            mats=(mats, router) if blocks is None else None,
        )
        far_parts.append(far_part)
        full_in, full_out = (
            lax.all_gather(one[layer, 0], "gx", axis=0, tiled=False, axis_index_groups=same_core)
            for one in (w_in, w_out)
        )
        state = (hidden, gains, (mats, router), (q, k, v), attended, lse, middle, logits)
        if last:
            made, d_back, grad_in_full, grad_out_full, d_logits = expert_both(
                sent, gates[0], far_parts, slot_col, chosen_f, logits, full_in, full_out, grid_shape, 7
            )
            kept.append(state)
        else:
            arrived, combined, hidden, blocks = expert_forward(
                sent,
                slot_col,
                chosen_f,
                logits,
                middle,
                full_in,
                full_out,
                grid_shape,
                5 + layer,
                column=later[layer],
            )
            kept.append(state + (combined, arrived, full_in, full_out))

    grad_now = cotangent
    parts = []
    partials = []
    returned = []
    for layer in reversed(range(layers)):
        last = layer == layers - 1
        (prior, gains, mats, q_k_v, attended, lse, middle, logits) = kept[layer][:8]
        if not last:
            arrived, full_in, full_out = kept[layer][9:]
            d_back, grad_in_full, grad_out_full, upper, lower, out_first = expert_backward(
                d_sent, arrived, parts[-1][0], full_in, full_out, grid_shape, layer
            )
            partials.append((upper, lower[:1]))
        experts_parts = []
        if layer > 0:
            experts_parts = [
                lax.psum_scatter(
                    one, "gx", scatter_dimension=0, tiled=False, axis_index_groups=same_core
                )
                for one in (grad_in_full, grad_out_full)
            ]
        below = None
        if layer > 0:
            below = (kept[layer - 1][8], slot_row, chosen_f, kept[layer - 1][7])
        got = attention_backward(
            d_back,
            slot_col,
            d_logits,
            grad_now,
            middle,
            prior,
            gains,
            mats,
            q_k_v,
            attended,
            bias,
            lse,
            grid_shape,
            below=below,
            after=[array for part in parts for array in part[4]],
            made=made,
            returns=last,
            push=(grad_out_full, grad_in_full) if layer == 0 else None,
            identifier=18 + layer,
        )
        grad_now, blocked, gwr, gga, ggf, offset_sums = got[:6]
        if layer > 0:
            d_sent, d_logits = got[6:8]
        if layer == 0:
            *got, out_second, in_first = got
        returned.append(got[-1])
        parts.append((blocked, gwr, gga, ggf, experts_parts, offset_sums))
    parts = parts[::-1]
    buckets_count = rel_table.shape[0]
    smalls = [part[which] for which in (1, 2, 3, 5) for part in parts]
    top = kept[-1]
    packed, small, hidden_out, in_second = final_sums(
        parts[0][0],
        partials[::-1],
        smalls + [buckets_row],
        (slot_col, chosen_f, top[7], top[6]),
        returned,
        grad_in_full,
        grid_shape,
        buckets_count,
    )
    first, second = lax.axis_index("gx"), lax.axis_index("gy")
    grad_in, grad_out, hidden_out, grad_now, gwq, gwk, gwv, gwo, gwr, gga_all, ggf_all, d_table = emit(
        jnp.stack([first, second, first // 2]).astype(jnp.int32),
        (grad_in_full, in_first, in_second, parts[1][4][0]),
        (grad_out_full, out_first, out_second, parts[1][4][1]),
        hidden_out,
        grad_now,
        packed,
        small,
        rel_table.shape,
    )
    return (
        hidden_out,
        grad_now,
        d_table.T,
        gga_all,
        ggf_all,
        gwq,
        gwk,
        gwv,
        gwo,
        gwr.transpose(0, 2, 1),
        grad_in,
        grad_out,
    )


def solution(mesh):
    rows = P(("gx", "gy"), None)
    square = P(None, "gx", "gy")
    expert = P(None, "gy", None, "gx")
    return jax.shard_map(
        body,
        mesh=mesh,
        in_specs=(rows, rows, P(("gx", "gy")), P(), P(), P(), P())
        + (square,) * 5
        + (expert, expert, rows),
        out_specs=(rows, rows, P(), P(), P()) + (square,) * 5 + (expert, expert),
        check_vma=False,
    )
```

```python
from functools import partial

import jax
import jax.numpy as jnp
from jax import lax
from jax.experimental import pallas as pl
from jax.experimental.pallas import tpu as pltpu
from jax.sharding import PartitionSpec as P

eps_norm = 1e-06
highest = lax.Precision.HIGHEST
f32 = jnp.float32
bf16 = jnp.bfloat16
masked_out = -1e30
tile_rows = 16
MESH = pl.DeviceIdType.MESH
vmem_spec = pl.BlockSpec(memory_space=pltpu.VMEM)
any_spec = pl.BlockSpec(memory_space=pl.ANY)
vmem_bytes = 60 * 1024 * 1024


def whole(shape):
    zeros = (0,) * len(shape)
    return pl.BlockSpec(shape, lambda *_: zeros, pipeline_mode=pl.Buffered(1))


def whole_of(arrays):
    return [whole(array.shape) for array in arrays]


def params(identifier=None):
    if identifier is None:
        return pltpu.CompilerParams(vmem_limit_bytes=vmem_bytes)
    return pltpu.CompilerParams(
        vmem_limit_bytes=vmem_bytes, collective_id=identifier, has_side_effects=True
    )


def lasting(microseconds):
    return pl.CostEstimate(
        flops=int(microseconds * 1e9), bytes_accessed=1 << 20, transcendentals=0
    )


def dot(lhs, rhs, lhs_dim=1, rhs_dim=0):
    return lax.dot_general(
        lhs, rhs, (((lhs_dim,), (rhs_dim,)), ((), ())), preferred_element_type=f32
    )


def rms_factor(hidden):
    return lax.rsqrt(jnp.mean(hidden * hidden, axis=-1, keepdims=True) + eps_norm)


def rms_pull(hidden, gain_row, d_normed):
    factor = rms_factor(hidden)
    scaled = gain_row * d_normed
    inner = jnp.mean(hidden * scaled, axis=-1, keepdims=True)
    d_hidden = factor * scaled - hidden * (factor * factor * factor * inner)
    d_gain = jnp.sum(d_normed * hidden * factor, axis=0, keepdims=True)
    return d_hidden, d_gain


def xor_of(index, other, bits):
    total = 0
    for bit in range(bits):
        power = 1 << bit
        total = total + ((index // power + other // power) % 2) * power
    return total


def placing_rows(slot_row, slots):
    places = lax.broadcasted_iota(jnp.int32, (slots, slot_row.shape[1]), 0)
    return (places == slot_row).astype(f32).astype(bf16)


def placing_cols(slot_col, slots):
    places = lax.broadcasted_iota(jnp.int32, (slot_col.shape[0], slots), 1)
    return (places == slot_col).astype(f32).astype(bf16)


def greet(peers):
    barrier = pltpu.get_barrier_semaphore()
    for peer in peers:
        pl.semaphore_signal(barrier, inc=1, device_id=peer, device_id_type=MESH)
    pl.semaphore_wait(barrier, len(peers))


def bits_of(count):
    return count.bit_length() - 1


class Place:
    def __init__(self, grid_shape):
        self.count_y, self.count_z = grid_shape[0] // 2, grid_shape[1] // 2
        first, second = lax.axis_index("gx"), lax.axis_index("gy")
        self.c, self.y = first % 2, first // 2
        self.x, self.z = second % 2, second // 2

    def core_peer(self):
        return {"gx": self.y * 2 + 1 - self.c}

    def x_peer(self):
        return {"gy": self.z * 2 + 1 - self.x}

    def y_at(self, apart):
        return xor_of(self.y, apart, bits_of(self.count_y))

    def y_peer(self, apart):
        return {"gx": self.y_at(apart) * 2 + self.c}

    def y_peers(self):
        return [self.y_peer(apart) for apart in range(1, self.count_y)]

    def z_at(self, apart):
        return xor_of(self.z, apart, bits_of(self.count_z))

    def z_peer(self, apart):
        return {"gy": self.z_at(apart) * 2 + self.x}

    def z_peers(self):
        return [self.z_peer(apart) for apart in range(1, self.count_z)]


def send(src, dst, sems, index, peer):
    return pltpu.make_async_remote_copy(
        src_ref=src,
        dst_ref=dst,
        send_sem=sems[0].at[index],
        recv_sem=sems[1].at[index],
        device_id=peer,
        device_id_type=MESH,
    )


def start_all(copies):
    for copy in copies:
        copy.start()


def wait_all(copies):
    for copy in copies:
        copy.wait()


def local_copies(pairs, sems, base=0):
    return [
        pltpu.make_async_copy(src, dst, sems.at[base + index])
        for index, (src, dst) in enumerate(pairs)
    ]


def scratch_of(arrays):
    return [pltpu.VMEM(array.shape, array.dtype) for array in arrays]


def gather_z(place, src, landing, sems):
    return [
        send(src, landing, sems, apart - 1, place.z_peer(apart)) for apart in range(1, place.count_z)
    ]


def gather_copies(grid_shape):
    return grid_shape[1] // 2 - 1, 2 * (grid_shape[0] // 2 - 1) + 3


def gather_second(place, column, full, split, sems):
    y, c, x = place.y, place.c, place.x
    upper, lower = pl.ds(0, split), pl.ds(split, full.shape[4] - split)
    copies = [
        send(column.at[:, upper], full.at[y, c, :, x, upper], sems, 0, place.x_peer())
    ]
    for apart in range(1, place.count_y):
        copies.append(
            send(column.at[:, lower], full.at[y, c, :, x, lower], sems, apart, place.y_peer(apart))
        )
    return copies


def gather_third(place, full, split, sems):
    y, c, x = place.y, place.c, place.x
    upper, lower = pl.ds(0, split), pl.ds(split, full.shape[4] - split)
    base = place.count_y
    ref = full.at[:, c, :, x, lower]
    copies = [send(ref, ref, sems, base, place.x_peer())]
    ref = full.at[y, c, :, :, upper]
    for apart in range(1, place.count_y):
        copies.append(send(ref, ref, sems, base + apart, place.y_peer(apart)))
    return copies


def gather_core(place, full, sems):
    ref = full.at[:, place.c]
    return [send(ref, ref, sems, 2 * place.count_y, place.core_peer())]


def whole_blocks(shape, split):
    count_y, _, count_z, _, tall, lanes = shape
    low = tall - split
    return [
        (count_y, count_z, 2, tall, lanes),
        (count_y - 1, count_z, 2, split, lanes),
        (count_y, count_z, low, lanes),
        (count_z, split, lanes),
        (count_y - 1, count_z, low, lanes),
        (count_z - 1, split, lanes),
        (count_z - 1, low, lanes),
    ]


def scatter_copies(grid_shape):
    return 1 + 2 * (grid_shape[0] // 2) + 2 * (grid_shape[1] // 2 - 1)


def add_low(dst, dst_at, *terms):
    total = terms[0].astype(f32)
    for term in terms[1:]:
        total = total + term.astype(f32)
    dst[dst_at] = total.astype(bf16)


class Scatter:
    def __init__(self, place, src, landings, sems, split, source=None):
        self.place, self.src, self.sems = place, src, sems
        self.source = src if source is None else source
        self.first, self.up2, self.low2, self.up3, self.low3, self.up4, self.low4 = landings
        tall = src.shape[4]
        self.upper, self.lower = pl.ds(0, split), pl.ds(split, tall - split)

    def copies(self, stage):
        at, sems = self.place, self.sems
        count_y, count_z = at.count_y, at.count_z
        if stage == 0:
            return [send(self.source.at[:, 1 - at.c], self.first, sems, 0, at.core_peer())]
        if stage == 1:
            copies = [send(self.first.at[:, :, 1 - at.x, self.lower], self.low2, sems, 1, at.x_peer())]
            for apart in range(1, count_y):
                src = self.first.at[at.y_at(apart), :, :, self.upper]
                dst = self.up2.at[apart - 1]
                copies.append(send(src, dst, sems, 1 + apart, at.y_peer(apart)))
            return copies
        if stage == 2:
            base = 1 + count_y
            copies = [send(self.up2.at[0, :, 1 - at.x], self.up3, sems, base, at.x_peer())]
            for apart in range(1, count_y):
                src, dst = self.low2.at[at.y_at(apart)], self.low3.at[apart - 1]
                copies.append(send(src, dst, sems, base + apart, at.y_peer(apart)))
            return copies
        base = 2 * count_y
        copies = []
        for apart in range(1, count_z):
            there = at.z_at(apart)
            for src, dst, more in (
                (self.up3.at[there], self.up4.at[apart - 1], 0),
                (self.low3.at[0, there], self.low4.at[apart - 1], 1),
            ):
                index = base + 2 * apart - 1 + more
                copies.append(send(src, dst, sems, index, at.z_peer(apart)))
        return copies

    def add(self, stage):
        at = self.place
        count_y, count_z = at.count_y, at.count_z
        if stage == 0:

            @pl.loop(0, count_y * count_z)
            def _(index):
                y, z = index // count_z, index % count_z
                add_low(self.first, (y, z), self.first[y, z], self.src[y, at.c, z])

        elif stage == 1:

            @pl.loop(0, count_z)
            def _(z):
                for x in range(2):
                    terms = [self.up2[apart, z, x] for apart in range(count_y - 1)]
                    add_low(self.up2, (0, z, x), self.first[at.y, z, x, self.upper], *terms)

                @pl.loop(0, count_y)
                def _(y):
                    add_low(self.low2, (y, z), self.first[y, z, at.x, self.lower], self.low2[y, z])

        elif stage == 2:

            @pl.loop(0, count_z)
            def _(z):
                add_low(self.up3, (z,), self.up3[z], self.up2[0, z, at.x])
                terms = [self.low3[apart, z] for apart in range(count_y - 1)]
                add_low(self.low3, (0, z), self.low2[at.y, z], *terms)

    def result(self):
        at = self.place
        upper, lower = self.up3[at.z].astype(f32), self.low3[0, at.z].astype(f32)
        for apart in range(at.count_z - 1):
            upper = upper + self.up4[apart].astype(f32)
            lower = lower + self.low4[apart].astype(f32)
        return upper, lower


class SmallSum:
    def __init__(self, grid_shape, totals, landing, sems):
        self.totals, self.landing, self.sems = totals, landing, sems
        self.peers = []
        for name, count in (("gx", grid_shape[0]), ("gy", grid_shape[1])):
            me = lax.axis_index(name)
            for bit in range(bits_of(count)):
                self.peers.append({name: xor_of(me, 1 << bit, bits_of(count))})
        self.done = 0

    def copy(self):
        step = self.done
        return send(self.totals.at[step], self.landing.at[step], self.sems, step, self.peers[step])

    def begin(self):
        self.copy().start()

    def advance(self):
        if self.done == len(self.peers):
            return
        self.copy().wait()
        step = self.done
        self.totals[step + 1] = self.totals[step] + self.landing[step]
        self.done += 1
        if self.done < len(self.peers):
            self.begin()


def small_steps(grid_shape):
    return bits_of(grid_shape[0]) + bits_of(grid_shape[1])


def lane_parts(lanes):
    return lanes // 128 if lanes % 128 == 0 else 1


def lane_part(ref, part, parts):
    if parts == 1:
        return ref
    lanes = ref.shape[-1] // parts
    return ref.at[..., pl.ds(part * lanes, lanes)]


def final_kernel(grid_shape, layers, buckets_count, *refs):
    refs = list(refs)
    take = refs.pop
    partial_refs = [(take(0), take(0)) for _ in range(layers - 1)]
    router_refs, gga_refs, ggf_refs, offset_refs = ([take(0) for _ in range(layers)] for _ in range(4))
    buckets_ref, slot_col_ref, chosen_ref, logits_ref = (take(0) for _ in range(4))
    blocks_in_ref, middle_in_ref = take(0), take(0)
    first_ref, second_ref, push_ref = take(0), take(0), take(0)
    packed_ref, small_out_ref, result_ref, landing_ref = (take(0) for _ in range(4))
    blocks_ref, middle_ref, move_sems = (take(0) for _ in range(3))
    landings = [take(0) for _ in range(7)]
    z_landings = [(take(0), take(0)) for _ in range(layers - 1)]
    totals, landing, returned_s = take(0), take(0), take(0)
    sems = [(take(0), take(0)) for _ in range(layers)]
    small_sems, collect_sems, push_sems = (take(0), take(0)), take(0), (take(0), take(0))
    place = Place(grid_shape)
    tall = packed_ref.shape[1]
    split = tall // 2
    members = grid_shape[1]
    slots = returned_s.shape[0]
    upper_layers = []
    for layer in range(1, layers):
        upper, lower = partial_refs[layer - 1]
        places = (None, None, None, upper, lower, *z_landings[layer - 1])
        upper_layers.append(Scatter(place, blocks_ref, places, sems[layer], split))
    parts = lane_parts(packed_ref.shape[2])
    lowest = [
        Scatter(
            place,
            lane_part(blocks_ref, part, parts),
            [lane_part(landing_part, part, parts) for landing_part in landings],
            (sems[0][0].at[part], sems[0][1].at[part]),
            split,
            lane_part(blocks_in_ref, part, parts),
        )
        for part in range(parts)
    ]

    def step(stage):
        for one in lowest:
            wait_all(one.copies(stage))
            one.add(stage)
            start_all(one.copies(stage + 1))

    c = place.c
    moves = local_copies(
        [(blocks_in_ref.at[:, c], blocks_ref.at[:, c]), (middle_in_ref, middle_ref)], move_sems
    )
    start_all(moves)
    collected = collect(
        lax.axis_index("gy"),
        members,
        slots // members,
        (first_ref, second_ref),
        lambda apart: int(apart not in early(members)),
        returned_s,
        collect_sems,
    )
    start_all(collected)
    greet([place.core_peer(), place.x_peer()] + place.y_peers() + place.z_peers())
    for one in lowest:
        start_all(one.copies(0))
    for one in upper_layers:
        start_all(one.copies(3))

    experts = router_refs[0].shape[0]
    totals[0] = jnp.zeros(totals.shape[1:], f32)
    row = 0
    for refs_of in (router_refs, gga_refs, ggf_refs):
        for ref in refs_of:
            totals[0, row : row + ref.shape[0], :] = ref[...]
            row += ref.shape[0]
    heads = offset_refs[0].shape[0]
    offsets = offset_refs[0][...]
    for ref in offset_refs[1:]:
        offsets = offsets + ref[...]
    in_bucket = (
        lax.broadcasted_iota(jnp.int32, (buckets_count, offsets.shape[1]), 0) == buckets_ref[...]
    ).astype(f32)
    totals[0, row : row + heads, :buckets_count] = lax.dot_general(
        offsets, in_bucket, (((1,), (1,)), ((), ())), precision=highest, preferred_element_type=f32
    )
    small = SmallSum(grid_shape, totals, landing, small_sems)
    small.begin()
    wait_all(moves)
    step(0)
    small.advance()
    wait_all(collected)
    placing = placing_cols(slot_col_ref[...], slots)
    gate = jnp.sum(jax.nn.softmax(logits_ref[...], axis=-1) * chosen_ref[...], axis=1, keepdims=True)
    result_ref[...] = middle_ref[...] + gate * dot(placing, returned_s[...])
    small.advance()
    step(1)
    small.advance()

    def finish(layer, one, lanes=slice(None)):
        for part, rows in zip(one.result(), (slice(0, split), slice(split, tall))):
            packed_ref[layer, rows, lanes] = part

    for layer, one in enumerate(upper_layers):
        wait_all(one.copies(3))
        finish(layer + 1, one)
    step(2)
    pushed = push_blocks(
        place, push_ref, landing_ref, push_sems, push_ref.shape[1] - landing_ref.shape[1]
    )
    start_all(pushed)
    while small.done < len(small.peers):
        small.advance()
    small_out_ref[...] = totals[len(small.peers)]
    each = packed_ref.shape[2] // parts
    for part, one in enumerate(lowest):
        wait_all(one.copies(3))
        finish(0, one, slice(part * each, (part + 1) * each))
    wait_all(pushed)


def final_sums(blocks, partials, smalls, finishing, returned, push, grid_shape, buckets_count):
    layers = len(partials) + 1
    shape = blocks.shape
    tall = shape[4]
    width = finishing[-1].shape[1]
    landings = [pltpu.VMEM(one, bf16) for one in whole_blocks(shape, tall // 2)]
    steps = small_steps(grid_shape)
    rows = sum(one.shape[0] for one in smalls[: 3 * layers]) + smalls[3 * layers].shape[0]
    small_shape = (rows, width)
    sems = pltpu.SemaphoreType.DMA((scatter_copies(grid_shape),))
    first_sems = pltpu.SemaphoreType.DMA((lane_parts(shape[5]), scatter_copies(grid_shape)))
    small_sems = pltpu.SemaphoreType.DMA((steps,))
    outs = [jax.ShapeDtypeStruct((layers, tall, shape[5]), f32)]
    outs += [jax.ShapeDtypeStruct(small_shape, f32), jax.ShapeDtypeStruct(finishing[-1].shape, f32)]
    outs.append(landing_of(push, push.shape[1] - push.shape[1] // 2))
    ins = [*[array for pair in partials for array in pair], *smalls, *finishing[:3]]
    moved = [blocks, finishing[-1]]
    return pl.pallas_call(
        partial(final_kernel, grid_shape, layers, buckets_count),
        in_specs=[vmem_spec] * len(ins) + [any_spec] * 5,
        out_specs=[vmem_spec] * (len(outs) - 1) + [any_spec],
        out_shape=outs,
        scratch_shapes=scratch_of(moved)
        + [pltpu.SemaphoreType.DMA((2,))]
        + landings
        + landings[5:] * (layers - 1)
        + [pltpu.VMEM((steps + 1, *small_shape), f32), pltpu.VMEM((steps, *small_shape), f32)]
        + [pltpu.VMEM(returned[0].shape, bf16)]
        + [first_sems, first_sems]
        + [sems, sems] * (layers - 1)
        + [small_sems, small_sems, pltpu.SemaphoreType.DMA((grid_shape[1],))]
        + [pltpu.SemaphoreType.DMA((grid_shape[0] // 2 - 1,))] * 2,
        compiler_params=params(24),
        cost_estimate=lasting(60),
        name="final_sums",
    )(*ins, *moved, *returned, push)


def unblock(grid_shape, blocks_ref, mats_ref, router_ref):
    count_x, count_y = grid_shape
    tall = mats_ref.shape[1] // count_x
    wide = mats_ref.shape[2] // count_y
    router_rows = []
    for first in range(count_x):
        spots = [(first // 2, first % 2, second // 2, second % 2) for second in range(count_y)]
        rows = slice(first * tall, (first + 1) * tall)
        for which in range(4):
            lanes = slice(which * wide, (which + 1) * wide)
            mats_ref[which, rows, :] = jnp.concatenate(
                [blocks_ref[(*spot, slice(0, tall), lanes)] for spot in spots], axis=1
            )
        router_rows.append(
            jnp.concatenate(
                [blocks_ref[(*spot, slice(tall, tall + 1), slice(0, tall))] for spot in spots],
                axis=0,
            )
        )
    router_ref[...] = jnp.concatenate(router_rows, axis=1)


def turned(row):
    return jnp.broadcast_to(row, (128, row.shape[1])).T[:, 0:1]


def start_kernel(
    grid_shape,
    wq_ref,
    wk_ref,
    wv_ref,
    wo_ref,
    router_rows_ref,
    buckets_ref,
    table_ref,
    piece_row_ref,
    route_row_ref,
    cotangent_ref,
    mats_ref,
    router_ref,
    later_ref,
    bias_out_ref,
    slot_col_ref,
    slot_row_ref,
    chosen_ref,
    spread_out_ref,
    far_ref,
    bias_ref,
    spread_ref,
    write_sems,
    full_s,
    column_s,
    spread_send,
    spread_recv,
    later_send,
    later_recv,
    z_send,
    z_recv,
    send_sems,
    recv_sems,
):
    place = Place(grid_shape)
    layers, tall, wide = wq_ref.shape
    split = tall // 2
    y, c, z, x = place.y, place.c, place.z, place.x

    def packed(layer):
        return jnp.concatenate([ref[layer] for ref in (wq_ref, wk_ref, wv_ref, wo_ref)], axis=1)

    column_s[z, :tall] = packed(0)
    column_s[z, tall:] = router_rows_ref[0]
    members = grid_shape[1]
    spread = Exchange(
        members, spread_ref.shape[0] // members, spread_ref, far_ref, spread_send, spread_recv
    )
    spread_copies = [spread.copy(apart) for apart in in_third(members, 0)]
    mine_here = spread.block(spread.me)
    half_heads = bias_ref.shape[0] // 2
    parts = [pl.ds(0, half_heads), pl.ds(half_heads, half_heads)]
    write_spread, write_own, *write_bias = local_copies(
        [(spread_ref, spread_out_ref), (spread_ref.at[mine_here, :], far_ref.at[mine_here, :])]
        + [(bias_ref.at[part], bias_out_ref.at[part]) for part in parts],
        write_sems,
    )
    greet(
        [place.core_peer(), place.x_peer()]
        + place.y_peers()
        + place.z_peers()
        + [spread.peer(apart) for apart in in_third(members, 0)]
    )
    first = gather_z(place, column_s.at[z], column_s.at[z], (z_send, z_recv))
    start_all(first)
    along_z = []
    for layer in range(1, layers):
        later_ref[layer - 1, z, :tall] = packed(layer)
        later_ref[layer - 1, z, tall:] = router_rows_ref[layer]
        mine = later_ref.at[layer - 1, z]
        along_z += gather_z(place, mine, mine, (later_send.at[layer - 1], later_recv.at[layer - 1]))

    seq_len, experts = chosen_ref.shape
    capacity = 2 * seq_len // experts
    heads = bias_ref.shape[0]
    buckets_count = table_ref.shape[1]
    in_bucket = (
        lax.broadcasted_iota(jnp.int32, (buckets_count, 2 * seq_len), 0) == buckets_ref[...]
    )
    offsets = dot(table_ref[...], in_bucket.astype(f32).astype(bf16))
    key_pos = lax.broadcasted_iota(jnp.int32, (seq_len, seq_len), 0)
    query_pos = lax.broadcasted_iota(jnp.int32, (seq_len, seq_len), 1)
    route_row, piece_row = route_row_ref[...], piece_row_ref[...]
    route_col, piece_col = turned(route_row), turned(piece_row)
    chosen = (lax.broadcasted_iota(jnp.int32, (seq_len, experts), 1) == route_col).astype(f32)
    chosen_t = (lax.broadcasted_iota(jnp.int32, (experts, seq_len), 0) == route_row).astype(f32)
    chosen_ref[...] = chosen
    earlier = (key_pos < query_pos).astype(f32).astype(bf16)
    before_t = dot(chosen_t.astype(bf16), earlier)
    rank_row = jnp.sum(before_t * chosen_t, axis=0, keepdims=True)
    slot_row_ref[...] = route_row * capacity + rank_row.astype(jnp.int32)
    later = (key_pos > query_pos).astype(f32).astype(bf16)
    before = dot(later, chosen.astype(bf16))
    rank_col = jnp.sum(before * chosen, axis=1, keepdims=True)
    slot_col_ref[...] = route_col * capacity + rank_col.astype(jnp.int32)
    placing = placing_rows(slot_row_ref[...], spread_ref.shape[0])
    spread_ref[...] = dot(placing, cotangent_ref[...]).astype(bf16)
    start_all([write_spread, write_own])

    same = (piece_col == piece_row) & (piece_col > 0)
    allowed = (key_pos <= query_pos) | same

    def bias_for(head):
        row = jnp.broadcast_to(offsets[head : head + 1], (seq_len, 2 * seq_len))
        shifted = pltpu.roll(row, seq_len + 1, 1, stride=1, stride_axis=0)[:, :seq_len]
        bias_ref[head] = jnp.where(allowed, shifted, masked_out).astype(bf16)

    for head in range(heads // 2):
        bias_for(head)
    wait_all(first)
    sems = (send_sems, recv_sems)
    second = gather_second(place, column_s, full_s, split, sems)
    start_all(second)
    start_all(along_z)
    start_all(spread_copies)
    write_bias[0].start()
    full_s[y, c, :, x] = column_s[...]
    for head in range(heads // 2, heads):
        bias_for(head)
    write_bias[1].start()
    wait_all(second)
    third = gather_third(place, full_s, split, sems)
    start_all(third)

    wait_all(third)
    fourth = gather_core(place, full_s, sems)
    start_all(fourth)
    wait_all(fourth)
    unblock(grid_shape, full_s, mats_ref, router_ref)
    wait_all(along_z)
    wait_all(spread_copies)
    wait_all([write_spread, write_own, *write_bias])


def start(mats, router_rows, buckets, table_t, piece_ids, route, cotangent, grid_shape):
    layers, tall, wide = mats[0].shape
    seq_len = piece_ids.shape[0]
    heads = table_t.shape[0]
    width = tall * grid_shape[0]
    experts = grid_shape[1]
    block = (router_rows.shape[1] + tall, 4 * wide)
    half = (grid_shape[0] // 2, 2, grid_shape[1] // 2, 2)
    ins = (
        *mats,
        router_rows,
        buckets,
        table_t,
        piece_ids[None, :],
        route.reshape(1, seq_len),
        cotangent,
    )
    outs = (
        jax.ShapeDtypeStruct((4, width, width), bf16),
        jax.ShapeDtypeStruct((experts, width), bf16),
        jax.ShapeDtypeStruct((layers - 1, half[2], *block), bf16),
        jax.ShapeDtypeStruct((heads, seq_len, seq_len), bf16),
        jax.ShapeDtypeStruct((seq_len, 1), jnp.int32),
        jax.ShapeDtypeStruct((1, seq_len), jnp.int32),
        jax.ShapeDtypeStruct((seq_len, experts), f32),
        jax.ShapeDtypeStruct((2 * seq_len, width), bf16),
        jax.ShapeDtypeStruct((2 * seq_len, width), bf16),
    )
    along_z, others = gather_copies(grid_shape)
    return pl.pallas_call(
        partial(start_kernel, grid_shape),
        in_specs=[vmem_spec] * len(ins),
        out_specs=[vmem_spec] * 3 + [any_spec] + [vmem_spec] * 3 + [any_spec] * 2,
        out_shape=outs,
        scratch_shapes=[
            *scratch_of([outs[3], outs[7]]),
            pltpu.SemaphoreType.DMA((4,)),
            pltpu.VMEM((*half, *block), bf16),
            pltpu.VMEM((half[2], *block), bf16),
            pltpu.SemaphoreType.DMA((experts,)),
            pltpu.SemaphoreType.DMA((experts,)),
            pltpu.SemaphoreType.DMA((layers - 1, along_z)),
            pltpu.SemaphoreType.DMA((layers - 1, along_z)),
            pltpu.SemaphoreType.DMA((along_z,)),
            pltpu.SemaphoreType.DMA((along_z,)),
            pltpu.SemaphoreType.DMA((others,)),
            pltpu.SemaphoreType.DMA((others,)),
        ],
        compiler_params=params(0),
        cost_estimate=lasting(45),
        name="start",
    )(*ins)


def half_masks(rows, width):
    lane = lax.broadcasted_iota(jnp.int32, (rows, width), 1)
    return lane < (width // 2)


def gates_of(logits, slot_col, chosen, gates_ref):
    experts = gates_ref.shape[0]
    seq_len = slot_col.shape[0]
    capacity = 2 * seq_len // experts
    gate = jnp.sum(jax.nn.softmax(logits, axis=-1) * chosen, axis=1, keepdims=True)
    places = lax.broadcasted_iota(jnp.int32, (seq_len, 2 * seq_len), 1)
    row = jnp.sum(jnp.where(places == slot_col, gate, 0.0), axis=0, keepdims=True)
    gates_ref[...] = jnp.zeros_like(gates_ref)
    for expert in range(experts):
        mine = row[:, expert * capacity : (expert + 1) * capacity]
        gates_ref[expert, :, :capacity] = jnp.broadcast_to(mine, (gates_ref.shape[1], capacity))


def forward_kernel(
    head_dim,
    grid_shape,
    blocked,
    last,
    hidden_ref,
    gain_attn_ref,
    gain_ffn_ref,
    slot_row_ref,
    slot_col_ref,
    chosen_ref,
    *refs,
):
    refs = list(refs)
    take = refs.pop
    blocks_ref = take(0) if blocked else None
    mats_ref, router_ref = (None, None) if blocked else (take(0), take(0))
    spread_ref = take(0)
    bias_ref = take(0)
    outs = []
    if blocked:
        outs.append(take(0))
        router_ref = take(0)
    outs += [take(0) for _ in range(3)]
    att_ref, lse_ref, middle_ref, logits_ref, sent_ref = (take(0) for _ in range(5))
    gates_ref = take(0) if last else None
    far_ref, send_sems, recv_sems, write_sems, *made_here = refs
    q_ref, k_ref, v_ref = made_here[-3:]
    if blocked:
        mats_ref = made_here[0]
    writes = local_copies(list(zip(made_here, outs)), write_sems)
    pair, pairs = pl.program_id(0), pl.num_programs(0)
    seq_len = hidden_ref.shape[0]
    width = 2 * head_dim
    step = min(512, seq_len)

    members = grid_shape[1]
    spread = Exchange(members, spread_ref.shape[0] // members, spread_ref, far_ref, send_sems, recv_sems)
    aparts = in_third(members, 2 if last else 1)

    @pl.when(pair == 0)
    def _():
        greet([spread.peer(apart) for apart in aparts])
        start_all([spread.copy(apart) for apart in aparts])

    @pl.when(pair == 0)
    def _():
        if blocked:
            unblock(grid_shape, blocks_ref, mats_ref, router_ref)
        hidden = hidden_ref[...].astype(f32)
        normed = (hidden * rms_factor(hidden) * gain_attn_ref[...]).astype(bf16)
        q_ref[...] = dot(normed, mats_ref[0]).astype(bf16)
        k_ref[...] = dot(normed, mats_ref[1]).astype(bf16)
        v_ref[...] = dot(normed, mats_ref[2]).astype(bf16)
        start_all(writes)

    lanes = pl.ds(pl.multiple_of(pair * width, width), width)
    q2 = q_ref[:, lanes] * jnp.asarray(head_dim**-0.5, bf16)
    k2 = k_ref[:, lanes]
    v2t = v_ref[:, lanes].T
    first = half_masks(seq_len, width)
    for half in range(2):
        q_one = jnp.where(first if half == 0 else ~first, q2, jnp.zeros_like(q2))
        v_one = v2t[half * head_dim : (half + 1) * head_dim]
        for begin in range(0, seq_len, step):
            cols = slice(begin, begin + step)
            scores = dot(k2, q_one[cols], 1, 1) + bias_ref[half, :, cols].astype(f32)
            top = jnp.max(scores, axis=0, keepdims=True)
            raised = jnp.exp(scores - top)
            total = jnp.sum(raised, axis=0, keepdims=True)
            probs = raised.astype(bf16)
            rows = pl.ds(pl.multiple_of(pair * width + half * head_dim, head_dim), head_dim)
            att_ref[rows, cols] = (dot(v_one, probs) * (1.0 / total)).astype(bf16)
            lse_ref[0, half : half + 1, cols] = top + jnp.log(total)

    @pl.when(pair == pairs - 1)
    def _():
        middle = hidden_ref[...].astype(f32) + dot(att_ref[...].T, mats_ref[3])
        middle_ref[...] = middle
        ffn_in = (middle * rms_factor(middle) * gain_ffn_ref[...]).astype(bf16)
        logits = dot(ffn_in, router_ref[...], 1, 1)
        logits_ref[...] = logits
        if gates_ref is not None:
            gates_of(logits, slot_col_ref[...], chosen_ref[...], gates_ref)
        placing = placing_rows(slot_row_ref[...], sent_ref.shape[0])
        sent_ref[...] = dot(placing, ffn_in).astype(bf16)

    @pl.when(pair == pairs - 1)
    def _():
        wait_all([spread.copy(apart) for apart in aparts])
        wait_all(writes)


def attention_forward(
    hidden,
    gain_attn,
    gain_ffn,
    slots_and_chosen,
    bias,
    grid_shape,
    identifier,
    spread,
    last,
    blocks=None,
    mats=None,
):
    seq_len, width = hidden.shape
    heads = bias.shape[0]
    head_dim = width // heads
    slots = 2 * seq_len
    experts = grid_shape[1]
    blocked = blocks is not None
    ins = [hidden, gain_attn, gain_ffn, *slots_and_chosen] + ([blocks] if blocked else list(mats))
    in_specs = whole_of(ins)
    ins.append(spread)
    in_specs.append(any_spec)
    ins.append(bias)
    in_specs.append(pl.BlockSpec((2, seq_len, seq_len), lambda p: (p, 0, 0)))
    tall = jax.ShapeDtypeStruct((seq_len, width), bf16)
    outs = [
        tall,
        tall,
        tall,
        jax.ShapeDtypeStruct((width, seq_len), bf16),
        jax.ShapeDtypeStruct((heads // 2, 2, seq_len), f32),
        jax.ShapeDtypeStruct((seq_len, width), f32),
        jax.ShapeDtypeStruct((seq_len, experts), f32),
        jax.ShapeDtypeStruct((slots, width), bf16),
    ]
    if last:
        outs.append(jax.ShapeDtypeStruct((experts, 8, max(128, slots // experts)), f32))
    out_specs = whole_of(outs)
    out_specs[:3] = [any_spec] * 3
    written = outs[:3]
    out_specs[4] = pl.BlockSpec((1, 2, seq_len), lambda p: (p, 0, 0))
    if blocked:
        more = [
            jax.ShapeDtypeStruct((4, width, width), bf16),
            jax.ShapeDtypeStruct((experts, width), bf16),
        ]
        outs = more + outs
        out_specs = [any_spec] + whole_of(more[1:]) + out_specs
        written = more[:1] + written
    outs.append(jax.ShapeDtypeStruct(spread.shape, bf16))
    out_specs.append(any_spec)
    sems = pltpu.SemaphoreType.DMA((experts,))
    scratch = [sems, sems, pltpu.SemaphoreType.DMA((len(written),)), *scratch_of(written)]
    got = pl.pallas_call(
        partial(forward_kernel, head_dim, grid_shape, blocked, last),
        grid=(heads // 2,),
        in_specs=in_specs,
        out_specs=out_specs,
        out_shape=outs,
        scratch_shapes=scratch,
        compiler_params=params(identifier),
        cost_estimate=lasting(25),
        name="attention_forward",
    )(*ins)
    return tuple(got) if blocked else tuple(mats) + tuple(got)


def diagonal_fold(values, seq_len):
    rows, wide = seq_len, 2 * seq_len
    folded = None
    tile = 128
    count = seq_len // tile
    for row_tile in range(count):
        piece = values[row_tile * tile : (row_tile + 1) * tile].astype(f32)
        before = (count - 1 - row_tile) * tile
        after = wide - seq_len - before
        parts = []
        if before:
            parts.append(jnp.zeros((tile, before), f32))
        parts.append(piece)
        if after:
            parts.append(jnp.zeros((tile, after), f32))
        padded = jnp.concatenate(parts, axis=1)
        folded = padded if folded is None else folded + padded
    rows = tile
    while rows > 1:
        rows //= 2
        folded = pltpu.roll(folded[:rows], rows, 1) + folded[rows:]
    return folded


def reblock(grid_shape, blocks_ref, which, values):
    count_x, count_y = grid_shape
    tall = values.shape[0] // count_x
    wide = values.shape[1] // count_y
    for first in range(count_x):
        for second in range(count_y):
            spot = (first // 2, first % 2, second // 2, second % 2)
            lanes = slice(which * wide, (which + 1) * wide)
            blocks_ref[(*spot, slice(None), lanes)] = values[
                first * tall : (first + 1) * tall, second * wide : (second + 1) * wide
            ]


def d_logits_of(d_gate, logits, chosen):
    shares = jax.nn.softmax(logits, axis=-1)
    gate = jnp.sum(shares * chosen, axis=1, keepdims=True)
    return (d_gate * shares * (chosen - gate)).astype(bf16)


def spread_into(grad_now, comb_ref, slot_row_ref, chosen_ref, logits_ref, d_sent_ref, d_logits_ref):
    d_gate = jnp.sum(grad_now * comb_ref[...], axis=1, keepdims=True)
    logits, chosen = logits_ref[...], chosen_ref[...]
    d_logits_ref[...] = d_logits_of(d_gate, logits, chosen)
    gate = jnp.sum(jax.nn.softmax(logits, axis=-1) * chosen, axis=1, keepdims=True)
    placing = placing_rows(slot_row_ref[...], d_sent_ref.shape[0])
    d_sent_ref[...] = dot(placing, (gate * grad_now).astype(bf16)).astype(bf16)


def backward_kernel(
    head_dim,
    grid_shape,
    spreads,
    returns,
    pushes,
    unread,
    d_back_ref,
    slot_col_ref,
    d_logits_ref,
    grad_ref,
    middle_ref,
    gain_attn_ref,
    gain_ffn_ref,
    router_ref,
    att_ref,
    *refs,
):
    refs = list(refs)
    take = refs.pop
    spread_in = [take(0) for _ in range(4)] if spreads else []
    bias_ref, lse_ref = take(0), take(0)
    made_ref = take(0)
    push_refs = (take(0), take(0)) if pushes else ()
    later = [take(0) for _ in range(5)]
    del refs[:unread]
    grad_new_ref, blocks_ref, gwr_ref, gga_ref, ggf_ref, offsets_ref = (take(0) for _ in range(6))
    spread_out = [take(0) for _ in range(2)] if spreads else []
    returned_ref = take(0)
    landing_refs = (take(0), take(0)) if pushes else ()
    d_att_s, d_middle_s, dqt_s, dk_s, dv_s, probs_s, scores_s = (take(0) for _ in range(7))
    loaded = [take(0) for _ in range(5)]
    load_sems = take(0)
    mats_ref, q_ref, k_ref, v_ref, hidden_ref = loaded
    mats_later = later[0]
    load_output = local_copies([(mats_later.at[3], mats_ref.at[3])], load_sems)
    load_heads = local_copies(list(zip(later[1:4], loaded[1:4])), load_sems, 1)
    first_three = pl.ds(0, 3)
    load_rest = local_copies(
        [(mats_later.at[first_three], mats_ref.at[first_three]), (later[4], hidden_ref)], load_sems, 4
    )
    own_sem, *sems = refs[:3]
    members = grid_shape[1]
    place = Place(grid_shape)
    pushed = []
    for src, landing, last_rows in zip(push_refs, landing_refs, (True, False)):
        begin = src.shape[1] - landing.shape[1] if last_rows else 0
        pushed += push_blocks(place, src, landing, refs[3:], begin, len(pushed))
    back = Exchange(members, made_ref.shape[0] // members, made_ref, returned_ref, *sems)
    mine = back.block(back.me)
    own = None
    if returns:
        own = pltpu.make_async_copy(made_ref.at[mine, :], returned_ref.at[mine, :], own_sem)
    aparts = part_of(members, returns)

    @pl.when(pl.program_id(0) == 0)
    def _():
        start_all(load_output + load_heads + load_rest)
        greet([back.peer(apart) for apart in aparts] + (place.y_peers() if pushes else []))
        start_all(pushed + [back.copy(apart) for apart in aparts])
        if returns:
            own.start()

    pair, pairs = pl.program_id(0), pl.num_programs(0)
    seq_len = att_ref.shape[1]
    width = 2 * head_dim
    step = min(512, seq_len)
    scale = head_dim**-0.5

    @pl.when(pair == 0)
    def _():
        placing = placing_cols(slot_col_ref[...], d_back_ref.shape[0])
        d_logits = d_logits_ref[...]
        d_ffn = dot(placing, d_back_ref[...]) + dot(d_logits, router_ref[...])
        middle = middle_ref[...]
        gain_row = gain_ffn_ref[...]
        ffn_in = (middle * rms_factor(middle) * gain_row).astype(bf16)
        gwr_ref[...] = dot(d_logits, ffn_in, 0, 0)
        d_middle, d_gain = rms_pull(middle, gain_row, d_ffn)
        ggf_ref[...] = d_gain
        d_middle = d_middle + grad_ref[...].astype(f32)
        d_middle_s[...] = d_middle
        d_low = d_middle.astype(bf16)
        wait_all(load_output)
        reblock(grid_shape, blocks_ref, 3, dot(att_ref[...], d_low).astype(bf16))
        d_att_s[...] = dot(d_low, mats_ref[3], 1, 1).astype(bf16)
        wait_all(load_heads)

    lanes = pl.ds(pl.multiple_of(pair * width, width), width)
    q2 = q_ref[:, lanes] * jnp.asarray(scale, bf16)
    k2 = k_ref[:, lanes]
    v2 = v_ref[:, lanes]
    da2 = d_att_s[:, lanes]
    k2t = k2.T
    first = half_masks(seq_len, width)
    d_key = jnp.zeros((seq_len, width), f32)
    d_value = jnp.zeros((seq_len, width), f32)
    for half in range(2):
        mask = first if half == 0 else ~first
        q_one = jnp.where(mask, q2, jnp.zeros_like(q2))
        da_one = jnp.where(mask, da2, jnp.zeros_like(da2))
        k_one = k2t[half * head_dim : (half + 1) * head_dim]
        rows = pl.ds(pl.multiple_of(pair * width + half * head_dim, head_dim), head_dim)
        for start in range(0, seq_len, step):
            cols = slice(start, start + step)
            scores = dot(k2, q_one[cols], 1, 1) + bias_ref[half, :, cols].astype(f32)
            probs = jnp.exp(scores - lse_ref[0, half : half + 1, cols])
            d_probs = dot(v2, da_one[cols], 1, 1)
            inner = jnp.sum(probs * d_probs, axis=0, keepdims=True)
            d_scores = (probs * (d_probs - inner)).astype(bf16)
            probs_s[:, cols] = probs.astype(bf16)
            scores_s[:, cols] = d_scores
            dqt_s[rows, cols] = (dot(k_one, d_scores) * scale).astype(bf16)
        d_key = d_key + dot(scores_s[...], q_one)
        d_value = d_value + dot(probs_s[...], da_one)
        offsets_ref[pl.ds(2 * pair + half, 1), :] = diagonal_fold(scores_s[...], seq_len)
    dk_s[:, lanes] = d_key.astype(bf16)
    dv_s[:, lanes] = d_value.astype(bf16)

    @pl.when(pair == pairs - 1)
    def _():
        wait_all(load_rest)
        hidden = hidden_ref[...].astype(f32)
        gain_row = gain_attn_ref[...]
        normed_t = (hidden * rms_factor(hidden) * gain_row).astype(bf16).T
        d_query = dqt_s[...].T
        d_normed = dot(d_query, mats_ref[0], 1, 1)
        reblock(grid_shape, blocks_ref, 0, dot(normed_t, d_query).astype(bf16))
        d_normed = d_normed + dot(dk_s[...], mats_ref[1], 1, 1)
        reblock(grid_shape, blocks_ref, 1, dot(normed_t, dk_s[...]).astype(bf16))
        d_normed = d_normed + dot(dv_s[...], mats_ref[2], 1, 1)
        reblock(grid_shape, blocks_ref, 2, dot(normed_t, dv_s[...]).astype(bf16))
        d_hidden, d_gain = rms_pull(hidden, gain_row, d_normed)
        gga_ref[...] = d_gain
        grad_new = d_hidden + d_middle_s[...]
        grad_new_ref[...] = grad_new
        if spreads:
            spread_into(grad_new, *spread_in, *spread_out)

    @pl.when(pair == pairs - 1)
    def _():
        wait_all(pushed + [back.copy(apart) for apart in aparts])
        if returns:
            own.wait()


def attention_backward(
    d_back,
    slot_col,
    d_logits,
    grad_now,
    middle,
    hidden,
    gains,
    mats,
    q_k_v,
    attended,
    bias,
    lse,
    grid_shape,
    below=None,
    after=(),
    made=None,
    returns=False,
    push=None,
    identifier=None,
):
    seq_len, width = hidden.shape
    heads = bias.shape[0]
    head_dim = width // heads
    experts = mats[1].shape[0]
    count_x, count_y = grid_shape
    ins = (
        d_back,
        slot_col,
        d_logits,
        grad_now,
        middle,
        *gains,
        mats[1],
        attended,
    )
    later = [mats[0], *q_k_v, hidden]
    spreads = below is not None
    if spreads:
        ins = ins + tuple(below)
    row = jax.ShapeDtypeStruct((1, width), f32)
    outs = (
        jax.ShapeDtypeStruct((seq_len, width), f32),
        jax.ShapeDtypeStruct(
            (count_x // 2, 2, count_y // 2, 2, width // count_x, 4 * (width // count_y)), bf16
        ),
        jax.ShapeDtypeStruct((experts, width), f32),
        row,
        row,
        jax.ShapeDtypeStruct((heads, 2 * seq_len), f32),
    )
    if spreads:
        outs = outs + (
            jax.ShapeDtypeStruct((2 * seq_len, width), bf16),
            jax.ShapeDtypeStruct(d_logits.shape, bf16),
        )
    outs = outs + (jax.ShapeDtypeStruct(made.shape, bf16),)
    pushes = push is not None
    out_specs = whole_of(outs)
    out_specs[-1] = any_spec
    if pushes:
        rows = [push[0].shape[1] - cut_of(push[0]), push[1].shape[1] // 2]
        outs = outs + tuple(landing_of(one, many) for one, many in zip(push, rows))
        out_specs += [any_spec] * 2
    return pl.pallas_call(
        partial(backward_kernel, head_dim, grid_shape, spreads, returns, pushes, len(after)),
        grid=(heads // 2,),
        in_specs=whole_of(ins)
        + [
            pl.BlockSpec((2, seq_len, seq_len), lambda p: (p, 0, 0)),
            pl.BlockSpec((1, 2, seq_len), lambda p: (p, 0, 0)),
        ]
        + [any_spec] * (len(after) + 6 + 2 * pushes),
        out_specs=out_specs,
        out_shape=outs,
        scratch_shapes=[
            pltpu.VMEM((seq_len, width), bf16),
            pltpu.VMEM((seq_len, width), f32),
            pltpu.VMEM((width, seq_len), bf16),
            pltpu.VMEM((seq_len, width), bf16),
            pltpu.VMEM((seq_len, width), bf16),
            pltpu.VMEM((seq_len, seq_len), bf16),
            pltpu.VMEM((seq_len, seq_len), bf16),
        ]
        + scratch_of(later)
        + [pltpu.SemaphoreType.DMA((6,)), pltpu.SemaphoreType.DMA]
        + [pltpu.SemaphoreType.DMA((count_y,))] * 2
        + [pltpu.SemaphoreType.DMA((2 * (count_x // 2 - 1),))] * (2 * pushes),
        compiler_params=params(identifier),
        cost_estimate=lasting(32),
        name="attention_backward",
    )(*ins, bias, lse, made, *(push if pushes else ()), *later, *after)


class Exchange:
    def __init__(self, members, rows, src, dst, send_sems, recv_sems):
        self.me = lax.axis_index("gy")
        self.bits = members.bit_length() - 1
        self.rows, self.src, self.dst = rows, src, dst
        self.send_sems, self.recv_sems = send_sems, recv_sems

    def block(self, index):
        return pl.ds(pl.multiple_of(index * self.rows, self.rows), self.rows)

    def peer(self, apart):
        return {"gy": xor_of(self.me, apart, self.bits)}

    def copy(self, apart):
        peer = xor_of(self.me, apart, self.bits)
        return pltpu.make_async_remote_copy(
            src_ref=self.src.at[self.block(peer), :],
            dst_ref=self.dst.at[self.block(self.me), :],
            send_sem=self.send_sems.at[apart],
            recv_sem=self.recv_sems.at[apart],
            device_id={"gy": peer},
            device_id_type=MESH,
        )

    def keep_own(self):
        self.dst[self.block(self.me), :] = self.src[self.block(self.me), :]


class Leading(Exchange):
    def __init__(self, members, src, dst, send_sems, recv_sems):
        super().__init__(members, 1, src, dst, send_sems, recv_sems)

    def copy(self, apart):
        peer = xor_of(self.me, apart, self.bits)
        sems = (self.send_sems, self.recv_sems)
        return send(self.src.at[peer], self.dst.at[self.me], sems, apart, {"gy": peer})

    def keep_own(self):
        self.dst[self.me] = self.src[self.me]


def peers_along_gy(members):
    me = lax.axis_index("gy")
    bits = members.bit_length() - 1
    return [{"gy": xor_of(me, apart, bits)} for apart in range(1, members)]


def gelu_and_slope(pre):
    inner_scale = 0.7978845608028654
    square = pre * pre
    bent = jnp.tanh(inner_scale * pre * (1.0 + 0.044715 * square))
    act = 0.5 * pre * (1.0 + bent)
    slope = 0.5 * (1.0 + bent) + 0.5 * pre * (1.0 - bent * bent) * (
        inner_scale * (1.0 + 3 * 0.044715 * square)
    )
    return act, slope


def gelu_only(pre):
    inner_scale = 0.7978845608028654
    return 0.5 * pre * (1.0 + jnp.tanh(inner_scale * pre * (1.0 + 0.044715 * pre * pre)))


def send_order(members):
    return range(1, members)


def early(members):
    quarter = max(1, members // 4)
    return [apart for apart in range(members) if (apart // quarter) % 2 == 0]


def part_of(members, first):
    chosen = early(members)
    return [a for a in range(1, members) if (a in chosen) == first]


def third_of(members, apart):
    quarter = max(1, members // 4)
    if (apart // quarter) % 2 == 0:
        return 0
    return 1 + (2 * (apart % quarter)) // quarter


def in_third(members, third):
    return [apart for apart in range(1, members) if third_of(members, apart) == third]


def collect(me, members, rows, refs, which_of, dst, sems):
    copies = []
    for apart in range(members):
        start = xor_of(me, apart, bits_of(members)) * rows
        here = pl.ds(pl.multiple_of(start, rows), rows)
        ref = refs[which_of(apart)]
        copies.append(pltpu.make_async_copy(ref.at[here, :], dst.at[here, :], sems.at[apart]))
    return copies


class Weights:
    def __init__(self, place, halves, whole_refs, local_sems, sems):
        blocks, _, units = halves[0].shape
        self.local, self.remote = [], []
        for which, (part, into) in enumerate(zip(halves, whole_refs)):
            for block in range(blocks):
                index = which * blocks + block
                begin = pl.multiple_of((place.c * blocks + block) * units, units)
                dst = into.at[:, pl.ds(begin, units)]
                src = part.at[block]
                self.local.append(pltpu.make_async_copy(src, dst, local_sems.at[index]))
                self.remote.append(send(src, dst, sems, index, place.core_peer()))
        self.blocks = blocks

    def start_local(self):
        start_all(self.local)

    def start_remote(self):
        start_all(self.remote)

    def wait(self, which):
        mine = slice(which * self.blocks, (which + 1) * self.blocks)
        for copy in self.local[mine] + self.remote[mine]:
            copy.wait()


def weight_gradients(place, products, sends, landings, outs, sems, after):
    blocks, _, units = outs[0].shape

    def product(lhs, rhs_ref, which, into_ref):
        @pl.loop(0, blocks)
        def _(block):
            begin = pl.multiple_of((which * blocks + block) * units, units)
            into_ref[block] = dot(lhs, rhs_ref[:, pl.ds(begin, units)]).astype(bf16)

    for index, (lhs_ref, rhs_ref) in enumerate(products):
        lhs = lhs_ref[...].T
        product(lhs, rhs_ref, 1 - place.c, sends[index])
        copy = send(sends[index], landings[index], sems, index, place.core_peer())
        copy.start()
        product(lhs, rhs_ref, place.c, outs[index])
        copy.wait()

        @pl.loop(0, blocks)
        def _(block, index=index):
            add_low(outs[index], (block,), outs[index][block], landings[index][block])

        start_all(after[index])


def push_blocks(place, src, landing, sems, begin, base=0):
    rows = pl.ds(begin, landing.shape[1])
    return [
        send(
            src.at[place.y_at(apart), rows],
            landing.at[apart - 1],
            sems,
            base + apart - 1,
            place.y_peer(apart),
        )
        for apart in range(1, place.count_y)
    ]


def cut_of(blocks):
    return blocks.shape[1] // 3 * 2


def landing_of(blocks, rows):
    return jax.ShapeDtypeStruct((blocks.shape[0] - 1, rows, blocks.shape[2]), bf16)


def chunk_of(members, rows):
    return max(1, min(members, 256 // rows))


def expert_forward_kernel(
    grid_shape,
    gathers,
    sent_ref,
    slot_col_ref,
    chosen_ref,
    logits_ref,
    middle_in_ref,
    win_ref,
    wout_ref,
    *refs,
):
    refs = list(refs)
    take = refs.pop
    column_ref = take(0) if gathers else None
    arrived_out_ref, comb_ref, out_ref = (take(0) for _ in range(3))
    full_ref = take(0) if gathers else None
    arrived_ref, middle_ref, move_sems = (take(0) for _ in range(3))
    load_middle, write_arrived = local_copies(
        [(middle_in_ref, middle_ref), (arrived_ref, arrived_out_ref)], move_sems
    )
    win_s, wout_s, made_s, returned_s, w_sems = (take(0) for _ in range(5))
    send_sems, recv_sems, back_send_sems, back_recv_sems = (take(0) for _ in range(4))
    weight_sems = (take(0), take(0))
    members = grid_shape[1]
    slots = sent_ref.shape[0]
    rows = slots // members
    group = chunk_of(members, rows)
    chunks = members // group
    chunk_bits = chunks.bit_length() - 1
    hidden_units = win_s.shape[1]
    tile = min(768, hidden_units)
    place = Place(grid_shape)
    weights = Weights(place, (win_ref, wout_ref), (win_s, wout_s), w_sems, weight_sems)
    weights.start_local()
    load_middle.start()
    more_peers = place.y_peers() if gathers else []
    greet(peers_along_gy(members) + [place.core_peer()] + more_peers)
    weights.start_remote()
    there = Exchange(members, rows, sent_ref, arrived_ref, send_sems, recv_sems)
    back = Exchange(members, rows, made_s, returned_s, back_send_sems, back_recv_sems)
    for apart in send_order(members):
        there.copy(apart).start()
    there.keep_own()
    if gathers:
        own_sem, *sems = refs
        split = (full_ref.shape[4] - tile_rows) // 2
        own = pltpu.make_async_copy(
            column_ref, full_ref.at[place.y, place.c, :, place.x], own_sem
        )
        own.start()
        second = gather_second(place, column_ref, full_ref, split, sems)
        third = gather_third(place, full_ref, split, sems)
        fourth = gather_core(place, full_ref, sems)
        start_all(second)
    weights.wait(0)
    weights.wait(1)
    my_chunk = there.me // group

    def chunk_rows(index):
        start = xor_of(my_chunk, index, chunk_bits) * (group * rows)
        return pl.ds(pl.multiple_of(start, group * rows), group * rows)

    def work(index, first):
        for member in range(first, group):
            there.copy(index * group + member).wait_recv()
        here = chunk_rows(index)
        taken = arrived_ref[here, :]
        total = jnp.zeros((group * rows, taken.shape[1]), f32)
        for start in range(0, hidden_units, tile):
            units = slice(start, start + tile)
            act = gelu_only(dot(taken, win_s[:, units])).astype(bf16)
            total = total + dot(act, wout_s[:, units], 1, 1)
        made_s[here, :] = total.astype(bf16)
        for member in range(first, group):
            back.copy(index * group + member).start()

    work(0, 1)
    back.keep_own()
    half = chunks // 2

    @pl.loop(1, half)
    def _(index):
        work(index, 0)

    if gathers:
        own.wait()
        wait_all(second)
        start_all(third)

    @pl.loop(half, chunks)
    def _(index):
        work(index, 0)

    if gathers:
        wait_all(third)
        start_all(fourth)
    write_arrived.start()
    slot_col = slot_col_ref[...]
    comb_ref[...] = jnp.zeros_like(comb_ref)

    def gather_back(index, first):
        for member in range(first, group):
            back.copy(index * group + member).wait_recv()
        begin = xor_of(my_chunk, index, chunk_bits) * (group * rows)
        places = lax.broadcasted_iota(jnp.int32, (slot_col.shape[0], group * rows), 1) + begin
        placing = (places == slot_col).astype(f32).astype(bf16)
        comb_ref[...] += dot(placing, returned_s[chunk_rows(index), :])

    gather_back(0, 1)

    @pl.loop(1, chunks)
    def _(index):
        gather_back(index, 0)

    load_middle.wait()
    gate = jnp.sum(jax.nn.softmax(logits_ref[...], axis=-1) * chosen_ref[...], axis=1, keepdims=True)
    out_ref[...] = middle_ref[...] + gate * comb_ref[...]
    if gathers:
        wait_all(fourth)

    @pl.loop(1, members)
    def _(apart):
        there.copy(apart).wait_send()
        back.copy(apart).wait_send()

    write_arrived.wait()


def doubled(half):
    return pltpu.VMEM((half.shape[1], 2 * half.shape[0] * half.shape[2]), bf16)


def expert_forward(
    sent, slot_col, chosen_f, logits, middle, full_in, full_out, grid_shape, identifier, column=None
):
    members = grid_shape[1]
    gathers = column is not None
    ins = [sent, slot_col, chosen_f, logits, middle, full_in, full_out]
    in_specs = [vmem_spec] * 4 + [any_spec] * 3
    outs = [
        jax.ShapeDtypeStruct(sent.shape, bf16),
        jax.ShapeDtypeStruct(middle.shape, f32),
        jax.ShapeDtypeStruct(middle.shape, f32),
    ]
    out_specs = [any_spec] + [vmem_spec] * 2
    sems = pltpu.SemaphoreType.DMA((members,))
    scratch = [
        *scratch_of([sent, middle]),
        pltpu.SemaphoreType.DMA((2,)),
        doubled(full_in),
        doubled(full_out),
        pltpu.VMEM(sent.shape, bf16),
        pltpu.VMEM(sent.shape, bf16),
        pltpu.SemaphoreType.DMA((2 * full_in.shape[0],)),
        sems,
        sems,
        sems,
        sems,
        pltpu.SemaphoreType.DMA((2 * full_in.shape[0],)),
        pltpu.SemaphoreType.DMA((2 * full_in.shape[0],)),
    ]
    if gathers:
        ins.append(column)
        in_specs.append(any_spec)
        half = (grid_shape[0] // 2, 2, grid_shape[1] // 2, 2)
        outs.append(jax.ShapeDtypeStruct((*half, *column.shape[1:]), bf16))
        out_specs.append(any_spec)
        others = pltpu.SemaphoreType.DMA((gather_copies(grid_shape)[1],))
        scratch += [pltpu.SemaphoreType.DMA, others, others]
    return pl.pallas_call(
        partial(expert_forward_kernel, grid_shape, gathers),
        in_specs=in_specs,
        out_specs=out_specs,
        out_shape=outs,
        scratch_shapes=scratch,
        compiler_params=params(identifier),
        cost_estimate=lasting(75),
        name="expert_forward",
    )(*ins)


def expert_both_kernel(
    grid_shape,
    sent_ref,
    gates_ref,
    slot_col_ref,
    chosen_ref,
    logits_ref,
    far_first_ref,
    far_second_ref,
    far_third_ref,
    win_ref,
    wout_ref,
    made_out_ref,
    d_back_ref,
    gin_out_ref,
    gout_out_ref,
    d_logits_ref,
    arrived_s,
    gates_s,
    win_s,
    wout_s,
    d_made_s,
    d_rows_s,
    act_s,
    d_pre_s,
    d_gates_s,
    d_gates_back_s,
    grads_ref,
    gin_send,
    gin_land,
    gout_send,
    gout_land,
    made_ref,
    gin_ref,
    gout_ref,
    write_sems,
    w_sems,
    *sems,
):
    far_refs = (far_first_ref, far_second_ref, far_third_ref)
    members = grid_shape[1]
    weight_sems, sum_sems = sems[9:11], sems[11:13]
    slots = sent_ref.shape[0]
    rows = slots // members
    group = chunk_of(members, rows)
    chunks = members // group
    chunk_bits = bits_of(chunks)
    hidden_units = win_s.shape[1]
    tile = min(256, hidden_units)
    place = Place(grid_shape)
    weights = Weights(place, (win_ref, wout_ref), (win_s, wout_s), w_sems, weight_sems)
    weights.start_local()
    greet(peers_along_gy(members) + [place.core_peer()])
    weights.start_remote()
    there = Exchange(members, rows, sent_ref, arrived_s, *sems[0:2])
    back = Exchange(members, rows, d_rows_s, d_back_ref, *sems[2:4])
    gates_there = Leading(members, gates_ref, gates_s, *sems[4:6])
    gates_back = Leading(members, d_gates_s, d_gates_back_s, *sems[6:8])

    for apart in send_order(members):
        gates_there.copy(apart).start()
        there.copy(apart).start()

    collected = collect(
        there.me, members, rows, far_refs, partial(third_of, members), grads_ref, sems[8]
    )
    start_all(collected)
    there.keep_own()
    gates_there.keep_own()
    weights.wait(0)
    weights.wait(1)
    wait_all(collected)
    my_chunk = there.me // group

    def work(index, first):
        for member in range(first, group):
            gates_there.copy(index * group + member).wait_recv()
            there.copy(index * group + member).wait_recv()
        chunk = xor_of(my_chunk, index, chunk_bits)
        here = pl.ds(pl.multiple_of(chunk * (group * rows), group * rows), group * rows)
        gate = jnp.concatenate(
            [gates_s[chunk * group + member].T[:rows, 0:1] for member in range(group)], axis=0
        )
        taken = arrived_s[here, :]
        grads = grads_ref[here, :].astype(f32)
        d_made = (gate * grads).astype(bf16)
        d_made_s[here, :] = d_made
        made = jnp.zeros((group * rows, taken.shape[1]), f32)
        d_rows = made
        for start in range(0, hidden_units, tile):
            units = slice(start, start + tile)
            act, slope = gelu_and_slope(dot(taken, win_s[:, units]))
            act = act.astype(bf16)
            act_s[here, units] = act
            d_pre = (dot(d_made, wout_s[:, units]) * slope).astype(bf16)
            d_pre_s[here, units] = d_pre
            d_rows = d_rows + dot(d_pre, win_s[:, units], 1, 1)
            made = made + dot(act, wout_s[:, units], 1, 1)
        d_rows_s[here, :] = d_rows.astype(bf16)
        made = made.astype(bf16)
        made_ref[here, :] = made
        d_gate = jnp.sum(grads * made.astype(f32), axis=1, keepdims=True)
        for member in range(group):
            part = jnp.broadcast_to(d_gate[member * rows : (member + 1) * rows], (rows, 128)).T
            d_gates_s[chunk * group + member, :, :rows] = part[: d_gates_s.shape[1]]
        for member in range(first, group):
            gates_back.copy(index * group + member).start()
            back.copy(index * group + member).start()

    work(0, 1)
    back.keep_own()
    gates_back.keep_own()

    @pl.loop(1, chunks)
    def _(index):
        work(index, 0)

    write_made, write_out, write_in = local_copies(
        [(made_ref, made_out_ref), (gout_ref, gout_out_ref), (gin_ref, gin_out_ref)], write_sems
    )
    write_made.start()
    weight_gradients(
        place,
        ((d_made_s, act_s), (arrived_s, d_pre_s)),
        (gout_send, gin_send),
        (gout_land, gin_land),
        (gout_ref, gin_ref),
        sum_sems,
        ([write_out], [write_in]),
    )

    @pl.loop(1, members)
    def _(apart):
        gates_back.copy(apart).wait_recv()

    row = jnp.concatenate(
        [d_gates_back_s[expert, 0:1, :rows] for expert in range(members)], axis=1
    )
    slot_col = slot_col_ref[...]
    places = lax.broadcasted_iota(jnp.int32, (slot_col.shape[0], slots), 1)
    d_gate = jnp.sum(jnp.where(places == slot_col, row, 0.0), axis=1, keepdims=True)
    d_logits_ref[...] = d_logits_of(d_gate, logits_ref[...], chosen_ref[...])

    @pl.loop(1, members)
    def _(apart):
        back.copy(apart).wait_recv()
        there.copy(apart).wait_send()
        back.copy(apart).wait_send()
        gates_there.copy(apart).wait_send()
        gates_back.copy(apart).wait_send()

    wait_all([write_made, write_out, write_in])


def expert_both(sent, gates, far_parts, slot_col, chosen_f, logits, full_in, full_out, grid_shape, identifier):
    members = grid_shape[1]
    slots = sent.shape[0]
    outs = (
        jax.ShapeDtypeStruct(sent.shape, bf16),
        jax.ShapeDtypeStruct(sent.shape, bf16),
        jax.ShapeDtypeStruct(full_in.shape, bf16),
        jax.ShapeDtypeStruct(full_out.shape, bf16),
        jax.ShapeDtypeStruct(logits.shape, bf16),
    )
    tall = pltpu.VMEM(sent.shape, bf16)
    wide = pltpu.VMEM((slots, 2 * full_in.shape[0] * full_in.shape[2]), bf16)
    half = pltpu.VMEM(full_in.shape, bf16)
    small = pltpu.VMEM(gates.shape, f32)
    weights = doubled(full_in)
    return pl.pallas_call(
        partial(expert_both_kernel, grid_shape),
        in_specs=[vmem_spec] * 5 + [any_spec] * 5,
        out_specs=[any_spec, vmem_spec, any_spec, any_spec, vmem_spec],
        out_shape=outs,
        scratch_shapes=[
            tall,
            small,
            weights,
            weights,
            tall,
            tall,
            wide,
            wide,
            small,
            small,
            tall,
            half,
            half,
            half,
            half,
            tall,
            half,
            half,
            pltpu.SemaphoreType.DMA((3,)),
            pltpu.SemaphoreType.DMA((2 * full_in.shape[0],)),
        ]
        + [pltpu.SemaphoreType.DMA((members,))] * 9
        + [pltpu.SemaphoreType.DMA((2 * full_in.shape[0],))] * 4,
        compiler_params=params(identifier),
        cost_estimate=lasting(85),
        name="expert_both",
    )(sent, gates, slot_col, chosen_f, logits, *far_parts, full_in, full_out)


def expert_backward_kernel(
    grid_shape,
    d_sent_ref,
    arrived_in_ref,
    blocks_in_ref,
    win_ref,
    wout_ref,
    d_back_ref,
    gin_out_ref,
    gout_out_ref,
    upper_ref,
    lower_ref,
    landing_ref,
    win_s,
    wout_s,
    d_arrived_s,
    d_rows_s,
    act_s,
    slope_s,
    first_s,
    up2_s,
    low2_s,
    gin_send,
    gin_land,
    gout_send,
    gout_land,
    arrived_ref,
    blocks_ref,
    gin_ref,
    gout_ref,
    move_sems,
    w_sems,
    send_sems,
    recv_sems,
    back_send_sems,
    back_recv_sems,
    *more_sems,
):
    members = grid_shape[1]
    sum_sems, weight_sems, gradient_sems = more_sems[0:2], more_sems[2:4], more_sems[4:6]
    push_sems = more_sems[6:8]
    slots = d_sent_ref.shape[0]
    rows = slots // members
    group = chunk_of(members, rows)
    chunks = members // group
    chunk_bits = chunks.bit_length() - 1
    hidden_units = win_s.shape[1]
    tile = min(768, hidden_units)
    place = Place(grid_shape)
    weights = Weights(place, (win_ref, wout_ref), (win_s, wout_s), w_sems, weight_sems)
    weights.start_local()
    moves = local_copies(
        [
            (arrived_in_ref, arrived_ref),
            (blocks_in_ref.at[:, place.c], blocks_ref.at[:, place.c]),
            (gout_ref, gout_out_ref),
            (gin_ref, gin_out_ref),
        ],
        move_sems,
    )
    start_all(moves[:2])
    greet(peers_along_gy(members) + [place.core_peer()] + place.y_peers())
    weights.start_remote()
    landings = (first_s, up2_s, low2_s, upper_ref, lower_ref, None, None)
    sums = Scatter(place, blocks_ref, landings, sum_sems, upper_ref.shape[1], blocks_in_ref)
    there = Exchange(members, rows, d_sent_ref, d_arrived_s, send_sems, recv_sems)
    back = Exchange(members, rows, d_rows_s, d_back_ref, back_send_sems, back_recv_sems)
    for apart in send_order(members):
        there.copy(apart).start()
    there.keep_own()
    my_chunk = there.me // group
    start_all(sums.copies(0))
    wait_all(moves[:2])
    weights.wait(0)

    @pl.loop(0, slots // 256)
    def _(index):
        here = pl.ds(pl.multiple_of(index * 256, 256), 256)
        taken = arrived_ref[here, :]
        for start in range(0, hidden_units, tile):
            units = slice(start, start + tile)
            act, slope = gelu_and_slope(dot(taken, win_s[:, units]))
            act_s[here, units] = act.astype(bf16)
            slope_s[here, units] = slope.astype(bf16)

    wait_all(sums.copies(0))
    sums.add(0)
    start_all(sums.copies(1))
    weights.wait(1)

    def chunk_rows(index):
        start = xor_of(my_chunk, index, chunk_bits) * (group * rows)
        return pl.ds(pl.multiple_of(start, group * rows), group * rows)

    def work(index, first):
        for member in range(first, group):
            there.copy(index * group + member).wait_recv()
        here = chunk_rows(index)
        taken = d_arrived_s[here, :]
        total = jnp.zeros((group * rows, taken.shape[1]), f32)
        for start in range(0, hidden_units, tile):
            units = slice(start, start + tile)
            d_pre = (dot(taken, wout_s[:, units]) * slope_s[here, units].astype(f32)).astype(bf16)
            slope_s[here, units] = d_pre
            total = total + dot(d_pre, win_s[:, units], 1, 1)
        d_rows_s[here, :] = total.astype(bf16)
        for member in range(first, group):
            back.copy(index * group + member).start()

    work(0, 1)
    back.keep_own()

    @pl.loop(1, chunks)
    def _(index):
        work(index, 0)

    wait_all(sums.copies(1))
    sums.add(1)
    start_all(sums.copies(2))
    pushed = push_blocks(place, gout_ref, landing_ref, push_sems, 0)
    weight_gradients(
        place,
        ((d_arrived_s, act_s), (arrived_ref, slope_s)),
        (gout_send, gin_send),
        (gout_land, gin_land),
        (gout_ref, gin_ref),
        gradient_sems,
        ([*pushed, moves[2]], [moves[3]]),
    )
    wait_all(sums.copies(2))
    sums.add(2)

    @pl.loop(1, members)
    def _(apart):
        back.copy(apart).wait_recv()
        there.copy(apart).wait_send()
        back.copy(apart).wait_send()

    wait_all(pushed + moves[2:])


def expert_backward(d_sent, arrived, blocks, full_in, full_out, grid_shape, identifier):
    members = grid_shape[1]
    landings = whole_blocks(blocks.shape, blocks.shape[4] // 2)
    outs = (
        jax.ShapeDtypeStruct(d_sent.shape, bf16),
        jax.ShapeDtypeStruct(full_in.shape, bf16),
        jax.ShapeDtypeStruct(full_out.shape, bf16),
        *[jax.ShapeDtypeStruct(one, bf16) for one in landings[3:5]],
        landing_of(full_out, cut_of(full_out)),
    )
    slots = d_sent.shape[0]
    sems = pltpu.SemaphoreType.DMA((members,))
    return pl.pallas_call(
        partial(expert_backward_kernel, grid_shape),
        in_specs=[vmem_spec] + [any_spec] * 4,
        out_specs=[vmem_spec] + [any_spec] * 2 + [vmem_spec] * 2 + [any_spec],
        out_shape=outs,
        scratch_shapes=[
            doubled(full_in),
            doubled(full_out),
            pltpu.VMEM(d_sent.shape, bf16),
            pltpu.VMEM(d_sent.shape, bf16),
            pltpu.VMEM((slots, 2 * full_in.shape[0] * full_in.shape[2]), bf16),
            pltpu.VMEM((slots, 2 * full_in.shape[0] * full_in.shape[2]), bf16),
            *[pltpu.VMEM(one, bf16) for one in landings[:3]],
            *[pltpu.VMEM(full_in.shape, bf16)] * 4,
            *scratch_of([arrived, blocks, full_in, full_out]),
            pltpu.SemaphoreType.DMA((4,)),
            pltpu.SemaphoreType.DMA((2 * full_in.shape[0],)),
            sems,
            sems,
            sems,
            sems,
            *[pltpu.SemaphoreType.DMA((scatter_copies(grid_shape),))] * 2,
            *[pltpu.SemaphoreType.DMA((2 * full_in.shape[0],))] * 4,
            *[pltpu.SemaphoreType.DMA((full_in.shape[0] - 1,))] * 2,
        ],
        compiler_params=params(10 + identifier),
        cost_estimate=lasting(85),
        name="expert_backward",
    )(d_sent, arrived, blocks, full_in, full_out)


def emit_kernel(
    table_shape,
    at_ref,
    gin_ref,
    gin_first_ref,
    gin_second_ref,
    gin_up_ref,
    gout_ref,
    gout_first_ref,
    gout_second_ref,
    gout_up_ref,
    result_ref,
    grad_ref,
    packed_ref,
    small_ref,
    gin_out_ref,
    gout_out_ref,
    result_out_ref,
    grad_out_ref,
    wq_ref,
    wk_ref,
    wv_ref,
    wo_ref,
    router_out_ref,
    gga_ref,
    ggf_ref,
    table_ref,
):
    step = pl.program_id(0)

    def landed(ref):
        total = ref[0].astype(f32)
        for index in range(1, ref.shape[0]):
            total = total + ref[index].astype(f32)
        return total

    steps = pl.num_programs(0)
    for own, first, second, up, out, early_steps in (
        (gin_ref, gin_first_ref, gin_second_ref, gin_up_ref, gin_out_ref, steps // 2),
        (gout_ref, gout_first_ref, gout_second_ref, gout_up_ref, gout_out_ref, steps // 3 * 2),
    ):
        out[0, 0] = own[0].astype(f32) + jnp.where(step < early_steps, landed(first), landed(second))
        out[1, 0] = up[...].astype(f32)

    @pl.when(step < 4)
    def _():
        result_out_ref[...] = result_ref[...]
        grad_out_ref[...] = grad_ref[...]

    @pl.when(step == 0)
    def _():
        layers, tall, wide = wq_ref.shape
        for which, ref in enumerate((wq_ref, wk_ref, wv_ref, wo_ref)):
            ref[...] = packed_ref[:, :, which * wide : (which + 1) * wide]
        buckets_count, heads = table_shape
        width = small_ref.shape[1]
        experts = (small_ref.shape[0] - 2 * layers - heads) // layers
        base = layers * experts
        gga_ref[...] = small_ref[base : base + layers, :]
        ggf_ref[...] = small_ref[base + layers : base + 2 * layers, :]
        base = base + 2 * layers
        table_ref[...] = small_ref[base : base + heads, :buckets_count]
        for layer in range(layers):
            row = small_ref[pl.ds(layer * experts + at_ref[1], 1), :]
            row = jnp.broadcast_to(row, (8, width))
            mine = pltpu.roll(row, lax.rem(width - at_ref[0] * tall, width), 1)
            router_out_ref[layer] = mine[0:1, :tall]


def emit(at, grads_in, grads_out, result, grad_now, packed, small, table_shape):
    layers, tall, lanes = packed.shape
    gin, gin_first, gin_second, gin_up = grads_in
    gout, gout_first, gout_second, gout_up = grads_out
    _, rows, units = gin.shape
    steps = 6
    tile = rows // steps
    wide = lanes // 4
    whole_in = [packed, small]
    passed = pl.BlockSpec((result.shape[0] // 4, result.shape[1]), lambda i, at: (jnp.minimum(i, 3), 0))
    own = pl.BlockSpec((1, tile, units), lambda i, at: (at[2], i, 0))
    up = pl.BlockSpec((tile, units), lambda i, at: (i, 0))

    def land(array, index):
        return pl.BlockSpec((array.shape[0], tile, units), lambda i, at: (0, index(i), 0))

    out = pl.BlockSpec((layers, 1, tile, units), lambda i, at: (0, 0, i, 0))
    expert = jax.ShapeDtypeStruct((layers, 1, rows, units), f32)
    square = jax.ShapeDtypeStruct((layers, tall, wide), f32)
    gain = jax.ShapeDtypeStruct((layers, small.shape[1]), f32)
    rest = [square] * 4
    rest += [jax.ShapeDtypeStruct((layers, 1, tall), f32), gain, gain]
    rest.append(jax.ShapeDtypeStruct(table_shape[::-1], f32))

    def expert_specs(first_land, second_land):
        early_steps = first_land.shape[1] // tile
        return [
            own,
            land(first_land, lambda i: jnp.minimum(i, early_steps - 1)),
            land(second_land, lambda i: jnp.maximum(i - early_steps, 0)),
            up,
        ]

    return pl.pallas_call(
        partial(emit_kernel, table_shape),
        grid_spec=pltpu.PrefetchScalarGridSpec(
            num_scalar_prefetch=1,
            grid=(steps,),
            in_specs=expert_specs(gin_first, gin_second)
            + expert_specs(gout_first, gout_second)
            + [passed, passed]
            + whole_of(whole_in),
            out_specs=[out, out, passed, passed] + whole_of(rest),
        ),
        out_shape=[expert, expert] + [jax.ShapeDtypeStruct(result.shape, f32)] * 2 + rest,
        compiler_params=params(),
        cost_estimate=lasting(7),
        name="emit",
    )(at, *grads_in, *grads_out, result, grad_now, *whole_in)


def body(
    hidden_in,
    route,
    piece_ids,
    buckets,
    rel_table,
    gain_attn,
    gain_ffn,
    w_query,
    w_key,
    w_value,
    w_output,
    w_router,
    w_in,
    w_out,
    cotangent,
):
    count_x = lax.axis_size("gx")
    count_y = lax.axis_size("gy")
    seq_len, width = hidden_in.shape
    layers = w_query.shape[0]
    heads = rel_table.shape[1]
    experts = w_router.shape[2] * count_y
    capacity = 2 * seq_len // experts
    wide_router = w_router.shape[2]
    tall, wide = w_query.shape[1], w_query.shape[2]
    grid_shape = (count_x, count_y)
    same_core = [list(range(core, count_x, 2)) for core in range(2)]
    router_rows = jnp.pad(
        w_router.transpose(0, 2, 1), ((0, 0), (0, tile_rows - wide_router), (0, 4 * wide - tall))
    )
    buckets_row = jnp.pad(buckets, (0, 1), constant_values=-1)[None, :]
    mats, router, later, bias, slot_col, slot_row, chosen_f, spread, far_part = start(
        (w_query, w_key, w_value, w_output),
        router_rows,
        buckets_row,
        rel_table.T,
        piece_ids,
        route,
        cotangent,
        grid_shape,
    )
    gain_attn_f = gain_attn.astype(f32)
    gain_ffn_f = gain_ffn.astype(f32)

    hidden = hidden_in
    kept = []
    blocks = None
    far_parts = [far_part]
    for layer in range(layers):
        last = layer == layers - 1
        gains = (gain_attn_f[layer][None], gain_ffn_f[layer][None])
        mats, router, q, k, v, attended, lse, middle, logits, sent, *gates, far_part = attention_forward(
            hidden,
            gains[0],
            gains[1],
            (slot_row, slot_col, chosen_f),
            bias,
            grid_shape,
            1 + layer,
            spread,
            last,
            blocks=blocks,
            mats=(mats, router) if blocks is None else None,
        )
        far_parts.append(far_part)
        full_in, full_out = (
            lax.all_gather(one[layer, 0], "gx", axis=0, tiled=False, axis_index_groups=same_core)
            for one in (w_in, w_out)
        )
        state = (hidden, gains, (mats, router), (q, k, v), attended, lse, middle, logits)
        if last:
            made, d_back, grad_in_full, grad_out_full, d_logits = expert_both(
                sent, gates[0], far_parts, slot_col, chosen_f, logits, full_in, full_out, grid_shape, 7
            )
            kept.append(state)
        else:
            arrived, combined, hidden, blocks = expert_forward(
                sent,
                slot_col,
                chosen_f,
                logits,
                middle,
                full_in,
                full_out,
                grid_shape,
                5 + layer,
                column=later[layer],
            )
            kept.append(state + (combined, arrived, full_in, full_out))

    grad_now = cotangent
    parts = []
    partials = []
    returned = []
    for layer in reversed(range(layers)):
        last = layer == layers - 1
        (prior, gains, mats, q_k_v, attended, lse, middle, logits) = kept[layer][:8]
        if not last:
            arrived, full_in, full_out = kept[layer][9:]
            d_back, grad_in_full, grad_out_full, upper, lower, out_first = expert_backward(
                d_sent, arrived, parts[-1][0], full_in, full_out, grid_shape, layer
            )
            partials.append((upper, lower[:1]))
        experts_parts = []
        if layer > 0:
            experts_parts = [
                lax.psum_scatter(
                    one, "gx", scatter_dimension=0, tiled=False, axis_index_groups=same_core
                )
                for one in (grad_in_full, grad_out_full)
            ]
        below = None
        if layer > 0:
            below = (kept[layer - 1][8], slot_row, chosen_f, kept[layer - 1][7])
        got = attention_backward(
            d_back,
            slot_col,
            d_logits,
            grad_now,
            middle,
            prior,
            gains,
            mats,
            q_k_v,
            attended,
            bias,
            lse,
            grid_shape,
            below=below,
            after=[array for part in parts for array in part[4]],
            made=made,
            returns=last,
            push=(grad_out_full, grad_in_full) if layer == 0 else None,
            identifier=18 + layer,
        )
        grad_now, blocked, gwr, gga, ggf, offset_sums = got[:6]
        if layer > 0:
            d_sent, d_logits = got[6:8]
        if layer == 0:
            *got, out_second, in_first = got
        returned.append(got[-1])
        parts.append((blocked, gwr, gga, ggf, experts_parts, offset_sums))
    parts = parts[::-1]
    buckets_count = rel_table.shape[0]
    smalls = [part[which] for which in (1, 2, 3, 5) for part in parts]
    top = kept[-1]
    packed, small, hidden_out, in_second = final_sums(
        parts[0][0],
        partials[::-1],
        smalls + [buckets_row],
        (slot_col, chosen_f, top[7], top[6]),
        returned,
        grad_in_full,
        grid_shape,
        buckets_count,
    )
    first, second = lax.axis_index("gx"), lax.axis_index("gy")
    grad_in, grad_out, hidden_out, grad_now, gwq, gwk, gwv, gwo, gwr, gga_all, ggf_all, d_table = emit(
        jnp.stack([first, second, first // 2]).astype(jnp.int32),
        (grad_in_full, in_first, in_second, parts[1][4][0]),
        (grad_out_full, out_first, out_second, parts[1][4][1]),
        hidden_out,
        grad_now,
        packed,
        small,
        rel_table.shape,
    )
    return (
        hidden_out,
        grad_now,
        d_table.T,
        gga_all,
        ggf_all,
        gwq,
        gwk,
        gwv,
        gwo,
        gwr.transpose(0, 2, 1),
        grad_in,
        grad_out,
    )


def solution(mesh):
    rows = P(("gx", "gy"), None)
    square = P(None, "gx", "gy")
    expert = P(None, "gy", None, "gx")
    return jax.shard_map(
        body,
        mesh=mesh,
        in_specs=(rows, rows, P(("gx", "gy")), P(), P(), P(), P())
        + (square,) * 5
        + (expert, expert, rows),
        out_specs=(rows, rows, P(), P(), P()) + (square,) * 5 + (expert, expert),
        check_vma=False,
    )
```
